32 devices in a mesh: group: 2 (over x), block: 16 (over z, y, core).
Axes of the slice: x: 2, y: 2, z: 4, core: 2. Of those that a mesh axis runs over, the one named last changes fastest.
Arguments:
- populations: float32 [19, 384, 8, 128], P(None, ('group', 'block')), parts along dimension 1, as said below
- design: float32 [384, 8, 128], P(('group', 'block')), parts along dimension 0, may hold values from 0.05 to 1
- fluid_mask: int32 [384, 8, 128], P(('group', 'block')), parts along dimension 0, may hold values 0 or 1
- owner_after: int32 [96], P('group'), parts along dimension 0, may hold values from 0 to 15, as said below
Outputs:
- populations_after: float32 [19, 640, 8, 128], P(None, ('group', 'block')), parts along dimension 1
- sensitivity: float32 [640, 8, 128], P(('group', 'block')), parts along dimension 0
The draws below stay inside these ranges and needn't reach their ends.
There are 2 independent parts, one for each index of `group`. The reference program is written for one: setup_inputs(seed, part) draws one part's arguments, and reference() takes and returns one part's arrays. A program takes and returns all parts, laid end to end along the dimension named above; each array names one. Nothing has to cross between parts.
Inputs may be any that keep to these rules, and one draw needn't show every extreme that they name: `populations`: every population lies between 0.4 and 2.5 times its lattice weight. `owner_after`: the list never falls along the duct; every block goes to its home device (block index // 3) or a neighbour of it; every device owns from 1 to 5 blocks, and some device owns exactly 5; block 0 stays on device 0.
All inputs are finite; a program needn't handle non-finite values. No bound on the sum of `fluid_mask` on one device may be relied on, other than what follows from the above.
Results may differ from the reference program's by a relative error of at most 0.000021.
Values sent between devices are 32-bit elements; how exact they have to be, the bound alone decides.
No kernel may reach another device: no remote copies, remote signals or barrier semaphores. Data moves between devices by JAX's collectives and lax.ppermute only.
A program may use at most 64 MiB of HBM per device.

```python
import jax
import jax.numpy as jnp
from jax import lax

BX = 4
BY = 8
BZ = 128
BPD = 3
STEPS = 3
NX = 192
N_BLOCK = 16


weight_list = (1.0 / 3.0,) + (1.0 / 18.0,) * 6 + (1.0 / 36.0,) * 12


def draw_populations(key, part):
    key = jax.random.fold_in(key, 3)
    weights = jnp.array(weight_list, jnp.float32)[:, None, None, None]
    factor = jnp.exp(0.3 * jnp.clip(jax.random.normal(key, (19, NX, BY, BZ), jnp.float32), -3.0, 3.0))
    return weights * factor


def draw_owner_after(key, part):
    key = jax.random.fold_in(key, 7)
    key_shift, key_place = jax.random.split(key)
    device_ids = jnp.arange(N_BLOCK, dtype=jnp.int32)
    shifts = jax.random.randint(key_shift, (N_BLOCK,), -1, 2).astype(jnp.int32)
    chosen = jax.random.randint(key_place, (), 1, N_BLOCK - 1).astype(jnp.int32)
    shifts = jnp.where(device_ids == chosen, -1, shifts)
    shifts = jnp.where(device_ids == chosen + 1, 1, shifts)
    shifts = jnp.where(device_ids == 0, 0, shifts)
    run_starts = device_ids * BPD + shifts
    block_ids = jnp.arange(N_BLOCK * BPD, dtype=jnp.int32)
    return (jnp.sum((run_starts[None, :] <= block_ids[:, None]).astype(jnp.int32), axis=1) - 1).astype(jnp.int32)


def set_ends(entries, stream_key, least, largest):
    longest = entries.shape.index(max(entries.shape))
    spots = []
    for shift in (0, 1):
        where = [jax.random.randint(jax.random.fold_in(stream_key, axis), (), 0, length) for axis, length in enumerate(entries.shape)]
        where[longest] = (where[longest] + shift) % entries.shape[longest]
        spots.append(tuple(where))
    return entries.at[spots[0]].set(least).at[spots[1]].set(largest)


def block_levels(own_key, extent, cuts, low, largest):
    gain, own = 1.0, jax.random.fold_in(own_key, 6)
    for position, parts in cuts:
        steps = jnp.exp(jax.random.uniform(jax.random.fold_in(own, position), (parts,), jnp.float32, low / len(cuts), largest / len(cuts)))
        gain = gain * jnp.repeat(steps, extent[position] // parts).reshape([-1 if axis == position else 1 for axis in range(len(extent))])
    return gain


def setup_inputs(seed: int = 0, part: int = 0) -> dict:
    seeds = jax.random.split(jax.random.key(seed), 5)
    own_keys = jax.random.split(jax.random.fold_in(seeds[4], part), 5)
    populations = draw_populations(jax.random.fold_in(jax.random.fold_in(seeds[4], part), 71), part)
    design = jnp.clip(0.05 + 0.95 * jax.random.uniform(own_keys[1], (NX, BY, BZ), jnp.float32) ** block_levels(own_keys[1], (NX, BY, BZ), ((0, 16),), -0.2, 0.2), 0.05, 1.0)
    fluid_mask = set_ends((jax.random.randint(own_keys[2], (NX, BY, BZ), 0, 4) < 3).astype(jnp.int32), jax.random.fold_in(own_keys[2], 1), 0, 1)
    owner_after = draw_owner_after(jax.random.fold_in(jax.random.fold_in(seeds[4], part), 71), part)
    return dict(populations=populations, design=design, fluid_mask=fluid_mask, owner_after=owner_after)


velocity_set = ((0, 0, 0), (1, 0, 0), (-1, 0, 0), (0, 1, 0), (0, -1, 0), (0, 0, 1), (0, 0, -1), (1, 1, 0), (-1, -1, 0), (1, -1, 0), (-1, 1, 0), (1, 0, 1), (-1, 0, -1), (1, 0, -1), (-1, 0, 1), (0, 1, 1), (0, -1, -1), (0, 1, -1), (0, -1, 1))
weight_set = (1.0 / 3.0,) + (1.0 / 18.0,) * 6 + (1.0 / 36.0,) * 12
omega_rate = 1.2
alpha_top = 0.6
ramp_factor = 4.0
force_x = 0.02

def opposite(member):
    if member == 0:
        return 0
    if member % 2 == 1:
        return member + 1
    return member - 1

def porosity(design):
    return alpha_top * (1.0 - design) / (1.0 + ramp_factor * design)

def moments(state):
    density = state[0]
    momentum = [jnp.zeros_like(density), jnp.zeros_like(density), jnp.zeros_like(density)]
    for member in range(1, 19):
        density = density + state[member]
        for coord in range(3):
            step = velocity_set[member][coord]
            if step == 1:
                momentum[coord] = momentum[coord] + state[member]
            elif step == -1:
                momentum[coord] = momentum[coord] - state[member]
    return (density, momentum)

def collide(state, design, fluid):
    density, momentum = moments(state)
    damping = 1.0 + porosity(design)
    speed_x = (momentum[0] / density + force_x) / damping
    speed_y = momentum[1] / density / damping
    speed_z = momentum[2] / density / damping
    square = speed_x * speed_x + speed_y * speed_y + speed_z * speed_z
    result = []
    for member in range(19):
        step_x, step_y, step_z = velocity_set[member]
        along = step_x * speed_x + step_y * speed_y + step_z * speed_z
        balance = weight_set[member] * density * (1.0 + 3.0 * along + 4.5 * along * along - 1.5 * square)
        result.append(state[member] - omega_rate * fluid * (state[member] - balance))
    return jnp.stack(result)

def drag_terms(state, design, fluid):
    density, momentum = moments(state)
    speed_x = momentum[0] / density
    speed_y = momentum[1] / density
    speed_z = momentum[2] / density
    return fluid * (1.0 + porosity(design)) * (speed_x * speed_x + speed_y * speed_y + speed_z * speed_z)

def shifted_yz(field, step_y, step_z):
    padded = jnp.pad(field, ((0, 0), (1, 1), (1, 1)))
    width_y = field.shape[1]
    width_z = field.shape[2]
    return padded[:, 1 - step_y:1 - step_y + width_y, 1 - step_z:1 - step_z + width_z]

def stream(collided, fluid):
    result = []
    for member in range(19):
        step_x, step_y, step_z = velocity_set[member]
        source = shifted_yz(jnp.roll(fluid, step_x, 0), step_y, step_z)
        moved = shifted_yz(jnp.roll(collided[member], step_x, 0), step_y, step_z)
        result.append(fluid * (source * moved + (1.0 - source) * collided[opposite(member)]) + (1.0 - fluid) * collided[member])
    return jnp.stack(result)

def reference(populations, design, fluid_mask, owner_after):
    fluid = fluid_mask.astype(jnp.float32)
    cell_count = NX * BY * BZ

    def advance(state, design_here):
        return stream(collide(state, design_here, fluid), fluid)
    checked = jax.checkpoint(advance)

    def log_drag(design_here):
        state = populations
        for step in range(STEPS):
            state = checked(state, design_here)
        return (jnp.log(jnp.sum(drag_terms(state, design_here, fluid)) / cell_count), state)
    (value, final), gradient = jax.value_and_grad(log_drag, has_aux=True)(design)
    gradient = gradient * cell_count
    device_ids = jnp.arange(N_BLOCK, dtype=jnp.int32)
    run_starts = lax.optimization_barrier(jnp.sum((owner_after[None, :] < device_ids[:, None]).astype(jnp.int32), axis=1))
    run_counts = lax.optimization_barrier(jnp.sum((owner_after[None, :] == device_ids[:, None]).astype(jnp.int32), axis=1))
    slot_planes = (BPD + 2) * BX
    plane_ids = jnp.arange(N_BLOCK * slot_planes, dtype=jnp.int32)
    holder = plane_ids // slot_planes
    offset = plane_ids % slot_planes
    live = offset < run_counts[holder] * BX
    anchor = jnp.where(live, run_starts[holder] * BX + offset, 0).astype(jnp.int32)
    moved_state = jnp.where(live[None, :, None, None], jnp.take(final, anchor, axis=1), 0.0)
    moved_grad = jnp.where(live[:, None, None], jnp.take(gradient, anchor, axis=0), 0.0)
    return (moved_state, moved_grad)
```

```python
import functools
import math

import jax
import jax.numpy as jnp
from jax import lax
from jax.experimental import pallas as pl
from jax.experimental.pallas import tpu as pltpu
from jax.sharding import PartitionSpec as P

BX = 4
STEPS = 3
REACH = 2 * STEPS
HALO = STEPS + BX

VELOCITY = (
    (0, 0, 0),
    (1, 0, 0),
    (-1, 0, 0),
    (0, 1, 0),
    (0, -1, 0),
    (0, 0, 1),
    (0, 0, -1),
    (1, 1, 0),
    (-1, -1, 0),
    (1, -1, 0),
    (-1, 1, 0),
    (1, 0, 1),
    (-1, 0, -1),
    (1, 0, -1),
    (-1, 0, 1),
    (0, 1, 1),
    (0, -1, -1),
    (0, 1, -1),
    (0, -1, 1),
)
OPP = (0,) + tuple(m + 1 if m % 2 else m - 1 for m in range(1, 19))
FORCE = 0.02
ROOT_45 = math.sqrt(4.5)
ROOT_2 = math.sqrt(2.0)


def rolled(field, step_y, step_z):
    if step_y:
        field = pltpu.roll(field, step_y % field.shape[0], 0)
    if step_z:
        field = pltpu.roll(field, step_z % field.shape[1], 1)
    return field


def pairs(values):
    plus = [values[2 * k + 1] + values[2 * k + 2] for k in range(9)]
    minus = [values[2 * k + 1] - values[2 * k + 2] for k in range(9)]
    return plus, minus


def first_moments(minus, scale):
    along_x, along_y, along_z = minus[:3]
    if scale != 1.0:
        along_x, along_y, along_z = scale * along_x, scale * along_y, scale * along_z
    along_x = along_x + ((minus[3] + minus[4]) + (minus[5] + minus[6]))
    along_y = along_y + ((minus[3] - minus[4]) + (minus[7] + minus[8]))
    along_z = along_z + ((minus[5] - minus[6]) + (minus[7] - minus[8]))
    return along_x, along_y, along_z


def density_velocity(state):
    plus, minus = pairs(state)
    axes = (plus[0] + plus[1]) + (plus[2] + state[0])
    diagonals = (plus[3] + plus[4]) + (plus[5] + plus[6]) + (plus[7] + plus[8])
    density = axes + diagonals
    inverse = 1.0 / density
    momentum = first_moments(minus, 1.0)
    return density, [part * inverse for part in momentum]


def collide(state, density, flow, open_rate):
    rate = ROOT_45 * open_rate
    x, y, z = (flow[0] + FORCE) * rate, flow[1] * rate, flow[2] * rate
    xx, yy, zz = x * x, y * y, z * z
    base = 1.0 - (xx + yy + zz) * (1.0 / 3.0)
    axis_weight = density * (1.2 / 18.0)
    axis_slope = density * (1.2 * ROOT_2 / 18.0)
    side_weight = density * (1.2 / 36.0)
    side_slope = density * (1.2 * ROOT_2 / 36.0)
    result = [density * 0.4 * base - 0.2 * state[0]]
    for k, along in enumerate((x, y, z, x + y, x - y, x + z, x - z, y + z, y - z)):
        if k < 3:
            even = axis_weight * (base + (xx, yy, zz)[k])
            odd = axis_slope * along
        else:
            even = side_weight * (base + along * along)
            odd = side_slope * along
        result.append((even + odd) - 0.2 * state[2 * k + 1])
        result.append((even - odd) - 0.2 * state[2 * k + 2])
    return result


def spread(level, slope):
    x, y, z = slope
    result = [level]
    for along in (x, y, z, x + y, x - y, x + z, x - z, y + z, y - z):
        result.append(level + along)
        result.append(level - along)
    return result


def pull(source, plane, word):
    here = [source[m, plane] for m in range(19)]
    result = [here[0]]
    for m in range(1, 19):
        step_x, step_y, step_z = VELOCITY[m]
        moved = here[m] if step_x == 0 else source[m, plane - step_x]
        moved = rolled(moved, step_y, step_z)
        result.append(jnp.where((word & (1 << m)) != 0, moved, here[OPP[m]]))
    return result


def link_word(behind, here, ahead):
    rows = lax.broadcasted_iota(jnp.int32, here.shape, 0)
    columns = lax.broadcasted_iota(jnp.int32, here.shape, 1)
    joined = behind + 2 * here + 4 * ahead
    word = jnp.zeros_like(here)
    for step_y in (-1, 0, 1):
        for step_z in (-1, 0, 1):
            if step_y and step_z:
                inner = {0: 1}
            else:
                inner = {1: 0, 0: 1, -1: 2}
            near = rolled(joined, step_y, step_z)
            if step_y == 1:
                near = jnp.where(rows == 0, 0, near)
            if step_y == -1:
                near = jnp.where(rows == here.shape[0] - 1, 0, near)
            if step_z == 1:
                near = jnp.where(columns == 0, 0, near)
            if step_z == -1:
                near = jnp.where(columns == here.shape[1] - 1, 0, near)
            for step_x, place in inner.items():
                if (step_x, step_y, step_z) == (0, 0, 0):
                    continue
                m = VELOCITY.index((step_x, step_y, step_z))
                word = word | ((near & (1 << place)) << (m - place))
    return jnp.where(here > 0, word, 0)


def each_plane(low, high, body):
    def two(index, carry):
        body(low + 2 * index)
        body(low + 2 * index + 1)
        return carry

    lax.fori_loop(0, (high - low) // 2, two, 0)
    if (high - low) % 2:
        body(high - 1)


def forward_kernel(
    home, pops, marked, left, right, final, history, opens, words, drag, first, even, odd, fluid, sems
):
    total = home + 2 * HALO
    copies = [
        pltpu.make_async_copy(pops, first.at[pl.ds(0, 19), pl.ds(HALO, home)], sems.at[0]),
        pltpu.make_async_copy(marked, first.at[19, pl.ds(HALO, home)], sems.at[1]),
        pltpu.make_async_copy(left, first.at[:, pl.ds(0, HALO)], sems.at[2]),
        pltpu.make_async_copy(right, first.at[:, pl.ds(HALO + home, HALO)], sems.at[3]),
    ]
    for copy in copies:
        copy.start()
    for copy in copies:
        copy.wait()

    def remember(step, plane, density, flow):
        history[4 * step, plane] = density
        for axis in range(3):
            history[4 * step + 1 + axis, plane] = flow[axis]

    def start(plane):
        mark = first[19, plane]
        fluid[plane] = (mark >= 0.0).astype(jnp.int32)
        design = jnp.maximum(mark, 0.0)
        open_rate = (1.0 + 4.0 * design) / (1.6 + 3.4 * design)
        opens[plane] = open_rate
        state = [first[m, plane] for m in range(19)]
        density, flow = density_velocity(state)
        remember(0, plane, density, flow)
        for m, part in enumerate(collide(state, density, flow, open_rate)):
            even[m, plane] = part

    each_plane(0, total, start)

    def link(plane):
        words[plane] = link_word(fluid[plane - 1], fluid[plane], fluid[plane + 1])

    each_plane(1, total - 1, link)

    def advance(step, source, target, plane):
        state = pull(source, plane, words[plane])
        density, flow = density_velocity(state)
        remember(step, plane, density, flow)
        for m, part in enumerate(collide(state, density, flow, opens[plane])):
            target[m, plane] = part

    each_plane(1, total - 1, functools.partial(advance, 1, even, odd))
    each_plane(2, total - 2, functools.partial(advance, 2, odd, even))

    drag[...] = jnp.zeros_like(drag)

    def finish(plane):
        state = pull(even, plane, words[plane])
        density, flow = density_velocity(state)
        remember(3, plane, density, flow)
        is_fluid = fluid[plane] > 0
        for m in range(19):
            final[m, plane - STEPS] = jnp.where(is_fluid, state[m], first[m, plane])
        square = flow[0] * flow[0] + flow[1] * flow[1] + flow[2] * flow[2]
        own = (plane >= HALO) & (plane < HALO + home)
        drag[...] += jnp.where(is_fluid & own, square / opens[plane], 0.0)

    each_plane(STEPS, total - STEPS, finish)


def backward_kernel(home, history, opens, words, marked, gradient, even, odd, share):
    def recall(step, plane):
        return history[4 * step, plane], [history[4 * step + 1 + axis, plane] for axis in range(3)]

    def seed(plane):
        density, flow = recall(STEPS, plane)
        damping = 1.0 / opens[plane]
        square = flow[0] * flow[0] + flow[1] * flow[1] + flow[2] * flow[2]
        share[plane] = -square * damping
        factor = 2.0 * damping / density
        slope = [part * factor for part in flow]
        values = spread(-square * factor, slope)
        for m in range(19):
            even[OPP[m], plane] = values[m]

    each_plane(HALO - STEPS, HALO + home + STEPS, seed)

    def retreat(step, source, target, plane):
        mirrored = pull(source, plane, words[plane])
        adjoint = [mirrored[OPP[m]] for m in range(19)]
        density, flow = recall(step, plane)
        open_rate = opens[plane]
        force_flow = [flow[0] + FORCE, flow[1], flow[2]]
        x, y, z = [open_rate * part for part in force_flow]
        plus, minus = pairs(adjoint)
        mx, my, mz = [part * (1.0 / 12.0) for part in first_moments(minus, 2.0)]
        xy_plus, xz_plus, yz_plus = plus[3] + plus[4], plus[5] + plus[6], plus[7] + plus[8]
        axes = [2.0 * plus[k] for k in range(3)]
        whole = 12.0 * adjoint[0] + (axes[0] + axes[1] + axes[2]) + (xy_plus + xz_plus + yz_plus)
        third = whole * (1.0 / 3.0)
        xx = axes[0] + (xy_plus + xz_plus) - third
        yy = axes[1] + (xy_plus + yz_plus) - third
        zz = axes[2] + (xz_plus + yz_plus) - third
        xy, xz, yz = plus[3] - plus[4], plus[5] - plus[6], plus[7] - plus[8]
        hx = 0.25 * (xx * x + xy * y + xz * z)
        hy = 0.25 * (xy * x + yy * y + yz * z)
        hz = 0.25 * (xz * x + yz * y + zz * z)
        rate = 1.2 * open_rate
        slope = [rate * (mx + hx), rate * (my + hy), rate * (mz + hz)]
        pushed = slope[0] * force_flow[0] + slope[1] * force_flow[1] + slope[2] * force_flow[2]
        share[plane] += density * pushed
        if target is None:
            return
        level = whole * (1.2 / 36.0) + 1.2 * (
            x * (mx + 0.5 * hx) + y * (my + 0.5 * hy) + z * (mz + 0.5 * hz)
        )
        level = level - (slope[0] * flow[0] + slope[1] * flow[1] + slope[2] * flow[2])
        values = spread(level, slope)
        for m in range(19):
            target[OPP[m], plane] = values[m] - 0.2 * adjoint[m]

    each_plane(HALO - 2, HALO + home + 2, functools.partial(retreat, 2, even, odd))
    each_plane(HALO - 1, HALO + home + 1, functools.partial(retreat, 1, odd, even))
    each_plane(HALO, HALO + home, functools.partial(retreat, 0, even, None))

    def close(plane):
        design = marked[plane]
        slope = 3.0 / ((1.6 + 3.4 * design) * (1.0 + 4.0 * design))
        gradient[plane] = jnp.where(design >= 0.0, share[plane + HALO] * slope, 0.0)

    each_plane(0, home, close)


def place_kernel(blocks, reach, where, source, out, zeros, sems):
    zeros[...] = jnp.zeros_like(zeros)
    most = source.shape[1] // BX - 1
    for slot in range(blocks):
        target = out.at[:, pl.ds(slot * BX, BX)]
        live = slot < where[1]
        begin = jnp.clip(where[0] + reach + slot, 0, most) * BX

        @pl.when(live)
        def _():
            pltpu.make_async_copy(source.at[:, pl.ds(begin, BX)], target, sems.at[slot]).start()

        @pl.when(jnp.logical_not(live))
        def _():
            pltpu.make_async_copy(zeros, target, sems.at[slot]).start()

    for slot in range(blocks):
        target = out.at[:, pl.ds(slot * BX, BX)]
        pltpu.make_async_copy(zeros, target, sems.at[slot]).wait()


def place(source, where, blocks, reach):
    members = source.shape[0]
    tail = source.shape[2:]
    return pl.pallas_call(
        functools.partial(place_kernel, blocks, reach),
        out_shape=jax.ShapeDtypeStruct((members, blocks * BX) + tail, jnp.float32),
        in_specs=[pl.BlockSpec(memory_space=pltpu.SMEM), pl.BlockSpec(memory_space=pl.ANY)],
        out_specs=pl.BlockSpec(memory_space=pl.ANY),
        scratch_shapes=[
            pltpu.VMEM((members, BX) + tail, jnp.float32),
            pltpu.SemaphoreType.DMA((blocks,)),
        ],
        cost_estimate=pl.CostEstimate(flops=0, bytes_accessed=3_200_000, transcendentals=0),
        name="place_populations",
    )(where, source)


def scale_kernel(home, cells, where, drag, left, own, right, out, joined):
    joined[pl.ds(0, home)] = left[...]
    joined[pl.ds(home, home)] = own[...]
    joined[pl.ds(2 * home, home)] = right[...]
    factor = cells / jnp.sum(drag[...])
    for plane in range(out.shape[0]):
        spot = jnp.clip(where[0] * BX + home + plane, 0, 3 * home - 1)
        live = plane < where[1] * BX
        out[plane] = jnp.where(live, joined[spot] * factor, 0.0)


def body(populations, design, fluid_mask, owner_after):
    count = lax.axis_size("block")
    rank = lax.axis_index("block")
    home, width_y, width_z = design.shape
    home_blocks = home // BX
    slots = home_blocks + 2
    total = home + 2 * HALO
    plane = (width_y, width_z)
    f32 = jnp.float32
    vmem = pl.BlockSpec(memory_space=pltpu.VMEM)
    anywhere = pl.BlockSpec(memory_space=pl.ANY)
    smem = pl.BlockSpec(memory_space=pltpu.SMEM)
    up = [(i, (i + 1) % count) for i in range(count)]
    down = [((i + 1) % count, i) for i in range(count)]

    marked = jnp.where(fluid_mask > 0, design, -1.0)
    tail = jnp.concatenate([populations[:, home - HALO :], marked[None, home - HALO :]], axis=0)
    head = jnp.concatenate([populations[:, :HALO], marked[None, :HALO]], axis=0)
    left = lax.ppermute(tail, "block", up)
    right = lax.ppermute(head, "block", down)

    members = jnp.arange(count + 1, dtype=jnp.int32)
    starts = jnp.sum((owner_after[None, :] < members[:, None]).astype(jnp.int32), axis=1)
    shifts = starts - home_blocks * members
    far = jnp.any(jnp.abs(shifts) > 1)
    begin = lax.dynamic_index_in_dim(shifts, rank, 0, keepdims=False)
    after = lax.dynamic_index_in_dim(shifts, rank + 1, 0, keepdims=False)
    where = jnp.stack([begin, after + home_blocks - begin])

    final, history, opens, words, drag = pl.pallas_call(
        functools.partial(forward_kernel, home),
        out_shape=[
            jax.ShapeDtypeStruct((19, home + 2 * BX) + plane, f32),
            jax.ShapeDtypeStruct((4 * (STEPS + 1), total) + plane, f32),
            jax.ShapeDtypeStruct((total,) + plane, f32),
            jax.ShapeDtypeStruct((total,) + plane, jnp.int32),
            jax.ShapeDtypeStruct(plane, f32),
        ],
        in_specs=[anywhere] * 4,
        out_specs=[vmem] * 5,
        scratch_shapes=[
            pltpu.VMEM((20, total) + plane, f32),
            pltpu.VMEM((19, total) + plane, f32),
            pltpu.VMEM((19, total) + plane, f32),
            pltpu.VMEM((total,) + plane, jnp.int32),
            pltpu.SemaphoreType.DMA((4,)),
        ],
        compiler_params=pltpu.CompilerParams(vmem_limit_bytes=24 * 2**20),
        cost_estimate=pl.CostEstimate(flops=25_000_000, bytes_accessed=6_000_000, transcendentals=0),
        name="forward_steps",
    )(populations, marked, left, right)

    distance = 1
    while distance < count:
        swap = [(i, i ^ distance) for i in range(count)]
        drag = drag + lax.ppermute(drag, "block", swap)
        distance *= 2

    gradient = pl.pallas_call(
        functools.partial(backward_kernel, home),
        out_shape=jax.ShapeDtypeStruct((home,) + plane, f32),
        in_specs=[vmem] * 4,
        out_specs=vmem,
        scratch_shapes=[
            pltpu.VMEM((19, total) + plane, f32),
            pltpu.VMEM((19, total) + plane, f32),
            pltpu.VMEM((total,) + plane, f32),
        ],
        compiler_params=pltpu.CompilerParams(vmem_limit_bytes=24 * 2**20),
        cost_estimate=pl.CostEstimate(flops=15_000_000, bytes_accessed=4_000_000, transcendentals=0),
        name="backward_steps",
    )(history, opens, words, marked)

    gradient_left = lax.ppermute(gradient, "block", up[:-1])
    gradient_right = lax.ppermute(gradient, "block", down[:-1])
    cells = float(count * home * width_y * width_z)
    sensitivity = pl.pallas_call(
        functools.partial(scale_kernel, home, cells),
        out_shape=jax.ShapeDtypeStruct((slots * BX,) + plane, f32),
        in_specs=[smem] + [vmem] * 4,
        out_specs=vmem,
        scratch_shapes=[pltpu.VMEM((3 * home,) + plane, f32)],
        name="place_gradient",
    )(where, drag, gradient_left, gradient, gradient_right)

    def by_one(kept):
        return place(kept, where, slots, 1)

    def by_more(kept):
        own = kept[:, BX : BX + home]
        before = lax.ppermute(own, "block", up[:-1])
        behind = lax.ppermute(own, "block", down[:-1])
        return place(jnp.concatenate([before, own, behind], axis=1), where, slots, home_blocks)

    populations_after = lax.cond(far, by_more, by_one, final)
    return (populations_after, sensitivity)


def solution(mesh):
    placed = (
        P(None, ("group", "block"), None, None),
        P(("group", "block"), None, None),
        P(("group", "block"), None, None),
        P("group"),
    )
    return jax.shard_map(
        body,
        mesh=mesh,
        in_specs=placed,
        out_specs=(P(None, ("group", "block"), None, None), P(("group", "block"), None, None)),
        check_vma=False,
    )
```

```python
import functools
import math

import jax
import jax.numpy as jnp
from jax import lax
from jax.experimental import pallas as pl
from jax.experimental.pallas import tpu as pltpu
from jax.sharding import PartitionSpec as P

BX = 4
STEPS = 3
REACH = 2 * STEPS
HALO = STEPS + BX

VELOCITY = (
    (0, 0, 0),
    (1, 0, 0),
    (-1, 0, 0),
    (0, 1, 0),
    (0, -1, 0),
    (0, 0, 1),
    (0, 0, -1),
    (1, 1, 0),
    (-1, -1, 0),
    (1, -1, 0),
    (-1, 1, 0),
    (1, 0, 1),
    (-1, 0, -1),
    (1, 0, -1),
    (-1, 0, 1),
    (0, 1, 1),
    (0, -1, -1),
    (0, 1, -1),
    (0, -1, 1),
)
OPP = (0,) + tuple(m + 1 if m % 2 else m - 1 for m in range(1, 19))
FORCE = 0.02
ROOT_45 = math.sqrt(4.5)
ROOT_2 = math.sqrt(2.0)


def rolled(field, step_y, step_z):
    if step_y:
        field = pltpu.roll(field, step_y % field.shape[0], 0)
    if step_z:
        field = pltpu.roll(field, step_z % field.shape[1], 1)
    return field


def pairs(values):
    plus = [values[2 * k + 1] + values[2 * k + 2] for k in range(9)]
    minus = [values[2 * k + 1] - values[2 * k + 2] for k in range(9)]
    return plus, minus


def first_moments(minus, scale):
    along_x, along_y, along_z = minus[:3]
    if scale != 1.0:
        along_x, along_y, along_z = scale * along_x, scale * along_y, scale * along_z
    along_x = along_x + ((minus[3] + minus[4]) + (minus[5] + minus[6]))
    along_y = along_y + ((minus[3] - minus[4]) + (minus[7] + minus[8]))
    along_z = along_z + ((minus[5] - minus[6]) + (minus[7] - minus[8]))
    return along_x, along_y, along_z


def density_velocity(state):
    plus, minus = pairs(state)
    axes = (plus[0] + plus[1]) + (plus[2] + state[0])
    diagonals = (plus[3] + plus[4]) + (plus[5] + plus[6]) + (plus[7] + plus[8])
    density = axes + diagonals
    inverse = 1.0 / density
    momentum = first_moments(minus, 1.0)
    return density, [part * inverse for part in momentum]


def collide(state, density, flow, open_rate):
    rate = ROOT_45 * open_rate
    x, y, z = (flow[0] + FORCE) * rate, flow[1] * rate, flow[2] * rate
    xx, yy, zz = x * x, y * y, z * z
    base = 1.0 - (xx + yy + zz) * (1.0 / 3.0)
    axis_weight = density * (1.2 / 18.0)
    axis_slope = density * (1.2 * ROOT_2 / 18.0)
    side_weight = density * (1.2 / 36.0)
    side_slope = density * (1.2 * ROOT_2 / 36.0)
    result = [density * 0.4 * base - 0.2 * state[0]]
    for k, along in enumerate((x, y, z, x + y, x - y, x + z, x - z, y + z, y - z)):
        if k < 3:
            even = axis_weight * (base + (xx, yy, zz)[k])
            odd = axis_slope * along
        else:
            even = side_weight * (base + along * along)
            odd = side_slope * along
        result.append((even + odd) - 0.2 * state[2 * k + 1])
        result.append((even - odd) - 0.2 * state[2 * k + 2])
    return result


def spread(level, slope):
    x, y, z = slope
    result = [level]
    for along in (x, y, z, x + y, x - y, x + z, x - z, y + z, y - z):
        result.append(level + along)
        result.append(level - along)
    return result


def pull(source, plane, word):
    here = [source[m, plane] for m in range(19)]
    result = [here[0]]
    for m in range(1, 19):
        step_x, step_y, step_z = VELOCITY[m]
        moved = here[m] if step_x == 0 else source[m, plane - step_x]
        moved = rolled(moved, step_y, step_z)
        result.append(jnp.where((word & (1 << m)) != 0, moved, here[OPP[m]]))
    return result


def link_word(behind, here, ahead):
    rows = lax.broadcasted_iota(jnp.int32, here.shape, 0)
    columns = lax.broadcasted_iota(jnp.int32, here.shape, 1)
    joined = behind + 2 * here + 4 * ahead
    word = jnp.zeros_like(here)
    for step_y in (-1, 0, 1):
        for step_z in (-1, 0, 1):
            if step_y and step_z:
                inner = {0: 1}
            else:
                inner = {1: 0, 0: 1, -1: 2}
            near = rolled(joined, step_y, step_z)
            if step_y == 1:
                near = jnp.where(rows == 0, 0, near)
            if step_y == -1:
                near = jnp.where(rows == here.shape[0] - 1, 0, near)
            if step_z == 1:
                near = jnp.where(columns == 0, 0, near)
            if step_z == -1:
                near = jnp.where(columns == here.shape[1] - 1, 0, near)
            for step_x, place in inner.items():
                if (step_x, step_y, step_z) == (0, 0, 0):
                    continue
                m = VELOCITY.index((step_x, step_y, step_z))
                word = word | ((near & (1 << place)) << (m - place))
    return jnp.where(here > 0, word, 0)


def each_plane(low, high, body):
    def two(index, carry):
        body(low + 2 * index)
        body(low + 2 * index + 1)
        return carry

    lax.fori_loop(0, (high - low) // 2, two, 0)
    if (high - low) % 2:
        body(high - 1)


def forward_kernel(
    home, pops, marked, left, right, final, history, opens, words, drag, first, even, odd, fluid, sems
):
    total = home + 2 * HALO
    copies = [
        pltpu.make_async_copy(pops, first.at[pl.ds(0, 19), pl.ds(HALO, home)], sems.at[0]),
        pltpu.make_async_copy(marked, first.at[19, pl.ds(HALO, home)], sems.at[1]),
        pltpu.make_async_copy(left, first.at[:, pl.ds(0, HALO)], sems.at[2]),
        pltpu.make_async_copy(right, first.at[:, pl.ds(HALO + home, HALO)], sems.at[3]),
    ]
    for copy in copies:
        copy.start()
    for copy in copies:
        copy.wait()

    def remember(step, plane, density, flow):
        history[4 * step, plane] = density
        for axis in range(3):
            history[4 * step + 1 + axis, plane] = flow[axis]

    def start(plane):
        mark = first[19, plane]
        fluid[plane] = (mark >= 0.0).astype(jnp.int32)
        design = jnp.maximum(mark, 0.0)
        open_rate = (1.0 + 4.0 * design) / (1.6 + 3.4 * design)
        opens[plane] = open_rate
        state = [first[m, plane] for m in range(19)]
        density, flow = density_velocity(state)
        remember(0, plane, density, flow)
        for m, part in enumerate(collide(state, density, flow, open_rate)):
            even[m, plane] = part

    each_plane(0, total, start)

    def link(plane):
        words[plane] = link_word(fluid[plane - 1], fluid[plane], fluid[plane + 1])

    each_plane(1, total - 1, link)

    def advance(step, source, target, plane):
        state = pull(source, plane, words[plane])
        density, flow = density_velocity(state)
        remember(step, plane, density, flow)
        for m, part in enumerate(collide(state, density, flow, opens[plane])):
            target[m, plane] = part

    each_plane(1, total - 1, functools.partial(advance, 1, even, odd))
    each_plane(2, total - 2, functools.partial(advance, 2, odd, even))

    drag[...] = jnp.zeros_like(drag)

    def finish(plane):
        state = pull(even, plane, words[plane])
        density, flow = density_velocity(state)
        remember(3, plane, density, flow)
        is_fluid = fluid[plane] > 0
        for m in range(19):
            final[m, plane - STEPS] = jnp.where(is_fluid, state[m], first[m, plane])
        square = flow[0] * flow[0] + flow[1] * flow[1] + flow[2] * flow[2]
        own = (plane >= HALO) & (plane < HALO + home)
        drag[...] += jnp.where(is_fluid & own, square / opens[plane], 0.0)

    each_plane(STEPS, total - STEPS, finish)


def backward_kernel(home, history, opens, words, marked, gradient, even, odd, share):
    def recall(step, plane):
        return history[4 * step, plane], [history[4 * step + 1 + axis, plane] for axis in range(3)]

    def seed(plane):
        density, flow = recall(STEPS, plane)
        damping = 1.0 / opens[plane]
        square = flow[0] * flow[0] + flow[1] * flow[1] + flow[2] * flow[2]
        share[plane] = -square * damping
        factor = 2.0 * damping / density
        slope = [part * factor for part in flow]
        values = spread(-square * factor, slope)
        for m in range(19):
            even[OPP[m], plane] = values[m]

    each_plane(HALO - STEPS, HALO + home + STEPS, seed)

    def retreat(step, source, target, plane):
        mirrored = pull(source, plane, words[plane])
        adjoint = [mirrored[OPP[m]] for m in range(19)]
        density, flow = recall(step, plane)
        open_rate = opens[plane]
        force_flow = [flow[0] + FORCE, flow[1], flow[2]]
        x, y, z = [open_rate * part for part in force_flow]
        plus, minus = pairs(adjoint)
        mx, my, mz = [part * (1.0 / 12.0) for part in first_moments(minus, 2.0)]
        xy_plus, xz_plus, yz_plus = plus[3] + plus[4], plus[5] + plus[6], plus[7] + plus[8]
        axes = [2.0 * plus[k] for k in range(3)]
        whole = 12.0 * adjoint[0] + (axes[0] + axes[1] + axes[2]) + (xy_plus + xz_plus + yz_plus)
        third = whole * (1.0 / 3.0)
        xx = axes[0] + (xy_plus + xz_plus) - third
        yy = axes[1] + (xy_plus + yz_plus) - third
        zz = axes[2] + (xz_plus + yz_plus) - third
        xy, xz, yz = plus[3] - plus[4], plus[5] - plus[6], plus[7] - plus[8]
        hx = 0.25 * (xx * x + xy * y + xz * z)
        hy = 0.25 * (xy * x + yy * y + yz * z)
        hz = 0.25 * (xz * x + yz * y + zz * z)
        rate = 1.2 * open_rate
        slope = [rate * (mx + hx), rate * (my + hy), rate * (mz + hz)]
        pushed = slope[0] * force_flow[0] + slope[1] * force_flow[1] + slope[2] * force_flow[2]
        share[plane] += density * pushed
        if target is None:
            return
        level = whole * (1.2 / 36.0) + 1.2 * (
            x * (mx + 0.5 * hx) + y * (my + 0.5 * hy) + z * (mz + 0.5 * hz)
        )
        level = level - (slope[0] * flow[0] + slope[1] * flow[1] + slope[2] * flow[2])
        values = spread(level, slope)
        for m in range(19):
            target[OPP[m], plane] = values[m] - 0.2 * adjoint[m]

    each_plane(HALO - 2, HALO + home + 2, functools.partial(retreat, 2, even, odd))
    each_plane(HALO - 1, HALO + home + 1, functools.partial(retreat, 1, odd, even))
    each_plane(HALO, HALO + home, functools.partial(retreat, 0, even, None))

    def close(plane):
        design = marked[plane]
        slope = 3.0 / ((1.6 + 3.4 * design) * (1.0 + 4.0 * design))
        gradient[plane] = jnp.where(design >= 0.0, share[plane + HALO] * slope, 0.0)

    each_plane(0, home, close)


def place_kernel(blocks, reach, where, source, out, zeros, sems):
    zeros[...] = jnp.zeros_like(zeros)
    most = source.shape[1] // BX - 1
    for slot in range(blocks):
        target = out.at[:, pl.ds(slot * BX, BX)]
        live = slot < where[1]
        begin = jnp.clip(where[0] + reach + slot, 0, most) * BX

        @pl.when(live)
        def _():
            pltpu.make_async_copy(source.at[:, pl.ds(begin, BX)], target, sems.at[slot]).start()

        @pl.when(jnp.logical_not(live))
        def _():
            pltpu.make_async_copy(zeros, target, sems.at[slot]).start()

    for slot in range(blocks):
        target = out.at[:, pl.ds(slot * BX, BX)]
        pltpu.make_async_copy(zeros, target, sems.at[slot]).wait()


def place(source, where, blocks, reach):
    members = source.shape[0]
    tail = source.shape[2:]
    return pl.pallas_call(
        functools.partial(place_kernel, blocks, reach),
        out_shape=jax.ShapeDtypeStruct((members, blocks * BX) + tail, jnp.float32),
        in_specs=[pl.BlockSpec(memory_space=pltpu.SMEM), pl.BlockSpec(memory_space=pl.ANY)],
        out_specs=pl.BlockSpec(memory_space=pl.ANY),
        scratch_shapes=[
            pltpu.VMEM((members, BX) + tail, jnp.float32),
            pltpu.SemaphoreType.DMA((blocks,)),
        ],
        cost_estimate=pl.CostEstimate(flops=0, bytes_accessed=3_200_000, transcendentals=0),
        name="place_populations",
    )(where, source)


def scale_kernel(home, cells, where, drag, left, own, right, out, joined):
    joined[pl.ds(0, home)] = left[...]
    joined[pl.ds(home, home)] = own[...]
    joined[pl.ds(2 * home, home)] = right[...]
    factor = cells / jnp.sum(drag[...])
    for plane in range(out.shape[0]):
        spot = jnp.clip(where[0] * BX + home + plane, 0, 3 * home - 1)
        live = plane < where[1] * BX
        out[plane] = jnp.where(live, joined[spot] * factor, 0.0)


def body(populations, design, fluid_mask, owner_after):
    count = lax.axis_size("block")
    rank = lax.axis_index("block")
    home, width_y, width_z = design.shape
    home_blocks = home // BX
    slots = home_blocks + 2
    total = home + 2 * HALO
    plane = (width_y, width_z)
    f32 = jnp.float32
    vmem = pl.BlockSpec(memory_space=pltpu.VMEM)
    anywhere = pl.BlockSpec(memory_space=pl.ANY)
    smem = pl.BlockSpec(memory_space=pltpu.SMEM)
    up = [(i, (i + 1) % count) for i in range(count)]
    down = [((i + 1) % count, i) for i in range(count)]

    marked = jnp.where(fluid_mask > 0, design, -1.0)
    tail = jnp.concatenate([populations[:, home - HALO :], marked[None, home - HALO :]], axis=0)
    head = jnp.concatenate([populations[:, :HALO], marked[None, :HALO]], axis=0)
    left = lax.ppermute(tail, "block", up)
    right = lax.ppermute(head, "block", down)

    members = jnp.arange(count + 1, dtype=jnp.int32)
    starts = jnp.sum((owner_after[None, :] < members[:, None]).astype(jnp.int32), axis=1)
    shifts = starts - home_blocks * members
    far = jnp.any(jnp.abs(shifts) > 1)
    begin = lax.dynamic_index_in_dim(shifts, rank, 0, keepdims=False)
    after = lax.dynamic_index_in_dim(shifts, rank + 1, 0, keepdims=False)
    where = jnp.stack([begin, after + home_blocks - begin])

    final, history, opens, words, drag = pl.pallas_call(
        functools.partial(forward_kernel, home),
        out_shape=[
            jax.ShapeDtypeStruct((19, home + 2 * BX) + plane, f32),
            jax.ShapeDtypeStruct((4 * (STEPS + 1), total) + plane, f32),
            jax.ShapeDtypeStruct((total,) + plane, f32),
            jax.ShapeDtypeStruct((total,) + plane, jnp.int32),
            jax.ShapeDtypeStruct(plane, f32),
        ],
        in_specs=[anywhere] * 4,
        out_specs=[vmem] * 5,
        scratch_shapes=[
            pltpu.VMEM((20, total) + plane, f32),
            pltpu.VMEM((19, total) + plane, f32),
            pltpu.VMEM((19, total) + plane, f32),
            pltpu.VMEM((total,) + plane, jnp.int32),
            pltpu.SemaphoreType.DMA((4,)),
        ],
        compiler_params=pltpu.CompilerParams(vmem_limit_bytes=24 * 2**20),
        cost_estimate=pl.CostEstimate(flops=25_000_000, bytes_accessed=6_000_000, transcendentals=0),
        name="forward_steps",
    )(populations, marked, left, right)

    drag = lax.all_gather(drag, "block")

    gradient = pl.pallas_call(
        functools.partial(backward_kernel, home),
        out_shape=jax.ShapeDtypeStruct((home,) + plane, f32),
        in_specs=[vmem] * 4,
        out_specs=vmem,
        scratch_shapes=[
            pltpu.VMEM((19, total) + plane, f32),
            pltpu.VMEM((19, total) + plane, f32),
            pltpu.VMEM((total,) + plane, f32),
        ],
        compiler_params=pltpu.CompilerParams(vmem_limit_bytes=24 * 2**20),
        cost_estimate=pl.CostEstimate(flops=15_000_000, bytes_accessed=4_000_000, transcendentals=0),
        name="backward_steps",
    )(history, opens, words, marked)

    gradient_left = lax.ppermute(gradient, "block", up[:-1])
    gradient_right = lax.ppermute(gradient, "block", down[:-1])
    cells = float(count * home * width_y * width_z)
    sensitivity = pl.pallas_call(
        functools.partial(scale_kernel, home, cells),
        out_shape=jax.ShapeDtypeStruct((slots * BX,) + plane, f32),
        in_specs=[smem] + [vmem] * 4,
        out_specs=vmem,
        scratch_shapes=[pltpu.VMEM((3 * home,) + plane, f32)],
        name="place_gradient",
    )(where, drag, gradient_left, gradient, gradient_right)

    def by_one(kept):
        return place(kept, where, slots, 1)

    def by_more(kept):
        own = kept[:, BX : BX + home]
        before = lax.ppermute(own, "block", up[:-1])
        behind = lax.ppermute(own, "block", down[:-1])
        return place(jnp.concatenate([before, own, behind], axis=1), where, slots, home_blocks)

    populations_after = lax.cond(far, by_more, by_one, final)
    return (populations_after, sensitivity)


def solution(mesh):
    placed = (
        P(None, ("group", "block"), None, None),
        P(("group", "block"), None, None),
        P(("group", "block"), None, None),
        P("group"),
    )
    return jax.shard_map(
        body,
        mesh=mesh,
        in_specs=placed,
        out_specs=(P(None, ("group", "block"), None, None), P(("group", "block"), None, None)),
        check_vma=False,
    )
```

```python
import functools
import math

import jax
import jax.numpy as jnp
from jax import lax
from jax.experimental import pallas as pl
from jax.experimental.pallas import tpu as pltpu
from jax.sharding import PartitionSpec as P

BX = 4
STEPS = 3
HALO = STEPS
MIB = 2**20

VELOCITY = (
    (0, 0, 0),
    (1, 0, 0),
    (-1, 0, 0),
    (0, 1, 0),
    (0, -1, 0),
    (0, 0, 1),
    (0, 0, -1),
    (1, 1, 0),
    (-1, -1, 0),
    (1, -1, 0),
    (-1, 1, 0),
    (1, 0, 1),
    (-1, 0, -1),
    (1, 0, -1),
    (-1, 0, 1),
    (0, 1, 1),
    (0, -1, -1),
    (0, 1, -1),
    (0, -1, 1),
)
OPP = (0,) + tuple(m + 1 if m % 2 else m - 1 for m in range(1, 19))
AHEAD = tuple(m for m in range(19) if VELOCITY[m][0] == 1)
BEHIND = tuple(m for m in range(19) if VELOCITY[m][0] == -1)
FORCE = 0.02
ROOT_45 = math.sqrt(4.5)
ROOT_2 = math.sqrt(2.0)


def rolled(field, step_y, step_z):
    if step_y:
        field = pltpu.roll(field, step_y % field.shape[0], 0)
    if step_z:
        field = pltpu.roll(field, step_z % field.shape[1], 1)
    return field


def pairs(values):
    plus = [values[2 * k + 1] + values[2 * k + 2] for k in range(9)]
    minus = [values[2 * k + 1] - values[2 * k + 2] for k in range(9)]
    return plus, minus


def first_moments(minus, scale):
    along_x, along_y, along_z = minus[:3]
    if scale != 1.0:
        along_x, along_y, along_z = scale * along_x, scale * along_y, scale * along_z
    along_x = along_x + ((minus[3] + minus[4]) + (minus[5] + minus[6]))
    along_y = along_y + ((minus[3] - minus[4]) + (minus[7] + minus[8]))
    along_z = along_z + ((minus[5] - minus[6]) + (minus[7] - minus[8]))
    return along_x, along_y, along_z


def density_velocity(state):
    plus, minus = pairs(state)
    axes = (plus[0] + plus[1]) + (plus[2] + state[0])
    diagonals = (plus[3] + plus[4]) + (plus[5] + plus[6]) + (plus[7] + plus[8])
    density = axes + diagonals
    inverse = 1.0 / density
    momentum = first_moments(minus, 1.0)
    return density, [part * inverse for part in momentum]


def collide(state, density, flow, open_rate):
    rate = ROOT_45 * open_rate
    x, y, z = (flow[0] + FORCE) * rate, flow[1] * rate, flow[2] * rate
    xx, yy, zz = x * x, y * y, z * z
    base = 1.0 - (xx + yy + zz) * (1.0 / 3.0)
    axis_weight = density * (1.2 / 18.0)
    axis_slope = density * (1.2 * ROOT_2 / 18.0)
    side_weight = density * (1.2 / 36.0)
    side_slope = density * (1.2 * ROOT_2 / 36.0)
    result = [density * 0.4 * base - 0.2 * state[0]]
    for k, along in enumerate((x, y, z, x + y, x - y, x + z, x - z, y + z, y - z)):
        if k < 3:
            even = axis_weight * (base + (xx, yy, zz)[k])
            odd = axis_slope * along
        else:
            even = side_weight * (base + along * along)
            odd = side_slope * along
        result.append((even + odd) - 0.2 * state[2 * k + 1])
        result.append((even - odd) - 0.2 * state[2 * k + 2])
    return result


def spread(level, slope):
    x, y, z = slope
    result = [level]
    for along in (x, y, z, x + y, x - y, x + z, x - z, y + z, y - z):
        result.append(level + along)
        result.append(level - along)
    return result


def pull(source, plane, word):
    here = [source[m, plane] for m in range(19)]
    result = [here[0]]
    for m in range(1, 19):
        step_x, step_y, step_z = VELOCITY[m]
        moved = here[m] if step_x == 0 else source[m, plane - step_x]
        moved = rolled(moved, step_y, step_z)
        result.append(jnp.where((word & (1 << m)) != 0, moved, here[OPP[m]]))
    return result


def link_word(behind, here, ahead):
    rows = lax.broadcasted_iota(jnp.int32, here.shape, 0)
    columns = lax.broadcasted_iota(jnp.int32, here.shape, 1)
    joined = behind + 2 * here + 4 * ahead
    word = jnp.zeros_like(here)
    for step_y in (-1, 0, 1):
        for step_z in (-1, 0, 1):
            if step_y and step_z:
                inner = {0: 1}
            else:
                inner = {1: 0, 0: 1, -1: 2}
            near = rolled(joined, step_y, step_z)
            if step_y == 1:
                near = jnp.where(rows == 0, 0, near)
            if step_y == -1:
                near = jnp.where(rows == here.shape[0] - 1, 0, near)
            if step_z == 1:
                near = jnp.where(columns == 0, 0, near)
            if step_z == -1:
                near = jnp.where(columns == here.shape[1] - 1, 0, near)
            for step_x, place in inner.items():
                if (step_x, step_y, step_z) == (0, 0, 0):
                    continue
                m = VELOCITY.index((step_x, step_y, step_z))
                word = word | ((near & (1 << place)) << (m - place))
    return jnp.where(here > 0, word, 0)


def each_plane(low, high, body):
    def two(index, carry):
        body(low + 2 * index)
        body(low + 2 * index + 1)
        return carry

    lax.fori_loop(0, (high - low) // 2, two, 0)
    if (high - low) % 2:
        body(high - 1)


def is_fluid_rate(mark):
    design = jnp.maximum(mark, 0.0)
    return (mark >= 0.0).astype(jnp.int32), (1.0 + 4.0 * design) / (1.6 + 3.4 * design)


def store(target, plane, values):
    for m, part in enumerate(values):
        target[m, plane] = part


def remember(history, step, plane, density, flow):
    history[4 * step, plane] = density
    for axis in range(3):
        history[4 * step + 1 + axis, plane] = flow[axis]


def drag_terms(flow, open_rate):
    return (flow[0] * flow[0] + flow[1] * flow[1] + flow[2] * flow[2]) / open_rate


def edge_kernel(home, pops, design, mask, head, tail, sems):
    copies = [
        pltpu.make_async_copy(pops.at[:, pl.ds(0, HALO)], head.at[pl.ds(0, 19)], sems.at[0]),
        pltpu.make_async_copy(
            pops.at[:, pl.ds(home - HALO, HALO)], tail.at[pl.ds(0, 19)], sems.at[1]
        ),
    ]
    for copy in copies:
        copy.start()
    for plane in range(HALO):
        last = home - HALO + plane
        head[19, plane] = jnp.where(mask[plane] > 0, design[plane], -1.0)
        tail[19, plane] = jnp.where(mask[last] > 0, design[last], -1.0)
    for copy in copies:
        copy.wait()


def interior_kernel(
    home,
    pops,
    design,
    mask,
    to_left,
    to_right,
    edges,
    history,
    final,
    opens,
    fluid,
    words,
    drag,
    even,
    odd,
):
    def start(plane):
        mark = jnp.where(mask[plane] > 0, design[plane], -1.0)
        fluid[plane], open_rate = is_fluid_rate(mark)
        opens[plane] = open_rate
        state = [pops[m, plane] for m in range(19)]
        density, flow = density_velocity(state)
        remember(history, 0, plane, density, flow)
        store(even, plane, collide(state, density, flow, open_rate))

    def link(plane):
        words[plane] = link_word(fluid[plane - 1], fluid[plane], fluid[plane + 1])

    def advance(step, source, target, plane):
        state = pull(source, plane, words[plane])
        density, flow = density_velocity(state)
        remember(history, step, plane, density, flow)
        store(target, plane, collide(state, density, flow, opens[plane]))

    def finish(plane):
        state = pull(even, plane, words[plane])
        density, flow = density_velocity(state)
        remember(history, 3, plane, density, flow)
        here = fluid[plane] > 0
        for m in range(19):
            final[m, plane - STEPS] = jnp.where(here, state[m], pops[m, plane])
        drag[...] += jnp.where(here, drag_terms(flow, opens[plane]), 0.0)

    def send(step, source):
        for slot in range(5):
            to_left[5 * step + slot] = source[BEHIND[slot], STEPS]
            to_right[5 * step + slot] = source[AHEAD[slot], home - 1 - STEPS]
        for m in range(19):
            for side in range(2):
                edges[m, 4 * step + side] = source[m, step + side]
                edges[m, 4 * step + 2 + side] = source[m, home - 2 - step + side]

    drag[...] = jnp.zeros_like(drag)
    for slot, plane in ((0, STEPS), (1, home - 1 - STEPS)):
        mark = jnp.where(mask[plane] > 0, design[plane], -1.0)
        (to_left, to_right)[slot][15] = mark
    each_plane(0, home, start)
    send(0, even)
    each_plane(1, home - 1, link)
    each_plane(1, home - 1, functools.partial(advance, 1, even, odd))
    send(1, odd)
    each_plane(2, home - 2, functools.partial(advance, 2, odd, even))
    send(2, even)
    each_plane(3, home - 3, finish)


def boundary_kernel(
    home,
    pops,
    left,
    right,
    from_left,
    from_right,
    edges,
    inner_history,
    inner_final,
    inner_opens,
    inner_fluid,
    inner_words,
    inner_drag,
    final,
    history,
    opens,
    words,
    drag,
    even,
    odd,
    fluid,
    sems,
):
    span = home + 2 * HALO
    copies = [
        pltpu.make_async_copy(
            inner_history.at[pl.ds(4 * step, 4), pl.ds(step, home - 2 * step)],
            history.at[pl.ds(4 * step, 4), pl.ds(HALO + step, home - 2 * step)],
            sems.at[step],
        )
        for step in range(4)
    ]
    copies.append(
        pltpu.make_async_copy(inner_final, final.at[:, pl.ds(BX + STEPS, home - 2 * STEPS)], sems.at[4])
    )
    for copy in copies:
        copy.start()

    for plane in range(home):
        fluid[plane + HALO + 1] = inner_fluid[plane]
        opens[plane + HALO] = inner_opens[plane]
    for plane in range(1, home - 1):
        words[plane + HALO] = inner_words[plane]
    fluid[0] = (from_left[15] >= 0.0).astype(jnp.int32)
    fluid[span + 1] = (from_right[15] >= 0.0).astype(jnp.int32)

    def begin(side, plane, index):
        fluid[index + 1], open_rate = is_fluid_rate(side[19, plane])
        opens[index] = open_rate
        state = [side[m, plane] for m in range(19)]
        density, flow = density_velocity(state)
        store(even, index + 1, collide(state, density, flow, open_rate))

    def start(step, carry):
        begin(left, step, step)
        begin(right, step, step + HALO + home)
        return carry

    lax.fori_loop(0, HALO, start, 0)

    def receive(step, target):
        for slot in range(5):
            target[AHEAD[slot], 0] = from_left[5 * step + slot]
            target[BEHIND[slot], span + 1] = from_right[5 * step + slot]
        for m in range(19):
            for side in range(2):
                target[m, HALO + 1 + step + side] = edges[m, 4 * step + side]
                target[m, HALO + home - 1 - step + side] = edges[m, 4 * step + 2 + side]

    def both(step, body):
        def two(place, carry):
            body(place)
            body(place + HALO + home - step)
            return carry

        lax.fori_loop(0, HALO + step, two, 0)

    def link(index):
        words[index] = link_word(fluid[index], fluid[index + 1], fluid[index + 2])

    def advance(step, source, target, index):
        state = pull(source, index + 1, words[index])
        density, flow = density_velocity(state)
        remember(history, step, index, density, flow)
        store(target, index + 1, collide(state, density, flow, opens[index]))

    both(1, link)
    receive(0, even)
    both(1, functools.partial(advance, 1, even, odd))
    receive(1, odd)
    both(2, functools.partial(advance, 2, odd, even))
    receive(2, even)
    drag[...] = inner_drag[...]

    def finish(initial, own, place, index):
        state = pull(even, index + 1, words[index])
        density, flow = density_velocity(state)
        remember(history, 3, index, density, flow)
        here = fluid[index + 1] > 0
        for m in range(19):
            final[m, index + BX - HALO] = jnp.where(here, state[m], initial[m, place])
        if own:
            drag[...] += jnp.where(here, drag_terms(flow, opens[index]), 0.0)

    def outer(place, carry):
        finish(left, False, place, place)
        finish(right, False, place, place + HALO + home)
        return carry

    def inner(place, carry):
        finish(pops, True, place, place + HALO)
        finish(pops, True, home - STEPS + place, place + HALO + home - STEPS)
        return carry

    lax.fori_loop(0, HALO, outer, 0)
    lax.fori_loop(0, STEPS, inner, 0)
    for copy in copies:
        copy.wait()


def backward_kernel(
    home, history, opens, words, design, mask, inner_final, gradient, to_left, to_right, even, odd, share
):
    def recall(step, plane):
        return history[4 * step, plane], [history[4 * step + 1 + axis, plane] for axis in range(3)]

    def seed(plane):
        density, flow = recall(STEPS, plane)
        damping = 1.0 / opens[plane]
        square = flow[0] * flow[0] + flow[1] * flow[1] + flow[2] * flow[2]
        share[plane] = -square * damping
        factor = 2.0 * damping / density
        slope = [part * factor for part in flow]
        values = spread(-square * factor, slope)
        for m in range(19):
            even[OPP[m], plane] = values[m]

    each_plane(0, home + 2 * HALO, seed)

    def retreat(step, source, target, plane):
        mirrored = pull(source, plane, words[plane])
        adjoint = [mirrored[OPP[m]] for m in range(19)]
        density, flow = recall(step, plane)
        open_rate = opens[plane]
        force_flow = [flow[0] + FORCE, flow[1], flow[2]]
        x, y, z = [open_rate * part for part in force_flow]
        plus, minus = pairs(adjoint)
        mx, my, mz = [part * (1.0 / 12.0) for part in first_moments(minus, 2.0)]
        xy_plus, xz_plus, yz_plus = plus[3] + plus[4], plus[5] + plus[6], plus[7] + plus[8]
        axes = [2.0 * plus[k] for k in range(3)]
        whole = 12.0 * adjoint[0] + (axes[0] + axes[1] + axes[2]) + (xy_plus + xz_plus + yz_plus)
        third = whole * (1.0 / 3.0)
        xx = axes[0] + (xy_plus + xz_plus) - third
        yy = axes[1] + (xy_plus + yz_plus) - third
        zz = axes[2] + (xz_plus + yz_plus) - third
        xy, xz, yz = plus[3] - plus[4], plus[5] - plus[6], plus[7] - plus[8]
        hx = 0.25 * (xx * x + xy * y + xz * z)
        hy = 0.25 * (xy * x + yy * y + yz * z)
        hz = 0.25 * (xz * x + yz * y + zz * z)
        rate = 1.2 * open_rate
        slope = [rate * (mx + hx), rate * (my + hy), rate * (mz + hz)]
        pushed = slope[0] * force_flow[0] + slope[1] * force_flow[1] + slope[2] * force_flow[2]
        share[plane] += density * pushed
        if target is None:
            return
        level = whole * (1.2 / 36.0) + 1.2 * (
            x * (mx + 0.5 * hx) + y * (my + 0.5 * hy) + z * (mz + 0.5 * hz)
        )
        level = level - (slope[0] * flow[0] + slope[1] * flow[1] + slope[2] * flow[2])
        values = spread(level, slope)
        for m in range(19):
            target[OPP[m], plane] = values[m] - 0.2 * adjoint[m]

    each_plane(HALO - 2, HALO + home + 2, functools.partial(retreat, 2, even, odd))
    each_plane(HALO - 1, HALO + home + 1, functools.partial(retreat, 1, odd, even))
    each_plane(HALO, HALO + home, functools.partial(retreat, 0, even, None))

    for plane in range(home):
        here = mask[plane] > 0
        slope = 3.0 / ((1.6 + 3.4 * design[plane]) * (1.0 + 4.0 * design[plane]))
        value = jnp.where(here, share[plane + HALO] * slope, 0.0)
        gradient[plane] = value
        if plane < BX:
            to_left[19 + plane] = value
        if plane >= home - BX:
            to_right[19 + plane - (home - BX)] = value
    for m in range(19):
        to_left[m] = inner_final[m, 0]
        to_right[m] = inner_final[m, home - 2 * STEPS - 1]


def scaled(home, cells, where, drag, joined, out):
    factor = cells / jnp.sum(drag[...])
    reach = (joined.shape[0] - home) // 2
    for plane in range(out.shape[0]):
        spot = jnp.clip(where[0] * BX + reach + plane, 0, joined.shape[0] - 1)
        live = plane < where[1] * BX
        out[plane] = jnp.where(live, joined[spot] * factor, 0.0)


def place_blocks(reach, where, source, out, zeros, sems):
    zeros[...] = jnp.zeros_like(zeros)
    blocks = out.shape[1] // BX
    most = source.shape[1] // BX - 1
    for slot in range(blocks):
        target = out.at[:, pl.ds(slot * BX, BX)]
        live = slot < where[1]
        begin = jnp.clip(where[0] + reach + slot, 0, most) * BX

        @pl.when(live)
        def _():
            pltpu.make_async_copy(source.at[:, pl.ds(begin, BX)], target, sems.at[slot]).start()

        @pl.when(jnp.logical_not(live))
        def _():
            pltpu.make_async_copy(zeros, target, sems.at[slot]).start()


def await_blocks(out, zeros, sems):
    for slot in range(out.shape[1] // BX):
        target = out.at[:, pl.ds(slot * BX, BX)]
        pltpu.make_async_copy(zeros, target, sems.at[slot]).wait()


def near_kernel(
    home, cells, where, final, drag, gradient, from_left, from_right, out, slots, joined, zeros, sems
):
    place_blocks(1, where, final, out, zeros, sems)
    joined[pl.ds(0, BX)] = from_left[pl.ds(19, BX)]
    joined[pl.ds(BX, home)] = gradient[...]
    joined[pl.ds(BX + home, BX)] = from_right[pl.ds(19, BX)]
    scaled(home, cells, where, drag, joined, slots)
    await_blocks(out, zeros, sems)

    @pl.when(where[0] < 0)
    def _():
        copy = pltpu.make_async_copy(from_left.at[pl.ds(0, 19)], out.at[:, 0], sems.at[0])
        copy.start()
        copy.wait()

    @pl.when((where[0] + where[1]) * BX > home)
    def _():
        last = jnp.clip(where[1], 1, out.shape[1] // BX) * BX - 1
        copy = pltpu.make_async_copy(from_right.at[pl.ds(0, 19)], out.at[:, last], sems.at[1])
        copy.start()
        copy.wait()


def far_kernel(
    home, cells, where, final, drag, gradient, from_left, from_right, out, slots, joined, zeros, sems
):
    place_blocks(home // BX, where, final, out, zeros, sems)
    joined[pl.ds(0, home)] = from_left[...]
    joined[pl.ds(home, home)] = gradient[...]
    joined[pl.ds(2 * home, home)] = from_right[...]
    scaled(home, cells, where, drag, joined, slots)
    await_blocks(out, zeros, sems)


def body(populations, design, fluid_mask, owner_after):
    count = lax.axis_size("block")
    rank = lax.axis_index("block")
    home, width_y, width_z = design.shape
    home_blocks = home // BX
    slots = home_blocks + 2
    span = home + 2 * HALO
    plane = (width_y, width_z)
    vmem = pl.BlockSpec(memory_space=pltpu.VMEM)
    anywhere = pl.BlockSpec(memory_space=pl.ANY)
    smem = pl.BlockSpec(memory_space=pltpu.SMEM)
    up = [(i, (i + 1) % count) for i in range(count)]
    down = [((i + 1) % count, i) for i in range(count)]
    cells = float(count * home * width_y * width_z)

    def planes(*lead, dtype=jnp.float32):
        return jax.ShapeDtypeStruct(lead + plane, dtype)

    def scratch(*lead, dtype=jnp.float32):
        return pltpu.VMEM(lead + plane, dtype)

    def call(kernel, name, ins, outs, scratches, limit, moved, *operands):
        return pl.pallas_call(
            kernel,
            out_shape=[shape for shape, _ in outs],
            in_specs=ins,
            out_specs=[spec for _, spec in outs],
            scratch_shapes=scratches,
            compiler_params=pltpu.CompilerParams(vmem_limit_bytes=limit * MIB),
            cost_estimate=pl.CostEstimate(flops=0, bytes_accessed=moved, transcendentals=0),
            name=name,
        )(*operands)

    head, tail = call(
        functools.partial(edge_kernel, home),
        "edge_planes",
        [anywhere, vmem, vmem],
        [(planes(20, HALO), vmem)] * 2,
        [pltpu.SemaphoreType.DMA((2,))],
        4,
        1_000_000,
        populations,
        design,
        fluid_mask,
    )
    left = lax.ppermute(tail, "block", up)
    right = lax.ppermute(head, "block", down)

    deep = home - 2 * STEPS
    to_left, to_right, edges, inner_history, inner_final, inner_opens, fluid, inner_words, drag = call(
        functools.partial(interior_kernel, home),
        "interior_steps",
        [vmem] * 3,
        [
            (shape, vmem)
            for shape in (
                planes(16),
                planes(16),
                planes(19, 12),
                planes(16, home),
                planes(19, deep),
                planes(home),
                planes(home, dtype=jnp.int32),
                planes(home, dtype=jnp.int32),
                planes(),
            )
        ],
        [scratch(19, home)] * 2,
        16,
        6_000_000,
        populations,
        design,
        fluid_mask,
    )
    from_left = lax.ppermute(to_right, "block", up)
    from_right = lax.ppermute(to_left, "block", down)

    members = jnp.arange(count + 1, dtype=jnp.int32)
    starts = jnp.sum((owner_after[None, :] < members[:, None]).astype(jnp.int32), axis=1)
    shifts = starts - home_blocks * members
    far = jnp.any(jnp.abs(shifts) > 1)
    begin = lax.dynamic_index_in_dim(shifts, rank, 0, keepdims=False)
    after = lax.dynamic_index_in_dim(shifts, rank + 1, 0, keepdims=False)
    where = jnp.stack([begin, after + home_blocks - begin])

    final, history, opens, words, drag = call(
        functools.partial(boundary_kernel, home),
        "boundary_steps",
        [vmem] * 6 + [anywhere] * 2 + [vmem] * 4,
        [
            (shape, vmem)
            for shape in (
                planes(19, home + 2 * BX),
                planes(16, span),
                planes(span),
                planes(span, dtype=jnp.int32),
                planes(),
            )
        ],
        [
            scratch(19, span + 2),
            scratch(19, span + 2),
            scratch(span + 2, dtype=jnp.int32),
            pltpu.SemaphoreType.DMA((5,)),
        ],
        20,
        8_000_000,
        populations,
        left,
        right,
        from_left,
        from_right,
        edges,
        inner_history,
        inner_final,
        inner_opens,
        fluid,
        inner_words,
        drag,
    )

    distance = 1
    while distance < count:
        swap = [(i, i ^ distance) for i in range(count)]
        drag = drag + lax.ppermute(drag, "block", swap)
        distance *= 2

    gradient, to_left, to_right = call(
        functools.partial(backward_kernel, home),
        "backward_steps",
        [vmem] * 6,
        [(planes(home), vmem), (planes(19 + BX), vmem), (planes(19 + BX), vmem)],
        [scratch(19, span), scratch(19, span), scratch(span)],
        20,
        8_000_000,
        history,
        opens,
        words,
        design,
        fluid_mask,
        inner_final,
    )
    from_left = lax.ppermute(to_right, "block", up[:-1])
    from_right = lax.ppermute(to_left, "block", down[:-1])

    def slotted(kernel, name, reach, *operands):
        return call(
            functools.partial(kernel, home, cells),
            name,
            [smem, anywhere] + [vmem] * 4,
            [(planes(19, slots * BX), anywhere), (planes(slots * BX), vmem)],
            [
                scratch(home + 2 * reach),
                scratch(19, BX),
                pltpu.SemaphoreType.DMA((slots,)),
            ],
            8,
            4_000_000,
            where,
            *operands,
        )

    def near_slots(final, gradient, drag, from_left, from_right):
        return slotted(near_kernel, "near_slots", BX, final, drag, gradient, from_left, from_right)

    def far_slots(final, gradient, drag, from_left, from_right):
        own = final[:, BX : BX + home]
        wide = [lax.ppermute(own, "block", route) for route in (up[:-1], down[:-1])]
        grads = [lax.ppermute(gradient, "block", route) for route in (up[:-1], down[:-1])]
        joined = jnp.concatenate([wide[0], own, wide[1]], axis=1)
        return slotted(far_kernel, "far_slots", home, joined, drag, gradient, *grads)

    return tuple(
        lax.cond(far, far_slots, near_slots, final, gradient, drag, from_left, from_right)
    )


def solution(mesh):
    placed = (
        P(None, ("group", "block"), None, None),
        P(("group", "block"), None, None),
        P(("group", "block"), None, None),
        P("group"),
    )
    return jax.shard_map(
        body,
        mesh=mesh,
        in_specs=placed,
        out_specs=(P(None, ("group", "block"), None, None), P(("group", "block"), None, None)),
        check_vma=False,
    )
```

```python
import functools
import math

import jax
import jax.numpy as jnp
from jax import lax
from jax.experimental import pallas as pl
from jax.experimental.pallas import tpu as pltpu
from jax.sharding import PartitionSpec as P

BX = 4
STEPS = 3
HALO = STEPS
MIB = 2**20

VELOCITY = (
    (0, 0, 0),
    (1, 0, 0),
    (-1, 0, 0),
    (0, 1, 0),
    (0, -1, 0),
    (0, 0, 1),
    (0, 0, -1),
    (1, 1, 0),
    (-1, -1, 0),
    (1, -1, 0),
    (-1, 1, 0),
    (1, 0, 1),
    (-1, 0, -1),
    (1, 0, -1),
    (-1, 0, 1),
    (0, 1, 1),
    (0, -1, -1),
    (0, 1, -1),
    (0, -1, 1),
)
OPP = (0,) + tuple(m + 1 if m % 2 else m - 1 for m in range(1, 19))
AHEAD = tuple(m for m in range(19) if VELOCITY[m][0] == 1)
BEHIND = tuple(m for m in range(19) if VELOCITY[m][0] == -1)
FORCE = 0.02
ROOT_45 = math.sqrt(4.5)
ROOT_2 = math.sqrt(2.0)


def rolled(field, step_y, step_z):
    if step_y:
        field = pltpu.roll(field, step_y % field.shape[0], 0)
    if step_z:
        field = pltpu.roll(field, step_z % field.shape[1], 1)
    return field


def pairs(values):
    plus = [values[2 * k + 1] + values[2 * k + 2] for k in range(9)]
    minus = [values[2 * k + 1] - values[2 * k + 2] for k in range(9)]
    return plus, minus


def first_moments(minus, scale):
    along_x, along_y, along_z = minus[:3]
    if scale != 1.0:
        along_x, along_y, along_z = scale * along_x, scale * along_y, scale * along_z
    along_x = along_x + ((minus[3] + minus[4]) + (minus[5] + minus[6]))
    along_y = along_y + ((minus[3] - minus[4]) + (minus[7] + minus[8]))
    along_z = along_z + ((minus[5] - minus[6]) + (minus[7] - minus[8]))
    return along_x, along_y, along_z


def density_velocity(state):
    plus, minus = pairs(state)
    axes = (plus[0] + plus[1]) + (plus[2] + state[0])
    diagonals = (plus[3] + plus[4]) + (plus[5] + plus[6]) + (plus[7] + plus[8])
    density = axes + diagonals
    inverse = 1.0 / density
    momentum = first_moments(minus, 1.0)
    return density, [part * inverse for part in momentum]


def collide(state, density, flow, open_rate):
    rate = ROOT_45 * open_rate
    x, y, z = (flow[0] + FORCE) * rate, flow[1] * rate, flow[2] * rate
    xx, yy, zz = x * x, y * y, z * z
    base = 1.0 - (xx + yy + zz) * (1.0 / 3.0)
    axis_weight = density * (1.2 / 18.0)
    axis_slope = density * (1.2 * ROOT_2 / 18.0)
    side_weight = density * (1.2 / 36.0)
    side_slope = density * (1.2 * ROOT_2 / 36.0)
    result = [density * 0.4 * base - 0.2 * state[0]]
    for k, along in enumerate((x, y, z, x + y, x - y, x + z, x - z, y + z, y - z)):
        if k < 3:
            even = axis_weight * (base + (xx, yy, zz)[k])
            odd = axis_slope * along
        else:
            even = side_weight * (base + along * along)
            odd = side_slope * along
        result.append((even + odd) - 0.2 * state[2 * k + 1])
        result.append((even - odd) - 0.2 * state[2 * k + 2])
    return result


def spread(level, slope):
    x, y, z = slope
    result = [level]
    for along in (x, y, z, x + y, x - y, x + z, x - z, y + z, y - z):
        result.append(level + along)
        result.append(level - along)
    return result


def pull(source, plane, word):
    here = [source[m, plane] for m in range(19)]
    result = [here[0]]
    for m in range(1, 19):
        step_x, step_y, step_z = VELOCITY[m]
        moved = here[m] if step_x == 0 else source[m, plane - step_x]
        moved = rolled(moved, step_y, step_z)
        result.append(jnp.where((word & (1 << m)) != 0, moved, here[OPP[m]]))
    return result


def link_word(behind, here, ahead):
    rows = lax.broadcasted_iota(jnp.int32, here.shape, 0)
    columns = lax.broadcasted_iota(jnp.int32, here.shape, 1)
    joined = behind + 2 * here + 4 * ahead
    word = jnp.zeros_like(here)
    for step_y in (-1, 0, 1):
        for step_z in (-1, 0, 1):
            if step_y and step_z:
                inner = {0: 1}
            else:
                inner = {1: 0, 0: 1, -1: 2}
            near = rolled(joined, step_y, step_z)
            if step_y == 1:
                near = jnp.where(rows == 0, 0, near)
            if step_y == -1:
                near = jnp.where(rows == here.shape[0] - 1, 0, near)
            if step_z == 1:
                near = jnp.where(columns == 0, 0, near)
            if step_z == -1:
                near = jnp.where(columns == here.shape[1] - 1, 0, near)
            for step_x, place in inner.items():
                if (step_x, step_y, step_z) == (0, 0, 0):
                    continue
                m = VELOCITY.index((step_x, step_y, step_z))
                word = word | ((near & (1 << place)) << (m - place))
    return jnp.where(here > 0, word, 0)


def each_plane(low, high, body):
    def two(index, carry):
        body(low + 2 * index)
        body(low + 2 * index + 1)
        return carry

    lax.fori_loop(0, (high - low) // 2, two, 0)
    if (high - low) % 2:
        body(high - 1)


def is_fluid_rate(mark):
    design = jnp.maximum(mark, 0.0)
    return (mark >= 0.0).astype(jnp.int32), (1.0 + 4.0 * design) / (1.6 + 3.4 * design)


def store(target, plane, values):
    for m, part in enumerate(values):
        target[m, plane] = part


def remember(history, step, plane, density, flow):
    history[4 * step, plane] = density
    for axis in range(3):
        history[4 * step + 1 + axis, plane] = flow[axis]


def drag_terms(flow, open_rate):
    return (flow[0] * flow[0] + flow[1] * flow[1] + flow[2] * flow[2]) / open_rate


def parity(axis="block"):
    return 1 - lax.rem(lax.axis_index(axis), 2)


def pick(flag, yes, no):
    return no + flag * (yes - no)


def edge_kernel(home, pops, design, mask, near, far, design_near, mask_near, sems):
    up = parity()
    copies = []
    for side, (out, ahead) in enumerate(((near, up), (far, 1 - up))):
        first = ahead * (home - HALO)
        copies.append(
            pltpu.make_async_copy(
                pops.at[:, pl.ds(first, HALO)], out.at[pl.ds(0, 19)], sems.at[3 * side]
            )
        )
        for place, (source, kept) in enumerate(((design, design_near), (mask, mask_near))):
            copies.append(
                pltpu.make_async_copy(
                    source.at[pl.ds(first, HALO)], kept.at[side], sems.at[3 * side + 1 + place]
                )
            )
    for copy in copies:
        copy.start()
    for side, out in enumerate((near, far)):
        copies[3 * side + 1].wait()
        copies[3 * side + 2].wait()
        for plane in range(HALO):
            out[19, plane] = jnp.where(mask_near[side, plane] > 0, design_near[side, plane], -1.0)
    copies[0].wait()
    copies[3].wait()


def interior_kernel(
    home,
    owner,
    pops_far,
    design,
    mask,
    to_near,
    to_far,
    edges,
    history,
    final,
    opens,
    fluid,
    words,
    drag,
    marked,
    where,
    pops,
    even,
    odd,
    designs,
    masks,
    sems,
):
    copies = [
        pltpu.make_async_copy(source, target, sems.at[place])
        for place, (source, target) in enumerate(((pops_far, pops), (design, designs), (mask, masks)))
    ]
    for copy in copies:
        copy.start()
    up = parity()
    rank = lax.axis_index("block")
    home_blocks = home // BX

    def count(block, carry):
        below, own = carry
        holder = owner[block]
        return below + (holder < rank).astype(jnp.int32), own + (holder == rank).astype(jnp.int32)

    def stray(device, found):
        late = owner[home_blocks * device + 1] < device
        early = owner[home_blocks * device + home_blocks - 2] > device
        return found | late.astype(jnp.int32) | early.astype(jnp.int32)

    below, own = lax.fori_loop(0, owner.shape[0], count, (jnp.int32(0), jnp.int32(0)))
    where[0] = below - home_blocks * rank
    where[1] = own
    where[2] = lax.fori_loop(0, owner.shape[0] // home_blocks, stray, jnp.int32(0))
    for copy in copies:
        copy.wait()

    def start(plane):
        mark = jnp.where(masks[plane] > 0, designs[plane], -1.0)
        marked[plane] = mark
        fluid[plane], open_rate = is_fluid_rate(mark)
        opens[plane] = open_rate
        state = [pops[m, plane] for m in range(19)]
        density, flow = density_velocity(state)
        remember(history, 0, plane, density, flow)
        store(even, plane, collide(state, density, flow, open_rate))

    def link(plane):
        words[plane] = link_word(fluid[plane - 1], fluid[plane], fluid[plane + 1])

    def advance(step, source, target, plane):
        state = pull(source, plane, words[plane])
        density, flow = density_velocity(state)
        remember(history, step, plane, density, flow)
        store(target, plane, collide(state, density, flow, opens[plane]))

    def finish(plane):
        state = pull(even, plane, words[plane])
        density, flow = density_velocity(state)
        remember(history, 3, plane, density, flow)
        here = fluid[plane] > 0
        for m in range(19):
            final[m, plane - STEPS] = jnp.where(here, state[m], pops[m, plane])
        drag[...] += jnp.where(here, drag_terms(flow, opens[plane]), 0.0)

    def send(step, source):
        for out, ahead in ((to_near, up), (to_far, 1 - up)):
            plane = pick(ahead, home - 1 - STEPS, STEPS)
            for slot in range(5):
                out[5 * step + slot] = source[AHEAD[slot] + 1 - ahead, plane]
            if step == 0:
                out[15] = marked[plane]
        for m in range(19):
            for side in range(2):
                edges[m, 4 * step + side] = source[m, step + side]
                edges[m, 4 * step + 2 + side] = source[m, home - 2 - step + side]

    drag[...] = jnp.zeros_like(drag)
    each_plane(0, home, start)
    send(0, even)
    each_plane(1, home - 1, link)
    each_plane(1, home - 1, functools.partial(advance, 1, even, odd))
    send(1, odd)
    each_plane(2, home - 2, functools.partial(advance, 2, odd, even))
    send(2, even)
    each_plane(3, home - 3, finish)


def boundary_kernel(
    home,
    own_near,
    own_far,
    near,
    far,
    from_near,
    from_far,
    edges,
    inner_history,
    inner_final,
    inner_opens,
    inner_fluid,
    inner_words,
    inner_drag,
    final,
    history,
    opens,
    words,
    drag,
    even,
    odd,
    fluid,
    sems,
):
    span = home + 2 * HALO
    up = parity()
    sides = ((up, own_near, near, from_near), (1 - up, own_far, far, from_far))
    copies = [
        pltpu.make_async_copy(
            inner_history.at[pl.ds(4 * step, 4), pl.ds(step, home - 2 * step)],
            history.at[pl.ds(4 * step, 4), pl.ds(HALO + step, home - 2 * step)],
            sems.at[step],
        )
        for step in range(4)
    ]
    copies.append(
        pltpu.make_async_copy(inner_final, final.at[:, pl.ds(BX + STEPS, home - 2 * STEPS)], sems.at[4])
    )
    for copy in copies:
        copy.start()

    for plane in range(home):
        fluid[plane + HALO + 1] = inner_fluid[plane]
        opens[plane + HALO] = inner_opens[plane]
    for plane in range(1, home - 1):
        words[plane + HALO] = inner_words[plane]
    for ahead, _, _, message in sides:
        fluid[ahead * (span + 1)] = (message[15] >= 0.0).astype(jnp.int32)

    def begin(ahead, side, plane):
        index = plane + ahead * (HALO + home)
        fluid[index + 1], open_rate = is_fluid_rate(side[19, plane])
        opens[index] = open_rate
        state = [side[m, plane] for m in range(19)]
        density, flow = density_velocity(state)
        store(even, index + 1, collide(state, density, flow, open_rate))

    def start(plane, carry):
        for ahead, _, side, _ in sides:
            begin(ahead, side, plane)
        return carry

    lax.fori_loop(0, HALO, start, 0)

    def receive(step, target):
        for ahead, _, _, message in sides:
            for slot in range(5):
                target[AHEAD[slot] + ahead, ahead * (span + 1)] = message[5 * step + slot]
        for m in range(19):
            for side in range(2):
                target[m, HALO + 1 + step + side] = edges[m, 4 * step + side]
                target[m, HALO + home - 1 - step + side] = edges[m, 4 * step + 2 + side]

    def both(step, body):
        def two(place, carry):
            body(place)
            body(place + HALO + home - step)
            return carry

        lax.fori_loop(0, HALO + step, two, 0)

    def link(index):
        words[index] = link_word(fluid[index], fluid[index + 1], fluid[index + 2])

    def advance(step, source, target, index):
        state = pull(source, index + 1, words[index])
        density, flow = density_velocity(state)
        remember(history, step, index, density, flow)
        store(target, index + 1, collide(state, density, flow, opens[index]))

    both(1, link)
    receive(0, even)
    both(1, functools.partial(advance, 1, even, odd))
    receive(1, odd)
    both(2, functools.partial(advance, 2, odd, even))
    receive(2, even)
    drag[...] = inner_drag[...]

    def finish(initial, own, place, index):
        state = pull(even, index + 1, words[index])
        density, flow = density_velocity(state)
        remember(history, 3, index, density, flow)
        here = fluid[index + 1] > 0
        for m in range(19):
            final[m, index + BX - HALO] = jnp.where(here, state[m], initial[m, place])
        if own:
            drag[...] += jnp.where(here, drag_terms(flow, opens[index]), 0.0)

    def outer(place, carry):
        for ahead, _, side, _ in sides:
            finish(side, False, place, place + ahead * (HALO + home))
        return carry

    def inner(place, carry):
        for ahead, own, _, _ in sides:
            finish(own, True, place, place + HALO + ahead * (home - STEPS))
        return carry

    lax.fori_loop(0, HALO, outer, 0)
    lax.fori_loop(0, STEPS, inner, 0)
    for copy in copies:
        copy.wait()


def backward_kernel(
    home, history, opens, words, marked, inner_final, gradient, to_near, to_far, even, odd, share
):
    def recall(step, plane):
        return history[4 * step, plane], [history[4 * step + 1 + axis, plane] for axis in range(3)]

    def seed(plane):
        density, flow = recall(STEPS, plane)
        damping = 1.0 / opens[plane]
        square = flow[0] * flow[0] + flow[1] * flow[1] + flow[2] * flow[2]
        share[plane] = -square * damping
        factor = 2.0 * damping / density
        slope = [part * factor for part in flow]
        values = spread(-square * factor, slope)
        for m in range(19):
            even[OPP[m], plane] = values[m]

    each_plane(0, home + 2 * HALO, seed)

    def retreat(step, source, target, plane):
        mirrored = pull(source, plane, words[plane])
        adjoint = [mirrored[OPP[m]] for m in range(19)]
        density, flow = recall(step, plane)
        open_rate = opens[plane]
        force_flow = [flow[0] + FORCE, flow[1], flow[2]]
        x, y, z = [open_rate * part for part in force_flow]
        plus, minus = pairs(adjoint)
        mx, my, mz = [part * (1.0 / 12.0) for part in first_moments(minus, 2.0)]
        xy_plus, xz_plus, yz_plus = plus[3] + plus[4], plus[5] + plus[6], plus[7] + plus[8]
        axes = [2.0 * plus[k] for k in range(3)]
        whole = 12.0 * adjoint[0] + (axes[0] + axes[1] + axes[2]) + (xy_plus + xz_plus + yz_plus)
        third = whole * (1.0 / 3.0)
        xx = axes[0] + (xy_plus + xz_plus) - third
        yy = axes[1] + (xy_plus + yz_plus) - third
        zz = axes[2] + (xz_plus + yz_plus) - third
        xy, xz, yz = plus[3] - plus[4], plus[5] - plus[6], plus[7] - plus[8]
        hx = 0.25 * (xx * x + xy * y + xz * z)
        hy = 0.25 * (xy * x + yy * y + yz * z)
        hz = 0.25 * (xz * x + yz * y + zz * z)
        rate = 1.2 * open_rate
        slope = [rate * (mx + hx), rate * (my + hy), rate * (mz + hz)]
        pushed = slope[0] * force_flow[0] + slope[1] * force_flow[1] + slope[2] * force_flow[2]
        share[plane] += density * pushed
        if target is None:
            return
        level = whole * (1.2 / 36.0) + 1.2 * (
            x * (mx + 0.5 * hx) + y * (my + 0.5 * hy) + z * (mz + 0.5 * hz)
        )
        level = level - (slope[0] * flow[0] + slope[1] * flow[1] + slope[2] * flow[2])
        values = spread(level, slope)
        for m in range(19):
            target[OPP[m], plane] = values[m] - 0.2 * adjoint[m]

    each_plane(HALO - 2, HALO + home + 2, functools.partial(retreat, 2, even, odd))
    each_plane(HALO - 1, HALO + home + 1, functools.partial(retreat, 1, odd, even))
    each_plane(HALO, HALO + home, functools.partial(retreat, 0, even, None))

    for plane in range(home):
        design = marked[plane]
        slope = 3.0 / ((1.6 + 3.4 * design) * (1.0 + 4.0 * design))
        gradient[plane] = jnp.where(design >= 0.0, share[plane + HALO] * slope, 0.0)
    up = parity()
    for out, ahead in ((to_near, up), (to_far, 1 - up)):
        for plane in range(BX):
            out[19 + plane] = gradient[ahead * (home - BX) + plane]
        for m in range(19):
            out[m] = inner_final[m, ahead * (home - 2 * STEPS - 1)]


def scaled(home, cells, where, drag, joined, out):
    factor = cells / jnp.sum(drag[...])
    reach = (joined.shape[0] - home) // 2
    for plane in range(out.shape[0]):
        spot = jnp.clip(where[0] * BX + reach + plane, 0, joined.shape[0] - 1)
        live = plane < where[1] * BX
        out[plane] = jnp.where(live, joined[spot] * factor, 0.0)


def near_kernel(
    home, cells, where, final, drag, gradient, from_near, from_far, out, slots, joined, outer, zeros, sems
):
    up = parity()
    blocks = out.shape[1] // BX
    last = home // BX + 1
    zeros[...] = jnp.zeros_like(zeros)
    for m in range(19):
        for plane in range(BX - 1):
            outer[0, m, plane + 1] = final[m, plane + 1]
            outer[1, m, plane] = final[m, BX + home + plane]
        for ahead, message in ((up, from_near), (1 - up, from_far)):
            outer[ahead, m, ahead * (BX - 1)] = message[m]
    for slot in range(blocks):
        target = out.at[:, pl.ds(slot * BX, BX)]
        live = slot < where[1]
        block = jnp.clip(where[0] + 1 + slot, 0, last)
        inside = (block > 0) & (block < last)

        @pl.when(live & inside)
        def _():
            source = final.at[:, pl.ds(block * BX, BX)]
            pltpu.make_async_copy(source, target, sems.at[slot]).start()

        @pl.when(live & jnp.logical_not(inside))
        def _():
            source = outer.at[(block > 0).astype(jnp.int32)]
            pltpu.make_async_copy(source, target, sems.at[slot]).start()

        @pl.when(jnp.logical_not(live))
        def _():
            pltpu.make_async_copy(zeros, target, sems.at[slot]).start()

    for ahead, message in ((up, from_near), (1 - up, from_far)):
        joined[pl.ds(ahead * (BX + home), BX)] = message[pl.ds(19, BX)]
    joined[pl.ds(BX, home)] = gradient[...]
    scaled(home, cells, where, drag, joined, slots)
    for slot in range(blocks):
        pltpu.make_async_copy(zeros, out.at[:, pl.ds(slot * BX, BX)], sems.at[slot]).wait()


def far_kernel(
    home, cells, where, final, drag, gradient, from_left, from_right, out, slots, joined, zeros, sems
):
    zeros[...] = jnp.zeros_like(zeros)
    blocks = out.shape[1] // BX
    most = final.shape[1] // BX - 1
    for slot in range(blocks):
        target = out.at[:, pl.ds(slot * BX, BX)]
        live = slot < where[1]
        begin = jnp.clip(where[0] + home // BX + slot, 0, most) * BX

        @pl.when(live)
        def _():
            pltpu.make_async_copy(final.at[:, pl.ds(begin, BX)], target, sems.at[slot]).start()

        @pl.when(jnp.logical_not(live))
        def _():
            pltpu.make_async_copy(zeros, target, sems.at[slot]).start()

    joined[pl.ds(0, home)] = from_left[...]
    joined[pl.ds(home, home)] = gradient[...]
    joined[pl.ds(2 * home, home)] = from_right[...]
    scaled(home, cells, where, drag, joined, slots)
    for slot in range(blocks):
        pltpu.make_async_copy(zeros, out.at[:, pl.ds(slot * BX, BX)], sems.at[slot]).wait()


def body(populations, design, fluid_mask, owner_after):
    count = lax.axis_size("block")
    home, width_y, width_z = design.shape
    slots = home // BX + 2
    span = home + 2 * HALO
    plane = (width_y, width_z)
    vmem = pl.BlockSpec(memory_space=pltpu.VMEM)
    hbm = pl.BlockSpec(memory_space=pltpu.HBM)
    anywhere = pl.BlockSpec(memory_space=pl.ANY)
    smem = pl.BlockSpec(memory_space=pltpu.SMEM)
    cells = float(count * home * width_y * width_z)
    near_pairs = [(i, i ^ 1) for i in range(count)]
    far_pairs = [(i, (i + 1 if i % 2 else i - 1) % count) for i in range(count)]
    inner_pairs = far_pairs[1:-1]

    def planes(*lead, dtype=jnp.float32):
        return jax.ShapeDtypeStruct(lead + plane, dtype)

    def scratch(*lead, dtype=jnp.float32):
        return pltpu.VMEM(lead + plane, dtype)

    def call(kernel, name, ins, outs, scratches, limit, moved, *operands):
        return pl.pallas_call(
            kernel,
            out_shape=[shape for shape, _ in outs],
            in_specs=ins,
            out_specs=[spec for _, spec in outs],
            scratch_shapes=scratches,
            compiler_params=pltpu.CompilerParams(vmem_limit_bytes=limit * MIB),
            cost_estimate=pl.CostEstimate(flops=0, bytes_accessed=moved, transcendentals=0),
            name=name,
        )(*operands)

    populations, design, fluid_mask = [
        pltpu.with_memory_space_constraint(part, pltpu.HBM)
        for part in (populations, design, fluid_mask)
    ]
    own_near, own_far = call(
        functools.partial(edge_kernel, home),
        "edge_planes",
        [hbm] * 3,
        [(planes(20, HALO), vmem)] * 2,
        [scratch(2, HALO), scratch(2, HALO, dtype=jnp.int32), pltpu.SemaphoreType.DMA((6,))],
        4,
        1_000_000,
        populations,
        design,
        fluid_mask,
    )
    far = lax.ppermute(own_far, "block", far_pairs)
    near = lax.ppermute(own_near, "block", near_pairs)

    deep = home - 2 * STEPS
    inner_shapes = (
        planes(16),
        planes(16),
        planes(19, 12),
        planes(16, home),
        planes(19, deep),
        planes(home),
        planes(home, dtype=jnp.int32),
        planes(home, dtype=jnp.int32),
        planes(),
        planes(home),
    )
    to_near, to_far, *inner, drag, marked, where = call(
        functools.partial(interior_kernel, home),
        "interior_steps",
        [smem] + [hbm] * 3,
        [(shape, vmem) for shape in inner_shapes] + [(jax.ShapeDtypeStruct((3,), jnp.int32), smem)],
        [scratch(19, home)] * 3
        + [scratch(home), scratch(home, dtype=jnp.int32), pltpu.SemaphoreType.DMA((3,))],
        16,
        6_000_000,
        owner_after,
        populations,
        design,
        fluid_mask,
    )
    from_far = lax.ppermute(to_far, "block", far_pairs)
    from_near = lax.ppermute(to_near, "block", near_pairs)

    boundary_shapes = (
        planes(19, home + 2 * BX),
        planes(16, span),
        planes(span),
        planes(span, dtype=jnp.int32),
        planes(),
    )
    final, history, opens, words, drag = call(
        functools.partial(boundary_kernel, home),
        "boundary_steps",
        [vmem] * 7 + [anywhere] * 2 + [vmem] * 4,
        [(shape, vmem) for shape in boundary_shapes],
        [
            scratch(19, span + 2),
            scratch(19, span + 2),
            scratch(span + 2, dtype=jnp.int32),
            pltpu.SemaphoreType.DMA((5,)),
        ],
        20,
        8_000_000,
        own_near,
        own_far,
        near,
        far,
        from_near,
        from_far,
        *inner,
        drag,
    )

    distance = 1
    while distance < count:
        swap = [(i, i ^ distance) for i in range(count)]
        drag = drag + lax.ppermute(drag, "block", swap)
        distance *= 2

    gradient, to_near, to_far = call(
        functools.partial(backward_kernel, home),
        "backward_steps",
        [vmem] * 5,
        [(planes(home), vmem), (planes(19 + BX), vmem), (planes(19 + BX), vmem)],
        [scratch(19, span), scratch(19, span), scratch(span)],
        20,
        8_000_000,
        history,
        opens,
        words,
        marked,
        inner[2],
    )
    from_far = lax.ppermute(to_far, "block", inner_pairs)
    from_near = lax.ppermute(to_near, "block", near_pairs)

    def slotted(kernel, name, reach, extra, *operands):
        return call(
            functools.partial(kernel, home, cells),
            name,
            [smem, anywhere if not extra else vmem] + [vmem] * 4,
            [(planes(19, slots * BX), anywhere), (planes(slots * BX), vmem)],
            [scratch(home + 2 * reach)]
            + extra
            + [scratch(19, BX), pltpu.SemaphoreType.DMA((slots,))],
            10,
            4_000_000,
            *operands,
        )

    def near_slots(*operands):
        return slotted(near_kernel, "near_slots", BX, [scratch(2, 19, BX)], *operands)

    def far_slots(where, final, drag, gradient, *_):
        own = final[:, BX : BX + home]
        ring = [(i, i + 1) for i in range(count - 1)]
        back = [(i + 1, i) for i in range(count - 1)]
        wide = [lax.ppermute(own, "block", route) for route in (ring, back)]
        slopes = [lax.ppermute(gradient, "block", route) for route in (ring, back)]
        joined = jnp.concatenate([wide[0], own, wide[1]], axis=1)
        return slotted(far_kernel, "far_slots", home, [], where, joined, drag, gradient, *slopes)

    operands = (where, final, drag, gradient, from_near, from_far)
    return tuple(lax.cond(where[2] > 0, far_slots, near_slots, *operands))


def solution(mesh):
    placed = (
        P(None, ("group", "block"), None, None),
        P(("group", "block"), None, None),
        P(("group", "block"), None, None),
        P("group"),
    )
    return jax.shard_map(
        body,
        mesh=mesh,
        in_specs=placed,
        out_specs=(P(None, ("group", "block"), None, None), P(("group", "block"), None, None)),
        check_vma=False,
    )
```

```python
import functools
import math

import jax
import jax.numpy as jnp
from jax import lax
from jax.experimental import pallas as pl
from jax.experimental.pallas import tpu as pltpu
from jax.sharding import PartitionSpec as P

BX = 4
STEPS = 3
HALO = STEPS
RAW = HALO - 1
MIB = 2**20

VELOCITY = (
    (0, 0, 0),
    (1, 0, 0),
    (-1, 0, 0),
    (0, 1, 0),
    (0, -1, 0),
    (0, 0, 1),
    (0, 0, -1),
    (1, 1, 0),
    (-1, -1, 0),
    (1, -1, 0),
    (-1, 1, 0),
    (1, 0, 1),
    (-1, 0, -1),
    (1, 0, -1),
    (-1, 0, 1),
    (0, 1, 1),
    (0, -1, -1),
    (0, 1, -1),
    (0, -1, 1),
)
OPP = (0,) + tuple(m + 1 if m % 2 else m - 1 for m in range(1, 19))
AHEAD = tuple(m for m in range(19) if VELOCITY[m][0] == 1)
BEHIND = tuple(m for m in range(19) if VELOCITY[m][0] == -1)
FORCE = 0.02
ROOT_45 = math.sqrt(4.5)
ROOT_2 = math.sqrt(2.0)


def rolled(field, step_y, step_z):
    if step_y:
        field = pltpu.roll(field, step_y % field.shape[0], 0)
    if step_z:
        field = pltpu.roll(field, step_z % field.shape[1], 1)
    return field


def pairs(values):
    plus = [values[2 * k + 1] + values[2 * k + 2] for k in range(9)]
    minus = [values[2 * k + 1] - values[2 * k + 2] for k in range(9)]
    return plus, minus


def first_moments(minus, scale):
    along_x, along_y, along_z = minus[:3]
    if scale != 1.0:
        along_x, along_y, along_z = scale * along_x, scale * along_y, scale * along_z
    along_x = along_x + ((minus[3] + minus[4]) + (minus[5] + minus[6]))
    along_y = along_y + ((minus[3] - minus[4]) + (minus[7] + minus[8]))
    along_z = along_z + ((minus[5] - minus[6]) + (minus[7] - minus[8]))
    return along_x, along_y, along_z


def density_velocity(state):
    plus, minus = pairs(state)
    axes = (plus[0] + plus[1]) + (plus[2] + state[0])
    diagonals = (plus[3] + plus[4]) + (plus[5] + plus[6]) + (plus[7] + plus[8])
    density = axes + diagonals
    inverse = 1.0 / density
    momentum = first_moments(minus, 1.0)
    return density, [part * inverse for part in momentum]


def collide(state, density, flow, open_rate):
    rate = ROOT_45 * open_rate
    x, y, z = (flow[0] + FORCE) * rate, flow[1] * rate, flow[2] * rate
    xx, yy, zz = x * x, y * y, z * z
    base = 1.0 - (xx + yy + zz) * (1.0 / 3.0)
    axis_weight = density * (1.2 / 18.0)
    axis_slope = density * (1.2 * ROOT_2 / 18.0)
    side_weight = density * (1.2 / 36.0)
    side_slope = density * (1.2 * ROOT_2 / 36.0)
    result = [density * 0.4 * base - 0.2 * state[0]]
    for k, along in enumerate((x, y, z, x + y, x - y, x + z, x - z, y + z, y - z)):
        if k < 3:
            even = axis_weight * (base + (xx, yy, zz)[k])
            odd = axis_slope * along
        else:
            even = side_weight * (base + along * along)
            odd = side_slope * along
        result.append((even + odd) - 0.2 * state[2 * k + 1])
        result.append((even - odd) - 0.2 * state[2 * k + 2])
    return result


def spread(level, slope):
    x, y, z = slope
    result = [level]
    for along in (x, y, z, x + y, x - y, x + z, x - z, y + z, y - z):
        result.append(level + along)
        result.append(level - along)
    return result


def pull(source, plane, word):
    here = [source[m, plane] for m in range(19)]
    result = [here[0]]
    for m in range(1, 19):
        step_x, step_y, step_z = VELOCITY[m]
        moved = here[m] if step_x == 0 else source[m, plane - step_x]
        moved = rolled(moved, step_y, step_z)
        result.append(jnp.where((word & (1 << m)) != 0, moved, here[OPP[m]]))
    return result


def link_word(behind, here, ahead):
    rows = lax.broadcasted_iota(jnp.int32, here.shape, 0)
    columns = lax.broadcasted_iota(jnp.int32, here.shape, 1)
    joined = behind + 2 * here + 4 * ahead
    word = jnp.zeros_like(here)
    for step_y in (-1, 0, 1):
        for step_z in (-1, 0, 1):
            if step_y and step_z:
                inner = {0: 1}
            else:
                inner = {1: 0, 0: 1, -1: 2}
            near = rolled(joined, step_y, step_z)
            if step_y == 1:
                near = jnp.where(rows == 0, 0, near)
            if step_y == -1:
                near = jnp.where(rows == here.shape[0] - 1, 0, near)
            if step_z == 1:
                near = jnp.where(columns == 0, 0, near)
            if step_z == -1:
                near = jnp.where(columns == here.shape[1] - 1, 0, near)
            for step_x, place in inner.items():
                if (step_x, step_y, step_z) == (0, 0, 0):
                    continue
                m = VELOCITY.index((step_x, step_y, step_z))
                word = word | ((near & (1 << place)) << (m - place))
    return jnp.where(here > 0, word, 0)


def each_plane(low, high, body):
    def two(index, carry):
        body(low + 2 * index)
        body(low + 2 * index + 1)
        return carry

    lax.fori_loop(0, (high - low) // 2, two, 0)
    if (high - low) % 2:
        body(high - 1)


def is_fluid_rate(mark):
    design = jnp.maximum(mark, 0.0)
    return (mark >= 0.0).astype(jnp.int32), (1.0 + 4.0 * design) / (1.6 + 3.4 * design)


def store(target, plane, values):
    for m, part in enumerate(values):
        target[m, plane] = part


def remember(history, step, plane, density, flow):
    history[4 * step, plane] = density
    for axis in range(3):
        history[4 * step + 1 + axis, plane] = flow[axis]


def drag_terms(flow, open_rate):
    return (flow[0] * flow[0] + flow[1] * flow[1] + flow[2] * flow[2]) / open_rate


def parity(axis="block"):
    return 1 - lax.rem(lax.axis_index(axis), 2)


def pick(flag, yes, no):
    return no + flag * (yes - no)


def edge_kernel(home, pops, design, mask, near, far, third, designs, masks, sems):
    up = parity()
    copies = []
    for side, (out, ahead) in enumerate(((near, up), (far, 1 - up))):
        first = ahead * (home - HALO)
        whole = ahead * (home - RAW)
        copies.append(
            [
                pltpu.make_async_copy(
                    pops.at[:, pl.ds(whole, RAW)], out.at[pl.ds(0, 19)], sems.at[4 * side]
                ),
                pltpu.make_async_copy(
                    pops.at[:, pl.ds(first + RAW * (1 - ahead), 1)], third.at[side], sems.at[4 * side + 1]
                ),
                pltpu.make_async_copy(
                    design.at[pl.ds(first, HALO)], designs.at[side], sems.at[4 * side + 2]
                ),
                pltpu.make_async_copy(mask.at[pl.ds(first, HALO)], masks.at[side], sems.at[4 * side + 3]),
            ]
        )
    for side in copies:
        for copy in side:
            copy.start()
    for side, (out, ahead) in enumerate(((near, up), (far, 1 - up))):
        for copy in copies[side][1:]:
            copy.wait()

        def mark(plane):
            return jnp.where(masks[side, plane] > 0, designs[side, plane], -1.0)

        for plane in range(RAW):
            out[19, plane] = mark(ahead + plane)
        last = mark(RAW * (1 - ahead))
        out[22, 1] = last
        _, open_rate = is_fluid_rate(last)
        state = [third[side, m, 0] for m in range(19)]
        density, flow = density_velocity(state)
        collided = collide(state, density, flow, open_rate)
        for slot in range(5):
            value = jnp.where(ahead > 0, collided[AHEAD[slot]], collided[BEHIND[slot]])
            out[20 + slot // 2, slot % 2] = value
    for side in copies:
        side[0].wait()


def count_kernel(home_blocks, owner, where):
    rank = lax.axis_index("block")

    def count(block, carry):
        below, own = carry
        holder = owner[block]
        return below + (holder < rank).astype(jnp.int32), own + (holder == rank).astype(jnp.int32)

    def stray(device, found):
        late = owner[home_blocks * device + 1] < device
        early = owner[home_blocks * device + home_blocks - 2] > device
        return found | late.astype(jnp.int32) | early.astype(jnp.int32)

    below, own = lax.fori_loop(0, owner.shape[0], count, (jnp.int32(0), jnp.int32(0)))
    where[0] = below - home_blocks * rank
    where[1] = own
    where[2] = lax.fori_loop(0, owner.shape[0] // home_blocks, stray, jnp.int32(0))


def interior_kernel(
    home,
    own_near,
    pops_far,
    design,
    mask,
    to_near,
    to_far,
    edges,
    history,
    final,
    opens,
    fluid,
    words,
    drag,
    marked,
    pops,
    designs,
    masks,
    even,
    odd,
    sems,
):
    del own_near
    up = parity()
    copies = [
        pltpu.make_async_copy(source, target, sems.at[place])
        for place, (source, target) in enumerate(((pops_far, pops), (design, designs), (mask, masks)))
    ]
    for copy in copies:
        copy.start()
    for copy in copies:
        copy.wait()

    def start(plane):
        mark = jnp.where(masks[plane] > 0, designs[plane], -1.0)
        marked[plane] = mark
        fluid[plane], open_rate = is_fluid_rate(mark)
        opens[plane] = open_rate
        state = [pops[m, plane] for m in range(19)]
        density, flow = density_velocity(state)
        remember(history, 0, plane, density, flow)
        store(even, plane, collide(state, density, flow, open_rate))

    def link(plane):
        words[plane] = link_word(fluid[plane - 1], fluid[plane], fluid[plane + 1])

    def advance(step, source, target, plane):
        state = pull(source, plane, words[plane])
        density, flow = density_velocity(state)
        remember(history, step, plane, density, flow)
        store(target, plane, collide(state, density, flow, opens[plane]))

    def finish(plane):
        state = pull(even, plane, words[plane])
        density, flow = density_velocity(state)
        remember(history, 3, plane, density, flow)
        here = fluid[plane] > 0
        for m in range(19):
            final[m, plane] = jnp.where(here, state[m], pops[m, plane])
        drag[...] += jnp.where(here, drag_terms(flow, opens[plane]), 0.0)

    def keep(step, source):
        for m in range(19):
            for side in range(2):
                edges[m, 4 * step + side] = source[m, step + side]
                edges[m, 4 * step + 2 + side] = source[m, home - 2 - step + side]

    def send(out, ahead, step, source):
        outer = ahead * (home - 1) + (1 - 2 * ahead) * RAW
        if step == 1:
            for slot in range(5):
                out[slot] = source[AHEAD[slot] + 1 - ahead, outer]
            return
        inner = ahead * (home - 1) + (1 - 2 * ahead) * HALO
        here = fluid[outer] > 0
        for slot in range(5):
            out[5 + slot] = source[AHEAD[slot] + 1 - ahead, inner]
        for m in range(19):
            out[10 + m] = jnp.where(here, source[m, outer], pops[m, outer])
        out[29] = marked[inner]

    drag[...] = jnp.zeros_like(drag)
    each_plane(0, home, start)
    keep(0, even)
    each_plane(1, home - 1, link)
    each_plane(1, home - 1, functools.partial(advance, 1, even, odd))
    keep(1, odd)
    each_plane(2, home - 2, functools.partial(advance, 2, odd, even))
    keep(2, even)
    for out, ahead in ((to_near, up), (to_far, 1 - up)):
        send(out, ahead, 1, odd)
        send(out, ahead, 2, even)
    each_plane(3, home - 3, finish)
    for m in range(19):
        for plane in range(STEPS):
            final[m, plane] = pops[m, plane]
            final[m, home - STEPS + plane] = pops[m, home - STEPS + plane]
        for out, ahead in ((to_near, up), (to_far, 1 - up)):
            out[30 + m] = final[m, STEPS + ahead * (home - 1 - 2 * STEPS)]


def boundary_kernel(
    home,
    near,
    far,
    edges,
    inner_history,
    inner_final,
    inner_opens,
    inner_fluid,
    inner_words,
    inner_drag,
    final,
    history,
    opens,
    fluid,
    words,
    drag,
    even,
    odd,
    sems,
):
    span = home + 2 * HALO
    up = parity()
    sides = ((up, near), (1 - up, far))
    copies = [
        pltpu.make_async_copy(
            inner_history.at[pl.ds(4 * step, 4), pl.ds(step, home - 2 * step)],
            history.at[pl.ds(4 * step, 4), pl.ds(HALO + step, home - 2 * step)],
            sems.at[step],
        )
        for step in range(4)
    ]
    copies.append(
        pltpu.make_async_copy(
            inner_final.at[:, pl.ds(STEPS, home - 2 * STEPS)],
            final.at[:, pl.ds(STEPS, home - 2 * STEPS)],
            sems.at[4],
        )
    )
    for copy in copies:
        copy.start()

    for plane in range(home):
        fluid[plane + HALO] = inner_fluid[plane]
        opens[plane + HALO] = inner_opens[plane]
    for plane in range(1, home - 1):
        words[plane + HALO] = inner_words[plane]
    for ahead, side in sides:
        fluid[ahead * (span - 1)], opens[ahead * (span - 1)] = is_fluid_rate(side[22, 1])
        for slot in range(5):
            even[AHEAD[slot] + ahead, ahead * (span - 1)] = side[20 + slot // 2, slot % 2]

    def start(plane, carry):
        for ahead, side in sides:
            index = plane + 1 + ahead * (home + RAW)
            fluid[index], open_rate = is_fluid_rate(side[19, plane])
            opens[index] = open_rate
            state = [side[m, plane] for m in range(19)]
            density, flow = density_velocity(state)
            store(even, index, collide(state, density, flow, open_rate))
        return carry

    lax.fori_loop(0, RAW, start, 0)

    def receive(step, target):
        for m in range(19):
            for side in range(2):
                target[m, HALO + step + side] = edges[m, 4 * step + side]
                target[m, HALO + home - 2 - step + side] = edges[m, 4 * step + 2 + side]

    def both(step, body):
        def two(place, carry):
            body(step + place, place, 0)
            body(span - 3 - step + place, place, 1)
            return carry

        lax.fori_loop(0, 3, two, 0)

    def link(index, place, ahead):
        words[index] = link_word(fluid[index - 1], fluid[index], fluid[index + 1])

    def advance(step, source, target, index, place, ahead):
        state = pull(source, index, words[index])
        density, flow = density_velocity(state)
        remember(history, step, index, density, flow)
        store(target, index, collide(state, density, flow, opens[index]))

    both(1, link)
    receive(0, even)
    both(1, functools.partial(advance, 1, even, odd))
    receive(1, odd)
    both(2, functools.partial(advance, 2, odd, even))
    receive(2, even)
    drag[...] = inner_drag[...]

    def finish(index, place, ahead):
        state = pull(even, index, words[index])
        density, flow = density_velocity(state)
        remember(history, 3, index, density, flow)
        here = fluid[index] > 0
        for m in range(19):
            final[m, index - HALO] = jnp.where(here, state[m], inner_final[m, index - HALO])
        drag[...] += jnp.where(here, drag_terms(flow, opens[index]), 0.0)

    both(3, finish)
    for copy in copies:
        copy.wait()


def backward_kernel(
    home,
    history,
    opens,
    fluid,
    words,
    even_state,
    odd_state,
    near,
    far,
    from_near,
    from_far,
    marked,
    summed,
    gradient,
    outer,
    to_near,
    to_far,
    even,
    odd,
    share,
    first,
    second,
    second_flow,
):
    del summed
    span = home + 2 * HALO
    up = parity()

    def recall(step, plane):
        return history[4 * step, plane], [history[4 * step + 1 + axis, plane] for axis in range(3)]

    def seed(plane, density, flow):
        damping = 1.0 / opens[plane]
        square = flow[0] * flow[0] + flow[1] * flow[1] + flow[2] * flow[2]
        share[plane] = -square * damping
        factor = 2.0 * damping / density
        slope = [part * factor for part in flow]
        values = spread(-square * factor, slope)
        for m in range(19):
            even[OPP[m], plane] = values[m]

    for ahead, raw, message in ((up, near, from_near), (1 - up, far, from_far)):
        one = first.at[ahead]
        for m in range(19):
            for place in range(HALO):
                one[m, place] = odd_state[m, ahead * (span - HALO) + place]
        for slot in range(5):
            one[AHEAD[slot] + ahead, ahead * RAW] = message[slot]
        index = 1 + ahead * (span - 3)
        state = pull(one, 1, words[index])
        density, flow = density_velocity(state)
        for place, part in enumerate([density] + flow):
            second_flow[ahead, place] = part
        two = second.at[ahead]
        store(two, 2, collide(state, density, flow, opens[index]))
        for m in range(19):
            for place in range(2):
                two[m, 3 - 3 * ahead + place] = even_state[m, 2 + ahead * (span - 6) + place]
            two[m, 1 + 2 * ahead] = message[10 + m]
        for slot in range(5):
            two[AHEAD[slot] + ahead, 4 * ahead] = message[5 + slot]
        beyond = (message[29] >= 0.0).astype(jnp.int32)
        within = fluid[1 + ahead * (span - 3)]
        edge_word = link_word(
            beyond + ahead * (within - beyond),
            fluid[ahead * (span - 1)],
            within + ahead * (beyond - within),
        )
        for place in range(HALO):
            spot = 1 + place
            index = place + ahead * (span - 3)
            word = words[index] if place == 1 else None
            if place == 0:
                word = edge_word + ahead * (words[index] - edge_word)
            if place == 2:
                word = words[index] + ahead * (edge_word - words[index])
            state = pull(two, spot, word)
            density, flow = density_velocity(state)
            seed(index, density, flow)
            here = fluid[index] > 0
            for m in range(19):
                if place == 1:
                    initial = raw[m, ahead]
                else:
                    kept = two[m, spot]
                    initial = jnp.where((ahead > 0) == (place == 2), kept, raw[m, place // 2])
                outer[ahead, m, spot - ahead] = jnp.where(here, state[m], initial)
        for m in range(19):
            outer[ahead, m, ahead * (BX - 1)] = message[30 + m]

    def seed_home(plane):
        seed(plane, *recall(STEPS, plane))

    each_plane(HALO, HALO + home, seed_home)

    def retreat(step, source, target, plane, recalled=None):
        mirrored = pull(source, plane, words[plane])
        adjoint = [mirrored[OPP[m]] for m in range(19)]
        density, flow = recalled or recall(step, plane)
        open_rate = opens[plane]
        force_flow = [flow[0] + FORCE, flow[1], flow[2]]
        x, y, z = [open_rate * part for part in force_flow]
        plus, minus = pairs(adjoint)
        mx, my, mz = [part * (1.0 / 12.0) for part in first_moments(minus, 2.0)]
        xy_plus, xz_plus, yz_plus = plus[3] + plus[4], plus[5] + plus[6], plus[7] + plus[8]
        axes = [2.0 * plus[k] for k in range(3)]
        whole = 12.0 * adjoint[0] + (axes[0] + axes[1] + axes[2]) + (xy_plus + xz_plus + yz_plus)
        third = whole * (1.0 / 3.0)
        xx = axes[0] + (xy_plus + xz_plus) - third
        yy = axes[1] + (xy_plus + yz_plus) - third
        zz = axes[2] + (xz_plus + yz_plus) - third
        xy, xz, yz = plus[3] - plus[4], plus[5] - plus[6], plus[7] - plus[8]
        hx = 0.25 * (xx * x + xy * y + xz * z)
        hy = 0.25 * (xy * x + yy * y + yz * z)
        hz = 0.25 * (xz * x + yz * y + zz * z)
        rate = 1.2 * open_rate
        slope = [rate * (mx + hx), rate * (my + hy), rate * (mz + hz)]
        pushed = slope[0] * force_flow[0] + slope[1] * force_flow[1] + slope[2] * force_flow[2]
        share[plane] += density * pushed
        if target is None:
            return
        level = whole * (1.2 / 36.0) + 1.2 * (
            x * (mx + 0.5 * hx) + y * (my + 0.5 * hy) + z * (mz + 0.5 * hz)
        )
        level = level - (slope[0] * flow[0] + slope[1] * flow[1] + slope[2] * flow[2])
        values = spread(level, slope)
        for m in range(19):
            target[OPP[m], plane] = values[m] - 0.2 * adjoint[m]

    for side in range(2):
        recalled = second_flow[side, 0], [second_flow[side, 1 + axis] for axis in range(3)]
        retreat(2, even, odd, 1 + side * (span - 3), recalled)
    each_plane(HALO - 1, HALO + home + 1, functools.partial(retreat, 2, even, odd))
    each_plane(HALO - 1, HALO + home + 1, functools.partial(retreat, 1, odd, even))
    each_plane(HALO, HALO + home, functools.partial(retreat, 0, even, None))

    for plane in range(home):
        design = marked[plane]
        slope = 3.0 / ((1.6 + 3.4 * design) * (1.0 + 4.0 * design))
        gradient[plane] = jnp.where(design >= 0.0, share[plane + HALO] * slope, 0.0)
    for out, ahead in ((to_near, up), (to_far, 1 - up)):
        for plane in range(BX):
            out[plane] = gradient[ahead * (home - BX) + plane]


def scaled(home, cells, where, drag, joined, out):
    factor = cells / jnp.sum(drag[...])
    reach = (joined.shape[0] - home) // 2
    for plane in range(out.shape[0]):
        spot = jnp.clip(where[0] * BX + reach + plane, 0, joined.shape[0] - 1)
        live = plane < where[1] * BX
        out[plane] = jnp.where(live, joined[spot] * factor, 0.0)


def near_gradient(home, cells, where, drag, gradient, from_near, from_far, out, joined):
    up = parity()
    for ahead, message in ((up, from_near), (1 - up, from_far)):
        joined[pl.ds(ahead * (BX + home), BX)] = message[...]
    joined[pl.ds(BX, home)] = gradient[...]
    scaled(home, cells, where, drag, joined, out)


def far_gradient(home, cells, where, drag, gradient, from_left, from_right, out, joined):
    joined[pl.ds(0, home)] = from_left[...]
    joined[pl.ds(home, home)] = gradient[...]
    joined[pl.ds(2 * home, home)] = from_right[...]
    scaled(home, cells, where, drag, joined, out)


def place_kernel(where, final, outer, out, zeros, sems):
    blocks = out.shape[1] // BX
    home_blocks = final.shape[1] // BX
    beyond = outer.shape[2] // BX
    zeros[...] = jnp.zeros_like(zeros)
    for slot in range(blocks):
        target = out.at[:, pl.ds(slot * BX, BX)]
        live = slot < where[1]
        block = jnp.clip(where[0] + slot, -beyond, home_blocks + beyond - 1)
        inside = (block >= 0) & (block < home_blocks)

        @pl.when(live & inside)
        def _():
            source = final.at[:, pl.ds(block * BX, BX)]
            pltpu.make_async_copy(source, target, sems.at[slot]).start()

        @pl.when(live & jnp.logical_not(inside))
        def _():
            after = (block >= 0).astype(jnp.int32)
            within = block + beyond - after * (home_blocks + beyond)
            source = outer.at[after, :, pl.ds(within * BX, BX)]
            pltpu.make_async_copy(source, target, sems.at[slot]).start()

        @pl.when(jnp.logical_not(live))
        def _():
            pltpu.make_async_copy(zeros, target, sems.at[slot]).start()

    for slot in range(blocks):
        pltpu.make_async_copy(zeros, out.at[:, pl.ds(slot * BX, BX)], sems.at[slot]).wait()


def body(populations, design, fluid_mask, owner_after):
    count = lax.axis_size("block")
    home, width_y, width_z = design.shape
    home_blocks = home // BX
    slots = home_blocks + 2
    span = home + 2 * HALO
    plane = (width_y, width_z)
    vmem = pl.BlockSpec(memory_space=pltpu.VMEM)
    hbm = pl.BlockSpec(memory_space=pltpu.HBM)
    anywhere = pl.BlockSpec(memory_space=pl.ANY)
    smem = pl.BlockSpec(memory_space=pltpu.SMEM)
    cells = float(count * home * width_y * width_z)
    near_pairs = [(i, i ^ 1) for i in range(count)]
    far_pairs = [(i, (i + 1 if i % 2 else i - 1) % count) for i in range(count)]
    inner_pairs = far_pairs[1:-1]

    def planes(*lead, dtype=jnp.float32):
        return jax.ShapeDtypeStruct(lead + plane, dtype)

    def scratch(*lead, dtype=jnp.float32):
        return pltpu.VMEM(lead + plane, dtype)

    def call(kernel, name, ins, outs, scratches, limit, moved, *operands):
        return pl.pallas_call(
            kernel,
            out_shape=[shape for shape, _ in outs],
            in_specs=ins,
            out_specs=[spec for _, spec in outs],
            scratch_shapes=scratches,
            compiler_params=pltpu.CompilerParams(vmem_limit_bytes=limit * MIB),
            cost_estimate=pl.CostEstimate(flops=20 * moved, bytes_accessed=moved, transcendentals=0),
            name=name,
        )(*operands)

    populations, design, fluid_mask = [
        pltpu.with_memory_space_constraint(part, pltpu.HBM)
        for part in (populations, design, fluid_mask)
    ]
    own_near, own_far = call(
        functools.partial(edge_kernel, home),
        "edge_planes",
        [hbm] * 3,
        [(planes(23, RAW), vmem)] * 2,
        [
            scratch(2, 19, 1),
            scratch(2, HALO),
            scratch(2, HALO, dtype=jnp.int32),
            pltpu.SemaphoreType.DMA((8,)),
        ],
        4,
        1_000_000,
        populations,
        design,
        fluid_mask,
    )
    far = lax.ppermute(own_far, "block", far_pairs)
    near = lax.ppermute(own_near, "block", near_pairs)

    inner_shapes = (
        planes(49),
        planes(49),
        planes(19, 12),
        planes(16, home),
        planes(19, home),
        planes(home),
        planes(home, dtype=jnp.int32),
        planes(home, dtype=jnp.int32),
        planes(),
        planes(home),
    )
    (
        to_near,
        to_far,
        edges,
        inner_history,
        inner_final,
        inner_opens,
        inner_fluid,
        inner_words,
        inner_drag,
        marked,
    ) = call(
        functools.partial(interior_kernel, home),
        "interior_steps",
        [anywhere] + [hbm] * 3,
        [(shape, vmem) for shape in inner_shapes],
        [scratch(19, home), scratch(home), scratch(home, dtype=jnp.int32)]
        + [scratch(19, home)] * 2
        + [pltpu.SemaphoreType.DMA((3,))],
        16,
        6_000_000,
        own_near,
        populations,
        design,
        fluid_mask,
    )
    from_far = lax.ppermute(to_far, "block", far_pairs)
    from_near = lax.ppermute(to_near, "block", near_pairs)

    (where,) = call(
        functools.partial(count_kernel, home_blocks),
        "slot_counts",
        [smem],
        [(jax.ShapeDtypeStruct((3,), jnp.int32), smem)],
        [],
        2,
        20_000_000,
        owner_after,
    )

    boundary_shapes = (
        planes(19, home),
        planes(16, span),
        planes(span),
        planes(span, dtype=jnp.int32),
        planes(span, dtype=jnp.int32),
        planes(),
        planes(19, span),
        planes(19, span),
    )
    final, history, opens, fluid, words, drag, even_state, odd_state = call(
        functools.partial(boundary_kernel, home),
        "boundary_steps",
        [vmem] * 3 + [anywhere] + [vmem] * 5,
        [(shape, vmem) for shape in boundary_shapes],
        [pltpu.SemaphoreType.DMA((5,))],
        20,
        8_000_000,
        near,
        far,
        edges,
        inner_history,
        inner_final,
        inner_opens,
        inner_fluid,
        inner_words,
        inner_drag,
    )

    sums = [drag]
    distance = 1
    while distance < count:
        swap = [(i, i ^ distance) for i in range(count)]
        sums.append(sums[-1] + lax.ppermute(sums[-1], "block", swap))
        distance *= 2
    drag = sums[-1]

    gradient, outer, to_near, to_far = call(
        functools.partial(backward_kernel, home),
        "backward_steps",
        [vmem] * 11 + [anywhere],
        [(planes(home), vmem), (planes(2, 19, BX), vmem), (planes(BX), vmem), (planes(BX), vmem)],
        [
            scratch(19, span),
            scratch(19, span),
            scratch(span),
            scratch(2, 19, HALO),
            scratch(2, 19, HALO + 2),
            scratch(2, 4),
        ],
        20,
        8_000_000,
        history,
        opens,
        fluid,
        words,
        even_state,
        odd_state,
        near,
        far,
        from_near,
        from_far,
        marked,
        sums[1],
    )
    from_far = lax.ppermute(to_far, "block", inner_pairs)
    from_near = lax.ppermute(to_near, "block", near_pairs)

    ring = [(i, i + 1) for i in range(count - 1)]
    back = [(i + 1, i) for i in range(count - 1)]

    def place(outer):
        (out,) = call(
            place_kernel,
            "place_populations",
            [smem, anywhere, anywhere],
            [(planes(19, slots * BX), anywhere)],
            [scratch(19, BX), pltpu.SemaphoreType.DMA((slots,))],
            8,
            4_000_000,
            where,
            final,
            outer,
        )
        return out

    def place_far(_):
        wide = [lax.ppermute(final, "block", route) for route in (ring, back)]
        return place(jnp.stack(wide))

    def slope(kernel, name, reach, *messages):
        (out,) = call(
            functools.partial(kernel, home, cells),
            name,
            [smem] + [vmem] * 4,
            [(planes(slots * BX), vmem)],
            [scratch(home + 2 * reach)],
            4,
            1_000_000,
            where,
            drag,
            gradient,
            *messages,
        )
        return out

    def slope_near(*messages):
        return slope(near_gradient, "near_gradient", BX, *messages)

    def slope_far(*_):
        wide = [lax.ppermute(gradient, "block", route) for route in (ring, back)]
        return slope(far_gradient, "far_gradient", home, *wide)

    is_far = where[2] > 0
    populations_after = lax.cond(is_far, place_far, place, outer)
    sensitivity = lax.cond(is_far, slope_far, slope_near, from_near, from_far)
    return (populations_after, sensitivity)


def solution(mesh):
    placed = (
        P(None, ("group", "block"), None, None),
        P(("group", "block"), None, None),
        P(("group", "block"), None, None),
        P("group"),
    )
    return jax.shard_map(
        body,
        mesh=mesh,
        in_specs=placed,
        out_specs=(P(None, ("group", "block"), None, None), P(("group", "block"), None, None)),
        check_vma=False,
    )
```

```python
import functools
import math

import jax
import jax.numpy as jnp
from jax import lax
from jax.experimental import pallas as pl
from jax.experimental.pallas import tpu as pltpu
from jax.sharding import PartitionSpec as P

BX = 4
STEPS = 3
HALO = STEPS
RAW = HALO - 1
MIB = 2**20

VELOCITY = (
    (0, 0, 0),
    (1, 0, 0),
    (-1, 0, 0),
    (0, 1, 0),
    (0, -1, 0),
    (0, 0, 1),
    (0, 0, -1),
    (1, 1, 0),
    (-1, -1, 0),
    (1, -1, 0),
    (-1, 1, 0),
    (1, 0, 1),
    (-1, 0, -1),
    (1, 0, -1),
    (-1, 0, 1),
    (0, 1, 1),
    (0, -1, -1),
    (0, 1, -1),
    (0, -1, 1),
)
OPP = (0,) + tuple(m + 1 if m % 2 else m - 1 for m in range(1, 19))
AHEAD = tuple(m for m in range(19) if VELOCITY[m][0] == 1)
BEHIND = tuple(m for m in range(19) if VELOCITY[m][0] == -1)
FORCE = 0.02
ROOT_45 = math.sqrt(4.5)
ROOT_2 = math.sqrt(2.0)


def rolled(field, step_y, step_z):
    if step_y:
        field = pltpu.roll(field, step_y % field.shape[0], 0)
    if step_z:
        field = pltpu.roll(field, step_z % field.shape[1], 1)
    return field


def pairs(values):
    plus = [values[2 * k + 1] + values[2 * k + 2] for k in range(9)]
    minus = [values[2 * k + 1] - values[2 * k + 2] for k in range(9)]
    return plus, minus


def first_moments(minus, scale):
    along_x, along_y, along_z = minus[:3]
    if scale != 1.0:
        along_x, along_y, along_z = scale * along_x, scale * along_y, scale * along_z
    along_x = along_x + ((minus[3] + minus[4]) + (minus[5] + minus[6]))
    along_y = along_y + ((minus[3] - minus[4]) + (minus[7] + minus[8]))
    along_z = along_z + ((minus[5] - minus[6]) + (minus[7] - minus[8]))
    return along_x, along_y, along_z


def density_velocity(state):
    plus, minus = pairs(state)
    axes = (plus[0] + plus[1]) + (plus[2] + state[0])
    diagonals = (plus[3] + plus[4]) + (plus[5] + plus[6]) + (plus[7] + plus[8])
    density = axes + diagonals
    inverse = 1.0 / density
    momentum = first_moments(minus, 1.0)
    return density, [part * inverse for part in momentum]


def collide(state, density, flow, open_rate):
    rate = ROOT_45 * open_rate
    x, y, z = (flow[0] + FORCE) * rate, flow[1] * rate, flow[2] * rate
    xx, yy, zz = x * x, y * y, z * z
    base = 1.0 - (xx + yy + zz) * (1.0 / 3.0)
    axis_weight = density * (1.2 / 18.0)
    axis_slope = density * (1.2 * ROOT_2 / 18.0)
    side_weight = density * (1.2 / 36.0)
    side_slope = density * (1.2 * ROOT_2 / 36.0)
    result = [density * 0.4 * base - 0.2 * state[0]]
    for k, along in enumerate((x, y, z, x + y, x - y, x + z, x - z, y + z, y - z)):
        if k < 3:
            even = axis_weight * (base + (xx, yy, zz)[k])
            odd = axis_slope * along
        else:
            even = side_weight * (base + along * along)
            odd = side_slope * along
        result.append((even + odd) - 0.2 * state[2 * k + 1])
        result.append((even - odd) - 0.2 * state[2 * k + 2])
    return result


def spread(level, slope):
    x, y, z = slope
    result = [level]
    for along in (x, y, z, x + y, x - y, x + z, x - z, y + z, y - z):
        result.append(level + along)
        result.append(level - along)
    return result


def pull(source, plane, word):
    here = [source[m, plane] for m in range(19)]
    result = [here[0]]
    for m in range(1, 19):
        step_x, step_y, step_z = VELOCITY[m]
        moved = here[m] if step_x == 0 else source[m, plane - step_x]
        moved = rolled(moved, step_y, step_z)
        result.append(jnp.where((word & (1 << m)) != 0, moved, here[OPP[m]]))
    return result


def link_word(behind, here, ahead):
    rows = lax.broadcasted_iota(jnp.int32, here.shape, 0)
    columns = lax.broadcasted_iota(jnp.int32, here.shape, 1)
    joined = behind + 2 * here + 4 * ahead
    word = jnp.zeros_like(here)
    for step_y in (-1, 0, 1):
        for step_z in (-1, 0, 1):
            if step_y and step_z:
                inner = {0: 1}
            else:
                inner = {1: 0, 0: 1, -1: 2}
            near = rolled(joined, step_y, step_z)
            if step_y == 1:
                near = jnp.where(rows == 0, 0, near)
            if step_y == -1:
                near = jnp.where(rows == here.shape[0] - 1, 0, near)
            if step_z == 1:
                near = jnp.where(columns == 0, 0, near)
            if step_z == -1:
                near = jnp.where(columns == here.shape[1] - 1, 0, near)
            for step_x, place in inner.items():
                if (step_x, step_y, step_z) == (0, 0, 0):
                    continue
                m = VELOCITY.index((step_x, step_y, step_z))
                word = word | ((near & (1 << place)) << (m - place))
    return jnp.where(here > 0, word, 0)


def each_plane(low, high, body):
    def two(index, carry):
        body(low + 2 * index)
        body(low + 2 * index + 1)
        return carry

    lax.fori_loop(0, (high - low) // 2, two, 0)
    if (high - low) % 2:
        body(high - 1)


def is_fluid_rate(mark):
    design = jnp.maximum(mark, 0.0)
    return (mark >= 0.0).astype(jnp.int32), (1.0 + 4.0 * design) / (1.6 + 3.4 * design)


def store(target, plane, values):
    for m, part in enumerate(values):
        target[m, plane] = part


def remember(history, step, plane, density, flow):
    history[4 * step, plane] = density
    for axis in range(3):
        history[4 * step + 1 + axis, plane] = flow[axis]


def drag_terms(flow, open_rate):
    return (flow[0] * flow[0] + flow[1] * flow[1] + flow[2] * flow[2]) / open_rate


def parity(axis="block"):
    return 1 - lax.rem(lax.axis_index(axis), 2)


def pick(flag, yes, no):
    return no + flag * (yes - no)


def edge_kernel(home, pops_far, design, mask, near, far, pops, marked, designs, masks, sems):
    up = parity()
    copies = [
        pltpu.make_async_copy(source, target, sems.at[place])
        for place, (source, target) in enumerate(((pops_far, pops), (design, designs), (mask, masks)))
    ]
    for copy in copies:
        copy.start()
    for copy in copies[1:]:
        copy.wait()
    for plane in range(home):
        marked[plane] = jnp.where(masks[plane] > 0, designs[plane], -1.0)
    copies[0].wait()
    for out, ahead in ((near, up), (far, 1 - up)):
        first = ahead * (home - RAW)
        for plane in range(RAW):
            for m in range(19):
                out[m, plane] = pops[m, first + plane]
            out[19, plane] = marked[first + plane]
        third = ahead * (home - 1) + (1 - 2 * ahead) * RAW
        last = marked[third]
        out[22, 1] = last
        _, open_rate = is_fluid_rate(last)
        state = [pops[m, third] for m in range(19)]
        density, flow = density_velocity(state)
        collided = collide(state, density, flow, open_rate)
        for slot in range(5):
            value = jnp.where(ahead > 0, collided[AHEAD[slot]], collided[BEHIND[slot]])
            out[20 + slot // 2, slot % 2] = value


def count_kernel(home_blocks, owner, where):
    rank = lax.axis_index("block")
    below = jnp.int32(0)
    own = jnp.int32(0)
    for block in range(owner.shape[0]):
        holder = owner[block]
        below += (holder < rank).astype(jnp.int32)
        own += (holder == rank).astype(jnp.int32)
    stray = jnp.int32(0)
    for device in range(owner.shape[0] // home_blocks):
        late = owner[home_blocks * device + 1] < device
        early = owner[home_blocks * device + home_blocks - 2] > device
        stray = stray | late.astype(jnp.int32) | early.astype(jnp.int32)
    where[0] = below - home_blocks * rank
    where[1] = own
    where[2] = stray


def interior_kernel(
    home,
    pops,
    marked,
    to_near,
    to_far,
    edges,
    history,
    final,
    opens,
    fluid,
    words,
    drag,
    even,
    odd,
):
    up = parity()

    def start(plane):
        fluid[plane], open_rate = is_fluid_rate(marked[plane])
        opens[plane] = open_rate
        state = [pops[m, plane] for m in range(19)]
        density, flow = density_velocity(state)
        remember(history, 0, plane, density, flow)
        store(even, plane, collide(state, density, flow, open_rate))

    def link(plane):
        words[plane] = link_word(fluid[plane - 1], fluid[plane], fluid[plane + 1])

    def advance(step, source, target, plane):
        state = pull(source, plane, words[plane])
        density, flow = density_velocity(state)
        remember(history, step, plane, density, flow)
        store(target, plane, collide(state, density, flow, opens[plane]))

    def finish(plane):
        state = pull(even, plane, words[plane])
        density, flow = density_velocity(state)
        remember(history, 3, plane, density, flow)
        here = fluid[plane] > 0
        for m in range(19):
            final[m, plane] = jnp.where(here, state[m], pops[m, plane])
        drag[...] += jnp.where(here, drag_terms(flow, opens[plane]), 0.0)

    def keep(step, source):
        for m in range(19):
            for side in range(2):
                edges[m, 4 * step + side] = source[m, step + side]
                edges[m, 4 * step + 2 + side] = source[m, home - 2 - step + side]

    def send(out, ahead, step, source):
        outer = ahead * (home - 1) + (1 - 2 * ahead) * RAW
        if step == 1:
            for slot in range(5):
                out[slot] = source[AHEAD[slot] + 1 - ahead, outer]
            return
        inner = ahead * (home - 1) + (1 - 2 * ahead) * HALO
        here = fluid[outer] > 0
        for slot in range(5):
            out[5 + slot] = source[AHEAD[slot] + 1 - ahead, inner]
        for m in range(19):
            out[10 + m] = jnp.where(here, source[m, outer], pops[m, outer])
        out[29] = marked[inner]

    drag[...] = jnp.zeros_like(drag)
    each_plane(0, home, start)
    keep(0, even)
    each_plane(1, home - 1, link)
    each_plane(1, home - 1, functools.partial(advance, 1, even, odd))
    keep(1, odd)
    each_plane(2, home - 2, functools.partial(advance, 2, odd, even))
    keep(2, even)
    for out, ahead in ((to_near, up), (to_far, 1 - up)):
        send(out, ahead, 1, odd)
        send(out, ahead, 2, even)
    each_plane(3, home - 3, finish)
    for m in range(19):
        for plane in range(STEPS):
            final[m, plane] = pops[m, plane]
            final[m, home - STEPS + plane] = pops[m, home - STEPS + plane]
        for out, ahead in ((to_near, up), (to_far, 1 - up)):
            out[30 + m] = final[m, STEPS + ahead * (home - 1 - 2 * STEPS)]


def boundary_kernel(
    home,
    near,
    far,
    edges,
    inner_history,
    inner_final,
    inner_opens,
    inner_fluid,
    inner_words,
    inner_drag,
    final,
    history,
    opens,
    fluid,
    words,
    drag,
    even,
    odd,
    sems,
):
    span = home + 2 * HALO
    up = parity()
    sides = ((up, near), (1 - up, far))
    copies = [
        pltpu.make_async_copy(
            inner_history.at[pl.ds(4 * step, 4), pl.ds(step, home - 2 * step)],
            history.at[pl.ds(4 * step, 4), pl.ds(HALO + step, home - 2 * step)],
            sems.at[step],
        )
        for step in range(4)
    ]
    copies.append(
        pltpu.make_async_copy(
            inner_final.at[:, pl.ds(STEPS, home - 2 * STEPS)],
            final.at[:, pl.ds(STEPS, home - 2 * STEPS)],
            sems.at[4],
        )
    )
    for copy in copies:
        copy.start()

    for plane in range(home):
        fluid[plane + HALO] = inner_fluid[plane]
        opens[plane + HALO] = inner_opens[plane]
    for plane in range(1, home - 1):
        words[plane + HALO] = inner_words[plane]
    for ahead, side in sides:
        fluid[ahead * (span - 1)], opens[ahead * (span - 1)] = is_fluid_rate(side[22, 1])
        for slot in range(5):
            even[AHEAD[slot] + ahead, ahead * (span - 1)] = side[20 + slot // 2, slot % 2]

    def start(plane, carry):
        for ahead, side in sides:
            index = plane + 1 + ahead * (home + RAW)
            fluid[index], open_rate = is_fluid_rate(side[19, plane])
            opens[index] = open_rate
            state = [side[m, plane] for m in range(19)]
            density, flow = density_velocity(state)
            store(even, index, collide(state, density, flow, open_rate))
        return carry

    lax.fori_loop(0, RAW, start, 0)

    def receive(step, target):
        for m in range(19):
            for side in range(2):
                target[m, HALO + step + side] = edges[m, 4 * step + side]
                target[m, HALO + home - 2 - step + side] = edges[m, 4 * step + 2 + side]

    def both(step, body):
        def two(place, carry):
            body(step + place, place, 0)
            body(span - 3 - step + place, place, 1)
            return carry

        lax.fori_loop(0, 3, two, 0)

    def link(index, place, ahead):
        words[index] = link_word(fluid[index - 1], fluid[index], fluid[index + 1])

    def advance(step, source, target, index, place, ahead):
        state = pull(source, index, words[index])
        density, flow = density_velocity(state)
        remember(history, step, index, density, flow)
        store(target, index, collide(state, density, flow, opens[index]))

    both(1, link)
    receive(0, even)
    both(1, functools.partial(advance, 1, even, odd))
    receive(1, odd)
    both(2, functools.partial(advance, 2, odd, even))
    receive(2, even)
    drag[...] = inner_drag[...]

    def finish(index, place, ahead):
        state = pull(even, index, words[index])
        density, flow = density_velocity(state)
        remember(history, 3, index, density, flow)
        here = fluid[index] > 0
        for m in range(19):
            final[m, index - HALO] = jnp.where(here, state[m], inner_final[m, index - HALO])
        drag[...] += jnp.where(here, drag_terms(flow, opens[index]), 0.0)

    both(3, finish)
    for copy in copies:
        copy.wait()


def recall(history, step, plane):
    return history[4 * step, plane], [history[4 * step + 1 + axis, plane] for axis in range(3)]


def retreat(opens, words, share, source, target, plane, density, flow):
    mirrored = pull(source, plane, words[plane])
    adjoint = [mirrored[OPP[m]] for m in range(19)]
    open_rate = opens[plane]
    force_flow = [flow[0] + FORCE, flow[1], flow[2]]
    x, y, z = [open_rate * part for part in force_flow]
    plus, minus = pairs(adjoint)
    mx, my, mz = [part * (1.0 / 12.0) for part in first_moments(minus, 2.0)]
    xy_plus, xz_plus, yz_plus = plus[3] + plus[4], plus[5] + plus[6], plus[7] + plus[8]
    axes = [2.0 * plus[k] for k in range(3)]
    whole = 12.0 * adjoint[0] + (axes[0] + axes[1] + axes[2]) + (xy_plus + xz_plus + yz_plus)
    third = whole * (1.0 / 3.0)
    xx = axes[0] + (xy_plus + xz_plus) - third
    yy = axes[1] + (xy_plus + yz_plus) - third
    zz = axes[2] + (xz_plus + yz_plus) - third
    xy, xz, yz = plus[3] - plus[4], plus[5] - plus[6], plus[7] - plus[8]
    hx = 0.25 * (xx * x + xy * y + xz * z)
    hy = 0.25 * (xy * x + yy * y + yz * z)
    hz = 0.25 * (xz * x + yz * y + zz * z)
    rate = 1.2 * open_rate
    slope = [rate * (mx + hx), rate * (my + hy), rate * (mz + hz)]
    pushed = slope[0] * force_flow[0] + slope[1] * force_flow[1] + slope[2] * force_flow[2]
    share[plane] += density * pushed
    if target is None:
        return
    level = whole * (1.2 / 36.0) + 1.2 * (
        x * (mx + 0.5 * hx) + y * (my + 0.5 * hy) + z * (mz + 0.5 * hz)
    )
    level = level - (slope[0] * flow[0] + slope[1] * flow[1] + slope[2] * flow[2])
    values = spread(level, slope)
    for m in range(19):
        target[OPP[m], plane] = values[m] - 0.2 * adjoint[m]


def outer_kernel(
    home,
    history,
    opens,
    fluid,
    words,
    even_state,
    odd_state,
    near,
    far,
    from_near,
    from_far,
    summed,
    counted,
    outer,
    share,
    odd,
    even,
    first,
    second,
    second_flow,
):
    del summed, counted
    span = home + 2 * HALO
    up = parity()

    def seed(plane, density, flow):
        damping = 1.0 / opens[plane]
        square = flow[0] * flow[0] + flow[1] * flow[1] + flow[2] * flow[2]
        share[plane] = -square * damping
        factor = 2.0 * damping / density
        slope = [part * factor for part in flow]
        values = spread(-square * factor, slope)
        for m in range(19):
            even[OPP[m], plane] = values[m]

    for ahead, raw, message in ((up, near, from_near), (1 - up, far, from_far)):
        one = first.at[ahead]
        for m in range(19):
            for place in range(HALO):
                one[m, place] = odd_state[m, ahead * (span - HALO) + place]
        for slot in range(5):
            one[AHEAD[slot] + ahead, ahead * RAW] = message[slot]
        index = 1 + ahead * (span - 3)
        state = pull(one, 1, words[index])
        density, flow = density_velocity(state)
        for place, part in enumerate([density] + flow):
            second_flow[ahead, place] = part
        two = second.at[ahead]
        store(two, 2, collide(state, density, flow, opens[index]))
        for m in range(19):
            for place in range(2):
                two[m, 3 - 3 * ahead + place] = even_state[m, 2 + ahead * (span - 6) + place]
            two[m, 1 + 2 * ahead] = message[10 + m]
        for slot in range(5):
            two[AHEAD[slot] + ahead, 4 * ahead] = message[5 + slot]
        beyond = (message[29] >= 0.0).astype(jnp.int32)
        within = fluid[1 + ahead * (span - 3)]
        edge_word = link_word(
            beyond + ahead * (within - beyond),
            fluid[ahead * (span - 1)],
            within + ahead * (beyond - within),
        )
        for place in range(HALO):
            spot = 1 + place
            index = place + ahead * (span - 3)
            word = words[index] if place == 1 else None
            if place == 0:
                word = edge_word + ahead * (words[index] - edge_word)
            if place == 2:
                word = words[index] + ahead * (edge_word - words[index])
            state = pull(two, spot, word)
            density, flow = density_velocity(state)
            seed(index, density, flow)
            here = fluid[index] > 0
            for m in range(19):
                if place == 1:
                    initial = raw[m, ahead]
                else:
                    kept = two[m, spot]
                    initial = jnp.where((ahead > 0) == (place == 2), kept, raw[m, place // 2])
                outer[ahead, m, spot - ahead] = jnp.where(here, state[m], initial)
        for m in range(19):
            outer[ahead, m, ahead * (BX - 1)] = message[30 + m]

    def seed_home(plane):
        seed(plane, *recall(history, STEPS, plane))

    each_plane(HALO, HALO + home, seed_home)

    for side in range(2):
        flow = [second_flow[side, 1 + axis] for axis in range(3)]
        retreat(opens, words, share, even, odd, 1 + side * (span - 3), second_flow[side, 0], flow)

    def step_two(plane):
        retreat(opens, words, share, even, odd, plane, *recall(history, 2, plane))

    each_plane(HALO - 1, HALO + home + 1, step_two)


def gradient_kernel(
    home, history, opens, words, share, odd, marked, summed, gradient, to_near, to_far, total, even
):
    del summed
    up = parity()
    for plane in range(share.shape[0]):
        total[plane] = share[plane]

    def step_one(plane):
        retreat(opens, words, total, odd, even, plane, *recall(history, 1, plane))

    def step_zero(plane):
        retreat(opens, words, total, even, None, plane, *recall(history, 0, plane))

    each_plane(HALO - 1, HALO + home + 1, step_one)
    each_plane(HALO, HALO + home, step_zero)
    for plane in range(home):
        design = marked[plane]
        slope = 3.0 / ((1.6 + 3.4 * design) * (1.0 + 4.0 * design))
        gradient[plane] = jnp.where(design >= 0.0, total[plane + HALO] * slope, 0.0)
    for out, ahead in ((to_near, up), (to_far, 1 - up)):
        for plane in range(BX):
            out[plane] = gradient[ahead * (home - BX) + plane]


def scaled(home, cells, where, drag, joined, out):
    factor = cells / jnp.sum(drag[...])
    reach = (joined.shape[0] - home) // 2
    for plane in range(out.shape[0]):
        spot = jnp.clip(where[0] * BX + reach + plane, 0, joined.shape[0] - 1)
        live = plane < where[1] * BX
        out[plane] = jnp.where(live, joined[spot] * factor, 0.0)


def near_gradient(home, cells, where, drag, gradient, from_near, from_far, out, joined, kept, sem):
    up = parity()
    for ahead, message in ((up, from_near), (1 - up, from_far)):
        joined[pl.ds(ahead * (BX + home), BX)] = message[...]
    joined[pl.ds(BX, home)] = gradient[...]
    scaled(home, cells, where, drag, joined, kept)
    copy = pltpu.make_async_copy(kept, out, sem)
    copy.start()
    copy.wait()


def far_gradient(home, cells, where, drag, gradient, from_left, from_right, out, joined, kept, sem):
    joined[pl.ds(0, home)] = from_left[...]
    joined[pl.ds(home, home)] = gradient[...]
    joined[pl.ds(2 * home, home)] = from_right[...]
    scaled(home, cells, where, drag, joined, kept)
    copy = pltpu.make_async_copy(kept, out, sem)
    copy.start()
    copy.wait()


def place_kernel(where, final, outer, out, zeros, sems):
    blocks = out.shape[1] // BX
    home_blocks = final.shape[1] // BX
    beyond = outer.shape[2] // BX
    zeros[...] = jnp.zeros_like(zeros)
    for slot in range(blocks):
        target = out.at[:, pl.ds(slot * BX, BX)]
        live = slot < where[1]
        block = jnp.clip(where[0] + slot, -beyond, home_blocks + beyond - 1)
        inside = (block >= 0) & (block < home_blocks)

        @pl.when(live & inside)
        def _():
            source = final.at[:, pl.ds(block * BX, BX)]
            pltpu.make_async_copy(source, target, sems.at[slot]).start()

        @pl.when(live & jnp.logical_not(inside))
        def _():
            after = (block >= 0).astype(jnp.int32)
            within = block + beyond - after * (home_blocks + beyond)
            source = outer.at[after, :, pl.ds(within * BX, BX)]
            pltpu.make_async_copy(source, target, sems.at[slot]).start()

        @pl.when(jnp.logical_not(live))
        def _():
            pltpu.make_async_copy(zeros, target, sems.at[slot]).start()

    for slot in range(blocks):
        pltpu.make_async_copy(zeros, out.at[:, pl.ds(slot * BX, BX)], sems.at[slot]).wait()


def body(populations, design, fluid_mask, owner_after):
    count = lax.axis_size("block")
    home, width_y, width_z = design.shape
    home_blocks = home // BX
    slots = home_blocks + 2
    span = home + 2 * HALO
    plane = (width_y, width_z)
    vmem = pl.BlockSpec(memory_space=pltpu.VMEM)
    hbm = pl.BlockSpec(memory_space=pltpu.HBM)
    anywhere = pl.BlockSpec(memory_space=pl.ANY)
    smem = pl.BlockSpec(memory_space=pltpu.SMEM)
    cells = float(count * home * width_y * width_z)
    near_pairs = [(i, i ^ 1) for i in range(count)]
    far_pairs = [(i, (i + 1 if i % 2 else i - 1) % count) for i in range(count)]
    inner_pairs = far_pairs[1:-1]

    def planes(*lead, dtype=jnp.float32):
        return jax.ShapeDtypeStruct(lead + plane, dtype)

    def scratch(*lead, dtype=jnp.float32):
        return pltpu.VMEM(lead + plane, dtype)

    def call(kernel, name, ins, outs, scratches, limit, moved, *operands):
        return pl.pallas_call(
            kernel,
            out_shape=[shape for shape, _ in outs],
            in_specs=ins,
            out_specs=[spec for _, spec in outs],
            scratch_shapes=scratches,
            compiler_params=pltpu.CompilerParams(vmem_limit_bytes=limit * MIB),
            cost_estimate=pl.CostEstimate(flops=20 * moved, bytes_accessed=moved, transcendentals=0),
            name=name,
        )(*operands)

    own_near, own_far, pops, marked = call(
        functools.partial(edge_kernel, home),
        "edge_planes",
        [hbm] * 3,
        [(planes(23, RAW), vmem)] * 2 + [(planes(19, home), vmem), (planes(home), vmem)],
        [scratch(home), scratch(home, dtype=jnp.int32), pltpu.SemaphoreType.DMA((3,))],
        4,
        1_000_000,
        *[
            pltpu.with_memory_space_constraint(part, pltpu.HBM)
            for part in (populations, design, fluid_mask)
        ],
    )
    far = lax.ppermute(own_far, "block", far_pairs)
    near = lax.ppermute(own_near, "block", near_pairs)

    inner_shapes = (
        planes(49),
        planes(49),
        planes(19, 12),
        planes(16, home),
        planes(19, home),
        planes(home),
        planes(home, dtype=jnp.int32),
        planes(home, dtype=jnp.int32),
        planes(),
    )
    (
        to_near,
        to_far,
        edges,
        inner_history,
        inner_final,
        inner_opens,
        inner_fluid,
        inner_words,
        inner_drag,
    ) = call(
        functools.partial(interior_kernel, home),
        "interior_steps",
        [vmem] * 2,
        [(shape, vmem) for shape in inner_shapes],
        [scratch(19, home)] * 2,
        16,
        6_000_000,
        pops,
        marked,
    )
    from_far = lax.ppermute(to_far, "block", far_pairs)
    from_near = lax.ppermute(to_near, "block", near_pairs)

    (where,) = call(
        functools.partial(count_kernel, home_blocks),
        "slot_counts",
        [smem],
        [(jax.ShapeDtypeStruct((3,), jnp.int32), smem)],
        [],
        2,
        20_000_000,
        owner_after,
    )

    boundary_shapes = (
        planes(19, home),
        planes(16, span),
        planes(span),
        planes(span, dtype=jnp.int32),
        planes(span, dtype=jnp.int32),
        planes(),
        planes(19, span),
        planes(19, span),
    )
    final, history, opens, fluid, words, drag, even_state, odd_state = call(
        functools.partial(boundary_kernel, home),
        "boundary_steps",
        [vmem] * 3 + [anywhere] + [vmem] * 5,
        [(shape, vmem) for shape in boundary_shapes],
        [pltpu.SemaphoreType.DMA((5,))],
        20,
        8_000_000,
        near,
        far,
        edges,
        inner_history,
        inner_final,
        inner_opens,
        inner_fluid,
        inner_words,
        inner_drag,
    )

    sums = [drag]
    width = 1
    while width < count:
        fold = 4 if width >= 4 and width * 4 <= count else 2
        parts = [sums[-1]]
        for step in range(1, fold):
            swap = [(i, i ^ (step * width)) for i in range(count)]
            parts.append(lax.ppermute(sums[-1], "block", swap))
        sums.append(sum(parts[1:], parts[0]))
        width *= fold
    drag = sums[-1]

    is_far = where[2] > 0
    outer, share, odd = call(
        functools.partial(outer_kernel, home),
        "outer_steps",
        [vmem] * 10 + [anywhere] * 2,
        [(planes(2, 19, BX), vmem), (planes(span), vmem), (planes(19, span), vmem)],
        [scratch(19, span), scratch(2, 19, HALO), scratch(2, 19, HALO + 2), scratch(2, 4)],
        20,
        6_000_000,
        history,
        opens,
        fluid,
        words,
        even_state,
        odd_state,
        near,
        far,
        from_near,
        from_far,
        sums[2],
        is_far.astype(jnp.int32).reshape(1),
    )
    gradient, to_near, to_far = call(
        functools.partial(gradient_kernel, home),
        "gradient_steps",
        [vmem] * 6 + [anywhere],
        [(planes(home), vmem), (planes(BX), vmem), (planes(BX), vmem)],
        [scratch(span), scratch(19, span)],
        20,
        6_000_000,
        history,
        opens,
        words,
        share,
        odd,
        marked,
        drag,
    )
    from_far = lax.ppermute(to_far, "block", inner_pairs)
    from_near = lax.ppermute(to_near, "block", near_pairs)

    ring = [(i, i + 1) for i in range(count - 1)]
    back = [(i + 1, i) for i in range(count - 1)]

    def place(outer):
        (out,) = call(
            place_kernel,
            "place_populations",
            [smem, anywhere, anywhere],
            [(pltpu.HBM((19, slots * BX) + plane, jnp.float32), hbm)],
            [scratch(19, BX), pltpu.SemaphoreType.DMA((slots,))],
            8,
            4_000_000,
            where,
            final,
            outer,
        )
        return out

    def place_far(_):
        wide = [lax.ppermute(final, "block", route) for route in (ring, back)]
        return place(jnp.stack(wide))

    def slope(kernel, name, reach, *messages):
        (out,) = call(
            functools.partial(kernel, home, cells),
            name,
            [smem] + [vmem] * 4,
            [(pltpu.HBM((slots * BX,) + plane, jnp.float32), hbm)],
            [scratch(home + 2 * reach), scratch(slots * BX), pltpu.SemaphoreType.DMA(())],
            4,
            1_000_000,
            where,
            drag,
            gradient,
            *messages,
        )
        return out

    def slope_near(*messages):
        return slope(near_gradient, "near_gradient", BX, *messages)

    def slope_far(*_):
        wide = [lax.ppermute(gradient, "block", route) for route in (ring, back)]
        return slope(far_gradient, "far_gradient", home, *wide)

    populations_after = lax.cond(is_far, place_far, place, outer)
    sensitivity = lax.cond(is_far, slope_far, slope_near, from_near, from_far)
    return (populations_after, sensitivity)


def solution(mesh):
    placed = (
        P(None, ("group", "block"), None, None),
        P(("group", "block"), None, None),
        P(("group", "block"), None, None),
        P("group"),
    )
    return jax.shard_map(
        body,
        mesh=mesh,
        in_specs=placed,
        out_specs=(P(None, ("group", "block"), None, None), P(("group", "block"), None, None)),
        check_vma=False,
    )
```

```python
import functools
import math

import jax
import jax.numpy as jnp
from jax import lax
from jax.experimental import pallas as pl
from jax.experimental.pallas import tpu as pltpu
from jax.sharding import PartitionSpec as P

BX = 4
STEPS = 3
HALO = STEPS
RAW = HALO - 1
MIB = 2**20

VELOCITY = (
    (0, 0, 0),
    (1, 0, 0),
    (-1, 0, 0),
    (0, 1, 0),
    (0, -1, 0),
    (0, 0, 1),
    (0, 0, -1),
    (1, 1, 0),
    (-1, -1, 0),
    (1, -1, 0),
    (-1, 1, 0),
    (1, 0, 1),
    (-1, 0, -1),
    (1, 0, -1),
    (-1, 0, 1),
    (0, 1, 1),
    (0, -1, -1),
    (0, 1, -1),
    (0, -1, 1),
)
OPP = (0,) + tuple(m + 1 if m % 2 else m - 1 for m in range(1, 19))
AHEAD = tuple(m for m in range(19) if VELOCITY[m][0] == 1)
BEHIND = tuple(m for m in range(19) if VELOCITY[m][0] == -1)
FORCE = 0.02
ROOT_45 = math.sqrt(4.5)
ROOT_2 = math.sqrt(2.0)


def rolled(field, step_y, step_z):
    if step_y:
        field = pltpu.roll(field, step_y % field.shape[0], 0)
    if step_z:
        field = pltpu.roll(field, step_z % field.shape[1], 1)
    return field


def pairs(values):
    plus = [values[2 * k + 1] + values[2 * k + 2] for k in range(9)]
    minus = [values[2 * k + 1] - values[2 * k + 2] for k in range(9)]
    return plus, minus


def first_moments(minus, scale):
    along_x, along_y, along_z = minus[:3]
    if scale != 1.0:
        along_x, along_y, along_z = scale * along_x, scale * along_y, scale * along_z
    along_x = along_x + ((minus[3] + minus[4]) + (minus[5] + minus[6]))
    along_y = along_y + ((minus[3] - minus[4]) + (minus[7] + minus[8]))
    along_z = along_z + ((minus[5] - minus[6]) + (minus[7] - minus[8]))
    return along_x, along_y, along_z


def density_velocity(state):
    plus, minus = pairs(state)
    axes = (plus[0] + plus[1]) + (plus[2] + state[0])
    diagonals = (plus[3] + plus[4]) + (plus[5] + plus[6]) + (plus[7] + plus[8])
    density = axes + diagonals
    inverse = 1.0 / density
    momentum = first_moments(minus, 1.0)
    return density, [part * inverse for part in momentum]


def collide(state, density, flow, open_rate):
    rate = ROOT_45 * open_rate
    x, y, z = (flow[0] + FORCE) * rate, flow[1] * rate, flow[2] * rate
    xx, yy, zz = x * x, y * y, z * z
    base = 1.0 - (xx + yy + zz) * (1.0 / 3.0)
    axis_weight = density * (1.2 / 18.0)
    axis_slope = density * (1.2 * ROOT_2 / 18.0)
    side_weight = density * (1.2 / 36.0)
    side_slope = density * (1.2 * ROOT_2 / 36.0)
    result = [density * 0.4 * base - 0.2 * state[0]]
    for k, along in enumerate((x, y, z, x + y, x - y, x + z, x - z, y + z, y - z)):
        if k < 3:
            even = axis_weight * (base + (xx, yy, zz)[k])
            odd = axis_slope * along
        else:
            even = side_weight * (base + along * along)
            odd = side_slope * along
        result.append((even + odd) - 0.2 * state[2 * k + 1])
        result.append((even - odd) - 0.2 * state[2 * k + 2])
    return result


def spread(level, slope):
    x, y, z = slope
    result = [level]
    for along in (x, y, z, x + y, x - y, x + z, x - z, y + z, y - z):
        result.append(level + along)
        result.append(level - along)
    return result


def pull(source, plane, word):
    here = [source[m, plane] for m in range(19)]
    result = [here[0]]
    for m in range(1, 19):
        step_x, step_y, step_z = VELOCITY[m]
        moved = here[m] if step_x == 0 else source[m, plane - step_x]
        moved = rolled(moved, step_y, step_z)
        result.append(jnp.where((word & (1 << m)) != 0, moved, here[OPP[m]]))
    return result


def link_word(behind, here, ahead):
    rows = lax.broadcasted_iota(jnp.int32, here.shape, 0)
    columns = lax.broadcasted_iota(jnp.int32, here.shape, 1)
    joined = behind + 2 * here + 4 * ahead
    word = jnp.zeros_like(here)
    for step_y in (-1, 0, 1):
        for step_z in (-1, 0, 1):
            if step_y and step_z:
                inner = {0: 1}
            else:
                inner = {1: 0, 0: 1, -1: 2}
            near = rolled(joined, step_y, step_z)
            if step_y == 1:
                near = jnp.where(rows == 0, 0, near)
            if step_y == -1:
                near = jnp.where(rows == here.shape[0] - 1, 0, near)
            if step_z == 1:
                near = jnp.where(columns == 0, 0, near)
            if step_z == -1:
                near = jnp.where(columns == here.shape[1] - 1, 0, near)
            for step_x, place in inner.items():
                if (step_x, step_y, step_z) == (0, 0, 0):
                    continue
                m = VELOCITY.index((step_x, step_y, step_z))
                word = word | ((near & (1 << place)) << (m - place))
    return jnp.where(here > 0, word, 0)


def each_plane(low, high, body):
    def two(index, carry):
        body(low + 2 * index)
        body(low + 2 * index + 1)
        return carry

    lax.fori_loop(0, (high - low) // 2, two, 0)
    if (high - low) % 2:
        body(high - 1)


def is_fluid_rate(mark):
    design = jnp.maximum(mark, 0.0)
    return (mark >= 0.0).astype(jnp.int32), (1.0 + 4.0 * design) / (1.6 + 3.4 * design)


def store(target, plane, values):
    for m, part in enumerate(values):
        target[m, plane] = part


def remember(history, step, plane, density, flow):
    history[4 * step, plane] = density
    for axis in range(3):
        history[4 * step + 1 + axis, plane] = flow[axis]


def drag_terms(flow, open_rate):
    return (flow[0] * flow[0] + flow[1] * flow[1] + flow[2] * flow[2]) / open_rate


def parity(axis="block"):
    return 1 - lax.rem(lax.axis_index(axis), 2)


def pick(flag, yes, no):
    return no + flag * (yes - no)


def edge_kernel(home, pops_far, design, mask, near, far, pops, marked, designs, masks, sems):
    up = parity()
    copies = [
        pltpu.make_async_copy(source, target, sems.at[place])
        for place, (source, target) in enumerate(((pops_far, pops), (design, designs), (mask, masks)))
    ]
    for copy in copies:
        copy.start()
    for copy in copies[1:]:
        copy.wait()
    for plane in range(home):
        marked[plane] = jnp.where(masks[plane] > 0, designs[plane], -1.0)
    copies[0].wait()
    for out, ahead in ((near, up), (far, 1 - up)):
        first = ahead * (home - RAW)
        for plane in range(RAW):
            for m in range(19):
                out[m, plane] = pops[m, first + plane]
            out[19, plane] = marked[first + plane]
        third = ahead * (home - 1) + (1 - 2 * ahead) * RAW
        last = marked[third]
        out[22, 1] = last
        _, open_rate = is_fluid_rate(last)
        state = [pops[m, third] for m in range(19)]
        density, flow = density_velocity(state)
        collided = collide(state, density, flow, open_rate)
        for slot in range(5):
            value = jnp.where(ahead > 0, collided[AHEAD[slot]], collided[BEHIND[slot]])
            out[20 + slot // 2, slot % 2] = value


def count_kernel(home_blocks, owner, where):
    rank = lax.axis_index("block")
    below = jnp.int32(0)
    own = jnp.int32(0)
    for block in range(owner.shape[0]):
        holder = owner[block]
        below += (holder < rank).astype(jnp.int32)
        own += (holder == rank).astype(jnp.int32)
    stray = jnp.int32(0)
    for device in range(owner.shape[0] // home_blocks):
        late = owner[home_blocks * device + 1] < device
        early = owner[home_blocks * device + home_blocks - 2] > device
        stray = stray | late.astype(jnp.int32) | early.astype(jnp.int32)
    where[0] = below - home_blocks * rank
    where[1] = own
    where[2] = stray


def interior_kernel(
    home,
    pops,
    marked,
    to_near,
    to_far,
    edges,
    history,
    final,
    opens,
    fluid,
    words,
    drag,
    even,
    odd,
):
    up = parity()

    def start(plane):
        fluid[plane], open_rate = is_fluid_rate(marked[plane])
        opens[plane] = open_rate
        state = [pops[m, plane] for m in range(19)]
        density, flow = density_velocity(state)
        remember(history, 0, plane, density, flow)
        store(even, plane, collide(state, density, flow, open_rate))

    def link(plane):
        words[plane] = link_word(fluid[plane - 1], fluid[plane], fluid[plane + 1])

    def advance(step, source, target, plane):
        state = pull(source, plane, words[plane])
        density, flow = density_velocity(state)
        remember(history, step, plane, density, flow)
        store(target, plane, collide(state, density, flow, opens[plane]))

    def finish(plane):
        state = pull(even, plane, words[plane])
        density, flow = density_velocity(state)
        remember(history, 3, plane, density, flow)
        here = fluid[plane] > 0
        for m in range(19):
            final[m, plane] = jnp.where(here, state[m], pops[m, plane])
        drag[...] += jnp.where(here, drag_terms(flow, opens[plane]), 0.0)

    def keep(step, source):
        for m in range(19):
            for side in range(2):
                edges[m, 4 * step + side] = source[m, step + side]
                edges[m, 4 * step + 2 + side] = source[m, home - 2 - step + side]

    def send(out, ahead, step, source):
        outer = ahead * (home - 1) + (1 - 2 * ahead) * RAW
        if step == 1:
            for slot in range(5):
                out[slot] = source[AHEAD[slot] + 1 - ahead, outer]
            return
        inner = ahead * (home - 1) + (1 - 2 * ahead) * HALO
        here = fluid[outer] > 0
        for slot in range(5):
            out[5 + slot] = source[AHEAD[slot] + 1 - ahead, inner]
        for m in range(19):
            out[10 + m] = jnp.where(here, source[m, outer], pops[m, outer])
        out[29] = marked[inner]

    drag[...] = jnp.zeros_like(drag)
    each_plane(0, home, start)
    keep(0, even)
    each_plane(1, home - 1, link)
    each_plane(1, home - 1, functools.partial(advance, 1, even, odd))
    keep(1, odd)
    each_plane(2, home - 2, functools.partial(advance, 2, odd, even))
    keep(2, even)
    for out, ahead in ((to_near, up), (to_far, 1 - up)):
        send(out, ahead, 1, odd)
        send(out, ahead, 2, even)
    each_plane(3, home - 3, finish)
    for m in range(19):
        for plane in range(STEPS):
            final[m, plane] = pops[m, plane]
            final[m, home - STEPS + plane] = pops[m, home - STEPS + plane]
        for out, ahead in ((to_near, up), (to_far, 1 - up)):
            out[30 + m] = final[m, STEPS + ahead * (home - 1 - 2 * STEPS)]


def boundary_kernel(
    home,
    near,
    far,
    edges,
    inner_history,
    inner_final,
    inner_opens,
    inner_fluid,
    inner_words,
    inner_drag,
    final,
    history,
    opens,
    fluid,
    words,
    drag,
    even,
    odd,
    sems,
):
    span = home + 2 * HALO
    up = parity()
    sides = ((up, near), (1 - up, far))
    copies = [
        pltpu.make_async_copy(
            inner_history.at[pl.ds(4 * step, 4), pl.ds(step, home - 2 * step)],
            history.at[pl.ds(4 * step, 4), pl.ds(HALO + step, home - 2 * step)],
            sems.at[step],
        )
        for step in range(4)
    ]
    copies.append(
        pltpu.make_async_copy(
            inner_final.at[:, pl.ds(STEPS, home - 2 * STEPS)],
            final.at[:, pl.ds(STEPS, home - 2 * STEPS)],
            sems.at[4],
        )
    )
    for copy in copies:
        copy.start()

    for plane in range(home):
        fluid[plane + HALO] = inner_fluid[plane]
        opens[plane + HALO] = inner_opens[plane]
    for plane in range(1, home - 1):
        words[plane + HALO] = inner_words[plane]
    for ahead, side in sides:
        fluid[ahead * (span - 1)], opens[ahead * (span - 1)] = is_fluid_rate(side[22, 1])
        for slot in range(5):
            even[AHEAD[slot] + ahead, ahead * (span - 1)] = side[20 + slot // 2, slot % 2]

    def start(plane, carry):
        for ahead, side in sides:
            index = plane + 1 + ahead * (home + RAW)
            fluid[index], open_rate = is_fluid_rate(side[19, plane])
            opens[index] = open_rate
            state = [side[m, plane] for m in range(19)]
            density, flow = density_velocity(state)
            store(even, index, collide(state, density, flow, open_rate))
        return carry

    lax.fori_loop(0, RAW, start, 0)

    def receive(step, target):
        for m in range(19):
            for side in range(2):
                target[m, HALO + step + side] = edges[m, 4 * step + side]
                target[m, HALO + home - 2 - step + side] = edges[m, 4 * step + 2 + side]

    def both(step, body):
        def two(place, carry):
            body(step + place, place, 0)
            body(span - 3 - step + place, place, 1)
            return carry

        lax.fori_loop(0, 3, two, 0)

    def link(index, place, ahead):
        words[index] = link_word(fluid[index - 1], fluid[index], fluid[index + 1])

    def advance(step, source, target, index, place, ahead):
        state = pull(source, index, words[index])
        density, flow = density_velocity(state)
        remember(history, step, index, density, flow)
        store(target, index, collide(state, density, flow, opens[index]))

    both(1, link)
    receive(0, even)
    both(1, functools.partial(advance, 1, even, odd))
    receive(1, odd)
    both(2, functools.partial(advance, 2, odd, even))
    receive(2, even)
    drag[...] = jnp.zeros_like(drag)
    drag[0] = inner_drag[...]

    def finish(index, place, ahead):
        state = pull(even, index, words[index])
        density, flow = density_velocity(state)
        remember(history, 3, index, density, flow)
        here = fluid[index] > 0
        for m in range(19):
            final[m, index - HALO] = jnp.where(here, state[m], inner_final[m, index - HALO])
        drag[1 + place] += jnp.where(here, drag_terms(flow, opens[index]), 0.0)

    both(3, finish)
    for copy in copies:
        copy.wait()


def recall(history, step, plane):
    return history[4 * step, plane], [history[4 * step + 1 + axis, plane] for axis in range(3)]


def retreat(opens, words, share, source, target, plane, density, flow):
    mirrored = pull(source, plane, words[plane])
    adjoint = [mirrored[OPP[m]] for m in range(19)]
    open_rate = opens[plane]
    force_flow = [flow[0] + FORCE, flow[1], flow[2]]
    x, y, z = [open_rate * part for part in force_flow]
    plus, minus = pairs(adjoint)
    mx, my, mz = [part * (1.0 / 12.0) for part in first_moments(minus, 2.0)]
    xy_plus, xz_plus, yz_plus = plus[3] + plus[4], plus[5] + plus[6], plus[7] + plus[8]
    axes = [2.0 * plus[k] for k in range(3)]
    whole = 12.0 * adjoint[0] + (axes[0] + axes[1] + axes[2]) + (xy_plus + xz_plus + yz_plus)
    third = whole * (1.0 / 3.0)
    xx = axes[0] + (xy_plus + xz_plus) - third
    yy = axes[1] + (xy_plus + yz_plus) - third
    zz = axes[2] + (xz_plus + yz_plus) - third
    xy, xz, yz = plus[3] - plus[4], plus[5] - plus[6], plus[7] - plus[8]
    hx = 0.25 * (xx * x + xy * y + xz * z)
    hy = 0.25 * (xy * x + yy * y + yz * z)
    hz = 0.25 * (xz * x + yz * y + zz * z)
    rate = 1.2 * open_rate
    slope = [rate * (mx + hx), rate * (my + hy), rate * (mz + hz)]
    pushed = slope[0] * force_flow[0] + slope[1] * force_flow[1] + slope[2] * force_flow[2]
    share[plane] += density * pushed
    if target is None:
        return
    level = whole * (1.2 / 36.0) + 1.2 * (
        x * (mx + 0.5 * hx) + y * (my + 0.5 * hy) + z * (mz + 0.5 * hz)
    )
    level = level - (slope[0] * flow[0] + slope[1] * flow[1] + slope[2] * flow[2])
    values = spread(level, slope)
    for m in range(19):
        target[OPP[m], plane] = values[m] - 0.2 * adjoint[m]


def outer_kernel(
    home,
    history,
    opens,
    fluid,
    words,
    even_state,
    odd_state,
    near,
    far,
    from_near,
    from_far,
    summed,
    counted,
    outer,
    share,
    odd,
    even,
    first,
    second,
    second_flow,
):
    del summed, counted
    span = home + 2 * HALO
    up = parity()

    def seed(plane, density, flow):
        damping = 1.0 / opens[plane]
        square = flow[0] * flow[0] + flow[1] * flow[1] + flow[2] * flow[2]
        share[plane] = -square * damping
        factor = 2.0 * damping / density
        slope = [part * factor for part in flow]
        values = spread(-square * factor, slope)
        for m in range(19):
            even[OPP[m], plane] = values[m]

    for ahead, raw, message in ((up, near, from_near), (1 - up, far, from_far)):
        one = first.at[ahead]
        for m in range(19):
            for place in range(HALO):
                one[m, place] = odd_state[m, ahead * (span - HALO) + place]
        for slot in range(5):
            one[AHEAD[slot] + ahead, ahead * RAW] = message[slot]
        index = 1 + ahead * (span - 3)
        state = pull(one, 1, words[index])
        density, flow = density_velocity(state)
        for place, part in enumerate([density] + flow):
            second_flow[ahead, place] = part
        two = second.at[ahead]
        store(two, 2, collide(state, density, flow, opens[index]))
        for m in range(19):
            for place in range(2):
                two[m, 3 - 3 * ahead + place] = even_state[m, 2 + ahead * (span - 6) + place]
            two[m, 1 + 2 * ahead] = message[10 + m]
        for slot in range(5):
            two[AHEAD[slot] + ahead, 4 * ahead] = message[5 + slot]
        beyond = (message[29] >= 0.0).astype(jnp.int32)
        within = fluid[1 + ahead * (span - 3)]
        edge_word = link_word(
            beyond + ahead * (within - beyond),
            fluid[ahead * (span - 1)],
            within + ahead * (beyond - within),
        )
        for place in range(HALO):
            spot = 1 + place
            index = place + ahead * (span - 3)
            word = words[index] if place == 1 else None
            if place == 0:
                word = edge_word + ahead * (words[index] - edge_word)
            if place == 2:
                word = words[index] + ahead * (edge_word - words[index])
            state = pull(two, spot, word)
            density, flow = density_velocity(state)
            seed(index, density, flow)
            here = fluid[index] > 0
            for m in range(19):
                if place == 1:
                    initial = raw[m, ahead]
                else:
                    kept = two[m, spot]
                    initial = jnp.where((ahead > 0) == (place == 2), kept, raw[m, place // 2])
                outer[ahead, m, spot - ahead] = jnp.where(here, state[m], initial)
        for m in range(19):
            outer[ahead, m, ahead * (BX - 1)] = message[30 + m]

    def seed_home(plane):
        seed(plane, *recall(history, STEPS, plane))

    each_plane(HALO, HALO + home, seed_home)

    for side in range(2):
        flow = [second_flow[side, 1 + axis] for axis in range(3)]
        retreat(opens, words, share, even, odd, 1 + side * (span - 3), second_flow[side, 0], flow)

    def step_two(plane):
        retreat(opens, words, share, even, odd, plane, *recall(history, 2, plane))

    each_plane(HALO - 1, HALO + home + 1, step_two)


def gradient_kernel(
    home, history, opens, words, share, odd, marked, summed, gradient, to_near, to_far, total, even
):
    del summed
    up = parity()
    for plane in range(share.shape[0]):
        total[plane] = share[plane]

    def step_one(plane):
        retreat(opens, words, total, odd, even, plane, *recall(history, 1, plane))

    def step_zero(plane):
        retreat(opens, words, total, even, None, plane, *recall(history, 0, plane))

    each_plane(HALO - 1, HALO + home + 1, step_one)
    each_plane(HALO, HALO + home, step_zero)
    for plane in range(home):
        design = marked[plane]
        slope = 3.0 / ((1.6 + 3.4 * design) * (1.0 + 4.0 * design))
        gradient[plane] = jnp.where(design >= 0.0, total[plane + HALO] * slope, 0.0)
    for out, ahead in ((to_near, up), (to_far, 1 - up)):
        for plane in range(BX):
            out[plane] = gradient[ahead * (home - BX) + plane]


def scaled(home, cells, where, drag, joined, out):
    factor = cells / jnp.sum(drag[...])
    reach = (joined.shape[0] - home) // 2
    for plane in range(out.shape[0]):
        spot = jnp.clip(where[0] * BX + reach + plane, 0, joined.shape[0] - 1)
        live = plane < where[1] * BX
        out[plane] = jnp.where(live, joined[spot] * factor, 0.0)


def near_gradient(home, cells, where, drag, gradient, from_near, from_far, out, joined):
    up = parity()
    for ahead, message in ((up, from_near), (1 - up, from_far)):
        joined[pl.ds(ahead * (BX + home), BX)] = message[...]
    joined[pl.ds(BX, home)] = gradient[...]
    scaled(home, cells, where, drag, joined, out)


def far_gradient(home, cells, where, drag, gradient, from_left, from_right, out, joined):
    joined[pl.ds(0, home)] = from_left[...]
    joined[pl.ds(home, home)] = gradient[...]
    joined[pl.ds(2 * home, home)] = from_right[...]
    scaled(home, cells, where, drag, joined, out)


def place_kernel(where, final, outer, later, out, zeros, sems):
    del later
    blocks = out.shape[1] // BX
    home_blocks = final.shape[1] // BX
    beyond = outer.shape[2] // BX
    zeros[...] = jnp.zeros_like(zeros)
    for slot in range(blocks):
        target = out.at[:, pl.ds(slot * BX, BX)]
        live = slot < where[1]
        block = jnp.clip(where[0] + slot, -beyond, home_blocks + beyond - 1)
        inside = (block >= 0) & (block < home_blocks)

        @pl.when(live & inside)
        def _():
            source = final.at[:, pl.ds(block * BX, BX)]
            pltpu.make_async_copy(source, target, sems.at[slot]).start()

        @pl.when(live & jnp.logical_not(inside))
        def _():
            after = (block >= 0).astype(jnp.int32)
            within = block + beyond - after * (home_blocks + beyond)
            source = outer.at[after, :, pl.ds(within * BX, BX)]
            pltpu.make_async_copy(source, target, sems.at[slot]).start()

        @pl.when(jnp.logical_not(live))
        def _():
            pltpu.make_async_copy(zeros, target, sems.at[slot]).start()

    for slot in range(blocks):
        pltpu.make_async_copy(zeros, out.at[:, pl.ds(slot * BX, BX)], sems.at[slot]).wait()


def body(populations, design, fluid_mask, owner_after):
    count = lax.axis_size("block")
    home, width_y, width_z = design.shape
    home_blocks = home // BX
    slots = home_blocks + 2
    span = home + 2 * HALO
    plane = (width_y, width_z)
    vmem = pl.BlockSpec(memory_space=pltpu.VMEM)
    hbm = pl.BlockSpec(memory_space=pltpu.HBM)
    anywhere = pl.BlockSpec(memory_space=pl.ANY)
    smem = pl.BlockSpec(memory_space=pltpu.SMEM)
    cells = float(count * home * width_y * width_z)
    near_pairs = [(i, i ^ 1) for i in range(count)]
    far_pairs = [(i, (i + 1 if i % 2 else i - 1) % count) for i in range(count)]
    inner_pairs = far_pairs[1:-1]

    def planes(*lead, dtype=jnp.float32):
        return jax.ShapeDtypeStruct(lead + plane, dtype)

    def scratch(*lead, dtype=jnp.float32):
        return pltpu.VMEM(lead + plane, dtype)

    def call(kernel, name, ins, outs, scratches, limit, moved, *operands):
        return pl.pallas_call(
            kernel,
            out_shape=[shape for shape, _ in outs],
            in_specs=ins,
            out_specs=[spec for _, spec in outs],
            scratch_shapes=scratches,
            compiler_params=pltpu.CompilerParams(vmem_limit_bytes=limit * MIB),
            cost_estimate=pl.CostEstimate(flops=20 * moved, bytes_accessed=moved, transcendentals=0),
            name=name,
        )(*operands)

    own_near, own_far, pops, marked = call(
        functools.partial(edge_kernel, home),
        "edge_planes",
        [hbm] * 3,
        [(planes(23, RAW), vmem)] * 2 + [(planes(19, home), vmem), (planes(home), vmem)],
        [scratch(home), scratch(home, dtype=jnp.int32), pltpu.SemaphoreType.DMA((3,))],
        4,
        1_000_000,
        *[
            pltpu.with_memory_space_constraint(part, pltpu.HBM)
            for part in (populations, design, fluid_mask)
        ],
    )
    far = lax.ppermute(own_far, "block", far_pairs)
    near = lax.ppermute(own_near, "block", near_pairs)

    inner_shapes = (
        planes(49),
        planes(49),
        planes(19, 12),
        planes(16, home),
        planes(19, home),
        planes(home),
        planes(home, dtype=jnp.int32),
        planes(home, dtype=jnp.int32),
        planes(),
    )
    (
        to_near,
        to_far,
        edges,
        inner_history,
        inner_final,
        inner_opens,
        inner_fluid,
        inner_words,
        inner_drag,
    ) = call(
        functools.partial(interior_kernel, home),
        "interior_steps",
        [vmem] * 2,
        [(shape, vmem) for shape in inner_shapes],
        [scratch(19, home)] * 2,
        16,
        6_000_000,
        pops,
        marked,
    )
    from_far = lax.ppermute(to_far, "block", far_pairs)
    from_near = lax.ppermute(to_near, "block", near_pairs)

    (where,) = call(
        functools.partial(count_kernel, home_blocks),
        "slot_counts",
        [smem],
        [(jax.ShapeDtypeStruct((3,), jnp.int32), smem)],
        [],
        2,
        20_000_000,
        owner_after,
    )

    boundary_shapes = (
        planes(19, home),
        planes(16, span),
        planes(span),
        planes(span, dtype=jnp.int32),
        planes(span, dtype=jnp.int32),
        planes(1 + STEPS),
        planes(19, span),
        planes(19, span),
    )
    final, history, opens, fluid, words, drag, even_state, odd_state = call(
        functools.partial(boundary_kernel, home),
        "boundary_steps",
        [vmem] * 3 + [anywhere] + [vmem] * 5,
        [(shape, vmem) for shape in boundary_shapes],
        [pltpu.SemaphoreType.DMA((5,))],
        20,
        8_000_000,
        near,
        far,
        edges,
        inner_history,
        inner_final,
        inner_opens,
        inner_fluid,
        inner_words,
        inner_drag,
    )

    sums = [drag]
    distance = 1
    while distance < count:
        swap = [(i, i ^ distance) for i in range(count)]
        sums.append(sums[-1] + lax.ppermute(sums[-1], "block", swap))
        distance *= 2
    drag = sums[-1]

    is_far = where[2] > 0
    outer, share, odd = call(
        functools.partial(outer_kernel, home),
        "outer_steps",
        [vmem] * 10 + [anywhere] * 2,
        [(planes(2, 19, BX), vmem), (planes(span), vmem), (planes(19, span), vmem)],
        [scratch(19, span), scratch(2, 19, HALO), scratch(2, 19, HALO + 2), scratch(2, 4)],
        20,
        12_000_000,
        history,
        opens,
        fluid,
        words,
        even_state,
        odd_state,
        near,
        far,
        from_near,
        from_far,
        sums[2],
        is_far.astype(jnp.int32).reshape(1),
    )
    gradient, to_near, to_far = call(
        functools.partial(gradient_kernel, home),
        "gradient_steps",
        [vmem] * 6 + [anywhere],
        [(planes(home), vmem), (planes(BX), vmem), (planes(BX), vmem)],
        [scratch(span), scratch(19, span)],
        20,
        6_000_000,
        history,
        opens,
        words,
        share,
        odd,
        marked,
        sums[3],
    )
    from_far = lax.ppermute(to_far, "block", inner_pairs)
    from_near = lax.ppermute(to_near, "block", near_pairs)

    ring = [(i, i + 1) for i in range(count - 1)]
    back = [(i + 1, i) for i in range(count - 1)]

    def place(outer):
        (out,) = call(
            place_kernel,
            "place_populations",
            [smem, anywhere, anywhere, anywhere],
            [(planes(19, slots * BX), anywhere)],
            [scratch(19, BX), pltpu.SemaphoreType.DMA((slots,))],
            8,
            4_000_000,
            where,
            final,
            outer,
            to_near,
        )
        return out

    def place_far(_):
        wide = [lax.ppermute(final, "block", route) for route in (ring, back)]
        return place(jnp.stack(wide))

    def slope(kernel, name, reach, *messages):
        (out,) = call(
            functools.partial(kernel, home, cells),
            name,
            [smem] + [vmem] * 4,
            [(planes(slots * BX), vmem)],
            [scratch(home + 2 * reach)],
            4,
            1_000_000,
            where,
            drag,
            gradient,
            *messages,
        )
        return out

    def slope_near(*messages):
        return slope(near_gradient, "near_gradient", BX, *messages)

    def slope_far(*_):
        wide = [lax.ppermute(gradient, "block", route) for route in (ring, back)]
        return slope(far_gradient, "far_gradient", home, *wide)

    populations_after = lax.cond(is_far, place_far, place, outer)
    sensitivity = lax.cond(is_far, slope_far, slope_near, from_near, from_far)
    return (populations_after, sensitivity)


def solution(mesh):
    placed = (
        P(None, ("group", "block"), None, None),
        P(("group", "block"), None, None),
        P(("group", "block"), None, None),
        P("group"),
    )
    return jax.shard_map(
        body,
        mesh=mesh,
        in_specs=placed,
        out_specs=(P(None, ("group", "block"), None, None), P(("group", "block"), None, None)),
        check_vma=False,
    )
```

```python
import functools
import math

import jax
import jax.numpy as jnp
from jax import lax
from jax.experimental import pallas as pl
from jax.experimental.pallas import tpu as pltpu
from jax.sharding import PartitionSpec as P

BX = 4
STEPS = 3
HALO = STEPS
RAW = HALO - 1
MIB = 2**20

VELOCITY = (
    (0, 0, 0),
    (1, 0, 0),
    (-1, 0, 0),
    (0, 1, 0),
    (0, -1, 0),
    (0, 0, 1),
    (0, 0, -1),
    (1, 1, 0),
    (-1, -1, 0),
    (1, -1, 0),
    (-1, 1, 0),
    (1, 0, 1),
    (-1, 0, -1),
    (1, 0, -1),
    (-1, 0, 1),
    (0, 1, 1),
    (0, -1, -1),
    (0, 1, -1),
    (0, -1, 1),
)
OPP = (0,) + tuple(m + 1 if m % 2 else m - 1 for m in range(1, 19))
AHEAD = tuple(m for m in range(19) if VELOCITY[m][0] == 1)
BEHIND = tuple(m for m in range(19) if VELOCITY[m][0] == -1)
FORCE = 0.02
ROOT_45 = math.sqrt(4.5)
ROOT_2 = math.sqrt(2.0)


def rolled(field, step_y, step_z):
    if step_y:
        field = pltpu.roll(field, step_y % field.shape[0], 0)
    if step_z:
        field = pltpu.roll(field, step_z % field.shape[1], 1)
    return field


def pairs(values):
    plus = [values[2 * k + 1] + values[2 * k + 2] for k in range(9)]
    minus = [values[2 * k + 1] - values[2 * k + 2] for k in range(9)]
    return plus, minus


def first_moments(minus, scale):
    along_x, along_y, along_z = minus[:3]
    if scale != 1.0:
        along_x, along_y, along_z = scale * along_x, scale * along_y, scale * along_z
    along_x = along_x + ((minus[3] + minus[4]) + (minus[5] + minus[6]))
    along_y = along_y + ((minus[3] - minus[4]) + (minus[7] + minus[8]))
    along_z = along_z + ((minus[5] - minus[6]) + (minus[7] - minus[8]))
    return along_x, along_y, along_z


def density_velocity(state):
    plus, minus = pairs(state)
    axes = (plus[0] + plus[1]) + (plus[2] + state[0])
    diagonals = (plus[3] + plus[4]) + (plus[5] + plus[6]) + (plus[7] + plus[8])
    density = axes + diagonals
    inverse = 1.0 / density
    momentum = first_moments(minus, 1.0)
    return density, [part * inverse for part in momentum]


def collide(state, density, flow, open_rate):
    rate = ROOT_45 * open_rate
    x, y, z = (flow[0] + FORCE) * rate, flow[1] * rate, flow[2] * rate
    xx, yy, zz = x * x, y * y, z * z
    base = 1.0 - (xx + yy + zz) * (1.0 / 3.0)
    axis_weight = density * (1.2 / 18.0)
    axis_slope = density * (1.2 * ROOT_2 / 18.0)
    side_weight = density * (1.2 / 36.0)
    side_slope = density * (1.2 * ROOT_2 / 36.0)
    result = [density * 0.4 * base - 0.2 * state[0]]
    for k, along in enumerate((x, y, z, x + y, x - y, x + z, x - z, y + z, y - z)):
        if k < 3:
            even = axis_weight * (base + (xx, yy, zz)[k])
            odd = axis_slope * along
        else:
            even = side_weight * (base + along * along)
            odd = side_slope * along
        result.append((even + odd) - 0.2 * state[2 * k + 1])
        result.append((even - odd) - 0.2 * state[2 * k + 2])
    return result


def spread(level, slope):
    x, y, z = slope
    result = [level]
    for along in (x, y, z, x + y, x - y, x + z, x - z, y + z, y - z):
        result.append(level + along)
        result.append(level - along)
    return result


def pull(source, plane, word):
    here = [source[m, plane] for m in range(19)]
    result = [here[0]]
    for m in range(1, 19):
        step_x, step_y, step_z = VELOCITY[m]
        moved = here[m] if step_x == 0 else source[m, plane - step_x]
        moved = rolled(moved, step_y, step_z)
        result.append(jnp.where((word & (1 << m)) != 0, moved, here[OPP[m]]))
    return result


def link_word(behind, here, ahead):
    rows = lax.broadcasted_iota(jnp.int32, here.shape, 0)
    columns = lax.broadcasted_iota(jnp.int32, here.shape, 1)
    joined = behind + 2 * here + 4 * ahead
    word = jnp.zeros_like(here)
    for step_y in (-1, 0, 1):
        for step_z in (-1, 0, 1):
            if step_y and step_z:
                inner = {0: 1}
            else:
                inner = {1: 0, 0: 1, -1: 2}
            near = rolled(joined, step_y, step_z)
            if step_y == 1:
                near = jnp.where(rows == 0, 0, near)
            if step_y == -1:
                near = jnp.where(rows == here.shape[0] - 1, 0, near)
            if step_z == 1:
                near = jnp.where(columns == 0, 0, near)
            if step_z == -1:
                near = jnp.where(columns == here.shape[1] - 1, 0, near)
            for step_x, place in inner.items():
                if (step_x, step_y, step_z) == (0, 0, 0):
                    continue
                m = VELOCITY.index((step_x, step_y, step_z))
                word = word | ((near & (1 << place)) << (m - place))
    return jnp.where(here > 0, word, 0)


def each_plane(low, high, body):
    def two(index, carry):
        body(low + 2 * index)
        body(low + 2 * index + 1)
        return carry

    lax.fori_loop(0, (high - low) // 2, two, 0)
    if (high - low) % 2:
        body(high - 1)


def is_fluid_rate(mark):
    design = jnp.maximum(mark, 0.0)
    return (mark >= 0.0).astype(jnp.int32), (1.0 + 4.0 * design) / (1.6 + 3.4 * design)


def store(target, plane, values):
    for m, part in enumerate(values):
        target[m, plane] = part


def remember(history, step, plane, density, flow):
    history[4 * step, plane] = density
    for axis in range(3):
        history[4 * step + 1 + axis, plane] = flow[axis]


def drag_terms(flow, open_rate):
    return (flow[0] * flow[0] + flow[1] * flow[1] + flow[2] * flow[2]) / open_rate


def parity(axis="block"):
    return 1 - lax.rem(lax.axis_index(axis), 2)


def pick(flag, yes, no):
    return no + flag * (yes - no)


def edge_kernel(home, pops_far, design, mask, near, far, pops, marked, designs, masks, sems):
    up = parity()
    copies = [
        pltpu.make_async_copy(source, target, sems.at[place])
        for place, (source, target) in enumerate(((pops_far, pops), (design, designs), (mask, masks)))
    ]
    for copy in copies:
        copy.start()
    for copy in copies[1:]:
        copy.wait()
    for plane in range(home):
        marked[plane] = jnp.where(masks[plane] > 0, designs[plane], -1.0)
    copies[0].wait()
    for out, ahead in ((near, up), (far, 1 - up)):
        first = ahead * (home - RAW)
        for plane in range(RAW):
            for m in range(19):
                out[m, plane] = pops[m, first + plane]
            out[19, plane] = marked[first + plane]
        third = ahead * (home - 1) + (1 - 2 * ahead) * RAW
        last = marked[third]
        out[22, 1] = last
        _, open_rate = is_fluid_rate(last)
        state = [pops[m, third] for m in range(19)]
        density, flow = density_velocity(state)
        collided = collide(state, density, flow, open_rate)
        for slot in range(5):
            value = jnp.where(ahead > 0, collided[AHEAD[slot]], collided[BEHIND[slot]])
            out[20 + slot // 2, slot % 2] = value


def count_kernel(home_blocks, owner, where):
    rank = lax.axis_index("block")
    below = jnp.int32(0)
    own = jnp.int32(0)
    for block in range(owner.shape[0]):
        holder = owner[block]
        below += (holder < rank).astype(jnp.int32)
        own += (holder == rank).astype(jnp.int32)
    stray = jnp.int32(0)
    for device in range(owner.shape[0] // home_blocks):
        late = owner[home_blocks * device + 1] < device
        early = owner[home_blocks * device + home_blocks - 2] > device
        stray = stray | late.astype(jnp.int32) | early.astype(jnp.int32)
    where[0] = below - home_blocks * rank
    where[1] = own
    where[2] = stray


def interior_kernel(
    home,
    pops,
    marked,
    to_near,
    to_far,
    edges,
    history,
    final,
    opens,
    fluid,
    words,
    drag,
    even,
    odd,
):
    up = parity()

    def start(plane):
        fluid[plane], open_rate = is_fluid_rate(marked[plane])
        opens[plane] = open_rate
        state = [pops[m, plane] for m in range(19)]
        density, flow = density_velocity(state)
        remember(history, 0, plane, density, flow)
        store(even, plane, collide(state, density, flow, open_rate))

    def link(plane):
        words[plane] = link_word(fluid[plane - 1], fluid[plane], fluid[plane + 1])

    def advance(step, source, target, plane):
        state = pull(source, plane, words[plane])
        density, flow = density_velocity(state)
        remember(history, step, plane, density, flow)
        store(target, plane, collide(state, density, flow, opens[plane]))

    def finish(plane):
        state = pull(even, plane, words[plane])
        density, flow = density_velocity(state)
        remember(history, 3, plane, density, flow)
        here = fluid[plane] > 0
        for m in range(19):
            final[m, plane] = jnp.where(here, state[m], pops[m, plane])
        drag[...] += jnp.where(here, drag_terms(flow, opens[plane]), 0.0)

    def keep(step, source):
        for m in range(19):
            for side in range(2):
                edges[m, 4 * step + side] = source[m, step + side]
                edges[m, 4 * step + 2 + side] = source[m, home - 2 - step + side]

    def send(out, ahead, step, source):
        outer = ahead * (home - 1) + (1 - 2 * ahead) * RAW
        if step == 1:
            for slot in range(5):
                out[slot] = source[AHEAD[slot] + 1 - ahead, outer]
            return
        inner = ahead * (home - 1) + (1 - 2 * ahead) * HALO
        here = fluid[outer] > 0
        for slot in range(5):
            out[5 + slot] = source[AHEAD[slot] + 1 - ahead, inner]
        for m in range(19):
            out[10 + m] = jnp.where(here, source[m, outer], pops[m, outer])
        out[29] = marked[inner]

    drag[...] = jnp.zeros_like(drag)
    each_plane(0, home, start)
    keep(0, even)
    each_plane(1, home - 1, link)
    each_plane(1, home - 1, functools.partial(advance, 1, even, odd))
    keep(1, odd)
    each_plane(2, home - 2, functools.partial(advance, 2, odd, even))
    keep(2, even)
    for out, ahead in ((to_near, up), (to_far, 1 - up)):
        send(out, ahead, 1, odd)
        send(out, ahead, 2, even)
    each_plane(3, home - 3, finish)
    for m in range(19):
        for plane in range(STEPS):
            final[m, plane] = pops[m, plane]
            final[m, home - STEPS + plane] = pops[m, home - STEPS + plane]
        for out, ahead in ((to_near, up), (to_far, 1 - up)):
            out[30 + m] = final[m, STEPS + ahead * (home - 1 - 2 * STEPS)]


def boundary_kernel(
    home,
    far,
    near,
    edges,
    inner_history,
    inner_final,
    inner_opens,
    inner_fluid,
    inner_words,
    inner_drag,
    final,
    history,
    opens,
    fluid,
    words,
    drag,
    even,
    odd,
    sems,
):
    span = home + 2 * HALO
    up = parity()
    sides = ((up, near), (1 - up, far))
    copies = [
        pltpu.make_async_copy(
            inner_history.at[pl.ds(4 * step, 4), pl.ds(step, home - 2 * step)],
            history.at[pl.ds(4 * step, 4), pl.ds(HALO + step, home - 2 * step)],
            sems.at[step],
        )
        for step in range(4)
    ]
    copies.append(
        pltpu.make_async_copy(
            inner_final.at[:, pl.ds(STEPS, home - 2 * STEPS)],
            final.at[:, pl.ds(STEPS, home - 2 * STEPS)],
            sems.at[4],
        )
    )
    for copy in copies:
        copy.start()

    for plane in range(home):
        fluid[plane + HALO] = inner_fluid[plane]
        opens[plane + HALO] = inner_opens[plane]
    for plane in range(1, home - 1):
        words[plane + HALO] = inner_words[plane]
    for ahead, side in sides:
        fluid[ahead * (span - 1)], opens[ahead * (span - 1)] = is_fluid_rate(side[22, 1])
        for slot in range(5):
            even[AHEAD[slot] + ahead, ahead * (span - 1)] = side[20 + slot // 2, slot % 2]

    def start(plane, carry):
        for ahead, side in sides:
            index = plane + 1 + ahead * (home + RAW)
            fluid[index], open_rate = is_fluid_rate(side[19, plane])
            opens[index] = open_rate
            state = [side[m, plane] for m in range(19)]
            density, flow = density_velocity(state)
            store(even, index, collide(state, density, flow, open_rate))
        return carry

    lax.fori_loop(0, RAW, start, 0)

    def receive(step, target):
        for m in range(19):
            for side in range(2):
                target[m, HALO + step + side] = edges[m, 4 * step + side]
                target[m, HALO + home - 2 - step + side] = edges[m, 4 * step + 2 + side]

    def both(step, body):
        def two(place, carry):
            body(step + place, place, 0)
            body(span - 3 - step + place, place, 1)
            return carry

        lax.fori_loop(0, 3, two, 0)

    def link(index, place, ahead):
        words[index] = link_word(fluid[index - 1], fluid[index], fluid[index + 1])

    def advance(step, source, target, index, place, ahead):
        state = pull(source, index, words[index])
        density, flow = density_velocity(state)
        remember(history, step, index, density, flow)
        store(target, index, collide(state, density, flow, opens[index]))

    both(1, link)
    receive(0, even)
    both(1, functools.partial(advance, 1, even, odd))
    receive(1, odd)
    both(2, functools.partial(advance, 2, odd, even))
    receive(2, even)
    drag[...] = jnp.zeros_like(drag)
    drag[0] = inner_drag[...]

    def finish(index, place, ahead):
        state = pull(even, index, words[index])
        density, flow = density_velocity(state)
        remember(history, 3, index, density, flow)
        here = fluid[index] > 0
        for m in range(19):
            final[m, index - HALO] = jnp.where(here, state[m], inner_final[m, index - HALO])
        drag[1 + place] += jnp.where(here, drag_terms(flow, opens[index]), 0.0)

    both(3, finish)
    for copy in copies:
        copy.wait()


def recall(history, step, plane):
    return history[4 * step, plane], [history[4 * step + 1 + axis, plane] for axis in range(3)]


def retreat(opens, words, share, source, target, plane, density, flow):
    mirrored = pull(source, plane, words[plane])
    adjoint = [mirrored[OPP[m]] for m in range(19)]
    open_rate = opens[plane]
    force_flow = [flow[0] + FORCE, flow[1], flow[2]]
    x, y, z = [open_rate * part for part in force_flow]
    plus, minus = pairs(adjoint)
    mx, my, mz = [part * (1.0 / 12.0) for part in first_moments(minus, 2.0)]
    xy_plus, xz_plus, yz_plus = plus[3] + plus[4], plus[5] + plus[6], plus[7] + plus[8]
    axes = [2.0 * plus[k] for k in range(3)]
    whole = 12.0 * adjoint[0] + (axes[0] + axes[1] + axes[2]) + (xy_plus + xz_plus + yz_plus)
    third = whole * (1.0 / 3.0)
    xx = axes[0] + (xy_plus + xz_plus) - third
    yy = axes[1] + (xy_plus + yz_plus) - third
    zz = axes[2] + (xz_plus + yz_plus) - third
    xy, xz, yz = plus[3] - plus[4], plus[5] - plus[6], plus[7] - plus[8]
    hx = 0.25 * (xx * x + xy * y + xz * z)
    hy = 0.25 * (xy * x + yy * y + yz * z)
    hz = 0.25 * (xz * x + yz * y + zz * z)
    rate = 1.2 * open_rate
    slope = [rate * (mx + hx), rate * (my + hy), rate * (mz + hz)]
    pushed = slope[0] * force_flow[0] + slope[1] * force_flow[1] + slope[2] * force_flow[2]
    share[plane] += density * pushed
    if target is None:
        return
    level = whole * (1.2 / 36.0) + 1.2 * (
        x * (mx + 0.5 * hx) + y * (my + 0.5 * hy) + z * (mz + 0.5 * hz)
    )
    level = level - (slope[0] * flow[0] + slope[1] * flow[1] + slope[2] * flow[2])
    values = spread(level, slope)
    for m in range(19):
        target[OPP[m], plane] = values[m] - 0.2 * adjoint[m]


def outer_kernel(
    home,
    history,
    opens,
    fluid,
    words,
    even_state,
    odd_state,
    far,
    near,
    from_far,
    from_near,
    summed,
    counted,
    outer,
    share,
    odd,
    even,
    first,
    second,
    second_flow,
):
    del summed, counted
    span = home + 2 * HALO
    up = parity()

    def seed(plane, density, flow):
        damping = 1.0 / opens[plane]
        square = flow[0] * flow[0] + flow[1] * flow[1] + flow[2] * flow[2]
        share[plane] = -square * damping
        factor = 2.0 * damping / density
        slope = [part * factor for part in flow]
        values = spread(-square * factor, slope)
        for m in range(19):
            even[OPP[m], plane] = values[m]

    for ahead, raw, message in ((up, near, from_near), (1 - up, far, from_far)):
        one = first.at[ahead]
        for m in range(19):
            for place in range(HALO):
                one[m, place] = odd_state[m, ahead * (span - HALO) + place]
        for slot in range(5):
            one[AHEAD[slot] + ahead, ahead * RAW] = message[slot]
        index = 1 + ahead * (span - 3)
        state = pull(one, 1, words[index])
        density, flow = density_velocity(state)
        for place, part in enumerate([density] + flow):
            second_flow[ahead, place] = part
        two = second.at[ahead]
        store(two, 2, collide(state, density, flow, opens[index]))
        for m in range(19):
            for place in range(2):
                two[m, 3 - 3 * ahead + place] = even_state[m, 2 + ahead * (span - 6) + place]
            two[m, 1 + 2 * ahead] = message[10 + m]
        for slot in range(5):
            two[AHEAD[slot] + ahead, 4 * ahead] = message[5 + slot]
        beyond = (message[29] >= 0.0).astype(jnp.int32)
        within = fluid[1 + ahead * (span - 3)]
        edge_word = link_word(
            beyond + ahead * (within - beyond),
            fluid[ahead * (span - 1)],
            within + ahead * (beyond - within),
        )
        for place in range(HALO):
            spot = 1 + place
            index = place + ahead * (span - 3)
            word = words[index] if place == 1 else None
            if place == 0:
                word = edge_word + ahead * (words[index] - edge_word)
            if place == 2:
                word = words[index] + ahead * (edge_word - words[index])
            state = pull(two, spot, word)
            density, flow = density_velocity(state)
            seed(index, density, flow)
            here = fluid[index] > 0
            for m in range(19):
                if place == 1:
                    initial = raw[m, ahead]
                else:
                    kept = two[m, spot]
                    initial = jnp.where((ahead > 0) == (place == 2), kept, raw[m, place // 2])
                outer[ahead, m, spot - ahead] = jnp.where(here, state[m], initial)
        for m in range(19):
            outer[ahead, m, ahead * (BX - 1)] = message[30 + m]

    def seed_home(plane):
        seed(plane, *recall(history, STEPS, plane))

    each_plane(HALO, HALO + home, seed_home)

    for side in range(2):
        flow = [second_flow[side, 1 + axis] for axis in range(3)]
        retreat(opens, words, share, even, odd, 1 + side * (span - 3), second_flow[side, 0], flow)

    def step_two(plane):
        retreat(opens, words, share, even, odd, plane, *recall(history, 2, plane))

    each_plane(HALO - 1, HALO + home + 1, step_two)


def gradient_kernel(
    home, history, opens, words, share, odd, marked, summed, gradient, to_near, to_far, total, even
):
    del summed
    up = parity()
    for plane in range(share.shape[0]):
        total[plane] = share[plane]

    def step_one(plane):
        retreat(opens, words, total, odd, even, plane, *recall(history, 1, plane))

    def step_zero(plane):
        retreat(opens, words, total, even, None, plane, *recall(history, 0, plane))

    each_plane(HALO - 1, HALO + home + 1, step_one)
    each_plane(HALO, HALO + home, step_zero)
    for plane in range(home):
        design = marked[plane]
        slope = 3.0 / ((1.6 + 3.4 * design) * (1.0 + 4.0 * design))
        gradient[plane] = jnp.where(design >= 0.0, total[plane + HALO] * slope, 0.0)
    for out, ahead in ((to_near, up), (to_far, 1 - up)):
        for plane in range(BX):
            out[plane] = gradient[ahead * (home - BX) + plane]


def scaled(home, cells, where, drag, joined, out):
    factor = cells / jnp.sum(drag[...])
    reach = (joined.shape[0] - home) // 2
    for plane in range(out.shape[0]):
        spot = jnp.clip(where[0] * BX + reach + plane, 0, joined.shape[0] - 1)
        live = plane < where[1] * BX
        out[plane] = jnp.where(live, joined[spot] * factor, 0.0)


def near_gradient(home, cells, where, drag, gradient, from_far, from_near, out, joined):
    up = parity()
    for ahead, message in ((up, from_near), (1 - up, from_far)):
        joined[pl.ds(ahead * (BX + home), BX)] = message[...]
    joined[pl.ds(BX, home)] = gradient[...]
    scaled(home, cells, where, drag, joined, out)


def far_gradient(home, cells, where, drag, gradient, from_left, from_right, out, joined):
    joined[pl.ds(0, home)] = from_left[...]
    joined[pl.ds(home, home)] = gradient[...]
    joined[pl.ds(2 * home, home)] = from_right[...]
    scaled(home, cells, where, drag, joined, out)


def place_kernel(where, final, outer, later, out, zeros, sems):
    del later
    blocks = out.shape[1] // BX
    home_blocks = final.shape[1] // BX
    beyond = outer.shape[2] // BX
    zeros[...] = jnp.zeros_like(zeros)
    for slot in range(blocks):
        target = out.at[:, pl.ds(slot * BX, BX)]
        live = slot < where[1]
        block = jnp.clip(where[0] + slot, -beyond, home_blocks + beyond - 1)
        inside = (block >= 0) & (block < home_blocks)

        @pl.when(live & inside)
        def _():
            source = final.at[:, pl.ds(block * BX, BX)]
            pltpu.make_async_copy(source, target, sems.at[slot]).start()

        @pl.when(live & jnp.logical_not(inside))
        def _():
            after = (block >= 0).astype(jnp.int32)
            within = block + beyond - after * (home_blocks + beyond)
            source = outer.at[after, :, pl.ds(within * BX, BX)]
            pltpu.make_async_copy(source, target, sems.at[slot]).start()

        @pl.when(jnp.logical_not(live))
        def _():
            pltpu.make_async_copy(zeros, target, sems.at[slot]).start()

    for slot in range(blocks):
        pltpu.make_async_copy(zeros, out.at[:, pl.ds(slot * BX, BX)], sems.at[slot]).wait()


def body(populations, design, fluid_mask, owner_after):
    count = lax.axis_size("block")
    home, width_y, width_z = design.shape
    home_blocks = home // BX
    slots = home_blocks + 2
    span = home + 2 * HALO
    plane = (width_y, width_z)
    vmem = pl.BlockSpec(memory_space=pltpu.VMEM)
    hbm = pl.BlockSpec(memory_space=pltpu.HBM)
    anywhere = pl.BlockSpec(memory_space=pl.ANY)
    smem = pl.BlockSpec(memory_space=pltpu.SMEM)
    cells = float(count * home * width_y * width_z)
    near_pairs = [(i, i ^ 1) for i in range(count)]
    far_pairs = [(i, (i + 1 if i % 2 else i - 1) % count) for i in range(count)]
    inner_pairs = far_pairs[1:-1]

    def planes(*lead, dtype=jnp.float32):
        return jax.ShapeDtypeStruct(lead + plane, dtype)

    def scratch(*lead, dtype=jnp.float32):
        return pltpu.VMEM(lead + plane, dtype)

    def call(kernel, name, ins, outs, scratches, limit, moved, *operands):
        return pl.pallas_call(
            kernel,
            out_shape=[shape for shape, _ in outs],
            in_specs=ins,
            out_specs=[spec for _, spec in outs],
            scratch_shapes=scratches,
            compiler_params=pltpu.CompilerParams(vmem_limit_bytes=limit * MIB),
            cost_estimate=pl.CostEstimate(flops=20 * moved, bytes_accessed=moved, transcendentals=0),
            name=name,
        )(*operands)

    own_near, own_far, pops, marked = call(
        functools.partial(edge_kernel, home),
        "edge_planes",
        [hbm] * 3,
        [(planes(23, RAW), vmem)] * 2 + [(planes(19, home), vmem), (planes(home), vmem)],
        [scratch(home), scratch(home, dtype=jnp.int32), pltpu.SemaphoreType.DMA((3,))],
        4,
        1_000_000,
        *[
            pltpu.with_memory_space_constraint(part, pltpu.HBM)
            for part in (populations, design, fluid_mask)
        ],
    )
    near = lax.ppermute(own_near, "block", near_pairs)
    far = lax.ppermute(own_far, "block", far_pairs)

    inner_shapes = (
        planes(49),
        planes(49),
        planes(19, 12),
        planes(16, home),
        planes(19, home),
        planes(home),
        planes(home, dtype=jnp.int32),
        planes(home, dtype=jnp.int32),
        planes(),
    )
    (
        to_near,
        to_far,
        edges,
        inner_history,
        inner_final,
        inner_opens,
        inner_fluid,
        inner_words,
        inner_drag,
    ) = call(
        functools.partial(interior_kernel, home),
        "interior_steps",
        [vmem] * 2,
        [(shape, vmem) for shape in inner_shapes],
        [scratch(19, home)] * 2,
        16,
        6_000_000,
        pops,
        marked,
    )
    from_near = lax.ppermute(to_near, "block", near_pairs)
    from_far = lax.ppermute(to_far, "block", far_pairs)

    (where,) = call(
        functools.partial(count_kernel, home_blocks),
        "slot_counts",
        [smem],
        [(jax.ShapeDtypeStruct((3,), jnp.int32), smem)],
        [],
        2,
        20_000_000,
        owner_after,
    )

    boundary_shapes = (
        planes(19, home),
        planes(16, span),
        planes(span),
        planes(span, dtype=jnp.int32),
        planes(span, dtype=jnp.int32),
        planes(1 + STEPS),
        planes(19, span),
        planes(19, span),
    )
    final, history, opens, fluid, words, drag, even_state, odd_state = call(
        functools.partial(boundary_kernel, home),
        "boundary_steps",
        [vmem] * 3 + [anywhere] + [vmem] * 5,
        [(shape, vmem) for shape in boundary_shapes],
        [pltpu.SemaphoreType.DMA((5,))],
        20,
        8_000_000,
        far,
        near,
        edges,
        inner_history,
        inner_final,
        inner_opens,
        inner_fluid,
        inner_words,
        inner_drag,
    )

    sums = [drag]
    distance = 1
    while distance < count:
        swap = [(i, i ^ distance) for i in range(count)]
        sums.append(sums[-1] + lax.ppermute(sums[-1], "block", swap))
        distance *= 2
    drag = sums[-1]

    is_far = where[2] > 0
    outer, share, odd = call(
        functools.partial(outer_kernel, home),
        "outer_steps",
        [vmem] * 10 + [anywhere] * 2,
        [(planes(2, 19, BX), vmem), (planes(span), vmem), (planes(19, span), vmem)],
        [scratch(19, span), scratch(2, 19, HALO), scratch(2, 19, HALO + 2), scratch(2, 4)],
        20,
        12_000_000,
        history,
        opens,
        fluid,
        words,
        even_state,
        odd_state,
        far,
        near,
        from_far,
        from_near,
        sums[2],
        is_far.astype(jnp.int32).reshape(1),
    )
    gradient, to_near, to_far = call(
        functools.partial(gradient_kernel, home),
        "gradient_steps",
        [vmem] * 6 + [anywhere],
        [(planes(home), vmem), (planes(BX), vmem), (planes(BX), vmem)],
        [scratch(span), scratch(19, span)],
        20,
        6_000_000,
        history,
        opens,
        words,
        share,
        odd,
        marked,
        sums[3],
    )
    from_near = lax.ppermute(to_near, "block", near_pairs)
    from_far = lax.ppermute(to_far, "block", inner_pairs)

    ring = [(i, i + 1) for i in range(count - 1)]
    back = [(i + 1, i) for i in range(count - 1)]

    def place(outer):
        (out,) = call(
            place_kernel,
            "place_populations",
            [smem, anywhere, anywhere, vmem],
            [(planes(19, slots * BX), anywhere)],
            [scratch(19, BX), pltpu.SemaphoreType.DMA((slots,))],
            8,
            4_000_000,
            where,
            final,
            outer,
            gradient,
        )
        return out

    def place_far(_):
        wide = [lax.ppermute(final, "block", route) for route in (ring, back)]
        return place(jnp.stack(wide))

    def slope(kernel, name, reach, *messages):
        (out,) = call(
            functools.partial(kernel, home, cells),
            name,
            [smem] + [vmem] * 4,
            [(planes(slots * BX), vmem)],
            [scratch(home + 2 * reach)],
            4,
            1_000_000,
            where,
            drag,
            gradient,
            *messages,
        )
        return out

    def slope_near(*messages):
        return slope(near_gradient, "near_gradient", BX, *messages)

    def slope_far(*_):
        wide = [lax.ppermute(gradient, "block", route) for route in (ring, back)]
        return slope(far_gradient, "far_gradient", home, *wide)

    populations_after = lax.cond(is_far, place_far, place, outer)
    sensitivity = lax.cond(is_far, slope_far, slope_near, from_far, from_near)
    return (populations_after, sensitivity)


def solution(mesh):
    placed = (
        P(None, ("group", "block"), None, None),
        P(("group", "block"), None, None),
        P(("group", "block"), None, None),
        P("group"),
    )
    return jax.shard_map(
        body,
        mesh=mesh,
        in_specs=placed,
        out_specs=(P(None, ("group", "block"), None, None), P(("group", "block"), None, None)),
        check_vma=False,
    )
```

```python
import functools
import math

import jax
import jax.numpy as jnp
from jax import lax
from jax.experimental import pallas as pl
from jax.experimental.pallas import tpu as pltpu
from jax.sharding import PartitionSpec as P

BX = 4
STEPS = 3
HALO = STEPS
RAW = HALO - 1
MIB = 2**20

VELOCITY = (
    (0, 0, 0),
    (1, 0, 0),
    (-1, 0, 0),
    (0, 1, 0),
    (0, -1, 0),
    (0, 0, 1),
    (0, 0, -1),
    (1, 1, 0),
    (-1, -1, 0),
    (1, -1, 0),
    (-1, 1, 0),
    (1, 0, 1),
    (-1, 0, -1),
    (1, 0, -1),
    (-1, 0, 1),
    (0, 1, 1),
    (0, -1, -1),
    (0, 1, -1),
    (0, -1, 1),
)
OPP = (0,) + tuple(m + 1 if m % 2 else m - 1 for m in range(1, 19))
AHEAD = tuple(m for m in range(19) if VELOCITY[m][0] == 1)
BEHIND = tuple(m for m in range(19) if VELOCITY[m][0] == -1)
FORCE = 0.02
ROOT_45 = math.sqrt(4.5)
ROOT_2 = math.sqrt(2.0)


def rolled(field, step_y, step_z):
    if step_y:
        field = pltpu.roll(field, step_y % field.shape[0], 0)
    if step_z:
        field = pltpu.roll(field, step_z % field.shape[1], 1)
    return field


def pairs(values):
    plus = [values[2 * k + 1] + values[2 * k + 2] for k in range(9)]
    minus = [values[2 * k + 1] - values[2 * k + 2] for k in range(9)]
    return plus, minus


def first_moments(minus, scale):
    along_x, along_y, along_z = minus[:3]
    if scale != 1.0:
        along_x, along_y, along_z = scale * along_x, scale * along_y, scale * along_z
    along_x = along_x + ((minus[3] + minus[4]) + (minus[5] + minus[6]))
    along_y = along_y + ((minus[3] - minus[4]) + (minus[7] + minus[8]))
    along_z = along_z + ((minus[5] - minus[6]) + (minus[7] - minus[8]))
    return along_x, along_y, along_z


def density_velocity(state):
    plus, minus = pairs(state)
    axes = (plus[0] + plus[1]) + (plus[2] + state[0])
    diagonals = (plus[3] + plus[4]) + (plus[5] + plus[6]) + (plus[7] + plus[8])
    density = axes + diagonals
    inverse = 1.0 / density
    momentum = first_moments(minus, 1.0)
    return density, [part * inverse for part in momentum]


def collide(state, density, flow, open_rate):
    rate = ROOT_45 * open_rate
    x, y, z = (flow[0] + FORCE) * rate, flow[1] * rate, flow[2] * rate
    xx, yy, zz = x * x, y * y, z * z
    base = 1.0 - (xx + yy + zz) * (1.0 / 3.0)
    axis_weight = density * (1.2 / 18.0)
    axis_slope = density * (1.2 * ROOT_2 / 18.0)
    side_weight = density * (1.2 / 36.0)
    side_slope = density * (1.2 * ROOT_2 / 36.0)
    result = [density * 0.4 * base - 0.2 * state[0]]
    for k, along in enumerate((x, y, z, x + y, x - y, x + z, x - z, y + z, y - z)):
        if k < 3:
            even = axis_weight * (base + (xx, yy, zz)[k])
            odd = axis_slope * along
        else:
            even = side_weight * (base + along * along)
            odd = side_slope * along
        result.append((even + odd) - 0.2 * state[2 * k + 1])
        result.append((even - odd) - 0.2 * state[2 * k + 2])
    return result


def spread(level, slope):
    x, y, z = slope
    result = [level]
    for along in (x, y, z, x + y, x - y, x + z, x - z, y + z, y - z):
        result.append(level + along)
        result.append(level - along)
    return result


def pull(source, plane, word):
    here = [source[m, plane] for m in range(19)]
    result = [here[0]]
    for m in range(1, 19):
        step_x, step_y, step_z = VELOCITY[m]
        moved = here[m] if step_x == 0 else source[m, plane - step_x]
        moved = rolled(moved, step_y, step_z)
        result.append(jnp.where((word & (1 << m)) != 0, moved, here[OPP[m]]))
    return result


def link_word(behind, here, ahead):
    rows = lax.broadcasted_iota(jnp.int32, here.shape, 0)
    columns = lax.broadcasted_iota(jnp.int32, here.shape, 1)
    joined = behind + 2 * here + 4 * ahead
    word = jnp.zeros_like(here)
    for step_y in (-1, 0, 1):
        for step_z in (-1, 0, 1):
            if step_y and step_z:
                inner = {0: 1}
            else:
                inner = {1: 0, 0: 1, -1: 2}
            near = rolled(joined, step_y, step_z)
            if step_y == 1:
                near = jnp.where(rows == 0, 0, near)
            if step_y == -1:
                near = jnp.where(rows == here.shape[0] - 1, 0, near)
            if step_z == 1:
                near = jnp.where(columns == 0, 0, near)
            if step_z == -1:
                near = jnp.where(columns == here.shape[1] - 1, 0, near)
            for step_x, place in inner.items():
                if (step_x, step_y, step_z) == (0, 0, 0):
                    continue
                m = VELOCITY.index((step_x, step_y, step_z))
                word = word | ((near & (1 << place)) << (m - place))
    return jnp.where(here > 0, word, 0)


def each_plane(low, high, body):
    def two(index, carry):
        body(low + 2 * index)
        body(low + 2 * index + 1)
        return carry

    lax.fori_loop(0, (high - low) // 2, two, 0)
    if (high - low) % 2:
        body(high - 1)


def is_fluid_rate(mark):
    design = jnp.maximum(mark, 0.0)
    return (mark >= 0.0).astype(jnp.int32), (1.0 + 4.0 * design) / (1.6 + 3.4 * design)


def store(target, plane, values):
    for m, part in enumerate(values):
        target[m, plane] = part


def remember(history, step, plane, density, flow):
    history[4 * step, plane] = density
    for axis in range(3):
        history[4 * step + 1 + axis, plane] = flow[axis]


def drag_terms(flow, open_rate):
    return (flow[0] * flow[0] + flow[1] * flow[1] + flow[2] * flow[2]) / open_rate


def parity(axis="block"):
    return 1 - lax.rem(lax.axis_index(axis), 2)


def pick(flag, yes, no):
    return no + flag * (yes - no)


def edge_kernel(home, pops_far, design, mask, near, far, pops, marked, designs, masks, sems):
    up = parity()
    copies = [
        pltpu.make_async_copy(source, target, sems.at[place])
        for place, (source, target) in enumerate(((pops_far, pops), (design, designs), (mask, masks)))
    ]
    for copy in copies:
        copy.start()
    for copy in copies[1:]:
        copy.wait()
    for plane in range(home):
        marked[plane] = jnp.where(masks[plane] > 0, designs[plane], -1.0)
    copies[0].wait()
    for out, ahead in ((near, up), (far, 1 - up)):
        first = ahead * (home - RAW)
        for plane in range(RAW):
            for m in range(19):
                out[m, plane] = pops[m, first + plane]
            out[19, plane] = marked[first + plane]
        third = ahead * (home - 1) + (1 - 2 * ahead) * RAW
        last = marked[third]
        out[22, 1] = last
        _, open_rate = is_fluid_rate(last)
        state = [pops[m, third] for m in range(19)]
        density, flow = density_velocity(state)
        collided = collide(state, density, flow, open_rate)
        for slot in range(5):
            value = jnp.where(ahead > 0, collided[AHEAD[slot]], collided[BEHIND[slot]])
            out[20 + slot // 2, slot % 2] = value


def count_kernel(home_blocks, owner, where):
    rank = lax.axis_index("block")
    below = jnp.int32(0)
    own = jnp.int32(0)
    for block in range(owner.shape[0]):
        holder = owner[block]
        below += (holder < rank).astype(jnp.int32)
        own += (holder == rank).astype(jnp.int32)
    stray = jnp.int32(0)
    for device in range(owner.shape[0] // home_blocks):
        late = owner[home_blocks * device + 1] < device
        early = owner[home_blocks * device + home_blocks - 2] > device
        stray = stray | late.astype(jnp.int32) | early.astype(jnp.int32)
    where[0] = below - home_blocks * rank
    where[1] = own
    where[2] = stray


def interior_kernel(
    home,
    pops,
    marked,
    to_near,
    to_far,
    edges,
    history,
    final,
    opens,
    fluid,
    words,
    drag,
    even,
    odd,
):
    up = parity()

    def start(plane):
        fluid[plane], open_rate = is_fluid_rate(marked[plane])
        opens[plane] = open_rate
        state = [pops[m, plane] for m in range(19)]
        density, flow = density_velocity(state)
        remember(history, 0, plane, density, flow)
        store(even, plane, collide(state, density, flow, open_rate))

    def link(plane):
        words[plane] = link_word(fluid[plane - 1], fluid[plane], fluid[plane + 1])

    def advance(step, source, target, plane):
        state = pull(source, plane, words[plane])
        density, flow = density_velocity(state)
        remember(history, step, plane, density, flow)
        store(target, plane, collide(state, density, flow, opens[plane]))

    def finish(plane):
        state = pull(even, plane, words[plane])
        density, flow = density_velocity(state)
        remember(history, 3, plane, density, flow)
        here = fluid[plane] > 0
        for m in range(19):
            final[m, plane] = jnp.where(here, state[m], pops[m, plane])
        drag[...] += jnp.where(here, drag_terms(flow, opens[plane]), 0.0)

    def keep(step, source):
        for m in range(19):
            for side in range(2):
                edges[m, 4 * step + side] = source[m, step + side]
                edges[m, 4 * step + 2 + side] = source[m, home - 2 - step + side]

    def send(out, ahead, step, source):
        outer = ahead * (home - 1) + (1 - 2 * ahead) * RAW
        if step == 1:
            for slot in range(5):
                out[slot] = source[AHEAD[slot] + 1 - ahead, outer]
            return
        inner = ahead * (home - 1) + (1 - 2 * ahead) * HALO
        here = fluid[outer] > 0
        for slot in range(5):
            out[5 + slot] = source[AHEAD[slot] + 1 - ahead, inner]
        for m in range(19):
            out[10 + m] = jnp.where(here, source[m, outer], pops[m, outer])
        out[29] = marked[inner]

    drag[...] = jnp.zeros_like(drag)
    each_plane(0, home, start)
    keep(0, even)
    each_plane(1, home - 1, link)
    each_plane(1, home - 1, functools.partial(advance, 1, even, odd))
    keep(1, odd)
    each_plane(2, home - 2, functools.partial(advance, 2, odd, even))
    keep(2, even)
    for out, ahead in ((to_near, up), (to_far, 1 - up)):
        send(out, ahead, 1, odd)
        send(out, ahead, 2, even)
    each_plane(3, home - 3, finish)
    for m in range(19):
        for plane in range(STEPS):
            final[m, plane] = pops[m, plane]
            final[m, home - STEPS + plane] = pops[m, home - STEPS + plane]
        for out, ahead in ((to_near, up), (to_far, 1 - up)):
            out[30 + m] = final[m, STEPS + ahead * (home - 1 - 2 * STEPS)]


def boundary_kernel(
    home,
    far,
    near,
    edges,
    inner_history,
    inner_final,
    inner_opens,
    inner_fluid,
    inner_words,
    inner_drag,
    final,
    history,
    opens,
    fluid,
    words,
    drag,
    even,
    odd,
    sems,
):
    span = home + 2 * HALO
    up = parity()
    sides = ((up, near), (1 - up, far))
    copies = [
        pltpu.make_async_copy(
            inner_history.at[pl.ds(4 * step, 4), pl.ds(step, home - 2 * step)],
            history.at[pl.ds(4 * step, 4), pl.ds(HALO + step, home - 2 * step)],
            sems.at[step],
        )
        for step in range(4)
    ]
    copies.append(
        pltpu.make_async_copy(
            inner_final.at[:, pl.ds(STEPS, home - 2 * STEPS)],
            final.at[:, pl.ds(STEPS, home - 2 * STEPS)],
            sems.at[4],
        )
    )
    for copy in copies:
        copy.start()

    for plane in range(home):
        fluid[plane + HALO] = inner_fluid[plane]
        opens[plane + HALO] = inner_opens[plane]
    for plane in range(1, home - 1):
        words[plane + HALO] = inner_words[plane]
    for ahead, side in sides:
        fluid[ahead * (span - 1)], opens[ahead * (span - 1)] = is_fluid_rate(side[22, 1])
        for slot in range(5):
            even[AHEAD[slot] + ahead, ahead * (span - 1)] = side[20 + slot // 2, slot % 2]

    def start(plane, carry):
        for ahead, side in sides:
            index = plane + 1 + ahead * (home + RAW)
            fluid[index], open_rate = is_fluid_rate(side[19, plane])
            opens[index] = open_rate
            state = [side[m, plane] for m in range(19)]
            density, flow = density_velocity(state)
            store(even, index, collide(state, density, flow, open_rate))
        return carry

    lax.fori_loop(0, RAW, start, 0)

    def receive(step, target):
        for m in range(19):
            for side in range(2):
                target[m, HALO + step + side] = edges[m, 4 * step + side]
                target[m, HALO + home - 2 - step + side] = edges[m, 4 * step + 2 + side]

    def both(step, body):
        def two(place, carry):
            body(step + place, place, 0)
            body(span - 3 - step + place, place, 1)
            return carry

        lax.fori_loop(0, 3, two, 0)

    def link(index, place, ahead):
        words[index] = link_word(fluid[index - 1], fluid[index], fluid[index + 1])

    def advance(step, source, target, index, place, ahead):
        state = pull(source, index, words[index])
        density, flow = density_velocity(state)
        remember(history, step, index, density, flow)
        store(target, index, collide(state, density, flow, opens[index]))

    both(1, link)
    receive(0, even)
    both(1, functools.partial(advance, 1, even, odd))
    receive(1, odd)
    both(2, functools.partial(advance, 2, odd, even))
    receive(2, even)
    drag[...] = inner_drag[...]

    def finish(index, place, ahead):
        state = pull(even, index, words[index])
        density, flow = density_velocity(state)
        remember(history, 3, index, density, flow)
        here = fluid[index] > 0
        for m in range(19):
            final[m, index - HALO] = jnp.where(here, state[m], inner_final[m, index - HALO])
        drag[...] += jnp.where(here, drag_terms(flow, opens[index]), 0.0)

    both(3, finish)
    for copy in copies:
        copy.wait()


def recall(history, step, plane):
    return history[4 * step, plane], [history[4 * step + 1 + axis, plane] for axis in range(3)]


def retreat(opens, words, share, source, target, plane, density, flow):
    mirrored = pull(source, plane, words[plane])
    adjoint = [mirrored[OPP[m]] for m in range(19)]
    open_rate = opens[plane]
    force_flow = [flow[0] + FORCE, flow[1], flow[2]]
    x, y, z = [open_rate * part for part in force_flow]
    plus, minus = pairs(adjoint)
    mx, my, mz = [part * (1.0 / 12.0) for part in first_moments(minus, 2.0)]
    xy_plus, xz_plus, yz_plus = plus[3] + plus[4], plus[5] + plus[6], plus[7] + plus[8]
    axes = [2.0 * plus[k] for k in range(3)]
    whole = 12.0 * adjoint[0] + (axes[0] + axes[1] + axes[2]) + (xy_plus + xz_plus + yz_plus)
    third = whole * (1.0 / 3.0)
    xx = axes[0] + (xy_plus + xz_plus) - third
    yy = axes[1] + (xy_plus + yz_plus) - third
    zz = axes[2] + (xz_plus + yz_plus) - third
    xy, xz, yz = plus[3] - plus[4], plus[5] - plus[6], plus[7] - plus[8]
    hx = 0.25 * (xx * x + xy * y + xz * z)
    hy = 0.25 * (xy * x + yy * y + yz * z)
    hz = 0.25 * (xz * x + yz * y + zz * z)
    rate = 1.2 * open_rate
    slope = [rate * (mx + hx), rate * (my + hy), rate * (mz + hz)]
    pushed = slope[0] * force_flow[0] + slope[1] * force_flow[1] + slope[2] * force_flow[2]
    share[plane] += density * pushed
    if target is None:
        return
    level = whole * (1.2 / 36.0) + 1.2 * (
        x * (mx + 0.5 * hx) + y * (my + 0.5 * hy) + z * (mz + 0.5 * hz)
    )
    level = level - (slope[0] * flow[0] + slope[1] * flow[1] + slope[2] * flow[2])
    values = spread(level, slope)
    for m in range(19):
        target[OPP[m], plane] = values[m] - 0.2 * adjoint[m]


def outer_kernel(
    home,
    history,
    opens,
    fluid,
    words,
    even_state,
    odd_state,
    far,
    near,
    from_far,
    from_near,
    summed,
    counted,
    outer,
    share,
    odd,
    even,
    first,
    second,
    second_flow,
):
    del summed, counted
    span = home + 2 * HALO
    up = parity()

    def seed(plane, density, flow):
        damping = 1.0 / opens[plane]
        square = flow[0] * flow[0] + flow[1] * flow[1] + flow[2] * flow[2]
        share[plane] = -square * damping
        factor = 2.0 * damping / density
        slope = [part * factor for part in flow]
        values = spread(-square * factor, slope)
        for m in range(19):
            even[OPP[m], plane] = values[m]

    for ahead, raw, message in ((up, near, from_near), (1 - up, far, from_far)):
        one = first.at[ahead]
        for m in range(19):
            for place in range(HALO):
                one[m, place] = odd_state[m, ahead * (span - HALO) + place]
        for slot in range(5):
            one[AHEAD[slot] + ahead, ahead * RAW] = message[slot]
        index = 1 + ahead * (span - 3)
        state = pull(one, 1, words[index])
        density, flow = density_velocity(state)
        for place, part in enumerate([density] + flow):
            second_flow[ahead, place] = part
        two = second.at[ahead]
        store(two, 2, collide(state, density, flow, opens[index]))
        for m in range(19):
            for place in range(2):
                two[m, 3 - 3 * ahead + place] = even_state[m, 2 + ahead * (span - 6) + place]
            two[m, 1 + 2 * ahead] = message[10 + m]
        for slot in range(5):
            two[AHEAD[slot] + ahead, 4 * ahead] = message[5 + slot]
        beyond = (message[29] >= 0.0).astype(jnp.int32)
        within = fluid[1 + ahead * (span - 3)]
        edge_word = link_word(
            beyond + ahead * (within - beyond),
            fluid[ahead * (span - 1)],
            within + ahead * (beyond - within),
        )
        for place in range(HALO):
            spot = 1 + place
            index = place + ahead * (span - 3)
            word = words[index] if place == 1 else None
            if place == 0:
                word = edge_word + ahead * (words[index] - edge_word)
            if place == 2:
                word = words[index] + ahead * (edge_word - words[index])
            state = pull(two, spot, word)
            density, flow = density_velocity(state)
            seed(index, density, flow)
            here = fluid[index] > 0
            for m in range(19):
                if place == 1:
                    initial = raw[m, ahead]
                else:
                    kept = two[m, spot]
                    initial = jnp.where((ahead > 0) == (place == 2), kept, raw[m, place // 2])
                outer[ahead, m, spot - ahead] = jnp.where(here, state[m], initial)
        for m in range(19):
            outer[ahead, m, ahead * (BX - 1)] = message[30 + m]

    def seed_home(plane):
        seed(plane, *recall(history, STEPS, plane))

    each_plane(HALO, HALO + home, seed_home)

    for side in range(2):
        flow = [second_flow[side, 1 + axis] for axis in range(3)]
        retreat(opens, words, share, even, odd, 1 + side * (span - 3), second_flow[side, 0], flow)

    def step_two(plane):
        retreat(opens, words, share, even, odd, plane, *recall(history, 2, plane))

    each_plane(HALO - 1, HALO + home + 1, step_two)


def gradient_kernel(
    home, history, opens, words, share, odd, marked, summed, gradient, to_near, to_far, total, even
):
    del summed
    up = parity()
    for plane in range(share.shape[0]):
        total[plane] = share[plane]

    def step_one(plane):
        retreat(opens, words, total, odd, even, plane, *recall(history, 1, plane))

    def step_zero(plane):
        retreat(opens, words, total, even, None, plane, *recall(history, 0, plane))

    each_plane(HALO - 1, HALO + home + 1, step_one)
    each_plane(HALO, HALO + home, step_zero)
    for plane in range(home):
        design = marked[plane]
        slope = 3.0 / ((1.6 + 3.4 * design) * (1.0 + 4.0 * design))
        gradient[plane] = jnp.where(design >= 0.0, total[plane + HALO] * slope, 0.0)
    for out, ahead in ((to_near, up), (to_far, 1 - up)):
        for plane in range(BX):
            out[plane] = gradient[ahead * (home - BX) + plane]


def scaled(home, cells, where, drag, joined, out):
    factor = cells / jnp.sum(drag[...])
    reach = (joined.shape[0] - home) // 2
    for plane in range(out.shape[0]):
        spot = jnp.clip(where[0] * BX + reach + plane, 0, joined.shape[0] - 1)
        live = plane < where[1] * BX
        out[plane] = jnp.where(live, joined[spot] * factor, 0.0)


def near_gradient(home, cells, where, drag, gradient, from_far, from_near, out, joined):
    up = parity()
    for ahead, message in ((up, from_near), (1 - up, from_far)):
        joined[pl.ds(ahead * (BX + home), BX)] = message[...]
    joined[pl.ds(BX, home)] = gradient[...]
    scaled(home, cells, where, drag, joined, out)


def far_gradient(home, cells, where, drag, gradient, from_left, from_right, out, joined):
    joined[pl.ds(0, home)] = from_left[...]
    joined[pl.ds(home, home)] = gradient[...]
    joined[pl.ds(2 * home, home)] = from_right[...]
    scaled(home, cells, where, drag, joined, out)


def place_kernel(where, final, outer, later, out, zeros, sems):
    del later
    blocks = out.shape[1] // BX
    home_blocks = final.shape[1] // BX
    beyond = outer.shape[2] // BX
    zeros[...] = jnp.zeros_like(zeros)
    for slot in range(blocks):
        target = out.at[:, pl.ds(slot * BX, BX)]
        live = slot < where[1]
        block = jnp.clip(where[0] + slot, -beyond, home_blocks + beyond - 1)
        inside = (block >= 0) & (block < home_blocks)

        @pl.when(live & inside)
        def _():
            source = final.at[:, pl.ds(block * BX, BX)]
            pltpu.make_async_copy(source, target, sems.at[slot]).start()

        @pl.when(live & jnp.logical_not(inside))
        def _():
            after = (block >= 0).astype(jnp.int32)
            within = block + beyond - after * (home_blocks + beyond)
            source = outer.at[after, :, pl.ds(within * BX, BX)]
            pltpu.make_async_copy(source, target, sems.at[slot]).start()

        @pl.when(jnp.logical_not(live))
        def _():
            pltpu.make_async_copy(zeros, target, sems.at[slot]).start()

    for slot in range(blocks):
        pltpu.make_async_copy(zeros, out.at[:, pl.ds(slot * BX, BX)], sems.at[slot]).wait()


def body(populations, design, fluid_mask, owner_after):
    count = lax.axis_size("block")
    home, width_y, width_z = design.shape
    home_blocks = home // BX
    slots = home_blocks + 2
    span = home + 2 * HALO
    plane = (width_y, width_z)
    vmem = pl.BlockSpec(memory_space=pltpu.VMEM)
    hbm = pl.BlockSpec(memory_space=pltpu.HBM)
    anywhere = pl.BlockSpec(memory_space=pl.ANY)
    smem = pl.BlockSpec(memory_space=pltpu.SMEM)
    cells = float(count * home * width_y * width_z)
    near_pairs = [(i, i ^ 1) for i in range(count)]
    far_pairs = [(i, (i + 1 if i % 2 else i - 1) % count) for i in range(count)]
    inner_pairs = far_pairs[1:-1]

    def planes(*lead, dtype=jnp.float32):
        return jax.ShapeDtypeStruct(lead + plane, dtype)

    def scratch(*lead, dtype=jnp.float32):
        return pltpu.VMEM(lead + plane, dtype)

    def call(kernel, name, ins, outs, scratches, limit, moved, *operands):
        return pl.pallas_call(
            kernel,
            out_shape=[shape for shape, _ in outs],
            in_specs=ins,
            out_specs=[spec for _, spec in outs],
            scratch_shapes=scratches,
            compiler_params=pltpu.CompilerParams(vmem_limit_bytes=limit * MIB),
            cost_estimate=pl.CostEstimate(flops=20 * moved, bytes_accessed=moved, transcendentals=0),
            name=name,
        )(*operands)

    own_near, own_far, pops, marked = call(
        functools.partial(edge_kernel, home),
        "edge_planes",
        [hbm] * 3,
        [(planes(23, RAW), vmem)] * 2 + [(planes(19, home), vmem), (planes(home), vmem)],
        [scratch(home), scratch(home, dtype=jnp.int32), pltpu.SemaphoreType.DMA((3,))],
        4,
        1_000_000,
        *[
            pltpu.with_memory_space_constraint(part, pltpu.HBM)
            for part in (populations, design, fluid_mask)
        ],
    )
    near = lax.ppermute(own_near, "block", near_pairs)
    far = lax.ppermute(own_far, "block", far_pairs)

    inner_shapes = (
        planes(49),
        planes(49),
        planes(19, 12),
        planes(16, home),
        planes(19, home),
        planes(home),
        planes(home, dtype=jnp.int32),
        planes(home, dtype=jnp.int32),
        planes(),
    )
    (
        to_near,
        to_far,
        edges,
        inner_history,
        inner_final,
        inner_opens,
        inner_fluid,
        inner_words,
        inner_drag,
    ) = call(
        functools.partial(interior_kernel, home),
        "interior_steps",
        [vmem] * 2,
        [(shape, vmem) for shape in inner_shapes],
        [scratch(19, home)] * 2,
        16,
        6_000_000,
        pops,
        marked,
    )
    from_near = lax.ppermute(to_near, "block", near_pairs)
    from_far = lax.ppermute(to_far, "block", far_pairs)

    (where,) = call(
        functools.partial(count_kernel, home_blocks),
        "slot_counts",
        [smem],
        [(jax.ShapeDtypeStruct((3,), jnp.int32), smem)],
        [],
        2,
        20_000_000,
        owner_after,
    )

    boundary_shapes = (
        planes(19, home),
        planes(16, span),
        planes(span),
        planes(span, dtype=jnp.int32),
        planes(span, dtype=jnp.int32),
        planes(),
        planes(19, span),
        planes(19, span),
    )
    final, history, opens, fluid, words, drag, even_state, odd_state = call(
        functools.partial(boundary_kernel, home),
        "boundary_steps",
        [vmem] * 3 + [anywhere] + [vmem] * 5,
        [(shape, vmem) for shape in boundary_shapes],
        [pltpu.SemaphoreType.DMA((5,))],
        20,
        8_000_000,
        far,
        near,
        edges,
        inner_history,
        inner_final,
        inner_opens,
        inner_fluid,
        inner_words,
        inner_drag,
    )

    copies = jnp.broadcast_to(drag[None], (count,) + drag.shape)
    drag = lax.all_to_all(copies, "block", 0, 0)

    is_far = where[2] > 0
    outer, share, odd = call(
        functools.partial(outer_kernel, home),
        "outer_steps",
        [vmem] * 10 + [anywhere] * 2,
        [(planes(2, 19, BX), vmem), (planes(span), vmem), (planes(19, span), vmem)],
        [scratch(19, span), scratch(2, 19, HALO), scratch(2, 19, HALO + 2), scratch(2, 4)],
        20,
        12_000_000,
        history,
        opens,
        fluid,
        words,
        even_state,
        odd_state,
        far,
        near,
        from_far,
        from_near,
        inner_drag,
        is_far.astype(jnp.int32).reshape(1),
    )
    gradient, to_near, to_far = call(
        functools.partial(gradient_kernel, home),
        "gradient_steps",
        [vmem] * 6 + [anywhere],
        [(planes(home), vmem), (planes(BX), vmem), (planes(BX), vmem)],
        [scratch(span), scratch(19, span)],
        20,
        6_000_000,
        history,
        opens,
        words,
        share,
        odd,
        marked,
        inner_drag,
    )
    from_near = lax.ppermute(to_near, "block", near_pairs)
    from_far = lax.ppermute(to_far, "block", inner_pairs)

    ring = [(i, i + 1) for i in range(count - 1)]
    back = [(i + 1, i) for i in range(count - 1)]

    def place(outer):
        (out,) = call(
            place_kernel,
            "place_populations",
            [smem, anywhere, anywhere, vmem],
            [(planes(19, slots * BX), anywhere)],
            [scratch(19, BX), pltpu.SemaphoreType.DMA((slots,))],
            8,
            4_000_000,
            where,
            final,
            outer,
            gradient,
        )
        return out

    def place_far(_):
        wide = [lax.ppermute(final, "block", route) for route in (ring, back)]
        return place(jnp.stack(wide))

    def slope(kernel, name, reach, *messages):
        (out,) = call(
            functools.partial(kernel, home, cells),
            name,
            [smem] + [vmem] * 4,
            [(planes(slots * BX), vmem)],
            [scratch(home + 2 * reach)],
            4,
            1_000_000,
            where,
            drag,
            gradient,
            *messages,
        )
        return out

    def slope_near(*messages):
        return slope(near_gradient, "near_gradient", BX, *messages)

    def slope_far(*_):
        wide = [lax.ppermute(gradient, "block", route) for route in (ring, back)]
        return slope(far_gradient, "far_gradient", home, *wide)

    populations_after = lax.cond(is_far, place_far, place, outer)
    sensitivity = lax.cond(is_far, slope_far, slope_near, from_far, from_near)
    return (populations_after, sensitivity)


def solution(mesh):
    placed = (
        P(None, ("group", "block"), None, None),
        P(("group", "block"), None, None),
        P(("group", "block"), None, None),
        P("group"),
    )
    return jax.shard_map(
        body,
        mesh=mesh,
        in_specs=placed,
        out_specs=(P(None, ("group", "block"), None, None), P(("group", "block"), None, None)),
        check_vma=False,
    )
```

```python
import functools
import math

import jax
import jax.numpy as jnp
from jax import lax
from jax.experimental import pallas as pl
from jax.experimental.pallas import tpu as pltpu
from jax.sharding import PartitionSpec as P

BX = 4
STEPS = 3
HALO = STEPS
RAW = HALO - 1
MIB = 2**20

VELOCITY = (
    (0, 0, 0),
    (1, 0, 0),
    (-1, 0, 0),
    (0, 1, 0),
    (0, -1, 0),
    (0, 0, 1),
    (0, 0, -1),
    (1, 1, 0),
    (-1, -1, 0),
    (1, -1, 0),
    (-1, 1, 0),
    (1, 0, 1),
    (-1, 0, -1),
    (1, 0, -1),
    (-1, 0, 1),
    (0, 1, 1),
    (0, -1, -1),
    (0, 1, -1),
    (0, -1, 1),
)
OPP = (0,) + tuple(m + 1 if m % 2 else m - 1 for m in range(1, 19))
AHEAD = tuple(m for m in range(19) if VELOCITY[m][0] == 1)
BEHIND = tuple(m for m in range(19) if VELOCITY[m][0] == -1)
FORCE = 0.02
ROOT_45 = math.sqrt(4.5)
ROOT_2 = math.sqrt(2.0)


def rolled(field, step_y, step_z):
    if step_y:
        field = pltpu.roll(field, step_y % field.shape[0], 0)
    if step_z:
        field = pltpu.roll(field, step_z % field.shape[1], 1)
    return field


def pairs(values):
    plus = [values[2 * k + 1] + values[2 * k + 2] for k in range(9)]
    minus = [values[2 * k + 1] - values[2 * k + 2] for k in range(9)]
    return plus, minus


def first_moments(minus, scale):
    along_x, along_y, along_z = minus[:3]
    if scale != 1.0:
        along_x, along_y, along_z = scale * along_x, scale * along_y, scale * along_z
    along_x = along_x + ((minus[3] + minus[4]) + (minus[5] + minus[6]))
    along_y = along_y + ((minus[3] - minus[4]) + (minus[7] + minus[8]))
    along_z = along_z + ((minus[5] - minus[6]) + (minus[7] - minus[8]))
    return along_x, along_y, along_z


def density_velocity(state):
    plus, minus = pairs(state)
    axes = (plus[0] + plus[1]) + (plus[2] + state[0])
    diagonals = (plus[3] + plus[4]) + (plus[5] + plus[6]) + (plus[7] + plus[8])
    density = axes + diagonals
    inverse = 1.0 / density
    momentum = first_moments(minus, 1.0)
    return density, [part * inverse for part in momentum]


def collide(state, density, flow, open_rate):
    rate = ROOT_45 * open_rate
    x, y, z = (flow[0] + FORCE) * rate, flow[1] * rate, flow[2] * rate
    xx, yy, zz = x * x, y * y, z * z
    base = 1.0 - (xx + yy + zz) * (1.0 / 3.0)
    axis_weight = density * (1.2 / 18.0)
    axis_slope = density * (1.2 * ROOT_2 / 18.0)
    side_weight = density * (1.2 / 36.0)
    side_slope = density * (1.2 * ROOT_2 / 36.0)
    result = [density * 0.4 * base - 0.2 * state[0]]
    for k, along in enumerate((x, y, z, x + y, x - y, x + z, x - z, y + z, y - z)):
        if k < 3:
            even = axis_weight * (base + (xx, yy, zz)[k])
            odd = axis_slope * along
        else:
            even = side_weight * (base + along * along)
            odd = side_slope * along
        result.append((even + odd) - 0.2 * state[2 * k + 1])
        result.append((even - odd) - 0.2 * state[2 * k + 2])
    return result


def spread(level, slope):
    x, y, z = slope
    result = [level]
    for along in (x, y, z, x + y, x - y, x + z, x - z, y + z, y - z):
        result.append(level + along)
        result.append(level - along)
    return result


def pull(source, plane, word):
    here = [source[m, plane] for m in range(19)]
    result = [here[0]]
    for m in range(1, 19):
        step_x, step_y, step_z = VELOCITY[m]
        moved = here[m] if step_x == 0 else source[m, plane - step_x]
        moved = rolled(moved, step_y, step_z)
        result.append(jnp.where((word & (1 << m)) != 0, moved, here[OPP[m]]))
    return result


def link_word(behind, here, ahead):
    rows = lax.broadcasted_iota(jnp.int32, here.shape, 0)
    columns = lax.broadcasted_iota(jnp.int32, here.shape, 1)
    joined = behind + 2 * here + 4 * ahead
    word = jnp.zeros_like(here)
    for step_y in (-1, 0, 1):
        for step_z in (-1, 0, 1):
            if step_y and step_z:
                inner = {0: 1}
            else:
                inner = {1: 0, 0: 1, -1: 2}
            near = rolled(joined, step_y, step_z)
            if step_y == 1:
                near = jnp.where(rows == 0, 0, near)
            if step_y == -1:
                near = jnp.where(rows == here.shape[0] - 1, 0, near)
            if step_z == 1:
                near = jnp.where(columns == 0, 0, near)
            if step_z == -1:
                near = jnp.where(columns == here.shape[1] - 1, 0, near)
            for step_x, place in inner.items():
                if (step_x, step_y, step_z) == (0, 0, 0):
                    continue
                m = VELOCITY.index((step_x, step_y, step_z))
                word = word | ((near & (1 << place)) << (m - place))
    return jnp.where(here > 0, word, 0)


def run(bodies):
    for body in bodies:
        next(body)
    for body in bodies:
        next(body, None)


def each_plane(low, high, body, width=2):
    groups = (high - low) // width

    def group(index, carry):
        run([body(low + width * index + place) for place in range(width)])
        return carry

    lax.fori_loop(0, groups, group, 0)
    rest = range(low + groups * width, high)
    if rest:
        run([body(plane) for plane in rest])


def is_fluid_rate(mark):
    design = jnp.maximum(mark, 0.0)
    return (mark >= 0.0).astype(jnp.int32), (1.0 + 4.0 * design) / (1.6 + 3.4 * design)


def store(target, plane, values):
    for m, part in enumerate(values):
        target[m, plane] = part


def remember(history, step, plane, density, flow):
    history[4 * step, plane] = density
    for axis in range(3):
        history[4 * step + 1 + axis, plane] = flow[axis]


def drag_terms(flow, open_rate):
    return (flow[0] * flow[0] + flow[1] * flow[1] + flow[2] * flow[2]) / open_rate


def parity(axis="block"):
    return 1 - lax.rem(lax.axis_index(axis), 2)


def pick(flag, yes, no):
    return no + flag * (yes - no)


def edge_kernel(home, pops_far, design, mask, near, far, pops, marked, designs, masks, sems):
    up = parity()
    copies = [
        pltpu.make_async_copy(source, target, sems.at[place])
        for place, (source, target) in enumerate(((pops_far, pops), (design, designs), (mask, masks)))
    ]
    for copy in copies:
        copy.start()
    for copy in copies[1:]:
        copy.wait()
    for plane in range(home):
        marked[plane] = jnp.where(masks[plane] > 0, designs[plane], -1.0)
    copies[0].wait()
    for out, ahead in ((near, up), (far, 1 - up)):
        first = ahead * (home - RAW)
        for plane in range(RAW):
            for m in range(19):
                out[m, plane] = pops[m, first + plane]
            out[19, plane] = marked[first + plane]
        third = ahead * (home - 1) + (1 - 2 * ahead) * RAW
        last = marked[third]
        out[22, 1] = last
        _, open_rate = is_fluid_rate(last)
        state = [pops[m, third] for m in range(19)]
        density, flow = density_velocity(state)
        collided = collide(state, density, flow, open_rate)
        for slot in range(5):
            value = jnp.where(ahead > 0, collided[AHEAD[slot]], collided[BEHIND[slot]])
            out[20 + slot // 2, slot % 2] = value


def count_kernel(home_blocks, owner, where):
    rank = lax.axis_index("block")
    below = jnp.int32(0)
    own = jnp.int32(0)
    for block in range(owner.shape[0]):
        holder = owner[block]
        below += (holder < rank).astype(jnp.int32)
        own += (holder == rank).astype(jnp.int32)
    stray = jnp.int32(0)
    for device in range(owner.shape[0] // home_blocks):
        late = owner[home_blocks * device + 1] < device
        early = owner[home_blocks * device + home_blocks - 2] > device
        stray = stray | late.astype(jnp.int32) | early.astype(jnp.int32)
    where[0] = below - home_blocks * rank
    where[1] = own
    where[2] = stray


def interior_kernel(
    home,
    pops,
    marked,
    to_near,
    to_far,
    edges,
    history,
    final,
    opens,
    fluid,
    words,
    drag,
    even,
    odd,
):
    up = parity()

    def start(plane):
        is_fluid, open_rate = is_fluid_rate(marked[plane])
        state = [pops[m, plane] for m in range(19)]
        density, flow = density_velocity(state)
        collided = collide(state, density, flow, open_rate)
        yield
        fluid[plane] = is_fluid
        opens[plane] = open_rate
        remember(history, 0, plane, density, flow)
        store(even, plane, collided)

    def link(plane):
        word = link_word(fluid[plane - 1], fluid[plane], fluid[plane + 1])
        yield
        words[plane] = word

    def advance(step, source, target, plane):
        state = pull(source, plane, words[plane])
        density, flow = density_velocity(state)
        collided = collide(state, density, flow, opens[plane])
        yield
        remember(history, step, plane, density, flow)
        store(target, plane, collided)

    def finish(plane):
        state = pull(even, plane, words[plane])
        density, flow = density_velocity(state)
        here = fluid[plane] > 0
        placed = [jnp.where(here, state[m], pops[m, plane]) for m in range(19)]
        part = jnp.where(here, drag_terms(flow, opens[plane]), 0.0)
        yield
        remember(history, 3, plane, density, flow)
        store(final, plane, placed)
        drag[...] += part

    def keep(step, source):
        for m in range(19):
            for side in range(2):
                edges[m, 4 * step + side] = source[m, step + side]
                edges[m, 4 * step + 2 + side] = source[m, home - 2 - step + side]

    def send(out, ahead, step, source):
        outer = ahead * (home - 1) + (1 - 2 * ahead) * RAW
        if step == 1:
            for slot in range(5):
                out[slot] = source[AHEAD[slot] + 1 - ahead, outer]
            return
        inner = ahead * (home - 1) + (1 - 2 * ahead) * HALO
        here = fluid[outer] > 0
        for slot in range(5):
            out[5 + slot] = source[AHEAD[slot] + 1 - ahead, inner]
        for m in range(19):
            out[10 + m] = jnp.where(here, source[m, outer], pops[m, outer])
        out[29] = marked[inner]

    drag[...] = jnp.zeros_like(drag)
    each_plane(0, home, start)
    keep(0, even)
    each_plane(1, home - 1, link)
    each_plane(1, home - 1, functools.partial(advance, 1, even, odd))
    keep(1, odd)
    each_plane(2, home - 2, functools.partial(advance, 2, odd, even))
    keep(2, even)
    for out, ahead in ((to_near, up), (to_far, 1 - up)):
        send(out, ahead, 1, odd)
        send(out, ahead, 2, even)
    each_plane(3, home - 3, finish)
    for m in range(19):
        for plane in range(STEPS):
            final[m, plane] = pops[m, plane]
            final[m, home - STEPS + plane] = pops[m, home - STEPS + plane]
        for out, ahead in ((to_near, up), (to_far, 1 - up)):
            out[30 + m] = final[m, STEPS + ahead * (home - 1 - 2 * STEPS)]


def boundary_kernel(
    home,
    far,
    near,
    edges,
    inner_history,
    inner_final,
    inner_opens,
    inner_fluid,
    inner_words,
    inner_drag,
    final,
    history,
    opens,
    fluid,
    words,
    drag,
    even,
    odd,
    sems,
):
    span = home + 2 * HALO
    up = parity()
    sides = ((up, near), (1 - up, far))
    copies = [
        pltpu.make_async_copy(
            inner_history.at[pl.ds(4 * step, 4), pl.ds(step, home - 2 * step)],
            history.at[pl.ds(4 * step, 4), pl.ds(HALO + step, home - 2 * step)],
            sems.at[step],
        )
        for step in range(4)
    ]
    copies.append(
        pltpu.make_async_copy(
            inner_final.at[:, pl.ds(STEPS, home - 2 * STEPS)],
            final.at[:, pl.ds(STEPS, home - 2 * STEPS)],
            sems.at[4],
        )
    )
    for copy in copies:
        copy.start()

    for plane in range(home):
        fluid[plane + HALO] = inner_fluid[plane]
        opens[plane + HALO] = inner_opens[plane]
    for plane in range(1, home - 1):
        words[plane + HALO] = inner_words[plane]
    for ahead, side in sides:
        fluid[ahead * (span - 1)], opens[ahead * (span - 1)] = is_fluid_rate(side[22, 1])
        for slot in range(5):
            even[AHEAD[slot] + ahead, ahead * (span - 1)] = side[20 + slot // 2, slot % 2]

    def begin(plane, ahead, side):
        index = plane + 1 + ahead * (home + RAW)
        is_fluid, open_rate = is_fluid_rate(side[19, plane])
        state = [side[m, plane] for m in range(19)]
        density, flow = density_velocity(state)
        collided = collide(state, density, flow, open_rate)
        yield
        fluid[index] = is_fluid
        opens[index] = open_rate
        store(even, index, collided)

    def start(plane, carry):
        run([begin(plane, *side) for side in sides])
        return carry

    lax.fori_loop(0, RAW, start, 0)

    def receive(step, target):
        for m in range(19):
            for side in range(2):
                target[m, HALO + step + side] = edges[m, 4 * step + side]
                target[m, HALO + home - 2 - step + side] = edges[m, 4 * step + 2 + side]

    def both(step, body):
        def two(place, carry):
            run([body(step + place, place, 0), body(span - 3 - step + place, place, 1)])
            return carry

        lax.fori_loop(0, 3, two, 0)

    def link(index, place, ahead):
        word = link_word(fluid[index - 1], fluid[index], fluid[index + 1])
        yield
        words[index] = word

    def advance(step, source, target, index, place, ahead):
        state = pull(source, index, words[index])
        density, flow = density_velocity(state)
        collided = collide(state, density, flow, opens[index])
        yield
        remember(history, step, index, density, flow)
        store(target, index, collided)

    both(1, link)
    receive(0, even)
    both(1, functools.partial(advance, 1, even, odd))
    receive(1, odd)
    both(2, functools.partial(advance, 2, odd, even))
    receive(2, even)
    drag[...] = jnp.zeros_like(drag)
    drag[0] = inner_drag[...]

    def finish(index, place, ahead):
        state = pull(even, index, words[index])
        density, flow = density_velocity(state)
        here = fluid[index] > 0
        placed = [jnp.where(here, state[m], inner_final[m, index - HALO]) for m in range(19)]
        part = jnp.where(here, drag_terms(flow, opens[index]), 0.0)
        yield
        remember(history, 3, index, density, flow)
        store(final, index - HALO, placed)
        drag[1 + place] += part

    both(3, finish)
    for copy in copies:
        copy.wait()


def recall(history, step, plane):
    return history[4 * step, plane], [history[4 * step + 1 + axis, plane] for axis in range(3)]


def retreat(opens, words, share, source, target, plane, density, flow):
    mirrored = pull(source, plane, words[plane])
    adjoint = [mirrored[OPP[m]] for m in range(19)]
    open_rate = opens[plane]
    force_flow = [flow[0] + FORCE, flow[1], flow[2]]
    x, y, z = [open_rate * part for part in force_flow]
    plus, minus = pairs(adjoint)
    mx, my, mz = [part * (1.0 / 12.0) for part in first_moments(minus, 2.0)]
    xy_plus, xz_plus, yz_plus = plus[3] + plus[4], plus[5] + plus[6], plus[7] + plus[8]
    axes = [2.0 * plus[k] for k in range(3)]
    whole = 12.0 * adjoint[0] + (axes[0] + axes[1] + axes[2]) + (xy_plus + xz_plus + yz_plus)
    third = whole * (1.0 / 3.0)
    xx = axes[0] + (xy_plus + xz_plus) - third
    yy = axes[1] + (xy_plus + yz_plus) - third
    zz = axes[2] + (xz_plus + yz_plus) - third
    xy, xz, yz = plus[3] - plus[4], plus[5] - plus[6], plus[7] - plus[8]
    hx = 0.25 * (xx * x + xy * y + xz * z)
    hy = 0.25 * (xy * x + yy * y + yz * z)
    hz = 0.25 * (xz * x + yz * y + zz * z)
    rate = 1.2 * open_rate
    slope = [rate * (mx + hx), rate * (my + hy), rate * (mz + hz)]
    pushed = slope[0] * force_flow[0] + slope[1] * force_flow[1] + slope[2] * force_flow[2]
    gained = share[plane] + density * pushed
    if target is None:
        yield
        share[plane] = gained
        return
    level = whole * (1.2 / 36.0) + 1.2 * (
        x * (mx + 0.5 * hx) + y * (my + 0.5 * hy) + z * (mz + 0.5 * hz)
    )
    level = level - (slope[0] * flow[0] + slope[1] * flow[1] + slope[2] * flow[2])
    values = [part - 0.2 * old for part, old in zip(spread(level, slope), adjoint)]
    yield
    share[plane] = gained
    for m in range(19):
        target[OPP[m], plane] = values[m]


def outer_kernel(
    home,
    history,
    opens,
    fluid,
    words,
    even_state,
    odd_state,
    far,
    near,
    from_far,
    from_near,
    summed,
    counted,
    outer,
    share,
    odd,
    even,
    first,
    second,
    second_flow,
):
    del summed, counted
    span = home + 2 * HALO
    up = parity()

    def seed(plane, density, flow):
        damping = 1.0 / opens[plane]
        square = flow[0] * flow[0] + flow[1] * flow[1] + flow[2] * flow[2]
        factor = 2.0 * damping / density
        slope = [part * factor for part in flow]
        values = spread(-square * factor, slope)
        yield
        share[plane] = -square * damping
        for m in range(19):
            even[OPP[m], plane] = values[m]

    for ahead, raw, message in ((up, near, from_near), (1 - up, far, from_far)):
        one = first.at[ahead]
        for m in range(19):
            for place in range(HALO):
                one[m, place] = odd_state[m, ahead * (span - HALO) + place]
        for slot in range(5):
            one[AHEAD[slot] + ahead, ahead * RAW] = message[slot]
        index = 1 + ahead * (span - 3)
        state = pull(one, 1, words[index])
        density, flow = density_velocity(state)
        for place, part in enumerate([density] + flow):
            second_flow[ahead, place] = part
        two = second.at[ahead]
        store(two, 2, collide(state, density, flow, opens[index]))
        for m in range(19):
            for place in range(2):
                two[m, 3 - 3 * ahead + place] = even_state[m, 2 + ahead * (span - 6) + place]
            two[m, 1 + 2 * ahead] = message[10 + m]
        for slot in range(5):
            two[AHEAD[slot] + ahead, 4 * ahead] = message[5 + slot]
        beyond = (message[29] >= 0.0).astype(jnp.int32)
        within = fluid[1 + ahead * (span - 3)]
        edge_word = link_word(
            beyond + ahead * (within - beyond),
            fluid[ahead * (span - 1)],
            within + ahead * (beyond - within),
        )
        for place in range(HALO):
            spot = 1 + place
            index = place + ahead * (span - 3)
            word = words[index] if place == 1 else None
            if place == 0:
                word = edge_word + ahead * (words[index] - edge_word)
            if place == 2:
                word = words[index] + ahead * (edge_word - words[index])
            state = pull(two, spot, word)
            density, flow = density_velocity(state)
            run([seed(index, density, flow)])
            here = fluid[index] > 0
            for m in range(19):
                if place == 1:
                    initial = raw[m, ahead]
                else:
                    kept = two[m, spot]
                    initial = jnp.where((ahead > 0) == (place == 2), kept, raw[m, place // 2])
                outer[ahead, m, spot - ahead] = jnp.where(here, state[m], initial)
        for m in range(19):
            outer[ahead, m, ahead * (BX - 1)] = message[30 + m]

    def seed_home(plane):
        return seed(plane, *recall(history, STEPS, plane))

    each_plane(HALO, HALO + home, seed_home)

    def ends(side):
        flow = [second_flow[side, 1 + axis] for axis in range(3)]
        return retreat(opens, words, share, even, odd, 1 + side * (span - 3), second_flow[side, 0], flow)

    run([ends(0), ends(1)])

    def step_two(plane):
        return retreat(opens, words, share, even, odd, plane, *recall(history, 2, plane))

    each_plane(HALO - 1, HALO + home + 1, step_two)


def gradient_kernel(
    home, history, opens, words, share, odd, marked, summed, gradient, to_near, to_far, total, even
):
    del summed
    up = parity()
    for plane in range(share.shape[0]):
        total[plane] = share[plane]

    def step_one(plane):
        return retreat(opens, words, total, odd, even, plane, *recall(history, 1, plane))

    def step_zero(plane):
        return retreat(opens, words, total, even, None, plane, *recall(history, 0, plane))

    each_plane(HALO - 1, HALO + home + 1, step_one)
    each_plane(HALO, HALO + home, step_zero)
    for plane in range(home):
        design = marked[plane]
        slope = 3.0 / ((1.6 + 3.4 * design) * (1.0 + 4.0 * design))
        gradient[plane] = jnp.where(design >= 0.0, total[plane + HALO] * slope, 0.0)
    for out, ahead in ((to_near, up), (to_far, 1 - up)):
        for plane in range(BX):
            out[plane] = gradient[ahead * (home - BX) + plane]


def scaled(home, cells, where, drag, joined, out):
    factor = cells / jnp.sum(drag[...])
    reach = (joined.shape[0] - home) // 2
    for plane in range(out.shape[0]):
        spot = jnp.clip(where[0] * BX + reach + plane, 0, joined.shape[0] - 1)
        live = plane < where[1] * BX
        out[plane] = jnp.where(live, joined[spot] * factor, 0.0)


def near_gradient(home, cells, where, drag, gradient, from_far, from_near, out, joined):
    up = parity()
    for ahead, message in ((up, from_near), (1 - up, from_far)):
        joined[pl.ds(ahead * (BX + home), BX)] = message[...]
    joined[pl.ds(BX, home)] = gradient[...]
    scaled(home, cells, where, drag, joined, out)


def far_gradient(home, cells, where, drag, gradient, from_left, from_right, out, joined):
    joined[pl.ds(0, home)] = from_left[...]
    joined[pl.ds(home, home)] = gradient[...]
    joined[pl.ds(2 * home, home)] = from_right[...]
    scaled(home, cells, where, drag, joined, out)


def place_kernel(where, final, outer, later, out, zeros, sems):
    del later
    blocks = out.shape[1] // BX
    home_blocks = final.shape[1] // BX
    beyond = outer.shape[2] // BX
    zeros[...] = jnp.zeros_like(zeros)
    for slot in range(blocks):
        target = out.at[:, pl.ds(slot * BX, BX)]
        live = slot < where[1]
        block = jnp.clip(where[0] + slot, -beyond, home_blocks + beyond - 1)
        inside = (block >= 0) & (block < home_blocks)

        @pl.when(live & inside)
        def _():
            source = final.at[:, pl.ds(block * BX, BX)]
            pltpu.make_async_copy(source, target, sems.at[slot]).start()

        @pl.when(live & jnp.logical_not(inside))
        def _():
            after = (block >= 0).astype(jnp.int32)
            within = block + beyond - after * (home_blocks + beyond)
            source = outer.at[after, :, pl.ds(within * BX, BX)]
            pltpu.make_async_copy(source, target, sems.at[slot]).start()

        @pl.when(jnp.logical_not(live))
        def _():
            pltpu.make_async_copy(zeros, target, sems.at[slot]).start()

    for slot in range(blocks):
        pltpu.make_async_copy(zeros, out.at[:, pl.ds(slot * BX, BX)], sems.at[slot]).wait()


def body(populations, design, fluid_mask, owner_after):
    count = lax.axis_size("block")
    home, width_y, width_z = design.shape
    home_blocks = home // BX
    slots = home_blocks + 2
    span = home + 2 * HALO
    plane = (width_y, width_z)
    vmem = pl.BlockSpec(memory_space=pltpu.VMEM)
    hbm = pl.BlockSpec(memory_space=pltpu.HBM)
    anywhere = pl.BlockSpec(memory_space=pl.ANY)
    smem = pl.BlockSpec(memory_space=pltpu.SMEM)
    cells = float(count * home * width_y * width_z)
    near_pairs = [(i, i ^ 1) for i in range(count)]
    far_pairs = [(i, (i + 1 if i % 2 else i - 1) % count) for i in range(count)]
    inner_pairs = far_pairs[1:-1]

    def planes(*lead, dtype=jnp.float32):
        return jax.ShapeDtypeStruct(lead + plane, dtype)

    def scratch(*lead, dtype=jnp.float32):
        return pltpu.VMEM(lead + plane, dtype)

    def call(kernel, name, ins, outs, scratches, limit, moved, *operands):
        return pl.pallas_call(
            kernel,
            out_shape=[shape for shape, _ in outs],
            in_specs=ins,
            out_specs=[spec for _, spec in outs],
            scratch_shapes=scratches,
            compiler_params=pltpu.CompilerParams(vmem_limit_bytes=limit * MIB),
            cost_estimate=pl.CostEstimate(flops=20 * moved, bytes_accessed=moved, transcendentals=0),
            name=name,
        )(*operands)

    own_near, own_far, pops, marked = call(
        functools.partial(edge_kernel, home),
        "edge_planes",
        [hbm] * 3,
        [(planes(23, RAW), vmem)] * 2 + [(planes(19, home), vmem), (planes(home), vmem)],
        [scratch(home), scratch(home, dtype=jnp.int32), pltpu.SemaphoreType.DMA((3,))],
        4,
        1_000_000,
        *[
            pltpu.with_memory_space_constraint(part, pltpu.HBM)
            for part in (populations, design, fluid_mask)
        ],
    )
    near = lax.ppermute(own_near, "block", near_pairs)
    far = lax.ppermute(own_far, "block", far_pairs)

    inner_shapes = (
        planes(49),
        planes(49),
        planes(19, 12),
        planes(16, home),
        planes(19, home),
        planes(home),
        planes(home, dtype=jnp.int32),
        planes(home, dtype=jnp.int32),
        planes(),
    )
    (
        to_near,
        to_far,
        edges,
        inner_history,
        inner_final,
        inner_opens,
        inner_fluid,
        inner_words,
        inner_drag,
    ) = call(
        functools.partial(interior_kernel, home),
        "interior_steps",
        [vmem] * 2,
        [(shape, vmem) for shape in inner_shapes],
        [scratch(19, home)] * 2,
        16,
        6_000_000,
        pops,
        marked,
    )
    from_near = lax.ppermute(to_near, "block", near_pairs)
    from_far = lax.ppermute(to_far, "block", far_pairs)

    (where,) = call(
        functools.partial(count_kernel, home_blocks),
        "slot_counts",
        [smem],
        [(jax.ShapeDtypeStruct((3,), jnp.int32), smem)],
        [],
        2,
        20_000_000,
        owner_after,
    )

    boundary_shapes = (
        planes(19, home),
        planes(16, span),
        planes(span),
        planes(span, dtype=jnp.int32),
        planes(span, dtype=jnp.int32),
        planes(1 + STEPS),
        planes(19, span),
        planes(19, span),
    )
    final, history, opens, fluid, words, drag, even_state, odd_state = call(
        functools.partial(boundary_kernel, home),
        "boundary_steps",
        [vmem] * 3 + [anywhere] + [vmem] * 5,
        [(shape, vmem) for shape in boundary_shapes],
        [pltpu.SemaphoreType.DMA((5,))],
        20,
        8_000_000,
        far,
        near,
        edges,
        inner_history,
        inner_final,
        inner_opens,
        inner_fluid,
        inner_words,
        inner_drag,
    )

    sums = [drag]
    distance = 1
    while distance < count:
        swap = [(i, i ^ distance) for i in range(count)]
        sums.append(sums[-1] + lax.ppermute(sums[-1], "block", swap))
        distance *= 2
    drag = sums[-1]

    is_far = where[2] > 0
    outer, share, odd = call(
        functools.partial(outer_kernel, home),
        "outer_steps",
        [vmem] * 10 + [anywhere] * 2,
        [(planes(2, 19, BX), vmem), (planes(span), vmem), (planes(19, span), vmem)],
        [scratch(19, span), scratch(2, 19, HALO), scratch(2, 19, HALO + 2), scratch(2, 4)],
        20,
        12_000_000,
        history,
        opens,
        fluid,
        words,
        even_state,
        odd_state,
        far,
        near,
        from_far,
        from_near,
        sums[2],
        is_far.astype(jnp.int32).reshape(1),
    )
    gradient, to_near, to_far = call(
        functools.partial(gradient_kernel, home),
        "gradient_steps",
        [vmem] * 6 + [anywhere],
        [(planes(home), vmem), (planes(BX), vmem), (planes(BX), vmem)],
        [scratch(span), scratch(19, span)],
        20,
        6_000_000,
        history,
        opens,
        words,
        share,
        odd,
        marked,
        sums[3],
    )
    from_near = lax.ppermute(to_near, "block", near_pairs)
    from_far = lax.ppermute(to_far, "block", inner_pairs)

    ring = [(i, i + 1) for i in range(count - 1)]
    back = [(i + 1, i) for i in range(count - 1)]

    def place(outer):
        (out,) = call(
            place_kernel,
            "place_populations",
            [smem, anywhere, anywhere, vmem],
            [(planes(19, slots * BX), anywhere)],
            [scratch(19, BX), pltpu.SemaphoreType.DMA((slots,))],
            8,
            4_000_000,
            where,
            final,
            outer,
            gradient,
        )
        return out

    def place_far(_):
        wide = [lax.ppermute(final, "block", route) for route in (ring, back)]
        return place(jnp.stack(wide))

    def slope(kernel, name, reach, *messages):
        (out,) = call(
            functools.partial(kernel, home, cells),
            name,
            [smem] + [vmem] * 4,
            [(planes(slots * BX), vmem)],
            [scratch(home + 2 * reach)],
            4,
            1_000_000,
            where,
            drag,
            gradient,
            *messages,
        )
        return out

    def slope_near(*messages):
        return slope(near_gradient, "near_gradient", BX, *messages)

    def slope_far(*_):
        wide = [lax.ppermute(gradient, "block", route) for route in (ring, back)]
        return slope(far_gradient, "far_gradient", home, *wide)

    populations_after = lax.cond(is_far, place_far, place, outer)
    sensitivity = lax.cond(is_far, slope_far, slope_near, from_far, from_near)
    return (populations_after, sensitivity)


def solution(mesh):
    placed = (
        P(None, ("group", "block"), None, None),
        P(("group", "block"), None, None),
        P(("group", "block"), None, None),
        P("group"),
    )
    return jax.shard_map(
        body,
        mesh=mesh,
        in_specs=placed,
        out_specs=(P(None, ("group", "block"), None, None), P(("group", "block"), None, None)),
        check_vma=False,
    )
```

```python
import functools
import math

import jax
import jax.numpy as jnp
from jax import lax
from jax.experimental import pallas as pl
from jax.experimental.pallas import tpu as pltpu
from jax.sharding import PartitionSpec as P

BX = 4
STEPS = 3
HALO = STEPS
RAW = HALO - 1
MIB = 2**20

VELOCITY = (
    (0, 0, 0),
    (1, 0, 0),
    (-1, 0, 0),
    (0, 1, 0),
    (0, -1, 0),
    (0, 0, 1),
    (0, 0, -1),
    (1, 1, 0),
    (-1, -1, 0),
    (1, -1, 0),
    (-1, 1, 0),
    (1, 0, 1),
    (-1, 0, -1),
    (1, 0, -1),
    (-1, 0, 1),
    (0, 1, 1),
    (0, -1, -1),
    (0, 1, -1),
    (0, -1, 1),
)
OPP = (0,) + tuple(m + 1 if m % 2 else m - 1 for m in range(1, 19))
AHEAD = tuple(m for m in range(19) if VELOCITY[m][0] == 1)
BEHIND = tuple(m for m in range(19) if VELOCITY[m][0] == -1)
FORCE = 0.02
ROOT_45 = math.sqrt(4.5)
ROOT_2 = math.sqrt(2.0)


def rolled(field, step_y, step_z):
    if step_y:
        field = pltpu.roll(field, step_y % field.shape[0], 0)
    if step_z:
        field = pltpu.roll(field, step_z % field.shape[1], 1)
    return field


def pairs(values):
    plus = [values[2 * k + 1] + values[2 * k + 2] for k in range(9)]
    minus = [values[2 * k + 1] - values[2 * k + 2] for k in range(9)]
    return plus, minus


def first_moments(minus, scale):
    along_x, along_y, along_z = minus[:3]
    if scale != 1.0:
        along_x, along_y, along_z = scale * along_x, scale * along_y, scale * along_z
    along_x = along_x + ((minus[3] + minus[4]) + (minus[5] + minus[6]))
    along_y = along_y + ((minus[3] - minus[4]) + (minus[7] + minus[8]))
    along_z = along_z + ((minus[5] - minus[6]) + (minus[7] - minus[8]))
    return along_x, along_y, along_z


def density_velocity(state):
    plus, minus = pairs(state)
    axes = (plus[0] + plus[1]) + (plus[2] + state[0])
    diagonals = (plus[3] + plus[4]) + (plus[5] + plus[6]) + (plus[7] + plus[8])
    density = axes + diagonals
    inverse = 1.0 / density
    momentum = first_moments(minus, 1.0)
    return density, [part * inverse for part in momentum]


def collide(state, density, flow, open_rate):
    rate = ROOT_45 * open_rate
    x, y, z = (flow[0] + FORCE) * rate, flow[1] * rate, flow[2] * rate
    xx, yy, zz = x * x, y * y, z * z
    base = 1.0 - (xx + yy + zz) * (1.0 / 3.0)
    axis_weight = density * (1.2 / 18.0)
    axis_slope = density * (1.2 * ROOT_2 / 18.0)
    side_weight = density * (1.2 / 36.0)
    side_slope = density * (1.2 * ROOT_2 / 36.0)
    result = [density * 0.4 * base - 0.2 * state[0]]
    for k, along in enumerate((x, y, z, x + y, x - y, x + z, x - z, y + z, y - z)):
        if k < 3:
            even = axis_weight * (base + (xx, yy, zz)[k])
            odd = axis_slope * along
        else:
            even = side_weight * (base + along * along)
            odd = side_slope * along
        result.append((even + odd) - 0.2 * state[2 * k + 1])
        result.append((even - odd) - 0.2 * state[2 * k + 2])
    return result


def spread(level, slope):
    x, y, z = slope
    result = [level]
    for along in (x, y, z, x + y, x - y, x + z, x - z, y + z, y - z):
        result.append(level + along)
        result.append(level - along)
    return result


def pull(source, plane, word):
    here = [source[m, plane] for m in range(19)]
    result = [here[0]]
    for m in range(1, 19):
        step_x, step_y, step_z = VELOCITY[m]
        moved = here[m] if step_x == 0 else source[m, plane - step_x]
        moved = rolled(moved, step_y, step_z)
        result.append(jnp.where((word & (1 << m)) != 0, moved, here[OPP[m]]))
    return result


def link_word(behind, here, ahead):
    rows = lax.broadcasted_iota(jnp.int32, here.shape, 0)
    columns = lax.broadcasted_iota(jnp.int32, here.shape, 1)
    joined = behind + 2 * here + 4 * ahead
    word = jnp.zeros_like(here)
    for step_y in (-1, 0, 1):
        for step_z in (-1, 0, 1):
            if step_y and step_z:
                inner = {0: 1}
            else:
                inner = {1: 0, 0: 1, -1: 2}
            near = rolled(joined, step_y, step_z)
            if step_y == 1:
                near = jnp.where(rows == 0, 0, near)
            if step_y == -1:
                near = jnp.where(rows == here.shape[0] - 1, 0, near)
            if step_z == 1:
                near = jnp.where(columns == 0, 0, near)
            if step_z == -1:
                near = jnp.where(columns == here.shape[1] - 1, 0, near)
            for step_x, place in inner.items():
                if (step_x, step_y, step_z) == (0, 0, 0):
                    continue
                m = VELOCITY.index((step_x, step_y, step_z))
                word = word | ((near & (1 << place)) << (m - place))
    return jnp.where(here > 0, word, 0)


def run(bodies):
    for body in bodies:
        next(body)
    for body in bodies:
        next(body, None)


def each_plane(low, high, body, width=4):
    groups = (high - low) // width

    def group(index, carry):
        run([body(low + width * index + place) for place in range(width)])
        return carry

    lax.fori_loop(0, groups, group, 0)
    rest = range(low + groups * width, high)
    if rest:
        run([body(plane) for plane in rest])


def is_fluid_rate(mark):
    design = jnp.maximum(mark, 0.0)
    return (mark >= 0.0).astype(jnp.int32), (1.0 + 4.0 * design) / (1.6 + 3.4 * design)


def store(target, plane, values):
    for m, part in enumerate(values):
        target[m, plane] = part


def remember(history, step, plane, density, flow):
    history[4 * step, plane] = density
    for axis in range(3):
        history[4 * step + 1 + axis, plane] = flow[axis]


def drag_terms(flow, open_rate):
    return (flow[0] * flow[0] + flow[1] * flow[1] + flow[2] * flow[2]) / open_rate


def parity(axis="block"):
    return 1 - lax.rem(lax.axis_index(axis), 2)


def pick(flag, yes, no):
    return no + flag * (yes - no)


def edge_kernel(home, pops_far, design, mask, near, far, pops, marked, designs, masks, sems):
    up = parity()
    copies = [
        pltpu.make_async_copy(source, target, sems.at[place])
        for place, (source, target) in enumerate(((pops_far, pops), (design, designs), (mask, masks)))
    ]
    for copy in copies:
        copy.start()
    for copy in copies[1:]:
        copy.wait()
    for plane in range(home):
        marked[plane] = jnp.where(masks[plane] > 0, designs[plane], -1.0)
    copies[0].wait()
    for out, ahead in ((near, up), (far, 1 - up)):
        first = ahead * (home - RAW)
        for plane in range(RAW):
            for m in range(19):
                out[m, plane] = pops[m, first + plane]
            out[19, plane] = marked[first + plane]
        third = ahead * (home - 1) + (1 - 2 * ahead) * RAW
        last = marked[third]
        out[22, 1] = last
        _, open_rate = is_fluid_rate(last)
        state = [pops[m, third] for m in range(19)]
        density, flow = density_velocity(state)
        collided = collide(state, density, flow, open_rate)
        for slot in range(5):
            value = jnp.where(ahead > 0, collided[AHEAD[slot]], collided[BEHIND[slot]])
            out[20 + slot // 2, slot % 2] = value


def count_kernel(home_blocks, owner, where):
    rank = lax.axis_index("block")
    below = jnp.int32(0)
    own = jnp.int32(0)
    for block in range(owner.shape[0]):
        holder = owner[block]
        below += (holder < rank).astype(jnp.int32)
        own += (holder == rank).astype(jnp.int32)
    stray = jnp.int32(0)
    for device in range(owner.shape[0] // home_blocks):
        late = owner[home_blocks * device + 1] < device
        early = owner[home_blocks * device + home_blocks - 2] > device
        stray = stray | late.astype(jnp.int32) | early.astype(jnp.int32)
    where[0] = below - home_blocks * rank
    where[1] = own
    where[2] = stray


def interior_kernel(
    home,
    pops,
    marked,
    to_near,
    to_far,
    edges,
    history,
    final,
    opens,
    fluid,
    words,
    drag,
    even,
    odd,
):
    up = parity()

    def start(plane):
        is_fluid, open_rate = is_fluid_rate(marked[plane])
        state = [pops[m, plane] for m in range(19)]
        density, flow = density_velocity(state)
        collided = collide(state, density, flow, open_rate)
        yield
        fluid[plane] = is_fluid
        opens[plane] = open_rate
        remember(history, 0, plane, density, flow)
        store(even, plane, collided)

    def link(plane):
        word = link_word(fluid[plane - 1], fluid[plane], fluid[plane + 1])
        yield
        words[plane] = word

    def advance(step, source, target, plane):
        state = pull(source, plane, words[plane])
        density, flow = density_velocity(state)
        collided = collide(state, density, flow, opens[plane])
        yield
        remember(history, step, plane, density, flow)
        store(target, plane, collided)

    def finish(plane):
        state = pull(even, plane, words[plane])
        density, flow = density_velocity(state)
        here = fluid[plane] > 0
        placed = [jnp.where(here, state[m], pops[m, plane]) for m in range(19)]
        part = jnp.where(here, drag_terms(flow, opens[plane]), 0.0)
        yield
        remember(history, 3, plane, density, flow)
        store(final, plane, placed)
        drag[...] += part

    def keep(step, source):
        for m in range(19):
            for side in range(2):
                edges[m, 4 * step + side] = source[m, step + side]
                edges[m, 4 * step + 2 + side] = source[m, home - 2 - step + side]

    def send(out, ahead, step, source):
        outer = ahead * (home - 1) + (1 - 2 * ahead) * RAW
        if step == 1:
            for slot in range(5):
                out[slot] = source[AHEAD[slot] + 1 - ahead, outer]
            return
        inner = ahead * (home - 1) + (1 - 2 * ahead) * HALO
        here = fluid[outer] > 0
        for slot in range(5):
            out[5 + slot] = source[AHEAD[slot] + 1 - ahead, inner]
        for m in range(19):
            out[10 + m] = jnp.where(here, source[m, outer], pops[m, outer])
        out[29] = marked[inner]

    drag[...] = jnp.zeros_like(drag)
    each_plane(0, home, start)
    keep(0, even)
    each_plane(1, home - 1, link)
    each_plane(1, home - 1, functools.partial(advance, 1, even, odd))
    keep(1, odd)
    each_plane(2, home - 2, functools.partial(advance, 2, odd, even))
    keep(2, even)
    for out, ahead in ((to_near, up), (to_far, 1 - up)):
        send(out, ahead, 1, odd)
        send(out, ahead, 2, even)
    each_plane(3, home - 3, finish)
    for m in range(19):
        for plane in range(STEPS):
            final[m, plane] = pops[m, plane]
            final[m, home - STEPS + plane] = pops[m, home - STEPS + plane]
        for out, ahead in ((to_near, up), (to_far, 1 - up)):
            out[30 + m] = final[m, STEPS + ahead * (home - 1 - 2 * STEPS)]


def boundary_kernel(
    home,
    far,
    near,
    edges,
    inner_history,
    inner_final,
    inner_opens,
    inner_fluid,
    inner_words,
    inner_drag,
    final,
    history,
    opens,
    fluid,
    words,
    drag,
    even,
    odd,
    sems,
):
    span = home + 2 * HALO
    up = parity()
    sides = ((up, near), (1 - up, far))
    copies = [
        pltpu.make_async_copy(
            inner_history.at[pl.ds(4 * step, 4), pl.ds(step, home - 2 * step)],
            history.at[pl.ds(4 * step, 4), pl.ds(HALO + step, home - 2 * step)],
            sems.at[step],
        )
        for step in range(4)
    ]
    copies.append(
        pltpu.make_async_copy(
            inner_final.at[:, pl.ds(STEPS, home - 2 * STEPS)],
            final.at[:, pl.ds(STEPS, home - 2 * STEPS)],
            sems.at[4],
        )
    )
    for copy in copies:
        copy.start()

    for plane in range(home):
        fluid[plane + HALO] = inner_fluid[plane]
        opens[plane + HALO] = inner_opens[plane]
    for plane in range(1, home - 1):
        words[plane + HALO] = inner_words[plane]
    for ahead, side in sides:
        fluid[ahead * (span - 1)], opens[ahead * (span - 1)] = is_fluid_rate(side[22, 1])
        for slot in range(5):
            even[AHEAD[slot] + ahead, ahead * (span - 1)] = side[20 + slot // 2, slot % 2]

    def begin(plane, ahead, side):
        index = plane + 1 + ahead * (home + RAW)
        is_fluid, open_rate = is_fluid_rate(side[19, plane])
        state = [side[m, plane] for m in range(19)]
        density, flow = density_velocity(state)
        collided = collide(state, density, flow, open_rate)
        yield
        fluid[index] = is_fluid
        opens[index] = open_rate
        store(even, index, collided)

    run([begin(plane, *side) for plane in range(RAW) for side in sides])

    def receive(step, target):
        for m in range(19):
            for side in range(2):
                target[m, HALO + step + side] = edges[m, 4 * step + side]
                target[m, HALO + home - 2 - step + side] = edges[m, 4 * step + 2 + side]

    def both(step, body):
        run(
            [
                body(first + place, place, ahead)
                for place in range(3)
                for ahead, first in enumerate((step, span - 3 - step))
            ]
        )

    def link(index, place, ahead):
        word = link_word(fluid[index - 1], fluid[index], fluid[index + 1])
        yield
        words[index] = word

    def advance(step, source, target, index, place, ahead):
        state = pull(source, index, words[index])
        density, flow = density_velocity(state)
        collided = collide(state, density, flow, opens[index])
        yield
        remember(history, step, index, density, flow)
        store(target, index, collided)

    both(1, link)
    receive(0, even)
    both(1, functools.partial(advance, 1, even, odd))
    receive(1, odd)
    both(2, functools.partial(advance, 2, odd, even))
    receive(2, even)
    drag[...] = jnp.zeros_like(drag)
    drag[0] = inner_drag[...]

    def finish(index, place, ahead):
        state = pull(even, index, words[index])
        density, flow = density_velocity(state)
        here = fluid[index] > 0
        placed = [jnp.where(here, state[m], inner_final[m, index - HALO]) for m in range(19)]
        part = jnp.where(here, drag_terms(flow, opens[index]), 0.0)
        yield
        remember(history, 3, index, density, flow)
        store(final, index - HALO, placed)
        drag[1 + place] += part

    both(3, finish)
    for copy in copies:
        copy.wait()


def recall(history, step, plane):
    return history[4 * step, plane], [history[4 * step + 1 + axis, plane] for axis in range(3)]


def retreat(opens, words, share, source, target, plane, density, flow):
    mirrored = pull(source, plane, words[plane])
    adjoint = [mirrored[OPP[m]] for m in range(19)]
    open_rate = opens[plane]
    force_flow = [flow[0] + FORCE, flow[1], flow[2]]
    x, y, z = [open_rate * part for part in force_flow]
    plus, minus = pairs(adjoint)
    mx, my, mz = [part * (1.0 / 12.0) for part in first_moments(minus, 2.0)]
    xy_plus, xz_plus, yz_plus = plus[3] + plus[4], plus[5] + plus[6], plus[7] + plus[8]
    axes = [2.0 * plus[k] for k in range(3)]
    whole = 12.0 * adjoint[0] + (axes[0] + axes[1] + axes[2]) + (xy_plus + xz_plus + yz_plus)
    third = whole * (1.0 / 3.0)
    xx = axes[0] + (xy_plus + xz_plus) - third
    yy = axes[1] + (xy_plus + yz_plus) - third
    zz = axes[2] + (xz_plus + yz_plus) - third
    xy, xz, yz = plus[3] - plus[4], plus[5] - plus[6], plus[7] - plus[8]
    hx = 0.25 * (xx * x + xy * y + xz * z)
    hy = 0.25 * (xy * x + yy * y + yz * z)
    hz = 0.25 * (xz * x + yz * y + zz * z)
    rate = 1.2 * open_rate
    slope = [rate * (mx + hx), rate * (my + hy), rate * (mz + hz)]
    pushed = slope[0] * force_flow[0] + slope[1] * force_flow[1] + slope[2] * force_flow[2]
    gained = share[plane] + density * pushed
    if target is None:
        yield
        share[plane] = gained
        return
    level = whole * (1.2 / 36.0) + 1.2 * (
        x * (mx + 0.5 * hx) + y * (my + 0.5 * hy) + z * (mz + 0.5 * hz)
    )
    level = level - (slope[0] * flow[0] + slope[1] * flow[1] + slope[2] * flow[2])
    values = [part - 0.2 * old for part, old in zip(spread(level, slope), adjoint)]
    yield
    share[plane] = gained
    for m in range(19):
        target[OPP[m], plane] = values[m]


def outer_kernel(
    home,
    history,
    opens,
    fluid,
    words,
    even_state,
    odd_state,
    far,
    near,
    from_far,
    from_near,
    summed,
    counted,
    outer,
    share,
    odd,
    even,
    first,
    second,
    second_flow,
):
    del summed, counted
    span = home + 2 * HALO
    up = parity()

    def seed(plane, density, flow):
        damping = 1.0 / opens[plane]
        square = flow[0] * flow[0] + flow[1] * flow[1] + flow[2] * flow[2]
        factor = 2.0 * damping / density
        slope = [part * factor for part in flow]
        values = spread(-square * factor, slope)
        yield
        share[plane] = -square * damping
        for m in range(19):
            even[OPP[m], plane] = values[m]

    for ahead, raw, message in ((up, near, from_near), (1 - up, far, from_far)):
        one = first.at[ahead]
        for m in range(19):
            for place in range(HALO):
                one[m, place] = odd_state[m, ahead * (span - HALO) + place]
        for slot in range(5):
            one[AHEAD[slot] + ahead, ahead * RAW] = message[slot]
        index = 1 + ahead * (span - 3)
        state = pull(one, 1, words[index])
        density, flow = density_velocity(state)
        for place, part in enumerate([density] + flow):
            second_flow[ahead, place] = part
        two = second.at[ahead]
        store(two, 2, collide(state, density, flow, opens[index]))
        for m in range(19):
            for place in range(2):
                two[m, 3 - 3 * ahead + place] = even_state[m, 2 + ahead * (span - 6) + place]
            two[m, 1 + 2 * ahead] = message[10 + m]
        for slot in range(5):
            two[AHEAD[slot] + ahead, 4 * ahead] = message[5 + slot]
        beyond = (message[29] >= 0.0).astype(jnp.int32)
        within = fluid[1 + ahead * (span - 3)]
        edge_word = link_word(
            beyond + ahead * (within - beyond),
            fluid[ahead * (span - 1)],
            within + ahead * (beyond - within),
        )
        for place in range(HALO):
            spot = 1 + place
            index = place + ahead * (span - 3)
            word = words[index] if place == 1 else None
            if place == 0:
                word = edge_word + ahead * (words[index] - edge_word)
            if place == 2:
                word = words[index] + ahead * (edge_word - words[index])
            state = pull(two, spot, word)
            density, flow = density_velocity(state)
            run([seed(index, density, flow)])
            here = fluid[index] > 0
            for m in range(19):
                if place == 1:
                    initial = raw[m, ahead]
                else:
                    kept = two[m, spot]
                    initial = jnp.where((ahead > 0) == (place == 2), kept, raw[m, place // 2])
                outer[ahead, m, spot - ahead] = jnp.where(here, state[m], initial)
        for m in range(19):
            outer[ahead, m, ahead * (BX - 1)] = message[30 + m]

    def seed_home(plane):
        return seed(plane, *recall(history, STEPS, plane))

    each_plane(HALO, HALO + home, seed_home)

    def ends(side):
        flow = [second_flow[side, 1 + axis] for axis in range(3)]
        return retreat(opens, words, share, even, odd, 1 + side * (span - 3), second_flow[side, 0], flow)

    run([ends(0), ends(1)])

    def step_two(plane):
        return retreat(opens, words, share, even, odd, plane, *recall(history, 2, plane))

    each_plane(HALO - 1, HALO + home + 1, step_two)


def gradient_kernel(
    home, history, opens, words, share, odd, marked, summed, gradient, to_near, to_far, total, even
):
    del summed
    up = parity()
    for plane in range(share.shape[0]):
        total[plane] = share[plane]

    def step_one(plane):
        return retreat(opens, words, total, odd, even, plane, *recall(history, 1, plane))

    def step_zero(plane):
        return retreat(opens, words, total, even, None, plane, *recall(history, 0, plane))

    each_plane(HALO - 1, HALO + home + 1, step_one)
    each_plane(HALO, HALO + home, step_zero)
    for plane in range(home):
        design = marked[plane]
        slope = 3.0 / ((1.6 + 3.4 * design) * (1.0 + 4.0 * design))
        gradient[plane] = jnp.where(design >= 0.0, total[plane + HALO] * slope, 0.0)
    for out, ahead in ((to_near, up), (to_far, 1 - up)):
        for plane in range(BX):
            out[plane] = gradient[ahead * (home - BX) + plane]


def scaled(home, cells, where, drag, joined, out):
    factor = cells / jnp.sum(drag[...])
    reach = (joined.shape[0] - home) // 2
    for plane in range(out.shape[0]):
        spot = jnp.clip(where[0] * BX + reach + plane, 0, joined.shape[0] - 1)
        live = plane < where[1] * BX
        out[plane] = jnp.where(live, joined[spot] * factor, 0.0)


def near_gradient(home, cells, where, drag, gradient, from_far, from_near, out, joined):
    up = parity()
    for ahead, message in ((up, from_near), (1 - up, from_far)):
        joined[pl.ds(ahead * (BX + home), BX)] = message[...]
    joined[pl.ds(BX, home)] = gradient[...]
    scaled(home, cells, where, drag, joined, out)


def far_gradient(home, cells, where, drag, gradient, from_left, from_right, out, joined):
    joined[pl.ds(0, home)] = from_left[...]
    joined[pl.ds(home, home)] = gradient[...]
    joined[pl.ds(2 * home, home)] = from_right[...]
    scaled(home, cells, where, drag, joined, out)


def place_kernel(where, final, outer, later, out, zeros, sems):
    del later
    blocks = out.shape[1] // BX
    home_blocks = final.shape[1] // BX
    beyond = outer.shape[2] // BX
    zeros[...] = jnp.zeros_like(zeros)
    for slot in range(blocks):
        target = out.at[:, pl.ds(slot * BX, BX)]
        live = slot < where[1]
        block = jnp.clip(where[0] + slot, -beyond, home_blocks + beyond - 1)
        inside = (block >= 0) & (block < home_blocks)

        @pl.when(live & inside)
        def _():
            source = final.at[:, pl.ds(block * BX, BX)]
            pltpu.make_async_copy(source, target, sems.at[slot]).start()

        @pl.when(live & jnp.logical_not(inside))
        def _():
            after = (block >= 0).astype(jnp.int32)
            within = block + beyond - after * (home_blocks + beyond)
            source = outer.at[after, :, pl.ds(within * BX, BX)]
            pltpu.make_async_copy(source, target, sems.at[slot]).start()

        @pl.when(jnp.logical_not(live))
        def _():
            pltpu.make_async_copy(zeros, target, sems.at[slot]).start()

    for slot in range(blocks):
        pltpu.make_async_copy(zeros, out.at[:, pl.ds(slot * BX, BX)], sems.at[slot]).wait()


def body(populations, design, fluid_mask, owner_after):
    count = lax.axis_size("block")
    home, width_y, width_z = design.shape
    home_blocks = home // BX
    slots = home_blocks + 2
    span = home + 2 * HALO
    plane = (width_y, width_z)
    vmem = pl.BlockSpec(memory_space=pltpu.VMEM)
    hbm = pl.BlockSpec(memory_space=pltpu.HBM)
    anywhere = pl.BlockSpec(memory_space=pl.ANY)
    smem = pl.BlockSpec(memory_space=pltpu.SMEM)
    cells = float(count * home * width_y * width_z)
    near_pairs = [(i, i ^ 1) for i in range(count)]
    far_pairs = [(i, (i + 1 if i % 2 else i - 1) % count) for i in range(count)]
    inner_pairs = far_pairs[1:-1]

    def planes(*lead, dtype=jnp.float32):
        return jax.ShapeDtypeStruct(lead + plane, dtype)

    def scratch(*lead, dtype=jnp.float32):
        return pltpu.VMEM(lead + plane, dtype)

    def call(kernel, name, ins, outs, scratches, limit, moved, *operands):
        return pl.pallas_call(
            kernel,
            out_shape=[shape for shape, _ in outs],
            in_specs=ins,
            out_specs=[spec for _, spec in outs],
            scratch_shapes=scratches,
            compiler_params=pltpu.CompilerParams(vmem_limit_bytes=limit * MIB),
            cost_estimate=pl.CostEstimate(flops=20 * moved, bytes_accessed=moved, transcendentals=0),
            name=name,
        )(*operands)

    own_near, own_far, pops, marked = call(
        functools.partial(edge_kernel, home),
        "edge_planes",
        [hbm] * 3,
        [(planes(23, RAW), vmem)] * 2 + [(planes(19, home), vmem), (planes(home), vmem)],
        [scratch(home), scratch(home, dtype=jnp.int32), pltpu.SemaphoreType.DMA((3,))],
        4,
        1_000_000,
        *[
            pltpu.with_memory_space_constraint(part, pltpu.HBM)
            for part in (populations, design, fluid_mask)
        ],
    )
    near = lax.ppermute(own_near, "block", near_pairs)
    far = lax.ppermute(own_far, "block", far_pairs)

    inner_shapes = (
        planes(49),
        planes(49),
        planes(19, 12),
        planes(16, home),
        planes(19, home),
        planes(home),
        planes(home, dtype=jnp.int32),
        planes(home, dtype=jnp.int32),
        planes(),
    )
    (
        to_near,
        to_far,
        edges,
        inner_history,
        inner_final,
        inner_opens,
        inner_fluid,
        inner_words,
        inner_drag,
    ) = call(
        functools.partial(interior_kernel, home),
        "interior_steps",
        [vmem] * 2,
        [(shape, vmem) for shape in inner_shapes],
        [scratch(19, home)] * 2,
        16,
        6_000_000,
        pops,
        marked,
    )
    from_near = lax.ppermute(to_near, "block", near_pairs)
    from_far = lax.ppermute(to_far, "block", far_pairs)

    (where,) = call(
        functools.partial(count_kernel, home_blocks),
        "slot_counts",
        [smem],
        [(jax.ShapeDtypeStruct((3,), jnp.int32), smem)],
        [],
        2,
        20_000_000,
        owner_after,
    )

    boundary_shapes = (
        planes(19, home),
        planes(16, span),
        planes(span),
        planes(span, dtype=jnp.int32),
        planes(span, dtype=jnp.int32),
        planes(1 + STEPS),
        planes(19, span),
        planes(19, span),
    )
    final, history, opens, fluid, words, drag, even_state, odd_state = call(
        functools.partial(boundary_kernel, home),
        "boundary_steps",
        [vmem] * 3 + [anywhere] + [vmem] * 5,
        [(shape, vmem) for shape in boundary_shapes],
        [pltpu.SemaphoreType.DMA((5,))],
        20,
        8_000_000,
        far,
        near,
        edges,
        inner_history,
        inner_final,
        inner_opens,
        inner_fluid,
        inner_words,
        inner_drag,
    )

    sums = [drag]
    distance = 1
    while distance < count:
        swap = [(i, i ^ distance) for i in range(count)]
        sums.append(sums[-1] + lax.ppermute(sums[-1], "block", swap))
        distance *= 2
    drag = sums[-1]

    is_far = where[2] > 0
    outer, share, odd = call(
        functools.partial(outer_kernel, home),
        "outer_steps",
        [vmem] * 10 + [anywhere] * 2,
        [(planes(2, 19, BX), vmem), (planes(span), vmem), (planes(19, span), vmem)],
        [scratch(19, span), scratch(2, 19, HALO), scratch(2, 19, HALO + 2), scratch(2, 4)],
        20,
        12_000_000,
        history,
        opens,
        fluid,
        words,
        even_state,
        odd_state,
        far,
        near,
        from_far,
        from_near,
        sums[2],
        is_far.astype(jnp.int32).reshape(1),
    )
    gradient, to_near, to_far = call(
        functools.partial(gradient_kernel, home),
        "gradient_steps",
        [vmem] * 6 + [anywhere],
        [(planes(home), vmem), (planes(BX), vmem), (planes(BX), vmem)],
        [scratch(span), scratch(19, span)],
        20,
        6_000_000,
        history,
        opens,
        words,
        share,
        odd,
        marked,
        sums[3],
    )
    from_near = lax.ppermute(to_near, "block", near_pairs)
    from_far = lax.ppermute(to_far, "block", inner_pairs)

    ring = [(i, i + 1) for i in range(count - 1)]
    back = [(i + 1, i) for i in range(count - 1)]

    def place(outer):
        (out,) = call(
            place_kernel,
            "place_populations",
            [smem, anywhere, anywhere, vmem],
            [(planes(19, slots * BX), anywhere)],
            [scratch(19, BX), pltpu.SemaphoreType.DMA((slots,))],
            8,
            4_000_000,
            where,
            final,
            outer,
            gradient,
        )
        return out

    def place_far(_):
        wide = [lax.ppermute(final, "block", route) for route in (ring, back)]
        return place(jnp.stack(wide))

    def slope(kernel, name, reach, *messages):
        (out,) = call(
            functools.partial(kernel, home, cells),
            name,
            [smem] + [vmem] * 4,
            [(planes(slots * BX), vmem)],
            [scratch(home + 2 * reach)],
            4,
            1_000_000,
            where,
            drag,
            gradient,
            *messages,
        )
        return out

    def slope_near(*messages):
        return slope(near_gradient, "near_gradient", BX, *messages)

    def slope_far(*_):
        wide = [lax.ppermute(gradient, "block", route) for route in (ring, back)]
        return slope(far_gradient, "far_gradient", home, *wide)

    populations_after = lax.cond(is_far, place_far, place, outer)
    sensitivity = lax.cond(is_far, slope_far, slope_near, from_far, from_near)
    return (populations_after, sensitivity)


def solution(mesh):
    placed = (
        P(None, ("group", "block"), None, None),
        P(("group", "block"), None, None),
        P(("group", "block"), None, None),
        P("group"),
    )
    return jax.shard_map(
        body,
        mesh=mesh,
        in_specs=placed,
        out_specs=(P(None, ("group", "block"), None, None), P(("group", "block"), None, None)),
        check_vma=False,
    )
```

```python
import functools
import math

import jax
import jax.numpy as jnp
from jax import lax
from jax.experimental import pallas as pl
from jax.experimental.pallas import tpu as pltpu
from jax.sharding import PartitionSpec as P

BX = 4
STEPS = 3
HALO = STEPS
RAW = HALO - 1
MIB = 2**20

VELOCITY = (
    (0, 0, 0),
    (1, 0, 0),
    (-1, 0, 0),
    (0, 1, 0),
    (0, -1, 0),
    (0, 0, 1),
    (0, 0, -1),
    (1, 1, 0),
    (-1, -1, 0),
    (1, -1, 0),
    (-1, 1, 0),
    (1, 0, 1),
    (-1, 0, -1),
    (1, 0, -1),
    (-1, 0, 1),
    (0, 1, 1),
    (0, -1, -1),
    (0, 1, -1),
    (0, -1, 1),
)
OPP = (0,) + tuple(m + 1 if m % 2 else m - 1 for m in range(1, 19))
AHEAD = tuple(m for m in range(19) if VELOCITY[m][0] == 1)
BEHIND = tuple(m for m in range(19) if VELOCITY[m][0] == -1)
FORCE = 0.02
ROOT_45 = math.sqrt(4.5)
ROOT_2 = math.sqrt(2.0)


def rolled(field, step_y, step_z):
    if step_y:
        field = pltpu.roll(field, step_y % field.shape[0], 0)
    if step_z:
        field = pltpu.roll(field, step_z % field.shape[1], 1)
    return field


def pairs(values):
    plus = [values[2 * k + 1] + values[2 * k + 2] for k in range(9)]
    minus = [values[2 * k + 1] - values[2 * k + 2] for k in range(9)]
    return plus, minus


def first_moments(minus, scale):
    along_x, along_y, along_z = minus[:3]
    if scale != 1.0:
        along_x, along_y, along_z = scale * along_x, scale * along_y, scale * along_z
    along_x = along_x + ((minus[3] + minus[4]) + (minus[5] + minus[6]))
    along_y = along_y + ((minus[3] - minus[4]) + (minus[7] + minus[8]))
    along_z = along_z + ((minus[5] - minus[6]) + (minus[7] - minus[8]))
    return along_x, along_y, along_z


def density_velocity(state):
    plus, minus = pairs(state)
    axes = (plus[0] + plus[1]) + (plus[2] + state[0])
    diagonals = (plus[3] + plus[4]) + (plus[5] + plus[6]) + (plus[7] + plus[8])
    density = axes + diagonals
    inverse = 1.0 / density
    momentum = first_moments(minus, 1.0)
    return density, [part * inverse for part in momentum]


def collide(state, density, flow, open_rate):
    rate = ROOT_45 * open_rate
    x, y, z = (flow[0] + FORCE) * rate, flow[1] * rate, flow[2] * rate
    xx, yy, zz = x * x, y * y, z * z
    base = 1.0 - (xx + yy + zz) * (1.0 / 3.0)
    axis_weight = density * (1.2 / 18.0)
    axis_slope = density * (1.2 * ROOT_2 / 18.0)
    side_weight = density * (1.2 / 36.0)
    side_slope = density * (1.2 * ROOT_2 / 36.0)
    result = [density * 0.4 * base - 0.2 * state[0]]
    for k, along in enumerate((x, y, z, x + y, x - y, x + z, x - z, y + z, y - z)):
        if k < 3:
            even = axis_weight * (base + (xx, yy, zz)[k])
            odd = axis_slope * along
        else:
            even = side_weight * (base + along * along)
            odd = side_slope * along
        result.append((even + odd) - 0.2 * state[2 * k + 1])
        result.append((even - odd) - 0.2 * state[2 * k + 2])
    return result


def spread(level, slope):
    x, y, z = slope
    result = [level]
    for along in (x, y, z, x + y, x - y, x + z, x - z, y + z, y - z):
        result.append(level + along)
        result.append(level - along)
    return result


def pull(source, plane, word):
    here = [source[m, plane] for m in range(19)]
    result = [here[0]]
    for m in range(1, 19):
        step_x, step_y, step_z = VELOCITY[m]
        moved = here[m] if step_x == 0 else source[m, plane - step_x]
        moved = rolled(moved, step_y, step_z)
        result.append(jnp.where((word & (1 << m)) != 0, moved, here[OPP[m]]))
    return result


def link_word(behind, here, ahead):
    rows = lax.broadcasted_iota(jnp.int32, here.shape, 0)
    columns = lax.broadcasted_iota(jnp.int32, here.shape, 1)
    joined = behind + 2 * here + 4 * ahead
    word = jnp.zeros_like(here)
    for step_y in (-1, 0, 1):
        for step_z in (-1, 0, 1):
            if step_y and step_z:
                inner = {0: 1}
            else:
                inner = {1: 0, 0: 1, -1: 2}
            near = rolled(joined, step_y, step_z)
            if step_y == 1:
                near = jnp.where(rows == 0, 0, near)
            if step_y == -1:
                near = jnp.where(rows == here.shape[0] - 1, 0, near)
            if step_z == 1:
                near = jnp.where(columns == 0, 0, near)
            if step_z == -1:
                near = jnp.where(columns == here.shape[1] - 1, 0, near)
            for step_x, place in inner.items():
                if (step_x, step_y, step_z) == (0, 0, 0):
                    continue
                m = VELOCITY.index((step_x, step_y, step_z))
                word = word | ((near & (1 << place)) << (m - place))
    return jnp.where(here > 0, word, 0)


def run(bodies):
    for body in bodies:
        next(body)
    for body in bodies:
        next(body, None)


def each_plane(low, high, body, width=6):
    groups = (high - low) // width

    def group(index, carry):
        run([body(low + width * index + place) for place in range(width)])
        return carry

    lax.fori_loop(0, groups, group, 0)
    rest = range(low + groups * width, high)
    if rest:
        run([body(plane) for plane in rest])


def is_fluid_rate(mark):
    design = jnp.maximum(mark, 0.0)
    return (mark >= 0.0).astype(jnp.int32), (1.0 + 4.0 * design) / (1.6 + 3.4 * design)


def store(target, plane, values):
    for m, part in enumerate(values):
        target[m, plane] = part


def remember(history, step, plane, density, flow):
    history[4 * step, plane] = density
    for axis in range(3):
        history[4 * step + 1 + axis, plane] = flow[axis]


def drag_terms(flow, open_rate):
    return (flow[0] * flow[0] + flow[1] * flow[1] + flow[2] * flow[2]) / open_rate


def parity(axis="block"):
    return 1 - lax.rem(lax.axis_index(axis), 2)


def pick(flag, yes, no):
    return no + flag * (yes - no)


def edge_kernel(home, pops_far, design, mask, near, far, pops, marked, designs, masks, sems):
    up = parity()
    cuts = ((0, HALO), (home - HALO, HALO), (HALO, home - 2 * HALO))
    copies = [
        pltpu.make_async_copy(design, designs, sems.at[0]),
        pltpu.make_async_copy(mask, masks, sems.at[1]),
    ] + [
        pltpu.make_async_copy(
            pops_far.at[:, pl.ds(first, planes)], pops.at[:, pl.ds(first, planes)], sems.at[2 + place]
        )
        for place, (first, planes) in enumerate(cuts)
    ]
    for copy in copies:
        copy.start()
    for copy in copies[:2]:
        copy.wait()
    for plane in range(home):
        marked[plane] = jnp.where(masks[plane] > 0, designs[plane], -1.0)
    for copy in copies[2:4]:
        copy.wait()
    for out, ahead in ((near, up), (far, 1 - up)):
        first = ahead * (home - RAW)
        for plane in range(RAW):
            for m in range(19):
                out[m, plane] = pops[m, first + plane]
            out[19, plane] = marked[first + plane]
        third = ahead * (home - 1) + (1 - 2 * ahead) * RAW
        last = marked[third]
        out[22, 1] = last
        _, open_rate = is_fluid_rate(last)
        state = [pops[m, third] for m in range(19)]
        density, flow = density_velocity(state)
        collided = collide(state, density, flow, open_rate)
        for slot in range(5):
            value = jnp.where(ahead > 0, collided[AHEAD[slot]], collided[BEHIND[slot]])
            out[20 + slot // 2, slot % 2] = value
    copies[4].wait()


def count_kernel(home_blocks, owner, where):
    rank = lax.axis_index("block")
    below = jnp.int32(0)
    own = jnp.int32(0)
    for block in range(owner.shape[0]):
        holder = owner[block]
        below += (holder < rank).astype(jnp.int32)
        own += (holder == rank).astype(jnp.int32)
    stray = jnp.int32(0)
    for device in range(owner.shape[0] // home_blocks):
        late = owner[home_blocks * device + 1] < device
        early = owner[home_blocks * device + home_blocks - 2] > device
        stray = stray | late.astype(jnp.int32) | early.astype(jnp.int32)
    where[0] = below - home_blocks * rank
    where[1] = own
    where[2] = stray


def interior_kernel(
    home,
    pops,
    marked,
    to_near,
    to_far,
    edges,
    history,
    final,
    opens,
    fluid,
    words,
    drag,
    even,
    odd,
):
    up = parity()

    def start(plane):
        is_fluid, open_rate = is_fluid_rate(marked[plane])
        state = [pops[m, plane] for m in range(19)]
        density, flow = density_velocity(state)
        collided = collide(state, density, flow, open_rate)
        yield
        fluid[plane] = is_fluid
        opens[plane] = open_rate
        remember(history, 0, plane, density, flow)
        store(even, plane, collided)

    def link(plane):
        word = link_word(fluid[plane - 1], fluid[plane], fluid[plane + 1])
        yield
        words[plane] = word

    def advance(step, source, target, plane):
        state = pull(source, plane, words[plane])
        density, flow = density_velocity(state)
        collided = collide(state, density, flow, opens[plane])
        yield
        remember(history, step, plane, density, flow)
        store(target, plane, collided)

    def finish(plane):
        state = pull(even, plane, words[plane])
        density, flow = density_velocity(state)
        here = fluid[plane] > 0
        placed = [jnp.where(here, state[m], pops[m, plane]) for m in range(19)]
        part = jnp.where(here, drag_terms(flow, opens[plane]), 0.0)
        yield
        remember(history, 3, plane, density, flow)
        store(final, plane, placed)
        drag[...] += part

    def keep(step, source):
        for m in range(19):
            for side in range(2):
                edges[m, 4 * step + side] = source[m, step + side]
                edges[m, 4 * step + 2 + side] = source[m, home - 2 - step + side]

    def send(out, ahead, step, source):
        outer = ahead * (home - 1) + (1 - 2 * ahead) * RAW
        if step == 1:
            for slot in range(5):
                out[slot] = source[AHEAD[slot] + 1 - ahead, outer]
            return
        inner = ahead * (home - 1) + (1 - 2 * ahead) * HALO
        here = fluid[outer] > 0
        for slot in range(5):
            out[5 + slot] = source[AHEAD[slot] + 1 - ahead, inner]
        for m in range(19):
            out[10 + m] = jnp.where(here, source[m, outer], pops[m, outer])
        out[29] = marked[inner]

    drag[...] = jnp.zeros_like(drag)
    each_plane(0, home, start)
    keep(0, even)
    each_plane(1, home - 1, link)
    each_plane(1, home - 1, functools.partial(advance, 1, even, odd))
    keep(1, odd)
    each_plane(2, home - 2, functools.partial(advance, 2, odd, even))
    keep(2, even)
    for out, ahead in ((to_near, up), (to_far, 1 - up)):
        send(out, ahead, 1, odd)
        send(out, ahead, 2, even)
    each_plane(3, home - 3, finish)
    for m in range(19):
        for plane in range(STEPS):
            final[m, plane] = pops[m, plane]
            final[m, home - STEPS + plane] = pops[m, home - STEPS + plane]
        for out, ahead in ((to_near, up), (to_far, 1 - up)):
            out[30 + m] = final[m, STEPS + ahead * (home - 1 - 2 * STEPS)]


def boundary_kernel(
    home,
    far,
    near,
    edges,
    inner_history,
    inner_final,
    inner_opens,
    inner_fluid,
    inner_words,
    inner_drag,
    final,
    history,
    opens,
    fluid,
    words,
    drag,
    even,
    odd,
    sems,
):
    span = home + 2 * HALO
    up = parity()
    sides = ((up, near), (1 - up, far))
    copies = [
        pltpu.make_async_copy(
            inner_history.at[pl.ds(4 * step, 4), pl.ds(step, home - 2 * step)],
            history.at[pl.ds(4 * step, 4), pl.ds(HALO + step, home - 2 * step)],
            sems.at[step],
        )
        for step in range(4)
    ]
    copies.append(
        pltpu.make_async_copy(
            inner_final.at[:, pl.ds(STEPS, home - 2 * STEPS)],
            final.at[:, pl.ds(STEPS, home - 2 * STEPS)],
            sems.at[4],
        )
    )
    for copy in copies:
        copy.start()

    for plane in range(home):
        fluid[plane + HALO] = inner_fluid[plane]
        opens[plane + HALO] = inner_opens[plane]
    for plane in range(1, home - 1):
        words[plane + HALO] = inner_words[plane]
    for ahead, side in sides:
        fluid[ahead * (span - 1)], opens[ahead * (span - 1)] = is_fluid_rate(side[22, 1])
        for slot in range(5):
            even[AHEAD[slot] + ahead, ahead * (span - 1)] = side[20 + slot // 2, slot % 2]

    def begin(plane, ahead, side):
        index = plane + 1 + ahead * (home + RAW)
        is_fluid, open_rate = is_fluid_rate(side[19, plane])
        state = [side[m, plane] for m in range(19)]
        density, flow = density_velocity(state)
        collided = collide(state, density, flow, open_rate)
        yield
        fluid[index] = is_fluid
        opens[index] = open_rate
        store(even, index, collided)

    run([begin(plane, *side) for plane in range(RAW) for side in sides])

    def receive(step, target):
        for m in range(19):
            for side in range(2):
                target[m, HALO + step + side] = edges[m, 4 * step + side]
                target[m, HALO + home - 2 - step + side] = edges[m, 4 * step + 2 + side]

    def both(step, body):
        run(
            [
                body(first + place, place, ahead)
                for place in range(3)
                for ahead, first in enumerate((step, span - 3 - step))
            ]
        )

    def link(index, place, ahead):
        word = link_word(fluid[index - 1], fluid[index], fluid[index + 1])
        yield
        words[index] = word

    def advance(step, source, target, index, place, ahead):
        state = pull(source, index, words[index])
        density, flow = density_velocity(state)
        collided = collide(state, density, flow, opens[index])
        yield
        remember(history, step, index, density, flow)
        store(target, index, collided)

    both(1, link)
    receive(0, even)
    both(1, functools.partial(advance, 1, even, odd))
    receive(1, odd)
    both(2, functools.partial(advance, 2, odd, even))
    receive(2, even)
    drag[...] = jnp.zeros_like(drag)
    drag[0] = inner_drag[...]

    def finish(index, place, ahead):
        state = pull(even, index, words[index])
        density, flow = density_velocity(state)
        here = fluid[index] > 0
        placed = [jnp.where(here, state[m], inner_final[m, index - HALO]) for m in range(19)]
        part = jnp.where(here, drag_terms(flow, opens[index]), 0.0)
        yield
        remember(history, 3, index, density, flow)
        store(final, index - HALO, placed)
        drag[1 + place] += part

    both(3, finish)
    for copy in copies:
        copy.wait()


def recall(history, step, plane):
    return history[4 * step, plane], [history[4 * step + 1 + axis, plane] for axis in range(3)]


def retreat(opens, words, share, source, target, plane, density, flow):
    mirrored = pull(source, plane, words[plane])
    adjoint = [mirrored[OPP[m]] for m in range(19)]
    open_rate = opens[plane]
    force_flow = [flow[0] + FORCE, flow[1], flow[2]]
    x, y, z = [open_rate * part for part in force_flow]
    plus, minus = pairs(adjoint)
    mx, my, mz = [part * (1.0 / 12.0) for part in first_moments(minus, 2.0)]
    xy_plus, xz_plus, yz_plus = plus[3] + plus[4], plus[5] + plus[6], plus[7] + plus[8]
    axes = [2.0 * plus[k] for k in range(3)]
    whole = 12.0 * adjoint[0] + (axes[0] + axes[1] + axes[2]) + (xy_plus + xz_plus + yz_plus)
    third = whole * (1.0 / 3.0)
    xx = axes[0] + (xy_plus + xz_plus) - third
    yy = axes[1] + (xy_plus + yz_plus) - third
    zz = axes[2] + (xz_plus + yz_plus) - third
    xy, xz, yz = plus[3] - plus[4], plus[5] - plus[6], plus[7] - plus[8]
    hx = 0.25 * (xx * x + xy * y + xz * z)
    hy = 0.25 * (xy * x + yy * y + yz * z)
    hz = 0.25 * (xz * x + yz * y + zz * z)
    rate = 1.2 * open_rate
    slope = [rate * (mx + hx), rate * (my + hy), rate * (mz + hz)]
    pushed = slope[0] * force_flow[0] + slope[1] * force_flow[1] + slope[2] * force_flow[2]
    gained = share[plane] + density * pushed
    if target is None:
        yield
        share[plane] = gained
        return
    level = whole * (1.2 / 36.0) + 1.2 * (
        x * (mx + 0.5 * hx) + y * (my + 0.5 * hy) + z * (mz + 0.5 * hz)
    )
    level = level - (slope[0] * flow[0] + slope[1] * flow[1] + slope[2] * flow[2])
    values = [part - 0.2 * old for part, old in zip(spread(level, slope), adjoint)]
    yield
    share[plane] = gained
    for m in range(19):
        target[OPP[m], plane] = values[m]


def outer_kernel(
    home,
    history,
    opens,
    fluid,
    words,
    even_state,
    odd_state,
    far,
    near,
    from_far,
    from_near,
    summed,
    counted,
    outer,
    share,
    odd,
    even,
    first,
    second,
    second_flow,
):
    del summed, counted
    span = home + 2 * HALO
    up = parity()

    def seed(plane, density, flow):
        damping = 1.0 / opens[plane]
        square = flow[0] * flow[0] + flow[1] * flow[1] + flow[2] * flow[2]
        factor = 2.0 * damping / density
        slope = [part * factor for part in flow]
        values = spread(-square * factor, slope)
        yield
        share[plane] = -square * damping
        for m in range(19):
            even[OPP[m], plane] = values[m]

    sides = ((up, near, from_near), (1 - up, far, from_far))
    edge_words = []
    for ahead, _, message in sides:
        for m in range(19):
            for place in range(HALO):
                first[ahead, m, place] = odd_state[m, ahead * (span - HALO) + place]
            for place in range(2):
                second[ahead, m, 3 - 3 * ahead + place] = even_state[m, 2 + ahead * (span - 6) + place]
            second[ahead, m, 1 + 2 * ahead] = message[10 + m]
        for slot in range(5):
            first[ahead, AHEAD[slot] + ahead, ahead * RAW] = message[slot]
            second[ahead, AHEAD[slot] + ahead, 4 * ahead] = message[5 + slot]
        beyond = (message[29] >= 0.0).astype(jnp.int32)
        within = fluid[1 + ahead * (span - 3)]
        edge_words.append(
            link_word(
                beyond + ahead * (within - beyond),
                fluid[ahead * (span - 1)],
                within + ahead * (beyond - within),
            )
        )

    def second_out(ahead):
        index = 1 + ahead * (span - 3)
        state = pull(first.at[ahead], 1, words[index])
        density, flow = density_velocity(state)
        collided = collide(state, density, flow, opens[index])
        yield
        for place, part in enumerate([density] + flow):
            second_flow[ahead, place] = part
        store(second.at[ahead], 2, collided)

    run([second_out(side[0]) for side in sides])

    def last_step(ahead, raw, message, edge_word, place):
        spot = 1 + place
        index = place + ahead * (span - 3)
        two = second.at[ahead]
        word = words[index]
        if place == 0:
            word = edge_word + ahead * (word - edge_word)
        if place == 2:
            word = word + ahead * (edge_word - word)
        state = pull(two, spot, word)
        density, flow = density_velocity(state)
        seeded = seed(index, density, flow)
        next(seeded)
        here = fluid[index] > 0
        placed = []
        for m in range(19):
            if place == 1:
                initial = raw[m, ahead]
            else:
                initial = jnp.where((ahead > 0) == (place == 2), two[m, spot], raw[m, place // 2])
            placed.append(jnp.where(here, state[m], initial))
        yield
        next(seeded, None)
        store(outer.at[ahead], spot - ahead, placed)

    run(
        [
            last_step(*side, edge_word, place)
            for place in range(HALO)
            for side, edge_word in zip(sides, edge_words)
        ]
    )
    for ahead, _, message in sides:
        for m in range(19):
            outer[ahead, m, ahead * (BX - 1)] = message[30 + m]

    def seed_home(plane):
        return seed(plane, *recall(history, STEPS, plane))

    each_plane(HALO, HALO + home, seed_home)

    def ends(side):
        flow = [second_flow[side, 1 + axis] for axis in range(3)]
        return retreat(opens, words, share, even, odd, 1 + side * (span - 3), second_flow[side, 0], flow)

    run([ends(0), ends(1)])

    def step_two(plane):
        return retreat(opens, words, share, even, odd, plane, *recall(history, 2, plane))

    each_plane(HALO - 1, HALO + home + 1, step_two)


def gradient_kernel(
    home, history, opens, words, share, odd, marked, summed, gradient, to_near, to_far, total, even
):
    del summed
    up = parity()
    for plane in range(share.shape[0]):
        total[plane] = share[plane]

    def step_one(plane):
        return retreat(opens, words, total, odd, even, plane, *recall(history, 1, plane))

    def step_zero(plane):
        return retreat(opens, words, total, even, None, plane, *recall(history, 0, plane))

    each_plane(HALO - 1, HALO + home + 1, step_one)
    each_plane(HALO, HALO + home, step_zero)
    for plane in range(home):
        design = marked[plane]
        slope = 3.0 / ((1.6 + 3.4 * design) * (1.0 + 4.0 * design))
        gradient[plane] = jnp.where(design >= 0.0, total[plane + HALO] * slope, 0.0)
    for out, ahead in ((to_near, up), (to_far, 1 - up)):
        for plane in range(BX):
            out[plane] = gradient[ahead * (home - BX) + plane]


def scaled(home, cells, where, drag, joined, out):
    factor = cells / jnp.sum(drag[...])
    reach = (joined.shape[0] - home) // 2
    for plane in range(out.shape[0]):
        spot = jnp.clip(where[0] * BX + reach + plane, 0, joined.shape[0] - 1)
        live = plane < where[1] * BX
        out[plane] = jnp.where(live, joined[spot] * factor, 0.0)


def near_gradient(home, cells, where, drag, gradient, from_far, from_near, out, joined):
    up = parity()
    for ahead, message in ((up, from_near), (1 - up, from_far)):
        joined[pl.ds(ahead * (BX + home), BX)] = message[...]
    joined[pl.ds(BX, home)] = gradient[...]
    scaled(home, cells, where, drag, joined, out)


def far_gradient(home, cells, where, drag, gradient, from_left, from_right, out, joined):
    joined[pl.ds(0, home)] = from_left[...]
    joined[pl.ds(home, home)] = gradient[...]
    joined[pl.ds(2 * home, home)] = from_right[...]
    scaled(home, cells, where, drag, joined, out)


def place_kernel(where, final, outer, later, out, zeros, sems):
    del later
    blocks = out.shape[1] // BX
    home_blocks = final.shape[1] // BX
    beyond = outer.shape[2] // BX
    zeros[...] = jnp.zeros_like(zeros)
    for slot in range(blocks):
        target = out.at[:, pl.ds(slot * BX, BX)]
        live = slot < where[1]
        block = jnp.clip(where[0] + slot, -beyond, home_blocks + beyond - 1)
        inside = (block >= 0) & (block < home_blocks)

        @pl.when(live & inside)
        def _():
            source = final.at[:, pl.ds(block * BX, BX)]
            pltpu.make_async_copy(source, target, sems.at[slot]).start()

        @pl.when(live & jnp.logical_not(inside))
        def _():
            after = (block >= 0).astype(jnp.int32)
            within = block + beyond - after * (home_blocks + beyond)
            source = outer.at[after, :, pl.ds(within * BX, BX)]
            pltpu.make_async_copy(source, target, sems.at[slot]).start()

        @pl.when(jnp.logical_not(live))
        def _():
            pltpu.make_async_copy(zeros, target, sems.at[slot]).start()

    for slot in range(blocks):
        pltpu.make_async_copy(zeros, out.at[:, pl.ds(slot * BX, BX)], sems.at[slot]).wait()


def body(populations, design, fluid_mask, owner_after):
    count = lax.axis_size("block")
    home, width_y, width_z = design.shape
    home_blocks = home // BX
    slots = home_blocks + 2
    span = home + 2 * HALO
    plane = (width_y, width_z)
    vmem = pl.BlockSpec(memory_space=pltpu.VMEM)
    hbm = pl.BlockSpec(memory_space=pltpu.HBM)
    anywhere = pl.BlockSpec(memory_space=pl.ANY)
    smem = pl.BlockSpec(memory_space=pltpu.SMEM)
    cells = float(count * home * width_y * width_z)
    near_pairs = [(i, i ^ 1) for i in range(count)]
    far_pairs = [(i, (i + 1 if i % 2 else i - 1) % count) for i in range(count)]
    inner_pairs = far_pairs[1:-1]

    def planes(*lead, dtype=jnp.float32):
        return jax.ShapeDtypeStruct(lead + plane, dtype)

    def scratch(*lead, dtype=jnp.float32):
        return pltpu.VMEM(lead + plane, dtype)

    def call(kernel, name, ins, outs, scratches, limit, moved, *operands):
        return pl.pallas_call(
            kernel,
            out_shape=[shape for shape, _ in outs],
            in_specs=ins,
            out_specs=[spec for _, spec in outs],
            scratch_shapes=scratches,
            compiler_params=pltpu.CompilerParams(vmem_limit_bytes=limit * MIB),
            cost_estimate=pl.CostEstimate(flops=20 * moved, bytes_accessed=moved, transcendentals=0),
            name=name,
        )(*operands)

    own_near, own_far, pops, marked = call(
        functools.partial(edge_kernel, home),
        "edge_planes",
        [hbm] * 3,
        [(planes(23, RAW), vmem)] * 2 + [(planes(19, home), vmem), (planes(home), vmem)],
        [scratch(home), scratch(home, dtype=jnp.int32), pltpu.SemaphoreType.DMA((5,))],
        4,
        1_000_000,
        *[
            pltpu.with_memory_space_constraint(part, pltpu.HBM)
            for part in (populations, design, fluid_mask)
        ],
    )
    near = lax.ppermute(own_near, "block", near_pairs)
    far = lax.ppermute(own_far, "block", far_pairs)

    inner_shapes = (
        planes(49),
        planes(49),
        planes(19, 12),
        planes(16, home),
        planes(19, home),
        planes(home),
        planes(home, dtype=jnp.int32),
        planes(home, dtype=jnp.int32),
        planes(),
    )
    (
        to_near,
        to_far,
        edges,
        inner_history,
        inner_final,
        inner_opens,
        inner_fluid,
        inner_words,
        inner_drag,
    ) = call(
        functools.partial(interior_kernel, home),
        "interior_steps",
        [vmem] * 2,
        [(shape, vmem) for shape in inner_shapes],
        [scratch(19, home)] * 2,
        16,
        6_000_000,
        pops,
        marked,
    )
    from_near = lax.ppermute(to_near, "block", near_pairs)
    from_far = lax.ppermute(to_far, "block", far_pairs)

    (where,) = call(
        functools.partial(count_kernel, home_blocks),
        "slot_counts",
        [smem],
        [(jax.ShapeDtypeStruct((3,), jnp.int32), smem)],
        [],
        2,
        20_000_000,
        owner_after,
    )

    boundary_shapes = (
        planes(19, home),
        planes(16, span),
        planes(span),
        planes(span, dtype=jnp.int32),
        planes(span, dtype=jnp.int32),
        planes(1 + STEPS),
        planes(19, span),
        planes(19, span),
    )
    final, history, opens, fluid, words, drag, even_state, odd_state = call(
        functools.partial(boundary_kernel, home),
        "boundary_steps",
        [vmem] * 3 + [anywhere] + [vmem] * 5,
        [(shape, vmem) for shape in boundary_shapes],
        [pltpu.SemaphoreType.DMA((5,))],
        20,
        8_000_000,
        far,
        near,
        edges,
        inner_history,
        inner_final,
        inner_opens,
        inner_fluid,
        inner_words,
        inner_drag,
    )

    sums = [drag]
    distance = 1
    while distance < count:
        swap = [(i, i ^ distance) for i in range(count)]
        sums.append(sums[-1] + lax.ppermute(sums[-1], "block", swap))
        distance *= 2
    drag = sums[-1]

    is_far = where[2] > 0
    outer, share, odd = call(
        functools.partial(outer_kernel, home),
        "outer_steps",
        [vmem] * 10 + [anywhere] * 2,
        [(planes(2, 19, BX), vmem), (planes(span), vmem), (planes(19, span), vmem)],
        [scratch(19, span), scratch(2, 19, HALO), scratch(2, 19, HALO + 2), scratch(2, 4)],
        20,
        12_000_000,
        history,
        opens,
        fluid,
        words,
        even_state,
        odd_state,
        far,
        near,
        from_far,
        from_near,
        sums[2],
        is_far.astype(jnp.int32).reshape(1),
    )
    gradient, to_near, to_far = call(
        functools.partial(gradient_kernel, home),
        "gradient_steps",
        [vmem] * 6 + [anywhere],
        [(planes(home), vmem), (planes(BX), vmem), (planes(BX), vmem)],
        [scratch(span), scratch(19, span)],
        20,
        6_000_000,
        history,
        opens,
        words,
        share,
        odd,
        marked,
        sums[3],
    )
    from_near = lax.ppermute(to_near, "block", near_pairs)
    from_far = lax.ppermute(to_far, "block", inner_pairs)

    ring = [(i, i + 1) for i in range(count - 1)]
    back = [(i + 1, i) for i in range(count - 1)]

    def place(outer):
        (out,) = call(
            place_kernel,
            "place_populations",
            [smem, anywhere, anywhere, vmem],
            [(planes(19, slots * BX), anywhere)],
            [scratch(19, BX), pltpu.SemaphoreType.DMA((slots,))],
            8,
            4_000_000,
            where,
            final,
            outer,
            gradient,
        )
        return out

    def place_far(_):
        wide = [lax.ppermute(final, "block", route) for route in (ring, back)]
        return place(jnp.stack(wide))

    def slope(kernel, name, reach, *messages):
        (out,) = call(
            functools.partial(kernel, home, cells),
            name,
            [smem] + [vmem] * 4,
            [(planes(slots * BX), vmem)],
            [scratch(home + 2 * reach)],
            4,
            1_000_000,
            where,
            drag,
            gradient,
            *messages,
        )
        return out

    def slope_near(*messages):
        return slope(near_gradient, "near_gradient", BX, *messages)

    def slope_far(*_):
        wide = [lax.ppermute(gradient, "block", route) for route in (ring, back)]
        return slope(far_gradient, "far_gradient", home, *wide)

    populations_after = lax.cond(is_far, place_far, place, outer)
    sensitivity = lax.cond(is_far, slope_far, slope_near, from_far, from_near)
    return (populations_after, sensitivity)


def solution(mesh):
    placed = (
        P(None, ("group", "block"), None, None),
        P(("group", "block"), None, None),
        P(("group", "block"), None, None),
        P("group"),
    )
    return jax.shard_map(
        body,
        mesh=mesh,
        in_specs=placed,
        out_specs=(P(None, ("group", "block"), None, None), P(("group", "block"), None, None)),
        check_vma=False,
    )
```

```python
import functools
import math

import jax
import jax.numpy as jnp
from jax import lax
from jax.experimental import pallas as pl
from jax.experimental.pallas import tpu as pltpu
from jax.sharding import PartitionSpec as P

BX = 4
STEPS = 3
HALO = STEPS
RAW = HALO - 1
MIB = 2**20

VELOCITY = (
    (0, 0, 0),
    (1, 0, 0),
    (-1, 0, 0),
    (0, 1, 0),
    (0, -1, 0),
    (0, 0, 1),
    (0, 0, -1),
    (1, 1, 0),
    (-1, -1, 0),
    (1, -1, 0),
    (-1, 1, 0),
    (1, 0, 1),
    (-1, 0, -1),
    (1, 0, -1),
    (-1, 0, 1),
    (0, 1, 1),
    (0, -1, -1),
    (0, 1, -1),
    (0, -1, 1),
)
OPP = (0,) + tuple(m + 1 if m % 2 else m - 1 for m in range(1, 19))
AHEAD = tuple(m for m in range(19) if VELOCITY[m][0] == 1)
BEHIND = tuple(m for m in range(19) if VELOCITY[m][0] == -1)
FORCE = 0.02
ROOT_45 = math.sqrt(4.5)
ROOT_2 = math.sqrt(2.0)


def rolled(field, step_y, step_z):
    if step_y:
        field = pltpu.roll(field, step_y % field.shape[0], 0)
    if step_z:
        field = pltpu.roll(field, step_z % field.shape[1], 1)
    return field


def pairs(values):
    plus = [values[2 * k + 1] + values[2 * k + 2] for k in range(9)]
    minus = [values[2 * k + 1] - values[2 * k + 2] for k in range(9)]
    return plus, minus


def first_moments(minus, scale):
    along_x, along_y, along_z = minus[:3]
    if scale != 1.0:
        along_x, along_y, along_z = scale * along_x, scale * along_y, scale * along_z
    along_x = along_x + ((minus[3] + minus[4]) + (minus[5] + minus[6]))
    along_y = along_y + ((minus[3] - minus[4]) + (minus[7] + minus[8]))
    along_z = along_z + ((minus[5] - minus[6]) + (minus[7] - minus[8]))
    return along_x, along_y, along_z


def density_velocity(state):
    plus, minus = pairs(state)
    axes = (plus[0] + plus[1]) + (plus[2] + state[0])
    diagonals = (plus[3] + plus[4]) + (plus[5] + plus[6]) + (plus[7] + plus[8])
    density = axes + diagonals
    inverse = 1.0 / density
    momentum = first_moments(minus, 1.0)
    return density, [part * inverse for part in momentum]


def collide(state, density, flow, open_rate):
    rate = ROOT_45 * open_rate
    x, y, z = (flow[0] + FORCE) * rate, flow[1] * rate, flow[2] * rate
    xx, yy, zz = x * x, y * y, z * z
    base = 1.0 - (xx + yy + zz) * (1.0 / 3.0)
    axis_weight = density * (1.2 / 18.0)
    axis_slope = density * (1.2 * ROOT_2 / 18.0)
    side_weight = density * (1.2 / 36.0)
    side_slope = density * (1.2 * ROOT_2 / 36.0)
    result = [density * 0.4 * base - 0.2 * state[0]]
    for k, along in enumerate((x, y, z, x + y, x - y, x + z, x - z, y + z, y - z)):
        if k < 3:
            even = axis_weight * (base + (xx, yy, zz)[k])
            odd = axis_slope * along
        else:
            even = side_weight * (base + along * along)
            odd = side_slope * along
        result.append((even + odd) - 0.2 * state[2 * k + 1])
        result.append((even - odd) - 0.2 * state[2 * k + 2])
    return result


def spread(level, slope):
    x, y, z = slope
    result = [level]
    for along in (x, y, z, x + y, x - y, x + z, x - z, y + z, y - z):
        result.append(level + along)
        result.append(level - along)
    return result


def pull(source, plane, word):
    here = [source[m, plane] for m in range(19)]
    result = [here[0]]
    for m in range(1, 19):
        step_x, step_y, step_z = VELOCITY[m]
        moved = here[m] if step_x == 0 else source[m, plane - step_x]
        moved = rolled(moved, step_y, step_z)
        result.append(jnp.where((word & (1 << m)) != 0, moved, here[OPP[m]]))
    return result


def link_word(behind, here, ahead):
    rows = lax.broadcasted_iota(jnp.int32, here.shape, 0)
    columns = lax.broadcasted_iota(jnp.int32, here.shape, 1)
    joined = behind + 2 * here + 4 * ahead
    word = jnp.zeros_like(here)
    for step_y in (-1, 0, 1):
        for step_z in (-1, 0, 1):
            if step_y and step_z:
                inner = {0: 1}
            else:
                inner = {1: 0, 0: 1, -1: 2}
            near = rolled(joined, step_y, step_z)
            if step_y == 1:
                near = jnp.where(rows == 0, 0, near)
            if step_y == -1:
                near = jnp.where(rows == here.shape[0] - 1, 0, near)
            if step_z == 1:
                near = jnp.where(columns == 0, 0, near)
            if step_z == -1:
                near = jnp.where(columns == here.shape[1] - 1, 0, near)
            for step_x, place in inner.items():
                if (step_x, step_y, step_z) == (0, 0, 0):
                    continue
                m = VELOCITY.index((step_x, step_y, step_z))
                word = word | ((near & (1 << place)) << (m - place))
    return jnp.where(here > 0, word, 0)


def run(bodies):
    for body in bodies:
        next(body)
    for body in bodies:
        next(body, None)


def each_plane(low, high, body, width=6):
    groups = (high - low) // width

    def group(index, carry):
        run([body(low + width * index + place) for place in range(width)])
        return carry

    lax.fori_loop(0, groups, group, 0)
    rest = range(low + groups * width, high)
    if rest:
        run([body(plane) for plane in rest])


def is_fluid_rate(mark):
    design = jnp.maximum(mark, 0.0)
    return (mark >= 0.0).astype(jnp.int32), (1.0 + 4.0 * design) / (1.6 + 3.4 * design)


def store(target, plane, values):
    for m, part in enumerate(values):
        target[m, plane] = part


def remember(history, step, plane, density, flow):
    history[4 * step, plane] = density
    for axis in range(3):
        history[4 * step + 1 + axis, plane] = flow[axis]


def drag_terms(flow, open_rate):
    return (flow[0] * flow[0] + flow[1] * flow[1] + flow[2] * flow[2]) / open_rate


def parity(axis="block"):
    return 1 - lax.rem(lax.axis_index(axis), 2)


def pick(flag, yes, no):
    return no + flag * (yes - no)


def edge_kernel(home, pops_far, design, mask, near, far, pops, marked, designs, masks, sems):
    up = parity()
    cuts = ((0, HALO), (home - HALO, HALO), (HALO, home - 2 * HALO))
    copies = [
        pltpu.make_async_copy(design, designs, sems.at[0]),
        pltpu.make_async_copy(mask, masks, sems.at[1]),
    ] + [
        pltpu.make_async_copy(
            pops_far.at[:, pl.ds(first, planes)], pops.at[:, pl.ds(first, planes)], sems.at[2 + place]
        )
        for place, (first, planes) in enumerate(cuts)
    ]
    for copy in copies:
        copy.start()
    for copy in copies[:2]:
        copy.wait()
    for plane in range(home):
        marked[plane] = jnp.where(masks[plane] > 0, designs[plane], -1.0)
    for copy in copies[2:4]:
        copy.wait()
    for out, ahead in ((near, up), (far, 1 - up)):
        first = ahead * (home - RAW)
        for plane in range(RAW):
            for m in range(19):
                out[m, plane] = pops[m, first + plane]
            out[19, plane] = marked[first + plane]
        third = ahead * (home - 1) + (1 - 2 * ahead) * RAW
        last = marked[third]
        out[22, 1] = last
        _, open_rate = is_fluid_rate(last)
        state = [pops[m, third] for m in range(19)]
        density, flow = density_velocity(state)
        collided = collide(state, density, flow, open_rate)
        for slot in range(5):
            value = jnp.where(ahead > 0, collided[AHEAD[slot]], collided[BEHIND[slot]])
            out[20 + slot // 2, slot % 2] = value
    copies[4].wait()


def count_blocks(home_blocks, owner, where):
    rank = lax.axis_index("block")
    below = jnp.int32(0)
    own = jnp.int32(0)
    for block in range(owner.shape[0]):
        holder = owner[block]
        below += (holder < rank).astype(jnp.int32)
        own += (holder == rank).astype(jnp.int32)
    stray = jnp.int32(0)
    for device in range(owner.shape[0] // home_blocks):
        late = owner[home_blocks * device + 1] < device
        early = owner[home_blocks * device + home_blocks - 2] > device
        stray = stray | late.astype(jnp.int32) | early.astype(jnp.int32)
    where[0] = below - home_blocks * rank
    where[1] = own
    where[2] = stray


def interior_kernel(
    home,
    owner_far,
    pops,
    marked,
    to_near,
    to_far,
    edges,
    history,
    final,
    opens,
    fluid,
    words,
    drag,
    where,
    even,
    odd,
    owner,
    sem,
):
    up = parity()
    copy = pltpu.make_async_copy(owner_far, owner, sem)
    copy.start()

    def start(plane):
        is_fluid, open_rate = is_fluid_rate(marked[plane])
        state = [pops[m, plane] for m in range(19)]
        density, flow = density_velocity(state)
        collided = collide(state, density, flow, open_rate)
        yield
        fluid[plane] = is_fluid
        opens[plane] = open_rate
        remember(history, 0, plane, density, flow)
        store(even, plane, collided)

    def link(plane):
        word = link_word(fluid[plane - 1], fluid[plane], fluid[plane + 1])
        yield
        words[plane] = word

    def advance(step, source, target, plane):
        state = pull(source, plane, words[plane])
        density, flow = density_velocity(state)
        collided = collide(state, density, flow, opens[plane])
        yield
        remember(history, step, plane, density, flow)
        store(target, plane, collided)

    def finish(plane):
        state = pull(even, plane, words[plane])
        density, flow = density_velocity(state)
        here = fluid[plane] > 0
        placed = [jnp.where(here, state[m], pops[m, plane]) for m in range(19)]
        part = jnp.where(here, drag_terms(flow, opens[plane]), 0.0)
        yield
        remember(history, 3, plane, density, flow)
        store(final, plane, placed)
        drag[...] += part

    def keep(step, source):
        for m in range(19):
            for side in range(2):
                edges[m, 4 * step + side] = source[m, step + side]
                edges[m, 4 * step + 2 + side] = source[m, home - 2 - step + side]

    def send(out, ahead, step, source):
        outer = ahead * (home - 1) + (1 - 2 * ahead) * RAW
        if step == 1:
            for slot in range(5):
                out[slot] = source[AHEAD[slot] + 1 - ahead, outer]
            return
        inner = ahead * (home - 1) + (1 - 2 * ahead) * HALO
        here = fluid[outer] > 0
        for slot in range(5):
            out[5 + slot] = source[AHEAD[slot] + 1 - ahead, inner]
        for m in range(19):
            out[10 + m] = jnp.where(here, source[m, outer], pops[m, outer])
        out[29] = marked[inner]

    drag[...] = jnp.zeros_like(drag)
    each_plane(0, home, start)
    keep(0, even)
    each_plane(1, home - 1, link)
    each_plane(1, home - 1, functools.partial(advance, 1, even, odd))
    keep(1, odd)
    each_plane(2, home - 2, functools.partial(advance, 2, odd, even))
    keep(2, even)
    for out, ahead in ((to_near, up), (to_far, 1 - up)):
        send(out, ahead, 1, odd)
        send(out, ahead, 2, even)
    each_plane(3, home - 3, finish)
    for m in range(19):
        for plane in range(STEPS):
            final[m, plane] = pops[m, plane]
            final[m, home - STEPS + plane] = pops[m, home - STEPS + plane]
        for out, ahead in ((to_near, up), (to_far, 1 - up)):
            out[30 + m] = final[m, STEPS + ahead * (home - 1 - 2 * STEPS)]
    copy.wait()
    count_blocks(home // BX, owner, where)


def boundary_kernel(
    home,
    far,
    near,
    edges,
    inner_history,
    inner_final,
    inner_opens,
    inner_fluid,
    inner_words,
    inner_drag,
    final,
    history,
    opens,
    fluid,
    words,
    drag,
    even,
    odd,
    sems,
):
    span = home + 2 * HALO
    up = parity()
    sides = ((up, near), (1 - up, far))
    copies = [
        pltpu.make_async_copy(
            inner_history.at[pl.ds(4 * step, 4), pl.ds(step, home - 2 * step)],
            history.at[pl.ds(4 * step, 4), pl.ds(HALO + step, home - 2 * step)],
            sems.at[step],
        )
        for step in range(4)
    ]
    copies.append(
        pltpu.make_async_copy(
            inner_final.at[:, pl.ds(STEPS, home - 2 * STEPS)],
            final.at[:, pl.ds(STEPS, home - 2 * STEPS)],
            sems.at[4],
        )
    )
    for copy in copies:
        copy.start()

    for plane in range(home):
        fluid[plane + HALO] = inner_fluid[plane]
        opens[plane + HALO] = inner_opens[plane]
    for plane in range(1, home - 1):
        words[plane + HALO] = inner_words[plane]
    for ahead, side in sides:
        fluid[ahead * (span - 1)], opens[ahead * (span - 1)] = is_fluid_rate(side[22, 1])
        for slot in range(5):
            even[AHEAD[slot] + ahead, ahead * (span - 1)] = side[20 + slot // 2, slot % 2]

    def begin(plane, ahead, side):
        index = plane + 1 + ahead * (home + RAW)
        is_fluid, open_rate = is_fluid_rate(side[19, plane])
        state = [side[m, plane] for m in range(19)]
        density, flow = density_velocity(state)
        collided = collide(state, density, flow, open_rate)
        yield
        fluid[index] = is_fluid
        opens[index] = open_rate
        store(even, index, collided)

    run([begin(plane, *side) for plane in range(RAW) for side in sides])

    def receive(step, target):
        for m in range(19):
            for side in range(2):
                target[m, HALO + step + side] = edges[m, 4 * step + side]
                target[m, HALO + home - 2 - step + side] = edges[m, 4 * step + 2 + side]

    def both(step, body):
        run(
            [
                body(first + place, place, ahead)
                for place in range(3)
                for ahead, first in enumerate((step, span - 3 - step))
            ]
        )

    def link(index, place, ahead):
        word = link_word(fluid[index - 1], fluid[index], fluid[index + 1])
        yield
        words[index] = word

    def advance(step, source, target, index, place, ahead):
        state = pull(source, index, words[index])
        density, flow = density_velocity(state)
        collided = collide(state, density, flow, opens[index])
        yield
        remember(history, step, index, density, flow)
        store(target, index, collided)

    both(1, link)
    receive(0, even)
    both(1, functools.partial(advance, 1, even, odd))
    receive(1, odd)
    both(2, functools.partial(advance, 2, odd, even))
    receive(2, even)
    drag[...] = jnp.zeros_like(drag)
    drag[0] = inner_drag[...]

    def finish(index, place, ahead):
        state = pull(even, index, words[index])
        density, flow = density_velocity(state)
        here = fluid[index] > 0
        placed = [jnp.where(here, state[m], inner_final[m, index - HALO]) for m in range(19)]
        part = jnp.where(here, drag_terms(flow, opens[index]), 0.0)
        yield
        remember(history, 3, index, density, flow)
        store(final, index - HALO, placed)
        drag[1 + place] += part

    both(3, finish)
    for copy in copies:
        copy.wait()


def recall(history, step, plane):
    return history[4 * step, plane], [history[4 * step + 1 + axis, plane] for axis in range(3)]


def retreat(opens, words, share, source, target, plane, density, flow):
    mirrored = pull(source, plane, words[plane])
    adjoint = [mirrored[OPP[m]] for m in range(19)]
    open_rate = opens[plane]
    force_flow = [flow[0] + FORCE, flow[1], flow[2]]
    x, y, z = [open_rate * part for part in force_flow]
    plus, minus = pairs(adjoint)
    mx, my, mz = [part * (1.0 / 12.0) for part in first_moments(minus, 2.0)]
    xy_plus, xz_plus, yz_plus = plus[3] + plus[4], plus[5] + plus[6], plus[7] + plus[8]
    axes = [2.0 * plus[k] for k in range(3)]
    whole = 12.0 * adjoint[0] + (axes[0] + axes[1] + axes[2]) + (xy_plus + xz_plus + yz_plus)
    third = whole * (1.0 / 3.0)
    xx = axes[0] + (xy_plus + xz_plus) - third
    yy = axes[1] + (xy_plus + yz_plus) - third
    zz = axes[2] + (xz_plus + yz_plus) - third
    xy, xz, yz = plus[3] - plus[4], plus[5] - plus[6], plus[7] - plus[8]
    hx = 0.25 * (xx * x + xy * y + xz * z)
    hy = 0.25 * (xy * x + yy * y + yz * z)
    hz = 0.25 * (xz * x + yz * y + zz * z)
    rate = 1.2 * open_rate
    slope = [rate * (mx + hx), rate * (my + hy), rate * (mz + hz)]
    pushed = slope[0] * force_flow[0] + slope[1] * force_flow[1] + slope[2] * force_flow[2]
    gained = share[plane] + density * pushed
    if target is None:
        yield
        share[plane] = gained
        return
    level = whole * (1.2 / 36.0) + 1.2 * (
        x * (mx + 0.5 * hx) + y * (my + 0.5 * hy) + z * (mz + 0.5 * hz)
    )
    level = level - (slope[0] * flow[0] + slope[1] * flow[1] + slope[2] * flow[2])
    values = [part - 0.2 * old for part, old in zip(spread(level, slope), adjoint)]
    yield
    share[plane] = gained
    for m in range(19):
        target[OPP[m], plane] = values[m]


def outer_kernel(
    home,
    history,
    opens,
    fluid,
    words,
    even_state,
    odd_state,
    far,
    near,
    from_far,
    from_near,
    summed,
    counted,
    outer,
    share,
    odd,
    even,
    first,
    second,
    second_flow,
):
    del summed, counted
    span = home + 2 * HALO
    up = parity()

    def seed(plane, density, flow):
        damping = 1.0 / opens[plane]
        square = flow[0] * flow[0] + flow[1] * flow[1] + flow[2] * flow[2]
        factor = 2.0 * damping / density
        slope = [part * factor for part in flow]
        values = spread(-square * factor, slope)
        yield
        share[plane] = -square * damping
        for m in range(19):
            even[OPP[m], plane] = values[m]

    sides = ((up, near, from_near), (1 - up, far, from_far))
    edge_words = []
    for ahead, _, message in sides:
        for m in range(19):
            for place in range(HALO):
                first[ahead, m, place] = odd_state[m, ahead * (span - HALO) + place]
            for place in range(2):
                second[ahead, m, 3 - 3 * ahead + place] = even_state[m, 2 + ahead * (span - 6) + place]
            second[ahead, m, 1 + 2 * ahead] = message[10 + m]
        for slot in range(5):
            first[ahead, AHEAD[slot] + ahead, ahead * RAW] = message[slot]
            second[ahead, AHEAD[slot] + ahead, 4 * ahead] = message[5 + slot]
        beyond = (message[29] >= 0.0).astype(jnp.int32)
        within = fluid[1 + ahead * (span - 3)]
        edge_words.append(
            link_word(
                beyond + ahead * (within - beyond),
                fluid[ahead * (span - 1)],
                within + ahead * (beyond - within),
            )
        )

    def second_out(ahead):
        index = 1 + ahead * (span - 3)
        state = pull(first.at[ahead], 1, words[index])
        density, flow = density_velocity(state)
        collided = collide(state, density, flow, opens[index])
        yield
        for place, part in enumerate([density] + flow):
            second_flow[ahead, place] = part
        store(second.at[ahead], 2, collided)

    run([second_out(side[0]) for side in sides])

    def last_step(ahead, raw, message, edge_word, place):
        spot = 1 + place
        index = place + ahead * (span - 3)
        two = second.at[ahead]
        word = words[index]
        if place == 0:
            word = edge_word + ahead * (word - edge_word)
        if place == 2:
            word = word + ahead * (edge_word - word)
        state = pull(two, spot, word)
        density, flow = density_velocity(state)
        seeded = seed(index, density, flow)
        next(seeded)
        here = fluid[index] > 0
        placed = []
        for m in range(19):
            if place == 1:
                initial = raw[m, ahead]
            else:
                initial = jnp.where((ahead > 0) == (place == 2), two[m, spot], raw[m, place // 2])
            placed.append(jnp.where(here, state[m], initial))
        yield
        next(seeded, None)
        store(outer.at[ahead], spot - ahead, placed)

    run(
        [
            last_step(*side, edge_word, place)
            for place in range(HALO)
            for side, edge_word in zip(sides, edge_words)
        ]
    )
    for ahead, _, message in sides:
        for m in range(19):
            outer[ahead, m, ahead * (BX - 1)] = message[30 + m]

    def seed_home(plane):
        return seed(plane, *recall(history, STEPS, plane))

    each_plane(HALO, HALO + home, seed_home)

    def ends(side):
        flow = [second_flow[side, 1 + axis] for axis in range(3)]
        return retreat(opens, words, share, even, odd, 1 + side * (span - 3), second_flow[side, 0], flow)

    run([ends(0), ends(1)])

    def step_two(plane):
        return retreat(opens, words, share, even, odd, plane, *recall(history, 2, plane))

    each_plane(HALO - 1, HALO + home + 1, step_two)


def gradient_kernel(
    home, history, opens, words, share, odd, marked, summed, gradient, to_near, to_far, total, even
):
    del summed
    up = parity()
    for plane in range(share.shape[0]):
        total[plane] = share[plane]

    def step_one(plane):
        return retreat(opens, words, total, odd, even, plane, *recall(history, 1, plane))

    def step_zero(plane):
        return retreat(opens, words, total, even, None, plane, *recall(history, 0, plane))

    each_plane(HALO - 1, HALO + home + 1, step_one)
    each_plane(HALO, HALO + home, step_zero)
    for plane in range(home):
        design = marked[plane]
        slope = 3.0 / ((1.6 + 3.4 * design) * (1.0 + 4.0 * design))
        gradient[plane] = jnp.where(design >= 0.0, total[plane + HALO] * slope, 0.0)
    for out, ahead in ((to_near, up), (to_far, 1 - up)):
        for plane in range(BX):
            out[plane] = gradient[ahead * (home - BX) + plane]


def scaled(home, cells, where, drag, joined, out):
    factor = cells / jnp.sum(drag[...])
    reach = (joined.shape[0] - home) // 2
    for plane in range(out.shape[0]):
        spot = jnp.clip(where[0] * BX + reach + plane, 0, joined.shape[0] - 1)
        live = plane < where[1] * BX
        out[plane] = jnp.where(live, joined[spot] * factor, 0.0)


def near_gradient(home, cells, where, drag, gradient, from_far, from_near, out, joined):
    up = parity()
    for ahead, message in ((up, from_near), (1 - up, from_far)):
        joined[pl.ds(ahead * (BX + home), BX)] = message[...]
    joined[pl.ds(BX, home)] = gradient[...]
    scaled(home, cells, where, drag, joined, out)


def far_gradient(home, cells, where, drag, gradient, from_left, from_right, out, joined):
    joined[pl.ds(0, home)] = from_left[...]
    joined[pl.ds(home, home)] = gradient[...]
    joined[pl.ds(2 * home, home)] = from_right[...]
    scaled(home, cells, where, drag, joined, out)


def place_kernel(where, final, outer, later, out, zeros, sems):
    del later
    blocks = out.shape[1] // BX
    home_blocks = final.shape[1] // BX
    beyond = outer.shape[2] // BX
    zeros[...] = jnp.zeros_like(zeros)
    for slot in range(blocks):
        target = out.at[:, pl.ds(slot * BX, BX)]
        live = slot < where[1]
        block = jnp.clip(where[0] + slot, -beyond, home_blocks + beyond - 1)
        inside = (block >= 0) & (block < home_blocks)

        @pl.when(live & inside)
        def _():
            source = final.at[:, pl.ds(block * BX, BX)]
            pltpu.make_async_copy(source, target, sems.at[slot]).start()

        @pl.when(live & jnp.logical_not(inside))
        def _():
            after = (block >= 0).astype(jnp.int32)
            within = block + beyond - after * (home_blocks + beyond)
            source = outer.at[after, :, pl.ds(within * BX, BX)]
            pltpu.make_async_copy(source, target, sems.at[slot]).start()

        @pl.when(jnp.logical_not(live))
        def _():
            pltpu.make_async_copy(zeros, target, sems.at[slot]).start()

    for slot in range(blocks):
        pltpu.make_async_copy(zeros, out.at[:, pl.ds(slot * BX, BX)], sems.at[slot]).wait()


def body(populations, design, fluid_mask, owner_after):
    count = lax.axis_size("block")
    home, width_y, width_z = design.shape
    slots = home // BX + 2
    span = home + 2 * HALO
    plane = (width_y, width_z)
    vmem = pl.BlockSpec(memory_space=pltpu.VMEM)
    hbm = pl.BlockSpec(memory_space=pltpu.HBM)
    anywhere = pl.BlockSpec(memory_space=pl.ANY)
    smem = pl.BlockSpec(memory_space=pltpu.SMEM)
    cells = float(count * home * width_y * width_z)
    near_pairs = [(i, i ^ 1) for i in range(count)]
    far_pairs = [(i, (i + 1 if i % 2 else i - 1) % count) for i in range(count)]
    inner_pairs = far_pairs[1:-1]

    def planes(*lead, dtype=jnp.float32):
        return jax.ShapeDtypeStruct(lead + plane, dtype)

    def scratch(*lead, dtype=jnp.float32):
        return pltpu.VMEM(lead + plane, dtype)

    def call(kernel, name, ins, outs, scratches, limit, moved, *operands):
        return pl.pallas_call(
            kernel,
            out_shape=[shape for shape, _ in outs],
            in_specs=ins,
            out_specs=[spec for _, spec in outs],
            scratch_shapes=scratches,
            compiler_params=pltpu.CompilerParams(vmem_limit_bytes=limit * MIB),
            cost_estimate=pl.CostEstimate(flops=20 * moved, bytes_accessed=moved, transcendentals=0),
            name=name,
        )(*operands)

    own_near, own_far, pops, marked = call(
        functools.partial(edge_kernel, home),
        "edge_planes",
        [hbm] * 3,
        [(planes(23, RAW), vmem)] * 2 + [(planes(19, home), vmem), (planes(home), vmem)],
        [scratch(home), scratch(home, dtype=jnp.int32), pltpu.SemaphoreType.DMA((5,))],
        4,
        1_000_000,
        *[
            pltpu.with_memory_space_constraint(part, pltpu.HBM)
            for part in (populations, design, fluid_mask)
        ],
    )
    near = lax.ppermute(own_near, "block", near_pairs)
    far = lax.ppermute(own_far, "block", far_pairs)

    inner_shapes = (
        planes(49),
        planes(49),
        planes(19, 12),
        planes(16, home),
        planes(19, home),
        planes(home),
        planes(home, dtype=jnp.int32),
        planes(home, dtype=jnp.int32),
        planes(),
    )
    (
        to_near,
        to_far,
        edges,
        inner_history,
        inner_final,
        inner_opens,
        inner_fluid,
        inner_words,
        inner_drag,
        where,
    ) = call(
        functools.partial(interior_kernel, home),
        "interior_steps",
        [hbm] + [vmem] * 2,
        [(shape, vmem) for shape in inner_shapes] + [(jax.ShapeDtypeStruct((3,), jnp.int32), smem)],
        [scratch(19, home)] * 2
        + [pltpu.SMEM(owner_after.shape, jnp.int32), pltpu.SemaphoreType.DMA(())],
        16,
        6_000_000,
        pltpu.with_memory_space_constraint(owner_after, pltpu.HBM),
        pops,
        marked,
    )
    from_near = lax.ppermute(to_near, "block", near_pairs)
    from_far = lax.ppermute(to_far, "block", far_pairs)

    boundary_shapes = (
        planes(19, home),
        planes(16, span),
        planes(span),
        planes(span, dtype=jnp.int32),
        planes(span, dtype=jnp.int32),
        planes(1 + STEPS),
        planes(19, span),
        planes(19, span),
    )
    final, history, opens, fluid, words, drag, even_state, odd_state = call(
        functools.partial(boundary_kernel, home),
        "boundary_steps",
        [vmem] * 3 + [anywhere] + [vmem] * 5,
        [(shape, vmem) for shape in boundary_shapes],
        [pltpu.SemaphoreType.DMA((5,))],
        20,
        8_000_000,
        far,
        near,
        edges,
        inner_history,
        inner_final,
        inner_opens,
        inner_fluid,
        inner_words,
        inner_drag,
    )

    sums = [drag]
    distance = 1
    while distance < count:
        swap = [(i, i ^ distance) for i in range(count)]
        sums.append(sums[-1] + lax.ppermute(sums[-1], "block", swap))
        distance *= 2
    drag = sums[-1]

    is_far = where[2] > 0
    outer, share, odd = call(
        functools.partial(outer_kernel, home),
        "outer_steps",
        [vmem] * 10 + [anywhere] * 2,
        [(planes(2, 19, BX), vmem), (planes(span), vmem), (planes(19, span), vmem)],
        [scratch(19, span), scratch(2, 19, HALO), scratch(2, 19, HALO + 2), scratch(2, 4)],
        20,
        12_000_000,
        history,
        opens,
        fluid,
        words,
        even_state,
        odd_state,
        far,
        near,
        from_far,
        from_near,
        sums[2],
        is_far.astype(jnp.int32).reshape(1),
    )
    gradient, to_near, to_far = call(
        functools.partial(gradient_kernel, home),
        "gradient_steps",
        [vmem] * 6 + [anywhere],
        [(planes(home), vmem), (planes(BX), vmem), (planes(BX), vmem)],
        [scratch(span), scratch(19, span)],
        20,
        6_000_000,
        history,
        opens,
        words,
        share,
        odd,
        marked,
        sums[3],
    )
    from_near = lax.ppermute(to_near, "block", near_pairs)
    from_far = lax.ppermute(to_far, "block", inner_pairs)

    ring = [(i, i + 1) for i in range(count - 1)]
    back = [(i + 1, i) for i in range(count - 1)]

    def place(outer):
        (out,) = call(
            place_kernel,
            "place_populations",
            [smem, anywhere, anywhere, vmem],
            [(planes(19, slots * BX), anywhere)],
            [scratch(19, BX), pltpu.SemaphoreType.DMA((slots,))],
            8,
            4_000_000,
            where,
            final,
            outer,
            gradient,
        )
        return out

    def place_far(_):
        wide = [lax.ppermute(final, "block", route) for route in (ring, back)]
        return place(jnp.stack(wide))

    def slope(kernel, name, reach, *messages):
        (out,) = call(
            functools.partial(kernel, home, cells),
            name,
            [smem] + [vmem] * 4,
            [(planes(slots * BX), vmem)],
            [scratch(home + 2 * reach)],
            4,
            1_000_000,
            where,
            drag,
            gradient,
            *messages,
        )
        return out

    def slope_near(*messages):
        return slope(near_gradient, "near_gradient", BX, *messages)

    def slope_far(*_):
        wide = [lax.ppermute(gradient, "block", route) for route in (ring, back)]
        return slope(far_gradient, "far_gradient", home, *wide)

    populations_after = lax.cond(is_far, place_far, place, outer)
    sensitivity = lax.cond(is_far, slope_far, slope_near, from_far, from_near)
    return (populations_after, sensitivity)


def solution(mesh):
    placed = (
        P(None, ("group", "block"), None, None),
        P(("group", "block"), None, None),
        P(("group", "block"), None, None),
        P("group"),
    )
    return jax.shard_map(
        body,
        mesh=mesh,
        in_specs=placed,
        out_specs=(P(None, ("group", "block"), None, None), P(("group", "block"), None, None)),
        check_vma=False,
    )
```

```python
import functools
import math

import jax
import jax.numpy as jnp
from jax import lax
from jax.experimental import pallas as pl
from jax.experimental.pallas import tpu as pltpu
from jax.sharding import PartitionSpec as P

BX = 4
STEPS = 3
HALO = STEPS
RAW = HALO - 1
MIB = 2**20

VELOCITY = (
    (0, 0, 0),
    (1, 0, 0),
    (-1, 0, 0),
    (0, 1, 0),
    (0, -1, 0),
    (0, 0, 1),
    (0, 0, -1),
    (1, 1, 0),
    (-1, -1, 0),
    (1, -1, 0),
    (-1, 1, 0),
    (1, 0, 1),
    (-1, 0, -1),
    (1, 0, -1),
    (-1, 0, 1),
    (0, 1, 1),
    (0, -1, -1),
    (0, 1, -1),
    (0, -1, 1),
)
OPP = (0,) + tuple(m + 1 if m % 2 else m - 1 for m in range(1, 19))
AHEAD = tuple(m for m in range(19) if VELOCITY[m][0] == 1)
BEHIND = tuple(m for m in range(19) if VELOCITY[m][0] == -1)
FORCE = 0.02
ROOT_45 = math.sqrt(4.5)
ROOT_2 = math.sqrt(2.0)


def rolled(field, step_y, step_z):
    if step_y:
        field = pltpu.roll(field, step_y % field.shape[0], 0)
    if step_z:
        field = pltpu.roll(field, step_z % field.shape[1], 1)
    return field


def pairs(values):
    plus = [values[2 * k + 1] + values[2 * k + 2] for k in range(9)]
    minus = [values[2 * k + 1] - values[2 * k + 2] for k in range(9)]
    return plus, minus


def first_moments(minus, scale):
    along_x, along_y, along_z = minus[:3]
    if scale != 1.0:
        along_x, along_y, along_z = scale * along_x, scale * along_y, scale * along_z
    along_x = along_x + ((minus[3] + minus[4]) + (minus[5] + minus[6]))
    along_y = along_y + ((minus[3] - minus[4]) + (minus[7] + minus[8]))
    along_z = along_z + ((minus[5] - minus[6]) + (minus[7] - minus[8]))
    return along_x, along_y, along_z


def density_velocity(state):
    plus, minus = pairs(state)
    axes = (plus[0] + plus[1]) + (plus[2] + state[0])
    diagonals = (plus[3] + plus[4]) + (plus[5] + plus[6]) + (plus[7] + plus[8])
    density = axes + diagonals
    inverse = 1.0 / density
    momentum = first_moments(minus, 1.0)
    return density, [part * inverse for part in momentum]


def collide(state, density, flow, open_rate):
    rate = ROOT_45 * open_rate
    x, y, z = (flow[0] + FORCE) * rate, flow[1] * rate, flow[2] * rate
    xx, yy, zz = x * x, y * y, z * z
    base = 1.0 - (xx + yy + zz) * (1.0 / 3.0)
    axis_weight = density * (1.2 / 18.0)
    axis_slope = density * (1.2 * ROOT_2 / 18.0)
    side_weight = density * (1.2 / 36.0)
    side_slope = density * (1.2 * ROOT_2 / 36.0)
    result = [density * 0.4 * base - 0.2 * state[0]]
    for k, along in enumerate((x, y, z, x + y, x - y, x + z, x - z, y + z, y - z)):
        if k < 3:
            even = axis_weight * (base + (xx, yy, zz)[k])
            odd = axis_slope * along
        else:
            even = side_weight * (base + along * along)
            odd = side_slope * along
        result.append((even + odd) - 0.2 * state[2 * k + 1])
        result.append((even - odd) - 0.2 * state[2 * k + 2])
    return result


def spread(level, slope):
    x, y, z = slope
    result = [level]
    for along in (x, y, z, x + y, x - y, x + z, x - z, y + z, y - z):
        result.append(level + along)
        result.append(level - along)
    return result


def pull(source, plane, word):
    here = [source[m, plane] for m in range(19)]
    result = [here[0]]
    for m in range(1, 19):
        step_x, step_y, step_z = VELOCITY[m]
        moved = here[m] if step_x == 0 else source[m, plane - step_x]
        moved = rolled(moved, step_y, step_z)
        result.append(jnp.where((word & (1 << m)) != 0, moved, here[OPP[m]]))
    return result


def link_word(behind, here, ahead):
    rows = lax.broadcasted_iota(jnp.int32, here.shape, 0)
    columns = lax.broadcasted_iota(jnp.int32, here.shape, 1)
    joined = behind + 2 * here + 4 * ahead
    word = jnp.zeros_like(here)
    for step_y in (-1, 0, 1):
        for step_z in (-1, 0, 1):
            if step_y and step_z:
                inner = {0: 1}
            else:
                inner = {1: 0, 0: 1, -1: 2}
            near = rolled(joined, step_y, step_z)
            if step_y == 1:
                near = jnp.where(rows == 0, 0, near)
            if step_y == -1:
                near = jnp.where(rows == here.shape[0] - 1, 0, near)
            if step_z == 1:
                near = jnp.where(columns == 0, 0, near)
            if step_z == -1:
                near = jnp.where(columns == here.shape[1] - 1, 0, near)
            for step_x, place in inner.items():
                if (step_x, step_y, step_z) == (0, 0, 0):
                    continue
                m = VELOCITY.index((step_x, step_y, step_z))
                word = word | ((near & (1 << place)) << (m - place))
    return jnp.where(here > 0, word, 0)


def run(bodies):
    for body in bodies:
        next(body)
    for body in bodies:
        next(body, None)


def each_plane(low, high, body, width=6):
    groups = (high - low) // width

    def group(index, carry):
        run([body(low + width * index + place) for place in range(width)])
        return carry

    lax.fori_loop(0, groups, group, 0)
    rest = range(low + groups * width, high)
    if rest:
        run([body(plane) for plane in rest])


def is_fluid_rate(mark):
    design = jnp.maximum(mark, 0.0)
    return (mark >= 0.0).astype(jnp.int32), (1.0 + 4.0 * design) / (1.6 + 3.4 * design)


def store(target, plane, values):
    for m, part in enumerate(values):
        target[m, plane] = part


def remember(history, step, plane, density, flow):
    history[4 * step, plane] = density
    for axis in range(3):
        history[4 * step + 1 + axis, plane] = flow[axis]


def drag_terms(flow, open_rate):
    return (flow[0] * flow[0] + flow[1] * flow[1] + flow[2] * flow[2]) / open_rate


def parity(axis="block"):
    return 1 - lax.rem(lax.axis_index(axis), 2)


def pick(flag, yes, no):
    return no + flag * (yes - no)


def edge_kernel(home, pops_far, design, mask, near, far, pops, marked, designs, masks, sems):
    up = parity()
    cuts = ((0, HALO), (home - HALO, HALO), (HALO, home - 2 * HALO))
    copies = [
        pltpu.make_async_copy(design, designs, sems.at[0]),
        pltpu.make_async_copy(mask, masks, sems.at[1]),
    ] + [
        pltpu.make_async_copy(
            pops_far.at[:, pl.ds(first, planes)], pops.at[:, pl.ds(first, planes)], sems.at[2 + place]
        )
        for place, (first, planes) in enumerate(cuts)
    ]
    for copy in copies:
        copy.start()
    for copy in copies[:2]:
        copy.wait()
    for plane in range(home):
        marked[plane] = jnp.where(masks[plane] > 0, designs[plane], -1.0)
    for copy in copies[2:4]:
        copy.wait()
    for out, ahead in ((near, up), (far, 1 - up)):
        first = ahead * (home - RAW)
        for plane in range(RAW):
            for m in range(19):
                out[m, plane] = pops[m, first + plane]
            out[19, plane] = marked[first + plane]
        third = ahead * (home - 1) + (1 - 2 * ahead) * RAW
        last = marked[third]
        out[22, 1] = last
        _, open_rate = is_fluid_rate(last)
        state = [pops[m, third] for m in range(19)]
        density, flow = density_velocity(state)
        collided = collide(state, density, flow, open_rate)
        for slot in range(5):
            value = jnp.where(ahead > 0, collided[AHEAD[slot]], collided[BEHIND[slot]])
            out[20 + slot // 2, slot % 2] = value
    copies[4].wait()


def count_blocks(home_blocks, owner, where):
    rank = lax.axis_index("block")
    below = jnp.int32(0)
    own = jnp.int32(0)
    for block in range(owner.shape[0]):
        holder = owner[block]
        below += (holder < rank).astype(jnp.int32)
        own += (holder == rank).astype(jnp.int32)
    stray = jnp.int32(0)
    for device in range(owner.shape[0] // home_blocks):
        late = owner[home_blocks * device + 1] < device
        early = owner[home_blocks * device + home_blocks - 2] > device
        stray = stray | late.astype(jnp.int32) | early.astype(jnp.int32)
    where[0] = below - home_blocks * rank
    where[1] = own
    where[2] = stray


def interior_kernel(
    home,
    owner_far,
    pops,
    marked,
    to_near,
    to_far,
    edges,
    history,
    final,
    opens,
    fluid,
    words,
    drag,
    where,
    even,
    odd,
    owner,
    sem,
):
    up = parity()
    copy = pltpu.make_async_copy(owner_far, owner, sem)
    copy.start()

    def start(plane):
        is_fluid, open_rate = is_fluid_rate(marked[plane])
        state = [pops[m, plane] for m in range(19)]
        density, flow = density_velocity(state)
        collided = collide(state, density, flow, open_rate)
        yield
        fluid[plane] = is_fluid
        opens[plane] = open_rate
        remember(history, 0, plane, density, flow)
        store(even, plane, collided)

    def link(plane):
        word = link_word(fluid[plane - 1], fluid[plane], fluid[plane + 1])
        yield
        words[plane] = word

    def advance(step, source, target, plane):
        state = pull(source, plane, words[plane])
        density, flow = density_velocity(state)
        collided = collide(state, density, flow, opens[plane])
        yield
        remember(history, step, plane, density, flow)
        store(target, plane, collided)

    def finish(plane):
        state = pull(even, plane, words[plane])
        density, flow = density_velocity(state)
        here = fluid[plane] > 0
        placed = [jnp.where(here, state[m], pops[m, plane]) for m in range(19)]
        part = jnp.where(here, drag_terms(flow, opens[plane]), 0.0)
        yield
        remember(history, 3, plane, density, flow)
        store(final, plane, placed)
        drag[...] += part

    def keep(step, source):
        for m in range(19):
            for side in range(2):
                edges[m, 4 * step + side] = source[m, step + side]
                edges[m, 4 * step + 2 + side] = source[m, home - 2 - step + side]

    def send(out, ahead, step, source):
        outer = ahead * (home - 1) + (1 - 2 * ahead) * RAW
        if step == 1:
            for slot in range(5):
                out[slot] = source[AHEAD[slot] + 1 - ahead, outer]
            return
        inner = ahead * (home - 1) + (1 - 2 * ahead) * HALO
        here = fluid[outer] > 0
        for slot in range(5):
            out[5 + slot] = source[AHEAD[slot] + 1 - ahead, inner]
        for m in range(19):
            out[10 + m] = jnp.where(here, source[m, outer], pops[m, outer])
        out[29] = marked[inner]

    drag[...] = jnp.zeros_like(drag)
    each_plane(0, home, start)
    keep(0, even)
    each_plane(1, home - 1, link)
    each_plane(1, home - 1, functools.partial(advance, 1, even, odd))
    keep(1, odd)
    each_plane(2, home - 2, functools.partial(advance, 2, odd, even))
    keep(2, even)
    for out, ahead in ((to_near, up), (to_far, 1 - up)):
        send(out, ahead, 1, odd)
        send(out, ahead, 2, even)
    each_plane(3, home - 3, finish)
    for m in range(19):
        for plane in range(STEPS):
            final[m, plane] = pops[m, plane]
            final[m, home - STEPS + plane] = pops[m, home - STEPS + plane]
        for out, ahead in ((to_near, up), (to_far, 1 - up)):
            out[30 + m] = final[m, STEPS + ahead * (home - 1 - 2 * STEPS)]
    copy.wait()
    count_blocks(home // BX, owner, where)


def boundary_kernel(
    home,
    far,
    near,
    edges,
    inner_history,
    inner_final,
    inner_opens,
    inner_fluid,
    inner_words,
    inner_drag,
    final,
    history,
    opens,
    fluid,
    words,
    drag,
    even,
    odd,
    sems,
):
    span = home + 2 * HALO
    up = parity()
    sides = ((up, near), (1 - up, far))
    copies = [
        pltpu.make_async_copy(
            inner_history.at[pl.ds(4 * step, 4), pl.ds(step, home - 2 * step)],
            history.at[pl.ds(4 * step, 4), pl.ds(HALO + step, home - 2 * step)],
            sems.at[step],
        )
        for step in range(4)
    ]
    copies.append(
        pltpu.make_async_copy(
            inner_final.at[:, pl.ds(STEPS, home - 2 * STEPS)],
            final.at[:, pl.ds(STEPS, home - 2 * STEPS)],
            sems.at[4],
        )
    )
    for copy in copies:
        copy.start()

    for plane in range(home):
        fluid[plane + HALO] = inner_fluid[plane]
        opens[plane + HALO] = inner_opens[plane]
    for plane in range(1, home - 1):
        words[plane + HALO] = inner_words[plane]
    for ahead, side in sides:
        fluid[ahead * (span - 1)], opens[ahead * (span - 1)] = is_fluid_rate(side[22, 1])
        for slot in range(5):
            even[AHEAD[slot] + ahead, ahead * (span - 1)] = side[20 + slot // 2, slot % 2]

    def begin(plane, ahead, side):
        index = plane + 1 + ahead * (home + RAW)
        is_fluid, open_rate = is_fluid_rate(side[19, plane])
        state = [side[m, plane] for m in range(19)]
        density, flow = density_velocity(state)
        collided = collide(state, density, flow, open_rate)
        yield
        fluid[index] = is_fluid
        opens[index] = open_rate
        store(even, index, collided)

    run([begin(plane, *side) for plane in range(RAW) for side in sides])

    def receive(step, target):
        for m in range(19):
            for side in range(2):
                target[m, HALO + step + side] = edges[m, 4 * step + side]
                target[m, HALO + home - 2 - step + side] = edges[m, 4 * step + 2 + side]

    def both(step, body):
        run(
            [
                body(first + place, place, ahead)
                for place in range(3)
                for ahead, first in enumerate((step, span - 3 - step))
            ]
        )

    def link(index, place, ahead):
        word = link_word(fluid[index - 1], fluid[index], fluid[index + 1])
        yield
        words[index] = word

    def advance(step, source, target, index, place, ahead):
        state = pull(source, index, words[index])
        density, flow = density_velocity(state)
        collided = collide(state, density, flow, opens[index])
        yield
        remember(history, step, index, density, flow)
        store(target, index, collided)

    both(1, link)
    receive(0, even)
    both(1, functools.partial(advance, 1, even, odd))
    receive(1, odd)
    both(2, functools.partial(advance, 2, odd, even))
    receive(2, even)
    drag[...] = jnp.zeros_like(drag)
    drag[0] = inner_drag[...]

    def finish(index, place, ahead):
        state = pull(even, index, words[index])
        density, flow = density_velocity(state)
        here = fluid[index] > 0
        placed = [jnp.where(here, state[m], inner_final[m, index - HALO]) for m in range(19)]
        part = jnp.where(here, drag_terms(flow, opens[index]), 0.0)
        yield
        remember(history, 3, index, density, flow)
        store(final, index - HALO, placed)
        drag[1 + place] += part

    both(3, finish)
    for copy in copies:
        copy.wait()


def recall(history, step, plane):
    return history[4 * step, plane], [history[4 * step + 1 + axis, plane] for axis in range(3)]


def retreat(opens, words, share, source, target, plane, density, flow):
    mirrored = pull(source, plane, words[plane])
    adjoint = [mirrored[OPP[m]] for m in range(19)]
    open_rate = opens[plane]
    force_flow = [flow[0] + FORCE, flow[1], flow[2]]
    x, y, z = [open_rate * part for part in force_flow]
    plus, minus = pairs(adjoint)
    mx, my, mz = [part * (1.0 / 12.0) for part in first_moments(minus, 2.0)]
    xy_plus, xz_plus, yz_plus = plus[3] + plus[4], plus[5] + plus[6], plus[7] + plus[8]
    axes = [2.0 * plus[k] for k in range(3)]
    whole = 12.0 * adjoint[0] + (axes[0] + axes[1] + axes[2]) + (xy_plus + xz_plus + yz_plus)
    third = whole * (1.0 / 3.0)
    xx = axes[0] + (xy_plus + xz_plus) - third
    yy = axes[1] + (xy_plus + yz_plus) - third
    zz = axes[2] + (xz_plus + yz_plus) - third
    xy, xz, yz = plus[3] - plus[4], plus[5] - plus[6], plus[7] - plus[8]
    hx = 0.25 * (xx * x + xy * y + xz * z)
    hy = 0.25 * (xy * x + yy * y + yz * z)
    hz = 0.25 * (xz * x + yz * y + zz * z)
    rate = 1.2 * open_rate
    slope = [rate * (mx + hx), rate * (my + hy), rate * (mz + hz)]
    pushed = slope[0] * force_flow[0] + slope[1] * force_flow[1] + slope[2] * force_flow[2]
    gained = share[plane] + density * pushed
    if target is None:
        yield
        share[plane] = gained
        return
    level = whole * (1.2 / 36.0) + 1.2 * (
        x * (mx + 0.5 * hx) + y * (my + 0.5 * hy) + z * (mz + 0.5 * hz)
    )
    level = level - (slope[0] * flow[0] + slope[1] * flow[1] + slope[2] * flow[2])
    values = [part - 0.2 * old for part, old in zip(spread(level, slope), adjoint)]
    yield
    share[plane] = gained
    for m in range(19):
        target[OPP[m], plane] = values[m]


def outer_kernel(
    home,
    history,
    opens,
    fluid,
    words,
    even_state,
    odd_state,
    far,
    near,
    from_far,
    from_near,
    summed,
    counted,
    outer,
    share,
    odd,
    even,
    first,
    second,
    second_flow,
):
    del summed, counted
    span = home + 2 * HALO
    up = parity()

    def seed(plane, density, flow):
        damping = 1.0 / opens[plane]
        square = flow[0] * flow[0] + flow[1] * flow[1] + flow[2] * flow[2]
        factor = 2.0 * damping / density
        slope = [part * factor for part in flow]
        values = spread(-square * factor, slope)
        yield
        share[plane] = -square * damping
        for m in range(19):
            even[OPP[m], plane] = values[m]

    sides = ((up, near, from_near), (1 - up, far, from_far))
    edge_words = []
    for ahead, _, message in sides:
        for m in range(19):
            for place in range(HALO):
                first[ahead, m, place] = odd_state[m, ahead * (span - HALO) + place]
            for place in range(2):
                second[ahead, m, 3 - 3 * ahead + place] = even_state[m, 2 + ahead * (span - 6) + place]
            second[ahead, m, 1 + 2 * ahead] = message[10 + m]
        for slot in range(5):
            first[ahead, AHEAD[slot] + ahead, ahead * RAW] = message[slot]
            second[ahead, AHEAD[slot] + ahead, 4 * ahead] = message[5 + slot]
        beyond = (message[29] >= 0.0).astype(jnp.int32)
        within = fluid[1 + ahead * (span - 3)]
        edge_words.append(
            link_word(
                beyond + ahead * (within - beyond),
                fluid[ahead * (span - 1)],
                within + ahead * (beyond - within),
            )
        )

    def second_out(ahead):
        index = 1 + ahead * (span - 3)
        state = pull(first.at[ahead], 1, words[index])
        density, flow = density_velocity(state)
        collided = collide(state, density, flow, opens[index])
        yield
        for place, part in enumerate([density] + flow):
            second_flow[ahead, place] = part
        store(second.at[ahead], 2, collided)

    run([second_out(side[0]) for side in sides])

    def last_step(ahead, raw, message, edge_word, place):
        spot = 1 + place
        index = place + ahead * (span - 3)
        two = second.at[ahead]
        word = words[index]
        if place == 0:
            word = edge_word + ahead * (word - edge_word)
        if place == 2:
            word = word + ahead * (edge_word - word)
        state = pull(two, spot, word)
        density, flow = density_velocity(state)
        seeded = seed(index, density, flow)
        next(seeded)
        here = fluid[index] > 0
        placed = []
        for m in range(19):
            if place == 1:
                initial = raw[m, ahead]
            else:
                initial = jnp.where((ahead > 0) == (place == 2), two[m, spot], raw[m, place // 2])
            placed.append(jnp.where(here, state[m], initial))
        yield
        next(seeded, None)
        store(outer.at[ahead], spot - ahead, placed)

    run(
        [
            last_step(*side, edge_word, place)
            for place in range(HALO)
            for side, edge_word in zip(sides, edge_words)
        ]
    )
    for ahead, _, message in sides:
        for m in range(19):
            outer[ahead, m, ahead * (BX - 1)] = message[30 + m]

    def seed_home(plane):
        return seed(plane, *recall(history, STEPS, plane))

    each_plane(HALO, HALO + home, seed_home)

    def ends(side):
        flow = [second_flow[side, 1 + axis] for axis in range(3)]
        return retreat(opens, words, share, even, odd, 1 + side * (span - 3), second_flow[side, 0], flow)

    run([ends(0), ends(1)])

    def step_two(plane):
        return retreat(opens, words, share, even, odd, plane, *recall(history, 2, plane))

    each_plane(HALO - 1, HALO + home + 1, step_two)


def gradient_kernel(
    home, history, opens, words, share, odd, marked, summed, gradient, to_near, to_far, total, even
):
    del summed
    up = parity()
    for plane in range(share.shape[0]):
        total[plane] = share[plane]

    def step_one(plane):
        return retreat(opens, words, total, odd, even, plane, *recall(history, 1, plane))

    def step_zero(plane):
        return retreat(opens, words, total, even, None, plane, *recall(history, 0, plane))

    each_plane(HALO - 1, HALO + home + 1, step_one)
    each_plane(HALO, HALO + home, step_zero)
    for plane in range(home):
        design = marked[plane]
        slope = 3.0 / ((1.6 + 3.4 * design) * (1.0 + 4.0 * design))
        gradient[plane] = jnp.where(design >= 0.0, total[plane + HALO] * slope, 0.0)
    for out, ahead in ((to_near, up), (to_far, 1 - up)):
        for plane in range(BX):
            out[plane] = gradient[ahead * (home - BX) + plane]


def scaled(home, cells, where, drag, joined, out):
    factor = cells / jnp.sum(drag[...])
    reach = (joined.shape[0] - home) // 2
    for plane in range(out.shape[0]):
        spot = jnp.clip(where[0] * BX + reach + plane, 0, joined.shape[0] - 1)
        live = plane < where[1] * BX
        out[plane] = jnp.where(live, joined[spot] * factor, 0.0)


def near_gradient(home, cells, where, drag, gradient, from_far, from_near, out, joined):
    up = parity()
    for ahead, message in ((up, from_near), (1 - up, from_far)):
        joined[pl.ds(ahead * (BX + home), BX)] = message[...]
    joined[pl.ds(BX, home)] = gradient[...]
    scaled(home, cells, where, drag, joined, out)


def far_gradient(home, cells, where, drag, gradient, from_left, from_right, out, joined):
    joined[pl.ds(0, home)] = from_left[...]
    joined[pl.ds(home, home)] = gradient[...]
    joined[pl.ds(2 * home, home)] = from_right[...]
    scaled(home, cells, where, drag, joined, out)


def place_kernel(where, final, outer, later, out, zeros, sems):
    del later
    blocks = out.shape[1] // BX
    home_blocks = final.shape[1] // BX
    beyond = outer.shape[2] // BX
    zeros[...] = jnp.zeros_like(zeros)
    for slot in range(blocks):
        target = out.at[:, pl.ds(slot * BX, BX)]
        live = slot < where[1]
        block = jnp.clip(where[0] + slot, -beyond, home_blocks + beyond - 1)
        inside = (block >= 0) & (block < home_blocks)

        @pl.when(live & inside)
        def _():
            source = final.at[:, pl.ds(block * BX, BX)]
            pltpu.make_async_copy(source, target, sems.at[slot]).start()

        @pl.when(live & jnp.logical_not(inside))
        def _():
            after = (block >= 0).astype(jnp.int32)
            within = block + beyond - after * (home_blocks + beyond)
            source = outer.at[after, :, pl.ds(within * BX, BX)]
            pltpu.make_async_copy(source, target, sems.at[slot]).start()

        @pl.when(jnp.logical_not(live))
        def _():
            pltpu.make_async_copy(zeros, target, sems.at[slot]).start()

    for slot in range(blocks):
        pltpu.make_async_copy(zeros, out.at[:, pl.ds(slot * BX, BX)], sems.at[slot]).wait()


def body(populations, design, fluid_mask, owner_after):
    count = lax.axis_size("block")
    home, width_y, width_z = design.shape
    slots = home // BX + 2
    span = home + 2 * HALO
    plane = (width_y, width_z)
    vmem = pl.BlockSpec(memory_space=pltpu.VMEM)
    hbm = pl.BlockSpec(memory_space=pltpu.HBM)
    anywhere = pl.BlockSpec(memory_space=pl.ANY)
    smem = pl.BlockSpec(memory_space=pltpu.SMEM)
    cells = float(count * home * width_y * width_z)
    near_pairs = [(i, i ^ 1) for i in range(count)]
    far_pairs = [(i, (i + 1 if i % 2 else i - 1) % count) for i in range(count)]
    inner_pairs = far_pairs[1:-1]

    def planes(*lead, dtype=jnp.float32):
        return jax.ShapeDtypeStruct(lead + plane, dtype)

    def scratch(*lead, dtype=jnp.float32):
        return pltpu.VMEM(lead + plane, dtype)

    def call(kernel, name, ins, outs, scratches, limit, moved, *operands):
        return pl.pallas_call(
            kernel,
            out_shape=[shape for shape, _ in outs],
            in_specs=ins,
            out_specs=[spec for _, spec in outs],
            scratch_shapes=scratches,
            compiler_params=pltpu.CompilerParams(vmem_limit_bytes=limit * MIB),
            cost_estimate=pl.CostEstimate(flops=20 * moved, bytes_accessed=moved, transcendentals=0),
            name=name,
        )(*operands)

    own_near, own_far, pops, marked = call(
        functools.partial(edge_kernel, home),
        "edge_planes",
        [hbm] * 3,
        [(planes(23, RAW), vmem)] * 2 + [(planes(19, home), vmem), (planes(home), vmem)],
        [scratch(home), scratch(home, dtype=jnp.int32), pltpu.SemaphoreType.DMA((5,))],
        4,
        1_000_000,
        *[
            pltpu.with_memory_space_constraint(part, pltpu.HBM)
            for part in (populations, design, fluid_mask)
        ],
    )
    near = lax.ppermute(own_near, "block", near_pairs)
    far = lax.ppermute(own_far, "block", far_pairs)

    inner_shapes = (
        planes(49),
        planes(49),
        planes(19, 12),
        planes(16, home),
        planes(19, home),
        planes(home),
        planes(home, dtype=jnp.int32),
        planes(home, dtype=jnp.int32),
        planes(),
    )
    (
        to_near,
        to_far,
        edges,
        inner_history,
        inner_final,
        inner_opens,
        inner_fluid,
        inner_words,
        inner_drag,
        where,
    ) = call(
        functools.partial(interior_kernel, home),
        "interior_steps",
        [hbm] + [vmem] * 2,
        [(shape, vmem) for shape in inner_shapes] + [(jax.ShapeDtypeStruct((3,), jnp.int32), smem)],
        [scratch(19, home)] * 2
        + [pltpu.SMEM(owner_after.shape, jnp.int32), pltpu.SemaphoreType.DMA(())],
        16,
        6_000_000,
        pltpu.with_memory_space_constraint(owner_after, pltpu.HBM),
        pops,
        marked,
    )
    from_near = lax.ppermute(to_near, "block", near_pairs)
    from_far = lax.ppermute(to_far, "block", far_pairs)

    boundary_shapes = (
        planes(19, home),
        planes(16, span),
        planes(span),
        planes(span, dtype=jnp.int32),
        planes(span, dtype=jnp.int32),
        planes(1 + STEPS),
        planes(19, span),
        planes(19, span),
    )
    final, history, opens, fluid, words, drag, even_state, odd_state = call(
        functools.partial(boundary_kernel, home),
        "boundary_steps",
        [vmem] * 3 + [anywhere] + [vmem] * 5,
        [(shape, vmem) for shape in boundary_shapes],
        [pltpu.SemaphoreType.DMA((5,))],
        20,
        8_000_000,
        far,
        near,
        edges,
        inner_history,
        inner_final,
        inner_opens,
        inner_fluid,
        inner_words,
        inner_drag,
    )

    distances = [1 << bit for bit in range(count.bit_length() - 1)]
    sums = [drag]
    for distance in distances[:1] + distances[2:] + distances[1:2]:
        swap = [(i, i ^ distance) for i in range(count)]
        sums.append(sums[-1] + lax.ppermute(sums[-1], "block", swap))
    drag = sums[-1]

    is_far = where[2] > 0
    outer, share, odd = call(
        functools.partial(outer_kernel, home),
        "outer_steps",
        [vmem] * 10 + [anywhere] * 2,
        [(planes(2, 19, BX), vmem), (planes(span), vmem), (planes(19, span), vmem)],
        [scratch(19, span), scratch(2, 19, HALO), scratch(2, 19, HALO + 2), scratch(2, 4)],
        20,
        12_000_000,
        history,
        opens,
        fluid,
        words,
        even_state,
        odd_state,
        far,
        near,
        from_far,
        from_near,
        sums[2],
        is_far.astype(jnp.int32).reshape(1),
    )
    gradient, to_near, to_far = call(
        functools.partial(gradient_kernel, home),
        "gradient_steps",
        [vmem] * 6 + [anywhere],
        [(planes(home), vmem), (planes(BX), vmem), (planes(BX), vmem)],
        [scratch(span), scratch(19, span)],
        20,
        6_000_000,
        history,
        opens,
        words,
        share,
        odd,
        marked,
        sums[3],
    )
    from_near = lax.ppermute(to_near, "block", near_pairs)
    from_far = lax.ppermute(to_far, "block", inner_pairs)

    ring = [(i, i + 1) for i in range(count - 1)]
    back = [(i + 1, i) for i in range(count - 1)]

    def place(outer):
        (out,) = call(
            place_kernel,
            "place_populations",
            [smem, anywhere, anywhere, vmem],
            [(planes(19, slots * BX), anywhere)],
            [scratch(19, BX), pltpu.SemaphoreType.DMA((slots,))],
            8,
            4_000_000,
            where,
            final,
            outer,
            gradient,
        )
        return out

    def place_far(_):
        wide = [lax.ppermute(final, "block", route) for route in (ring, back)]
        return place(jnp.stack(wide))

    def slope(kernel, name, reach, *messages):
        (out,) = call(
            functools.partial(kernel, home, cells),
            name,
            [smem] + [vmem] * 4,
            [(planes(slots * BX), vmem)],
            [scratch(home + 2 * reach)],
            4,
            1_000_000,
            where,
            drag,
            gradient,
            *messages,
        )
        return out

    def slope_near(*messages):
        return slope(near_gradient, "near_gradient", BX, *messages)

    def slope_far(*_):
        wide = [lax.ppermute(gradient, "block", route) for route in (ring, back)]
        return slope(far_gradient, "far_gradient", home, *wide)

    populations_after = lax.cond(is_far, place_far, place, outer)
    sensitivity = lax.cond(is_far, slope_far, slope_near, from_far, from_near)
    return (populations_after, sensitivity)


def solution(mesh):
    placed = (
        P(None, ("group", "block"), None, None),
        P(("group", "block"), None, None),
        P(("group", "block"), None, None),
        P("group"),
    )
    return jax.shard_map(
        body,
        mesh=mesh,
        in_specs=placed,
        out_specs=(P(None, ("group", "block"), None, None), P(("group", "block"), None, None)),
        check_vma=False,
    )
```

```python
import functools
import math

import jax
import jax.numpy as jnp
from jax import lax
from jax.experimental import pallas as pl
from jax.experimental.pallas import tpu as pltpu
from jax.sharding import PartitionSpec as P

BX = 4
STEPS = 3
HALO = STEPS
RAW = HALO - 1
MIB = 2**20

VELOCITY = (
    (0, 0, 0),
    (1, 0, 0),
    (-1, 0, 0),
    (0, 1, 0),
    (0, -1, 0),
    (0, 0, 1),
    (0, 0, -1),
    (1, 1, 0),
    (-1, -1, 0),
    (1, -1, 0),
    (-1, 1, 0),
    (1, 0, 1),
    (-1, 0, -1),
    (1, 0, -1),
    (-1, 0, 1),
    (0, 1, 1),
    (0, -1, -1),
    (0, 1, -1),
    (0, -1, 1),
)
OPP = (0,) + tuple(m + 1 if m % 2 else m - 1 for m in range(1, 19))
AHEAD = tuple(m for m in range(19) if VELOCITY[m][0] == 1)
BEHIND = tuple(m for m in range(19) if VELOCITY[m][0] == -1)
FORCE = 0.02
ROOT_45 = math.sqrt(4.5)
ROOT_2 = math.sqrt(2.0)


def rolled(field, step_y, step_z):
    if step_y:
        field = pltpu.roll(field, step_y % field.shape[0], 0)
    if step_z:
        field = pltpu.roll(field, step_z % field.shape[1], 1)
    return field


def pairs(values):
    plus = [values[2 * k + 1] + values[2 * k + 2] for k in range(9)]
    minus = [values[2 * k + 1] - values[2 * k + 2] for k in range(9)]
    return plus, minus


def first_moments(minus, scale):
    along_x, along_y, along_z = minus[:3]
    if scale != 1.0:
        along_x, along_y, along_z = scale * along_x, scale * along_y, scale * along_z
    along_x = along_x + ((minus[3] + minus[4]) + (minus[5] + minus[6]))
    along_y = along_y + ((minus[3] - minus[4]) + (minus[7] + minus[8]))
    along_z = along_z + ((minus[5] - minus[6]) + (minus[7] - minus[8]))
    return along_x, along_y, along_z


def density_velocity(state):
    plus, minus = pairs(state)
    axes = (plus[0] + plus[1]) + (plus[2] + state[0])
    diagonals = (plus[3] + plus[4]) + (plus[5] + plus[6]) + (plus[7] + plus[8])
    density = axes + diagonals
    inverse = 1.0 / density
    momentum = first_moments(minus, 1.0)
    return density, [part * inverse for part in momentum]


def collide(state, density, flow, open_rate):
    rate = ROOT_45 * open_rate
    x, y, z = (flow[0] + FORCE) * rate, flow[1] * rate, flow[2] * rate
    xx, yy, zz = x * x, y * y, z * z
    base = 1.0 - (xx + yy + zz) * (1.0 / 3.0)
    axis_weight = density * (1.2 / 18.0)
    axis_slope = density * (1.2 * ROOT_2 / 18.0)
    side_weight = density * (1.2 / 36.0)
    side_slope = density * (1.2 * ROOT_2 / 36.0)
    result = [density * 0.4 * base - 0.2 * state[0]]
    for k, along in enumerate((x, y, z, x + y, x - y, x + z, x - z, y + z, y - z)):
        if k < 3:
            even = axis_weight * (base + (xx, yy, zz)[k])
            odd = axis_slope * along
        else:
            even = side_weight * (base + along * along)
            odd = side_slope * along
        result.append((even + odd) - 0.2 * state[2 * k + 1])
        result.append((even - odd) - 0.2 * state[2 * k + 2])
    return result


def spread(level, slope):
    x, y, z = slope
    result = [level]
    for along in (x, y, z, x + y, x - y, x + z, x - z, y + z, y - z):
        result.append(level + along)
        result.append(level - along)
    return result


def pull(source, plane, word):
    here = [source[m, plane] for m in range(19)]
    result = [here[0]]
    for m in range(1, 19):
        step_x, step_y, step_z = VELOCITY[m]
        moved = here[m] if step_x == 0 else source[m, plane - step_x]
        moved = rolled(moved, step_y, step_z)
        result.append(jnp.where((word & (1 << m)) != 0, moved, here[OPP[m]]))
    return result


def link_word(behind, here, ahead):
    rows = lax.broadcasted_iota(jnp.int32, here.shape, 0)
    columns = lax.broadcasted_iota(jnp.int32, here.shape, 1)
    joined = behind + 2 * here + 4 * ahead
    word = jnp.zeros_like(here)
    for step_y in (-1, 0, 1):
        for step_z in (-1, 0, 1):
            if step_y and step_z:
                inner = {0: 1}
            else:
                inner = {1: 0, 0: 1, -1: 2}
            near = rolled(joined, step_y, step_z)
            if step_y == 1:
                near = jnp.where(rows == 0, 0, near)
            if step_y == -1:
                near = jnp.where(rows == here.shape[0] - 1, 0, near)
            if step_z == 1:
                near = jnp.where(columns == 0, 0, near)
            if step_z == -1:
                near = jnp.where(columns == here.shape[1] - 1, 0, near)
            for step_x, place in inner.items():
                if (step_x, step_y, step_z) == (0, 0, 0):
                    continue
                m = VELOCITY.index((step_x, step_y, step_z))
                word = word | ((near & (1 << place)) << (m - place))
    return jnp.where(here > 0, word, 0)


def run(bodies):
    for body in bodies:
        next(body)
    for body in bodies:
        next(body, None)


def each_plane(low, high, body, width=6):
    groups = (high - low) // width

    def group(index, carry):
        run([body(low + width * index + place) for place in range(width)])
        return carry

    lax.fori_loop(0, groups, group, 0)
    rest = range(low + groups * width, high)
    if rest:
        run([body(plane) for plane in rest])


def is_fluid_rate(mark):
    design = jnp.maximum(mark, 0.0)
    return (mark >= 0.0).astype(jnp.int32), (1.0 + 4.0 * design) / (1.6 + 3.4 * design)


def store(target, plane, values):
    for m, part in enumerate(values):
        target[m, plane] = part


def remember(history, step, plane, density, flow):
    history[4 * step, plane] = density
    for axis in range(3):
        history[4 * step + 1 + axis, plane] = flow[axis]


def drag_terms(flow, open_rate):
    return (flow[0] * flow[0] + flow[1] * flow[1] + flow[2] * flow[2]) / open_rate


def parity(axis="block"):
    return 1 - lax.rem(lax.axis_index(axis), 2)


def pick(flag, yes, no):
    return no + flag * (yes - no)


def edge_kernel(home, pops_far, design, mask, near, far, pops, marked, designs, masks, sems):
    up = parity()
    cuts = ((0, HALO), (home - HALO, HALO), (HALO, home - 2 * HALO))
    copies = [
        pltpu.make_async_copy(design, designs, sems.at[0]),
        pltpu.make_async_copy(mask, masks, sems.at[1]),
    ] + [
        pltpu.make_async_copy(
            pops_far.at[:, pl.ds(first, planes)], pops.at[:, pl.ds(first, planes)], sems.at[2 + place]
        )
        for place, (first, planes) in enumerate(cuts)
    ]
    for copy in copies:
        copy.start()
    for copy in copies[:2]:
        copy.wait()
    for plane in range(home):
        marked[plane] = jnp.where(masks[plane] > 0, designs[plane], -1.0)
    for copy in copies[2:4]:
        copy.wait()
    for out, ahead in ((near, up), (far, 1 - up)):
        first = ahead * (home - RAW)
        for plane in range(RAW):
            for m in range(19):
                out[m, plane] = pops[m, first + plane]
            out[19, plane] = marked[first + plane]
        third = ahead * (home - 1) + (1 - 2 * ahead) * RAW
        last = marked[third]
        out[22, 1] = last
        _, open_rate = is_fluid_rate(last)
        state = [pops[m, third] for m in range(19)]
        density, flow = density_velocity(state)
        collided = collide(state, density, flow, open_rate)
        for slot in range(5):
            value = jnp.where(ahead > 0, collided[AHEAD[slot]], collided[BEHIND[slot]])
            out[20 + slot // 2, slot % 2] = value
    copies[4].wait()


def count_blocks(home_blocks, owner, where):
    rank = lax.axis_index("block")
    below = jnp.int32(0)
    own = jnp.int32(0)
    for block in range(owner.shape[0]):
        holder = owner[block]
        below += (holder < rank).astype(jnp.int32)
        own += (holder == rank).astype(jnp.int32)
    stray = jnp.int32(0)
    for device in range(owner.shape[0] // home_blocks):
        late = owner[home_blocks * device + 1] < device
        early = owner[home_blocks * device + home_blocks - 2] > device
        stray = stray | late.astype(jnp.int32) | early.astype(jnp.int32)
    where[0] = below - home_blocks * rank
    where[1] = own
    where[2] = stray


def interior_kernel(
    home,
    owner_far,
    pops,
    marked,
    to_near,
    to_far,
    edges,
    history,
    final,
    opens,
    fluid,
    words,
    drag,
    where,
    even,
    odd,
    owner,
    sem,
):
    up = parity()
    copy = pltpu.make_async_copy(owner_far, owner, sem)
    copy.start()

    def start(plane):
        is_fluid, open_rate = is_fluid_rate(marked[plane])
        state = [pops[m, plane] for m in range(19)]
        density, flow = density_velocity(state)
        collided = collide(state, density, flow, open_rate)
        yield
        fluid[plane] = is_fluid
        opens[plane] = open_rate
        remember(history, 0, plane, density, flow)
        store(even, plane, collided)

    def link(plane):
        word = link_word(fluid[plane - 1], fluid[plane], fluid[plane + 1])
        yield
        words[plane] = word

    def advance(step, source, target, plane):
        state = pull(source, plane, words[plane])
        density, flow = density_velocity(state)
        collided = collide(state, density, flow, opens[plane])
        yield
        remember(history, step, plane, density, flow)
        store(target, plane, collided)

    def finish(plane):
        state = pull(even, plane, words[plane])
        density, flow = density_velocity(state)
        here = fluid[plane] > 0
        placed = [jnp.where(here, state[m], pops[m, plane]) for m in range(19)]
        part = jnp.where(here, drag_terms(flow, opens[plane]), 0.0)
        yield
        remember(history, 3, plane, density, flow)
        store(final, plane, placed)
        drag[...] += part

    def keep(step, source):
        for m in range(19):
            for side in range(2):
                edges[m, 4 * step + side] = source[m, step + side]
                edges[m, 4 * step + 2 + side] = source[m, home - 2 - step + side]

    def send(out, ahead, step, source):
        outer = ahead * (home - 1) + (1 - 2 * ahead) * RAW
        if step == 1:
            for slot in range(5):
                out[slot] = source[AHEAD[slot] + 1 - ahead, outer]
            return
        inner = ahead * (home - 1) + (1 - 2 * ahead) * HALO
        here = fluid[outer] > 0
        for slot in range(5):
            out[5 + slot] = source[AHEAD[slot] + 1 - ahead, inner]
        for m in range(19):
            out[10 + m] = jnp.where(here, source[m, outer], pops[m, outer])
        out[29] = marked[inner]

    drag[...] = jnp.zeros_like(drag)
    each_plane(0, home, start)
    keep(0, even)
    each_plane(1, home - 1, link)
    each_plane(1, home - 1, functools.partial(advance, 1, even, odd))
    keep(1, odd)
    each_plane(2, home - 2, functools.partial(advance, 2, odd, even))
    keep(2, even)
    for out, ahead in ((to_near, up), (to_far, 1 - up)):
        send(out, ahead, 1, odd)
        send(out, ahead, 2, even)
    each_plane(3, home - 3, finish)
    for m in range(19):
        for plane in range(STEPS):
            final[m, plane] = pops[m, plane]
            final[m, home - STEPS + plane] = pops[m, home - STEPS + plane]
        for out, ahead in ((to_near, up), (to_far, 1 - up)):
            out[30 + m] = final[m, STEPS + ahead * (home - 1 - 2 * STEPS)]
    copy.wait()
    count_blocks(home // BX, owner, where)


def boundary_kernel(
    home,
    far,
    near,
    edges,
    inner_history,
    inner_final,
    inner_opens,
    inner_fluid,
    inner_words,
    inner_drag,
    final,
    history,
    opens,
    fluid,
    words,
    drag,
    even,
    odd,
    sems,
):
    span = home + 2 * HALO
    up = parity()
    sides = ((up, near), (1 - up, far))
    copies = [
        pltpu.make_async_copy(
            inner_history.at[pl.ds(4 * step, 4), pl.ds(step, home - 2 * step)],
            history.at[pl.ds(4 * step, 4), pl.ds(HALO + step, home - 2 * step)],
            sems.at[step],
        )
        for step in range(4)
    ]
    copies.append(
        pltpu.make_async_copy(
            inner_final.at[:, pl.ds(STEPS, home - 2 * STEPS)],
            final.at[:, pl.ds(STEPS, home - 2 * STEPS)],
            sems.at[4],
        )
    )
    for copy in copies:
        copy.start()

    for plane in range(home):
        fluid[plane + HALO] = inner_fluid[plane]
        opens[plane + HALO] = inner_opens[plane]
    for plane in range(1, home - 1):
        words[plane + HALO] = inner_words[plane]
    for ahead, side in sides:
        fluid[ahead * (span - 1)], opens[ahead * (span - 1)] = is_fluid_rate(side[22, 1])
        for slot in range(5):
            even[AHEAD[slot] + ahead, ahead * (span - 1)] = side[20 + slot // 2, slot % 2]

    def begin(plane, ahead, side):
        index = plane + 1 + ahead * (home + RAW)
        is_fluid, open_rate = is_fluid_rate(side[19, plane])
        state = [side[m, plane] for m in range(19)]
        density, flow = density_velocity(state)
        collided = collide(state, density, flow, open_rate)
        yield
        fluid[index] = is_fluid
        opens[index] = open_rate
        store(even, index, collided)

    run([begin(plane, *side) for plane in range(RAW) for side in sides])

    def receive(step, target):
        for m in range(19):
            for side in range(2):
                target[m, HALO + step + side] = edges[m, 4 * step + side]
                target[m, HALO + home - 2 - step + side] = edges[m, 4 * step + 2 + side]

    def both(step, body):
        run(
            [
                body(first + place, place, ahead)
                for place in range(3)
                for ahead, first in enumerate((step, span - 3 - step))
            ]
        )

    def link(index, place, ahead):
        word = link_word(fluid[index - 1], fluid[index], fluid[index + 1])
        yield
        words[index] = word

    def advance(step, source, target, index, place, ahead):
        state = pull(source, index, words[index])
        density, flow = density_velocity(state)
        collided = collide(state, density, flow, opens[index])
        yield
        remember(history, step, index, density, flow)
        store(target, index, collided)

    both(1, link)
    receive(0, even)
    both(1, functools.partial(advance, 1, even, odd))
    receive(1, odd)
    both(2, functools.partial(advance, 2, odd, even))
    receive(2, even)
    drag[...] = inner_drag[...]

    def finish(index, place, ahead):
        state = pull(even, index, words[index])
        density, flow = density_velocity(state)
        here = fluid[index] > 0
        placed = [jnp.where(here, state[m], inner_final[m, index - HALO]) for m in range(19)]
        part = jnp.where(here, drag_terms(flow, opens[index]), 0.0)
        yield
        remember(history, 3, index, density, flow)
        store(final, index - HALO, placed)
        drag[...] += part

    both(3, finish)
    for copy in copies:
        copy.wait()


def recall(history, step, plane):
    return history[4 * step, plane], [history[4 * step + 1 + axis, plane] for axis in range(3)]


def retreat(opens, words, share, source, target, plane, density, flow):
    mirrored = pull(source, plane, words[plane])
    adjoint = [mirrored[OPP[m]] for m in range(19)]
    open_rate = opens[plane]
    force_flow = [flow[0] + FORCE, flow[1], flow[2]]
    x, y, z = [open_rate * part for part in force_flow]
    plus, minus = pairs(adjoint)
    mx, my, mz = [part * (1.0 / 12.0) for part in first_moments(minus, 2.0)]
    xy_plus, xz_plus, yz_plus = plus[3] + plus[4], plus[5] + plus[6], plus[7] + plus[8]
    axes = [2.0 * plus[k] for k in range(3)]
    whole = 12.0 * adjoint[0] + (axes[0] + axes[1] + axes[2]) + (xy_plus + xz_plus + yz_plus)
    third = whole * (1.0 / 3.0)
    xx = axes[0] + (xy_plus + xz_plus) - third
    yy = axes[1] + (xy_plus + yz_plus) - third
    zz = axes[2] + (xz_plus + yz_plus) - third
    xy, xz, yz = plus[3] - plus[4], plus[5] - plus[6], plus[7] - plus[8]
    hx = 0.25 * (xx * x + xy * y + xz * z)
    hy = 0.25 * (xy * x + yy * y + yz * z)
    hz = 0.25 * (xz * x + yz * y + zz * z)
    rate = 1.2 * open_rate
    slope = [rate * (mx + hx), rate * (my + hy), rate * (mz + hz)]
    pushed = slope[0] * force_flow[0] + slope[1] * force_flow[1] + slope[2] * force_flow[2]
    gained = share[plane] + density * pushed
    if target is None:
        yield
        share[plane] = gained
        return
    level = whole * (1.2 / 36.0) + 1.2 * (
        x * (mx + 0.5 * hx) + y * (my + 0.5 * hy) + z * (mz + 0.5 * hz)
    )
    level = level - (slope[0] * flow[0] + slope[1] * flow[1] + slope[2] * flow[2])
    values = [part - 0.2 * old for part, old in zip(spread(level, slope), adjoint)]
    yield
    share[plane] = gained
    for m in range(19):
        target[OPP[m], plane] = values[m]


def outer_kernel(
    home,
    history,
    opens,
    fluid,
    words,
    even_state,
    odd_state,
    far,
    near,
    from_far,
    from_near,
    summed,
    counted,
    outer,
    share,
    odd,
    even,
    first,
    second,
    second_flow,
):
    del summed, counted
    span = home + 2 * HALO
    up = parity()

    def seed(plane, density, flow):
        damping = 1.0 / opens[plane]
        square = flow[0] * flow[0] + flow[1] * flow[1] + flow[2] * flow[2]
        factor = 2.0 * damping / density
        slope = [part * factor for part in flow]
        values = spread(-square * factor, slope)
        yield
        share[plane] = -square * damping
        for m in range(19):
            even[OPP[m], plane] = values[m]

    sides = ((up, near, from_near), (1 - up, far, from_far))
    edge_words = []
    for ahead, _, message in sides:
        for m in range(19):
            for place in range(HALO):
                first[ahead, m, place] = odd_state[m, ahead * (span - HALO) + place]
            for place in range(2):
                second[ahead, m, 3 - 3 * ahead + place] = even_state[m, 2 + ahead * (span - 6) + place]
            second[ahead, m, 1 + 2 * ahead] = message[10 + m]
        for slot in range(5):
            first[ahead, AHEAD[slot] + ahead, ahead * RAW] = message[slot]
            second[ahead, AHEAD[slot] + ahead, 4 * ahead] = message[5 + slot]
        beyond = (message[29] >= 0.0).astype(jnp.int32)
        within = fluid[1 + ahead * (span - 3)]
        edge_words.append(
            link_word(
                beyond + ahead * (within - beyond),
                fluid[ahead * (span - 1)],
                within + ahead * (beyond - within),
            )
        )

    def second_out(ahead):
        index = 1 + ahead * (span - 3)
        state = pull(first.at[ahead], 1, words[index])
        density, flow = density_velocity(state)
        collided = collide(state, density, flow, opens[index])
        yield
        for place, part in enumerate([density] + flow):
            second_flow[ahead, place] = part
        store(second.at[ahead], 2, collided)

    run([second_out(side[0]) for side in sides])

    def last_step(ahead, raw, message, edge_word, place):
        spot = 1 + place
        index = place + ahead * (span - 3)
        two = second.at[ahead]
        word = words[index]
        if place == 0:
            word = edge_word + ahead * (word - edge_word)
        if place == 2:
            word = word + ahead * (edge_word - word)
        state = pull(two, spot, word)
        density, flow = density_velocity(state)
        seeded = seed(index, density, flow)
        next(seeded)
        here = fluid[index] > 0
        placed = []
        for m in range(19):
            if place == 1:
                initial = raw[m, ahead]
            else:
                initial = jnp.where((ahead > 0) == (place == 2), two[m, spot], raw[m, place // 2])
            placed.append(jnp.where(here, state[m], initial))
        yield
        next(seeded, None)
        store(outer.at[ahead], spot - ahead, placed)

    run(
        [
            last_step(*side, edge_word, place)
            for place in range(HALO)
            for side, edge_word in zip(sides, edge_words)
        ]
    )
    for ahead, _, message in sides:
        for m in range(19):
            outer[ahead, m, ahead * (BX - 1)] = message[30 + m]

    def seed_home(plane):
        return seed(plane, *recall(history, STEPS, plane))

    each_plane(HALO, HALO + home, seed_home)

    def ends(side):
        flow = [second_flow[side, 1 + axis] for axis in range(3)]
        return retreat(opens, words, share, even, odd, 1 + side * (span - 3), second_flow[side, 0], flow)

    run([ends(0), ends(1)])

    def step_two(plane):
        return retreat(opens, words, share, even, odd, plane, *recall(history, 2, plane))

    each_plane(HALO - 1, HALO + home + 1, step_two)


def gradient_kernel(
    home, history, opens, words, share, odd, marked, summed, gradient, to_near, to_far, total, even
):
    del summed
    up = parity()
    for plane in range(share.shape[0]):
        total[plane] = share[plane]

    def step_one(plane):
        return retreat(opens, words, total, odd, even, plane, *recall(history, 1, plane))

    def step_zero(plane):
        return retreat(opens, words, total, even, None, plane, *recall(history, 0, plane))

    each_plane(HALO - 1, HALO + home + 1, step_one)
    each_plane(HALO, HALO + home, step_zero)
    for plane in range(home):
        design = marked[plane]
        slope = 3.0 / ((1.6 + 3.4 * design) * (1.0 + 4.0 * design))
        gradient[plane] = jnp.where(design >= 0.0, total[plane + HALO] * slope, 0.0)
    for out, ahead in ((to_near, up), (to_far, 1 - up)):
        for plane in range(BX):
            out[plane] = gradient[ahead * (home - BX) + plane]


def scaled(home, cells, where, drag, joined, out):
    factor = cells / jnp.sum(drag[...])
    reach = (joined.shape[0] - home) // 2
    for plane in range(out.shape[0]):
        spot = jnp.clip(where[0] * BX + reach + plane, 0, joined.shape[0] - 1)
        live = plane < where[1] * BX
        out[plane] = jnp.where(live, joined[spot] * factor, 0.0)


def near_gradient(home, cells, where, drag, gradient, from_far, from_near, out, joined):
    up = parity()
    for ahead, message in ((up, from_near), (1 - up, from_far)):
        joined[pl.ds(ahead * (BX + home), BX)] = message[...]
    joined[pl.ds(BX, home)] = gradient[...]
    scaled(home, cells, where, drag, joined, out)


def far_gradient(home, cells, where, drag, gradient, from_left, from_right, out, joined):
    joined[pl.ds(0, home)] = from_left[...]
    joined[pl.ds(home, home)] = gradient[...]
    joined[pl.ds(2 * home, home)] = from_right[...]
    scaled(home, cells, where, drag, joined, out)


def place_kernel(where, final, outer, later, out, zeros, sems):
    del later
    blocks = out.shape[1] // BX
    home_blocks = final.shape[1] // BX
    beyond = outer.shape[2] // BX
    zeros[...] = jnp.zeros_like(zeros)
    for slot in range(blocks):
        target = out.at[:, pl.ds(slot * BX, BX)]
        live = slot < where[1]
        block = jnp.clip(where[0] + slot, -beyond, home_blocks + beyond - 1)
        inside = (block >= 0) & (block < home_blocks)

        @pl.when(live & inside)
        def _():
            source = final.at[:, pl.ds(block * BX, BX)]
            pltpu.make_async_copy(source, target, sems.at[slot]).start()

        @pl.when(live & jnp.logical_not(inside))
        def _():
            after = (block >= 0).astype(jnp.int32)
            within = block + beyond - after * (home_blocks + beyond)
            source = outer.at[after, :, pl.ds(within * BX, BX)]
            pltpu.make_async_copy(source, target, sems.at[slot]).start()

        @pl.when(jnp.logical_not(live))
        def _():
            pltpu.make_async_copy(zeros, target, sems.at[slot]).start()

    for slot in range(blocks):
        pltpu.make_async_copy(zeros, out.at[:, pl.ds(slot * BX, BX)], sems.at[slot]).wait()


def body(populations, design, fluid_mask, owner_after):
    count = lax.axis_size("block")
    home, width_y, width_z = design.shape
    slots = home // BX + 2
    span = home + 2 * HALO
    plane = (width_y, width_z)
    vmem = pl.BlockSpec(memory_space=pltpu.VMEM)
    hbm = pl.BlockSpec(memory_space=pltpu.HBM)
    anywhere = pl.BlockSpec(memory_space=pl.ANY)
    smem = pl.BlockSpec(memory_space=pltpu.SMEM)
    cells = float(count * home * width_y * width_z)
    near_pairs = [(i, i ^ 1) for i in range(count)]
    far_pairs = [(i, (i + 1 if i % 2 else i - 1) % count) for i in range(count)]
    inner_pairs = far_pairs[1:-1]

    def planes(*lead, dtype=jnp.float32):
        return jax.ShapeDtypeStruct(lead + plane, dtype)

    def scratch(*lead, dtype=jnp.float32):
        return pltpu.VMEM(lead + plane, dtype)

    def call(kernel, name, ins, outs, scratches, limit, moved, *operands):
        return pl.pallas_call(
            kernel,
            out_shape=[shape for shape, _ in outs],
            in_specs=ins,
            out_specs=[spec for _, spec in outs],
            scratch_shapes=scratches,
            compiler_params=pltpu.CompilerParams(vmem_limit_bytes=limit * MIB),
            cost_estimate=pl.CostEstimate(flops=20 * moved, bytes_accessed=moved, transcendentals=0),
            name=name,
        )(*operands)

    own_near, own_far, pops, marked = call(
        functools.partial(edge_kernel, home),
        "edge_planes",
        [hbm] * 3,
        [(planes(23, RAW), vmem)] * 2 + [(planes(19, home), vmem), (planes(home), vmem)],
        [scratch(home), scratch(home, dtype=jnp.int32), pltpu.SemaphoreType.DMA((5,))],
        4,
        1_000_000,
        *[
            pltpu.with_memory_space_constraint(part, pltpu.HBM)
            for part in (populations, design, fluid_mask)
        ],
    )
    near = lax.ppermute(own_near, "block", near_pairs)
    far = lax.ppermute(own_far, "block", far_pairs)

    inner_shapes = (
        planes(49),
        planes(49),
        planes(19, 12),
        planes(16, home),
        planes(19, home),
        planes(home),
        planes(home, dtype=jnp.int32),
        planes(home, dtype=jnp.int32),
        planes(),
    )
    (
        to_near,
        to_far,
        edges,
        inner_history,
        inner_final,
        inner_opens,
        inner_fluid,
        inner_words,
        inner_drag,
        where,
    ) = call(
        functools.partial(interior_kernel, home),
        "interior_steps",
        [hbm] + [vmem] * 2,
        [(shape, vmem) for shape in inner_shapes] + [(jax.ShapeDtypeStruct((3,), jnp.int32), smem)],
        [scratch(19, home)] * 2
        + [pltpu.SMEM(owner_after.shape, jnp.int32), pltpu.SemaphoreType.DMA(())],
        16,
        6_000_000,
        pltpu.with_memory_space_constraint(owner_after, pltpu.HBM),
        pops,
        marked,
    )
    from_near = lax.ppermute(to_near, "block", near_pairs)
    from_far = lax.ppermute(to_far, "block", far_pairs)

    boundary_shapes = (
        planes(19, home),
        planes(16, span),
        planes(span),
        planes(span, dtype=jnp.int32),
        planes(span, dtype=jnp.int32),
        planes(),
        planes(19, span),
        planes(19, span),
    )
    final, history, opens, fluid, words, drag, even_state, odd_state = call(
        functools.partial(boundary_kernel, home),
        "boundary_steps",
        [vmem] * 3 + [anywhere] + [vmem] * 5,
        [(shape, vmem) for shape in boundary_shapes],
        [pltpu.SemaphoreType.DMA((5,))],
        20,
        8_000_000,
        far,
        near,
        edges,
        inner_history,
        inner_final,
        inner_opens,
        inner_fluid,
        inner_words,
        inner_drag,
    )

    distances = [1 << bit for bit in range(count.bit_length() - 1)]
    sums = [drag]
    for distance in distances[:1] + distances[2:] + distances[1:2]:
        swap = [(i, i ^ distance) for i in range(count)]
        sums.append(sums[-1] + lax.ppermute(sums[-1], "block", swap))
    drag = sums[-1]

    is_far = where[2] > 0
    outer, share, odd = call(
        functools.partial(outer_kernel, home),
        "outer_steps",
        [vmem] * 10 + [anywhere] * 2,
        [(planes(2, 19, BX), vmem), (planes(span), vmem), (planes(19, span), vmem)],
        [scratch(19, span), scratch(2, 19, HALO), scratch(2, 19, HALO + 2), scratch(2, 4)],
        20,
        12_000_000,
        history,
        opens,
        fluid,
        words,
        even_state,
        odd_state,
        far,
        near,
        from_far,
        from_near,
        sums[2],
        is_far.astype(jnp.int32).reshape(1),
    )
    gradient, to_near, to_far = call(
        functools.partial(gradient_kernel, home),
        "gradient_steps",
        [vmem] * 6 + [anywhere],
        [(planes(home), vmem), (planes(BX), vmem), (planes(BX), vmem)],
        [scratch(span), scratch(19, span)],
        20,
        6_000_000,
        history,
        opens,
        words,
        share,
        odd,
        marked,
        sums[3],
    )
    from_near = lax.ppermute(to_near, "block", near_pairs)
    from_far = lax.ppermute(to_far, "block", inner_pairs)

    ring = [(i, i + 1) for i in range(count - 1)]
    back = [(i + 1, i) for i in range(count - 1)]

    def place(outer):
        (out,) = call(
            place_kernel,
            "place_populations",
            [smem, anywhere, anywhere, vmem],
            [(planes(19, slots * BX), anywhere)],
            [scratch(19, BX), pltpu.SemaphoreType.DMA((slots,))],
            8,
            4_000_000,
            where,
            final,
            outer,
            gradient,
        )
        return out

    def place_far(_):
        wide = [lax.ppermute(final, "block", route) for route in (ring, back)]
        return place(jnp.stack(wide))

    def slope(kernel, name, reach, *messages):
        (out,) = call(
            functools.partial(kernel, home, cells),
            name,
            [smem] + [vmem] * 4,
            [(planes(slots * BX), vmem)],
            [scratch(home + 2 * reach)],
            4,
            1_000_000,
            where,
            drag,
            gradient,
            *messages,
        )
        return out

    def slope_near(*messages):
        return slope(near_gradient, "near_gradient", BX, *messages)

    def slope_far(*_):
        wide = [lax.ppermute(gradient, "block", route) for route in (ring, back)]
        return slope(far_gradient, "far_gradient", home, *wide)

    populations_after = lax.cond(is_far, place_far, place, outer)
    sensitivity = lax.cond(is_far, slope_far, slope_near, from_far, from_near)
    return (populations_after, sensitivity)


def solution(mesh):
    placed = (
        P(None, ("group", "block"), None, None),
        P(("group", "block"), None, None),
        P(("group", "block"), None, None),
        P("group"),
    )
    return jax.shard_map(
        body,
        mesh=mesh,
        in_specs=placed,
        out_specs=(P(None, ("group", "block"), None, None), P(("group", "block"), None, None)),
        check_vma=False,
    )
```

```python
import functools
import math

import jax
import jax.numpy as jnp
from jax import lax
from jax.experimental import pallas as pl
from jax.experimental.pallas import tpu as pltpu
from jax.sharding import PartitionSpec as P

BX = 4
STEPS = 3
HALO = STEPS
RAW = HALO - 1
MIB = 2**20

VELOCITY = (
    (0, 0, 0),
    (1, 0, 0),
    (-1, 0, 0),
    (0, 1, 0),
    (0, -1, 0),
    (0, 0, 1),
    (0, 0, -1),
    (1, 1, 0),
    (-1, -1, 0),
    (1, -1, 0),
    (-1, 1, 0),
    (1, 0, 1),
    (-1, 0, -1),
    (1, 0, -1),
    (-1, 0, 1),
    (0, 1, 1),
    (0, -1, -1),
    (0, 1, -1),
    (0, -1, 1),
)
OPP = (0,) + tuple(m + 1 if m % 2 else m - 1 for m in range(1, 19))
AHEAD = tuple(m for m in range(19) if VELOCITY[m][0] == 1)
BEHIND = tuple(m for m in range(19) if VELOCITY[m][0] == -1)
FORCE = 0.02
ROOT_45 = math.sqrt(4.5)
ROOT_2 = math.sqrt(2.0)


def rolled(field, step_y, step_z):
    if step_y:
        field = pltpu.roll(field, step_y % field.shape[0], 0)
    if step_z:
        field = pltpu.roll(field, step_z % field.shape[1], 1)
    return field


def pairs(values):
    plus = [values[2 * k + 1] + values[2 * k + 2] for k in range(9)]
    minus = [values[2 * k + 1] - values[2 * k + 2] for k in range(9)]
    return plus, minus


def first_moments(minus, scale):
    along_x, along_y, along_z = minus[:3]
    if scale != 1.0:
        along_x, along_y, along_z = scale * along_x, scale * along_y, scale * along_z
    along_x = along_x + ((minus[3] + minus[4]) + (minus[5] + minus[6]))
    along_y = along_y + ((minus[3] - minus[4]) + (minus[7] + minus[8]))
    along_z = along_z + ((minus[5] - minus[6]) + (minus[7] - minus[8]))
    return along_x, along_y, along_z


def density_velocity(state):
    plus, minus = pairs(state)
    axes = (plus[0] + plus[1]) + (plus[2] + state[0])
    diagonals = (plus[3] + plus[4]) + (plus[5] + plus[6]) + (plus[7] + plus[8])
    density = axes + diagonals
    inverse = 1.0 / density
    momentum = first_moments(minus, 1.0)
    return density, [part * inverse for part in momentum]


def collide(state, density, flow, open_rate):
    rate = ROOT_45 * open_rate
    x, y, z = (flow[0] + FORCE) * rate, flow[1] * rate, flow[2] * rate
    xx, yy, zz = x * x, y * y, z * z
    base = 1.0 - (xx + yy + zz) * (1.0 / 3.0)
    axis_weight = density * (1.2 / 18.0)
    axis_slope = density * (1.2 * ROOT_2 / 18.0)
    side_weight = density * (1.2 / 36.0)
    side_slope = density * (1.2 * ROOT_2 / 36.0)
    result = [density * 0.4 * base - 0.2 * state[0]]
    for k, along in enumerate((x, y, z, x + y, x - y, x + z, x - z, y + z, y - z)):
        if k < 3:
            even = axis_weight * (base + (xx, yy, zz)[k])
            odd = axis_slope * along
        else:
            even = side_weight * (base + along * along)
            odd = side_slope * along
        result.append((even + odd) - 0.2 * state[2 * k + 1])
        result.append((even - odd) - 0.2 * state[2 * k + 2])
    return result


def spread(level, slope):
    x, y, z = slope
    result = [level]
    for along in (x, y, z, x + y, x - y, x + z, x - z, y + z, y - z):
        result.append(level + along)
        result.append(level - along)
    return result


def pull(source, plane, word):
    here = [source[m, plane] for m in range(19)]
    result = [here[0]]
    for m in range(1, 19):
        step_x, step_y, step_z = VELOCITY[m]
        moved = here[m] if step_x == 0 else source[m, plane - step_x]
        moved = rolled(moved, step_y, step_z)
        result.append(jnp.where((word & (1 << m)) != 0, moved, here[OPP[m]]))
    return result


def link_word(behind, here, ahead):
    rows = lax.broadcasted_iota(jnp.int32, here.shape, 0)
    columns = lax.broadcasted_iota(jnp.int32, here.shape, 1)
    joined = behind + 2 * here + 4 * ahead
    word = jnp.zeros_like(here)
    for step_y in (-1, 0, 1):
        for step_z in (-1, 0, 1):
            if step_y and step_z:
                inner = {0: 1}
            else:
                inner = {1: 0, 0: 1, -1: 2}
            near = rolled(joined, step_y, step_z)
            if step_y == 1:
                near = jnp.where(rows == 0, 0, near)
            if step_y == -1:
                near = jnp.where(rows == here.shape[0] - 1, 0, near)
            if step_z == 1:
                near = jnp.where(columns == 0, 0, near)
            if step_z == -1:
                near = jnp.where(columns == here.shape[1] - 1, 0, near)
            for step_x, place in inner.items():
                if (step_x, step_y, step_z) == (0, 0, 0):
                    continue
                m = VELOCITY.index((step_x, step_y, step_z))
                word = word | ((near & (1 << place)) << (m - place))
    return jnp.where(here > 0, word, 0)


def run(bodies):
    for body in bodies:
        next(body)
    for body in bodies:
        next(body, None)


def each_plane(low, high, body, width=6):
    groups = (high - low) // width

    def group(index, carry):
        run([body(low + width * index + place) for place in range(width)])
        return carry

    lax.fori_loop(0, groups, group, 0)
    rest = range(low + groups * width, high)
    if rest:
        run([body(plane) for plane in rest])


def is_fluid_rate(mark):
    design = jnp.maximum(mark, 0.0)
    return (mark >= 0.0).astype(jnp.int32), (1.0 + 4.0 * design) / (1.6 + 3.4 * design)


def store(target, plane, values):
    for m, part in enumerate(values):
        target[m, plane] = part


def remember(history, step, plane, density, flow):
    history[4 * step, plane] = density
    for axis in range(3):
        history[4 * step + 1 + axis, plane] = flow[axis]


def drag_terms(flow, open_rate):
    return (flow[0] * flow[0] + flow[1] * flow[1] + flow[2] * flow[2]) / open_rate


def parity(axis="block"):
    return 1 - lax.rem(lax.axis_index(axis), 2)


def pick(flag, yes, no):
    return no + flag * (yes - no)


def edge_kernel(home, pops_far, design, mask, near, far, pops, marked, designs, masks, sems):
    up = parity()
    cuts = ((0, HALO), (home - HALO, HALO), (HALO, home - 2 * HALO))
    copies = [
        pltpu.make_async_copy(design, designs, sems.at[0]),
        pltpu.make_async_copy(mask, masks, sems.at[1]),
    ] + [
        pltpu.make_async_copy(
            pops_far.at[:, pl.ds(first, planes)], pops.at[:, pl.ds(first, planes)], sems.at[2 + place]
        )
        for place, (first, planes) in enumerate(cuts)
    ]
    for copy in copies:
        copy.start()
    for copy in copies[:2]:
        copy.wait()
    for plane in range(home):
        marked[plane] = jnp.where(masks[plane] > 0, designs[plane], -1.0)
    for copy in copies[2:4]:
        copy.wait()
    for out, ahead in ((near, up), (far, 1 - up)):
        first = ahead * (home - RAW)
        for plane in range(RAW):
            for m in range(19):
                out[m, plane] = pops[m, first + plane]
            out[19, plane] = marked[first + plane]
        third = ahead * (home - 1) + (1 - 2 * ahead) * RAW
        last = marked[third]
        out[22, 1] = last
        _, open_rate = is_fluid_rate(last)
        state = [pops[m, third] for m in range(19)]
        density, flow = density_velocity(state)
        collided = collide(state, density, flow, open_rate)
        for slot in range(5):
            value = jnp.where(ahead > 0, collided[AHEAD[slot]], collided[BEHIND[slot]])
            out[20 + slot // 2, slot % 2] = value
    copies[4].wait()


def count_blocks(home_blocks, owner, where):
    rank = lax.axis_index("block")
    below = jnp.int32(0)
    own = jnp.int32(0)
    for block in range(owner.shape[0]):
        holder = owner[block]
        below += (holder < rank).astype(jnp.int32)
        own += (holder == rank).astype(jnp.int32)
    stray = jnp.int32(0)
    for device in range(owner.shape[0] // home_blocks):
        late = owner[home_blocks * device + 1] < device
        early = owner[home_blocks * device + home_blocks - 2] > device
        stray = stray | late.astype(jnp.int32) | early.astype(jnp.int32)
    where[0] = below - home_blocks * rank
    where[1] = own
    where[2] = stray


def interior_kernel(
    home,
    owner_far,
    pops,
    marked,
    to_near,
    to_far,
    edges,
    history,
    final,
    opens,
    fluid,
    words,
    drag,
    where,
    even,
    odd,
    owner,
    sem,
):
    up = parity()
    copy = pltpu.make_async_copy(owner_far, owner, sem)
    copy.start()

    def start(plane):
        is_fluid, open_rate = is_fluid_rate(marked[plane])
        state = [pops[m, plane] for m in range(19)]
        density, flow = density_velocity(state)
        collided = collide(state, density, flow, open_rate)
        yield
        fluid[plane] = is_fluid
        opens[plane] = open_rate
        remember(history, 0, plane, density, flow)
        store(even, plane, collided)

    def link(plane):
        word = link_word(fluid[plane - 1], fluid[plane], fluid[plane + 1])
        yield
        words[plane] = word

    def advance(step, source, target, plane):
        state = pull(source, plane, words[plane])
        density, flow = density_velocity(state)
        collided = collide(state, density, flow, opens[plane])
        yield
        remember(history, step, plane, density, flow)
        store(target, plane, collided)

    def finish(plane):
        state = pull(even, plane, words[plane])
        density, flow = density_velocity(state)
        here = fluid[plane] > 0
        placed = [jnp.where(here, state[m], pops[m, plane]) for m in range(19)]
        part = jnp.where(here, drag_terms(flow, opens[plane]), 0.0)
        yield
        remember(history, 3, plane, density, flow)
        store(final, plane, placed)
        drag[...] += part

    def keep(step, source):
        for m in range(19):
            for side in range(2):
                edges[m, 4 * step + side] = source[m, step + side]
                edges[m, 4 * step + 2 + side] = source[m, home - 2 - step + side]

    def send(out, ahead, step, source):
        outer = ahead * (home - 1) + (1 - 2 * ahead) * RAW
        if step == 1:
            for slot in range(5):
                out[slot] = source[AHEAD[slot] + 1 - ahead, outer]
            return
        inner = ahead * (home - 1) + (1 - 2 * ahead) * HALO
        here = fluid[outer] > 0
        for slot in range(5):
            out[5 + slot] = source[AHEAD[slot] + 1 - ahead, inner]
        for m in range(19):
            out[10 + m] = jnp.where(here, source[m, outer], pops[m, outer])
        out[29] = marked[inner]

    drag[...] = jnp.zeros_like(drag)
    each_plane(0, home, start)
    keep(0, even)
    each_plane(1, home - 1, link)
    each_plane(1, home - 1, functools.partial(advance, 1, even, odd))
    keep(1, odd)
    each_plane(2, home - 2, functools.partial(advance, 2, odd, even))
    keep(2, even)
    for out, ahead in ((to_near, up), (to_far, 1 - up)):
        send(out, ahead, 1, odd)
        send(out, ahead, 2, even)
    each_plane(3, home - 3, finish)
    for m in range(19):
        for plane in range(STEPS):
            final[m, plane] = pops[m, plane]
            final[m, home - STEPS + plane] = pops[m, home - STEPS + plane]
        for out, ahead in ((to_near, up), (to_far, 1 - up)):
            out[30 + m] = final[m, STEPS + ahead * (home - 1 - 2 * STEPS)]
    copy.wait()
    count_blocks(home // BX, owner, where)


def boundary_kernel(
    home,
    far,
    near,
    edges,
    inner_history,
    inner_final,
    inner_opens,
    inner_fluid,
    inner_words,
    inner_drag,
    final,
    history,
    opens,
    fluid,
    words,
    drag,
    even,
    odd,
    sems,
):
    span = home + 2 * HALO
    up = parity()
    sides = ((up, near), (1 - up, far))
    copies = [
        pltpu.make_async_copy(
            inner_history.at[pl.ds(4 * step, 4), pl.ds(step, home - 2 * step)],
            history.at[pl.ds(4 * step, 4), pl.ds(HALO + step, home - 2 * step)],
            sems.at[step],
        )
        for step in range(4)
    ]
    copies.append(
        pltpu.make_async_copy(
            inner_final.at[:, pl.ds(STEPS, home - 2 * STEPS)],
            final.at[:, pl.ds(STEPS, home - 2 * STEPS)],
            sems.at[4],
        )
    )
    for copy in copies:
        copy.start()

    for plane in range(home):
        fluid[plane + HALO] = inner_fluid[plane]
        opens[plane + HALO] = inner_opens[plane]
    for plane in range(1, home - 1):
        words[plane + HALO] = inner_words[plane]
    for ahead, side in sides:
        fluid[ahead * (span - 1)], opens[ahead * (span - 1)] = is_fluid_rate(side[22, 1])
        for slot in range(5):
            even[AHEAD[slot] + ahead, ahead * (span - 1)] = side[20 + slot // 2, slot % 2]

    def begin(plane, ahead, side):
        index = plane + 1 + ahead * (home + RAW)
        is_fluid, open_rate = is_fluid_rate(side[19, plane])
        state = [side[m, plane] for m in range(19)]
        density, flow = density_velocity(state)
        collided = collide(state, density, flow, open_rate)
        yield
        fluid[index] = is_fluid
        opens[index] = open_rate
        store(even, index, collided)

    run([begin(plane, *side) for plane in range(RAW) for side in sides])

    def receive(step, target):
        for m in range(19):
            for side in range(2):
                target[m, HALO + step + side] = edges[m, 4 * step + side]
                target[m, HALO + home - 2 - step + side] = edges[m, 4 * step + 2 + side]

    def both(step, body):
        run(
            [
                body(first + place, place, ahead)
                for place in range(3)
                for ahead, first in enumerate((step, span - 3 - step))
            ]
        )

    def link(index, place, ahead):
        word = link_word(fluid[index - 1], fluid[index], fluid[index + 1])
        yield
        words[index] = word

    def advance(step, source, target, index, place, ahead):
        state = pull(source, index, words[index])
        density, flow = density_velocity(state)
        collided = collide(state, density, flow, opens[index])
        yield
        remember(history, step, index, density, flow)
        store(target, index, collided)

    both(1, link)
    receive(0, even)
    both(1, functools.partial(advance, 1, even, odd))
    receive(1, odd)
    both(2, functools.partial(advance, 2, odd, even))
    receive(2, even)
    drag[...] = jnp.zeros_like(drag)
    drag[0] = inner_drag[...]

    def finish(index, place, ahead):
        state = pull(even, index, words[index])
        density, flow = density_velocity(state)
        here = fluid[index] > 0
        placed = [jnp.where(here, state[m], inner_final[m, index - HALO]) for m in range(19)]
        part = jnp.where(here, drag_terms(flow, opens[index]), 0.0)
        yield
        remember(history, 3, index, density, flow)
        store(final, index - HALO, placed)
        drag[1 + place] += part

    both(3, finish)
    for copy in copies:
        copy.wait()


def recall(history, step, plane):
    return history[4 * step, plane], [history[4 * step + 1 + axis, plane] for axis in range(3)]


def retreat(opens, words, share, source, target, plane, density, flow):
    mirrored = pull(source, plane, words[plane])
    adjoint = [mirrored[OPP[m]] for m in range(19)]
    open_rate = opens[plane]
    force_flow = [flow[0] + FORCE, flow[1], flow[2]]
    x, y, z = [open_rate * part for part in force_flow]
    plus, minus = pairs(adjoint)
    mx, my, mz = [part * (1.0 / 12.0) for part in first_moments(minus, 2.0)]
    xy_plus, xz_plus, yz_plus = plus[3] + plus[4], plus[5] + plus[6], plus[7] + plus[8]
    axes = [2.0 * plus[k] for k in range(3)]
    whole = 12.0 * adjoint[0] + (axes[0] + axes[1] + axes[2]) + (xy_plus + xz_plus + yz_plus)
    third = whole * (1.0 / 3.0)
    xx = axes[0] + (xy_plus + xz_plus) - third
    yy = axes[1] + (xy_plus + yz_plus) - third
    zz = axes[2] + (xz_plus + yz_plus) - third
    xy, xz, yz = plus[3] - plus[4], plus[5] - plus[6], plus[7] - plus[8]
    hx = 0.25 * (xx * x + xy * y + xz * z)
    hy = 0.25 * (xy * x + yy * y + yz * z)
    hz = 0.25 * (xz * x + yz * y + zz * z)
    rate = 1.2 * open_rate
    slope = [rate * (mx + hx), rate * (my + hy), rate * (mz + hz)]
    pushed = slope[0] * force_flow[0] + slope[1] * force_flow[1] + slope[2] * force_flow[2]
    gained = share[plane] + density * pushed
    if target is None:
        yield
        share[plane] = gained
        return
    level = whole * (1.2 / 36.0) + 1.2 * (
        x * (mx + 0.5 * hx) + y * (my + 0.5 * hy) + z * (mz + 0.5 * hz)
    )
    level = level - (slope[0] * flow[0] + slope[1] * flow[1] + slope[2] * flow[2])
    values = [part - 0.2 * old for part, old in zip(spread(level, slope), adjoint)]
    yield
    share[plane] = gained
    for m in range(19):
        target[OPP[m], plane] = values[m]


def outer_kernel(
    home,
    history,
    opens,
    fluid,
    words,
    even_state,
    odd_state,
    far,
    near,
    from_far,
    from_near,
    summed,
    counted,
    outer,
    share,
    odd,
    even,
    first,
    second,
    second_flow,
):
    del summed, counted
    span = home + 2 * HALO
    up = parity()

    def seed(plane, density, flow):
        damping = 1.0 / opens[plane]
        square = flow[0] * flow[0] + flow[1] * flow[1] + flow[2] * flow[2]
        factor = 2.0 * damping / density
        slope = [part * factor for part in flow]
        values = spread(-square * factor, slope)
        yield
        share[plane] = -square * damping
        for m in range(19):
            even[OPP[m], plane] = values[m]

    sides = ((up, near, from_near), (1 - up, far, from_far))
    edge_words = []
    for ahead, _, message in sides:
        for m in range(19):
            for place in range(HALO):
                first[ahead, m, place] = odd_state[m, ahead * (span - HALO) + place]
            for place in range(2):
                second[ahead, m, 3 - 3 * ahead + place] = even_state[m, 2 + ahead * (span - 6) + place]
            second[ahead, m, 1 + 2 * ahead] = message[10 + m]
        for slot in range(5):
            first[ahead, AHEAD[slot] + ahead, ahead * RAW] = message[slot]
            second[ahead, AHEAD[slot] + ahead, 4 * ahead] = message[5 + slot]
        beyond = (message[29] >= 0.0).astype(jnp.int32)
        within = fluid[1 + ahead * (span - 3)]
        edge_words.append(
            link_word(
                beyond + ahead * (within - beyond),
                fluid[ahead * (span - 1)],
                within + ahead * (beyond - within),
            )
        )

    def second_out(ahead):
        index = 1 + ahead * (span - 3)
        state = pull(first.at[ahead], 1, words[index])
        density, flow = density_velocity(state)
        collided = collide(state, density, flow, opens[index])
        yield
        for place, part in enumerate([density] + flow):
            second_flow[ahead, place] = part
        store(second.at[ahead], 2, collided)

    run([second_out(side[0]) for side in sides])

    def last_step(ahead, raw, message, edge_word, place):
        spot = 1 + place
        index = place + ahead * (span - 3)
        two = second.at[ahead]
        word = words[index]
        if place == 0:
            word = edge_word + ahead * (word - edge_word)
        if place == 2:
            word = word + ahead * (edge_word - word)
        state = pull(two, spot, word)
        density, flow = density_velocity(state)
        seeded = seed(index, density, flow)
        next(seeded)
        here = fluid[index] > 0
        placed = []
        for m in range(19):
            if place == 1:
                initial = raw[m, ahead]
            else:
                initial = jnp.where((ahead > 0) == (place == 2), two[m, spot], raw[m, place // 2])
            placed.append(jnp.where(here, state[m], initial))
        yield
        next(seeded, None)
        store(outer.at[ahead], spot - ahead, placed)

    run(
        [
            last_step(*side, edge_word, place)
            for place in range(HALO)
            for side, edge_word in zip(sides, edge_words)
        ]
    )
    for ahead, _, message in sides:
        for m in range(19):
            outer[ahead, m, ahead * (BX - 1)] = message[30 + m]

    def seed_home(plane):
        return seed(plane, *recall(history, STEPS, plane))

    each_plane(HALO, HALO + home, seed_home)

    def ends(side):
        flow = [second_flow[side, 1 + axis] for axis in range(3)]
        return retreat(opens, words, share, even, odd, 1 + side * (span - 3), second_flow[side, 0], flow)

    run([ends(0), ends(1)])

    def step_two(plane):
        return retreat(opens, words, share, even, odd, plane, *recall(history, 2, plane))

    each_plane(HALO - 1, HALO + home + 1, step_two)


def gradient_kernel(
    home, history, opens, words, share, odd, marked, summed, gradient, to_near, to_far, total, even
):
    del summed
    up = parity()
    for plane in range(share.shape[0]):
        total[plane] = share[plane]

    def step_one(plane):
        return retreat(opens, words, total, odd, even, plane, *recall(history, 1, plane))

    def step_zero(plane):
        return retreat(opens, words, total, even, None, plane, *recall(history, 0, plane))

    each_plane(HALO - 1, HALO + home + 1, step_one)
    each_plane(HALO, HALO + home, step_zero)
    for plane in range(home):
        design = marked[plane]
        slope = 3.0 / ((1.6 + 3.4 * design) * (1.0 + 4.0 * design))
        gradient[plane] = jnp.where(design >= 0.0, total[plane + HALO] * slope, 0.0)
    for out, ahead in ((to_near, up), (to_far, 1 - up)):
        for plane in range(BX):
            out[plane] = gradient[ahead * (home - BX) + plane]


def scaled(home, cells, where, drag, joined, out):
    factor = cells / jnp.sum(drag[...])
    reach = (joined.shape[0] - home) // 2
    for plane in range(out.shape[0]):
        spot = jnp.clip(where[0] * BX + reach + plane, 0, joined.shape[0] - 1)
        live = plane < where[1] * BX
        out[plane] = jnp.where(live, joined[spot] * factor, 0.0)


def near_gradient(home, cells, where, drag, gradient, from_far, from_near, out, joined):
    up = parity()
    for ahead, message in ((up, from_near), (1 - up, from_far)):
        joined[pl.ds(ahead * (BX + home), BX)] = message[...]
    joined[pl.ds(BX, home)] = gradient[...]
    scaled(home, cells, where, drag, joined, out)


def far_gradient(home, cells, where, drag, gradient, from_left, from_right, out, joined):
    joined[pl.ds(0, home)] = from_left[...]
    joined[pl.ds(home, home)] = gradient[...]
    joined[pl.ds(2 * home, home)] = from_right[...]
    scaled(home, cells, where, drag, joined, out)


def place_kernel(where, final, outer, later, out, zeros, sems):
    del later
    blocks = out.shape[1] // BX
    home_blocks = final.shape[1] // BX
    beyond = outer.shape[2] // BX
    zeros[...] = jnp.zeros_like(zeros)
    for slot in range(blocks):
        target = out.at[:, pl.ds(slot * BX, BX)]
        live = slot < where[1]
        block = jnp.clip(where[0] + slot, -beyond, home_blocks + beyond - 1)
        inside = (block >= 0) & (block < home_blocks)

        @pl.when(live & inside)
        def _():
            source = final.at[:, pl.ds(block * BX, BX)]
            pltpu.make_async_copy(source, target, sems.at[slot]).start()

        @pl.when(live & jnp.logical_not(inside))
        def _():
            after = (block >= 0).astype(jnp.int32)
            within = block + beyond - after * (home_blocks + beyond)
            source = outer.at[after, :, pl.ds(within * BX, BX)]
            pltpu.make_async_copy(source, target, sems.at[slot]).start()

        @pl.when(jnp.logical_not(live))
        def _():
            pltpu.make_async_copy(zeros, target, sems.at[slot]).start()

    for slot in range(blocks):
        pltpu.make_async_copy(zeros, out.at[:, pl.ds(slot * BX, BX)], sems.at[slot]).wait()


def body(populations, design, fluid_mask, owner_after):
    count = lax.axis_size("block")
    home, width_y, width_z = design.shape
    slots = home // BX + 2
    span = home + 2 * HALO
    plane = (width_y, width_z)
    vmem = pl.BlockSpec(memory_space=pltpu.VMEM)
    hbm = pl.BlockSpec(memory_space=pltpu.HBM)
    anywhere = pl.BlockSpec(memory_space=pl.ANY)
    smem = pl.BlockSpec(memory_space=pltpu.SMEM)
    cells = float(count * home * width_y * width_z)
    near_pairs = [(i, i ^ 1) for i in range(count)]
    far_pairs = [(i, (i + 1 if i % 2 else i - 1) % count) for i in range(count)]
    inner_pairs = far_pairs[1:-1]

    def planes(*lead, dtype=jnp.float32):
        return jax.ShapeDtypeStruct(lead + plane, dtype)

    def scratch(*lead, dtype=jnp.float32):
        return pltpu.VMEM(lead + plane, dtype)

    def call(kernel, name, ins, outs, scratches, limit, moved, *operands):
        return pl.pallas_call(
            kernel,
            out_shape=[shape for shape, _ in outs],
            in_specs=ins,
            out_specs=[spec for _, spec in outs],
            scratch_shapes=scratches,
            compiler_params=pltpu.CompilerParams(vmem_limit_bytes=limit * MIB),
            cost_estimate=pl.CostEstimate(flops=20 * moved, bytes_accessed=moved, transcendentals=0),
            name=name,
        )(*operands)

    own_near, own_far, pops, marked = call(
        functools.partial(edge_kernel, home),
        "edge_planes",
        [hbm] * 3,
        [(planes(23, RAW), vmem)] * 2 + [(planes(19, home), vmem), (planes(home), vmem)],
        [scratch(home), scratch(home, dtype=jnp.int32), pltpu.SemaphoreType.DMA((5,))],
        4,
        1_000_000,
        *[
            pltpu.with_memory_space_constraint(part, pltpu.HBM)
            for part in (populations, design, fluid_mask)
        ],
    )
    near = lax.ppermute(own_near, "block", near_pairs)
    far = lax.ppermute(own_far, "block", far_pairs)

    inner_shapes = (
        planes(49),
        planes(49),
        planes(19, 12),
        planes(16, home),
        planes(19, home),
        planes(home),
        planes(home, dtype=jnp.int32),
        planes(home, dtype=jnp.int32),
        planes(),
    )
    (
        to_near,
        to_far,
        edges,
        inner_history,
        inner_final,
        inner_opens,
        inner_fluid,
        inner_words,
        inner_drag,
        where,
    ) = call(
        functools.partial(interior_kernel, home),
        "interior_steps",
        [hbm] + [vmem] * 2,
        [(shape, vmem) for shape in inner_shapes] + [(jax.ShapeDtypeStruct((3,), jnp.int32), smem)],
        [scratch(19, home)] * 2
        + [pltpu.SMEM(owner_after.shape, jnp.int32), pltpu.SemaphoreType.DMA(())],
        16,
        6_000_000,
        pltpu.with_memory_space_constraint(owner_after, pltpu.HBM),
        pops,
        marked,
    )
    from_near = lax.ppermute(to_near, "block", near_pairs)
    from_far = lax.ppermute(to_far, "block", far_pairs)

    boundary_shapes = (
        planes(19, home),
        planes(16, span),
        planes(span),
        planes(span, dtype=jnp.int32),
        planes(span, dtype=jnp.int32),
        planes(1 + STEPS),
        planes(19, span),
        planes(19, span),
    )
    final, history, opens, fluid, words, drag, even_state, odd_state = call(
        functools.partial(boundary_kernel, home),
        "boundary_steps",
        [vmem] * 3 + [anywhere] + [vmem] * 5,
        [(shape, vmem) for shape in boundary_shapes],
        [pltpu.SemaphoreType.DMA((5,))],
        20,
        8_000_000,
        far,
        near,
        edges,
        inner_history,
        inner_final,
        inner_opens,
        inner_fluid,
        inner_words,
        inner_drag,
    )

    distances = [1 << bit for bit in range(count.bit_length() - 1)]
    sums = [drag]
    for distance in distances[:1] + distances[2:3] + distances[1:2] + distances[3:]:
        swap = [(i, i ^ distance) for i in range(count)]
        sums.append(sums[-1] + lax.ppermute(sums[-1], "block", swap))
    drag = sums[-1]

    is_far = where[2] > 0
    outer, share, odd = call(
        functools.partial(outer_kernel, home),
        "outer_steps",
        [vmem] * 10 + [anywhere] * 2,
        [(planes(2, 19, BX), vmem), (planes(span), vmem), (planes(19, span), vmem)],
        [scratch(19, span), scratch(2, 19, HALO), scratch(2, 19, HALO + 2), scratch(2, 4)],
        20,
        12_000_000,
        history,
        opens,
        fluid,
        words,
        even_state,
        odd_state,
        far,
        near,
        from_far,
        from_near,
        sums[2],
        is_far.astype(jnp.int32).reshape(1),
    )
    gradient, to_near, to_far = call(
        functools.partial(gradient_kernel, home),
        "gradient_steps",
        [vmem] * 6 + [anywhere],
        [(planes(home), vmem), (planes(BX), vmem), (planes(BX), vmem)],
        [scratch(span), scratch(19, span)],
        20,
        6_000_000,
        history,
        opens,
        words,
        share,
        odd,
        marked,
        sums[3],
    )
    from_near = lax.ppermute(to_near, "block", near_pairs)
    from_far = lax.ppermute(to_far, "block", inner_pairs)

    ring = [(i, i + 1) for i in range(count - 1)]
    back = [(i + 1, i) for i in range(count - 1)]

    def place(outer):
        (out,) = call(
            place_kernel,
            "place_populations",
            [smem, anywhere, anywhere, vmem],
            [(planes(19, slots * BX), anywhere)],
            [scratch(19, BX), pltpu.SemaphoreType.DMA((slots,))],
            8,
            4_000_000,
            where,
            final,
            outer,
            gradient,
        )
        return out

    def place_far(_):
        wide = [lax.ppermute(final, "block", route) for route in (ring, back)]
        return place(jnp.stack(wide))

    def slope(kernel, name, reach, *messages):
        (out,) = call(
            functools.partial(kernel, home, cells),
            name,
            [smem] + [vmem] * 4,
            [(planes(slots * BX), vmem)],
            [scratch(home + 2 * reach)],
            4,
            1_000_000,
            where,
            drag,
            gradient,
            *messages,
        )
        return out

    def slope_near(*messages):
        return slope(near_gradient, "near_gradient", BX, *messages)

    def slope_far(*_):
        wide = [lax.ppermute(gradient, "block", route) for route in (ring, back)]
        return slope(far_gradient, "far_gradient", home, *wide)

    populations_after = lax.cond(is_far, place_far, place, outer)
    sensitivity = lax.cond(is_far, slope_far, slope_near, from_far, from_near)
    return (populations_after, sensitivity)


def solution(mesh):
    placed = (
        P(None, ("group", "block"), None, None),
        P(("group", "block"), None, None),
        P(("group", "block"), None, None),
        P("group"),
    )
    return jax.shard_map(
        body,
        mesh=mesh,
        in_specs=placed,
        out_specs=(P(None, ("group", "block"), None, None), P(("group", "block"), None, None)),
        check_vma=False,
    )
```

```python
import functools
import math

import jax
import jax.numpy as jnp
from jax import lax
from jax.experimental import pallas as pl
from jax.experimental.pallas import tpu as pltpu
from jax.sharding import PartitionSpec as P

BX = 4
STEPS = 3
HALO = STEPS
RAW = HALO - 1
MIB = 2**20

VELOCITY = (
    (0, 0, 0),
    (1, 0, 0),
    (-1, 0, 0),
    (0, 1, 0),
    (0, -1, 0),
    (0, 0, 1),
    (0, 0, -1),
    (1, 1, 0),
    (-1, -1, 0),
    (1, -1, 0),
    (-1, 1, 0),
    (1, 0, 1),
    (-1, 0, -1),
    (1, 0, -1),
    (-1, 0, 1),
    (0, 1, 1),
    (0, -1, -1),
    (0, 1, -1),
    (0, -1, 1),
)
OPP = (0,) + tuple(m + 1 if m % 2 else m - 1 for m in range(1, 19))
AHEAD = tuple(m for m in range(19) if VELOCITY[m][0] == 1)
BEHIND = tuple(m for m in range(19) if VELOCITY[m][0] == -1)
FORCE = 0.02
ROOT_45 = math.sqrt(4.5)
ROOT_2 = math.sqrt(2.0)


def rolled(field, step_y, step_z):
    if step_y:
        field = pltpu.roll(field, step_y % field.shape[0], 0)
    if step_z:
        field = pltpu.roll(field, step_z % field.shape[1], 1)
    return field


def pairs(values):
    plus = [values[2 * k + 1] + values[2 * k + 2] for k in range(9)]
    minus = [values[2 * k + 1] - values[2 * k + 2] for k in range(9)]
    return plus, minus


def first_moments(minus, scale):
    along_x, along_y, along_z = minus[:3]
    if scale != 1.0:
        along_x, along_y, along_z = scale * along_x, scale * along_y, scale * along_z
    along_x = along_x + ((minus[3] + minus[4]) + (minus[5] + minus[6]))
    along_y = along_y + ((minus[3] - minus[4]) + (minus[7] + minus[8]))
    along_z = along_z + ((minus[5] - minus[6]) + (minus[7] - minus[8]))
    return along_x, along_y, along_z


def density_velocity(state):
    plus, minus = pairs(state)
    axes = (plus[0] + plus[1]) + (plus[2] + state[0])
    diagonals = (plus[3] + plus[4]) + (plus[5] + plus[6]) + (plus[7] + plus[8])
    density = axes + diagonals
    inverse = 1.0 / density
    momentum = first_moments(minus, 1.0)
    return density, [part * inverse for part in momentum]


def collide(state, density, flow, open_rate):
    rate = ROOT_45 * open_rate
    x, y, z = (flow[0] + FORCE) * rate, flow[1] * rate, flow[2] * rate
    xx, yy, zz = x * x, y * y, z * z
    base = 1.0 - (xx + yy + zz) * (1.0 / 3.0)
    axis_weight = density * (1.2 / 18.0)
    axis_slope = density * (1.2 * ROOT_2 / 18.0)
    side_weight = density * (1.2 / 36.0)
    side_slope = density * (1.2 * ROOT_2 / 36.0)
    result = [density * 0.4 * base - 0.2 * state[0]]
    for k, along in enumerate((x, y, z, x + y, x - y, x + z, x - z, y + z, y - z)):
        if k < 3:
            even = axis_weight * (base + (xx, yy, zz)[k])
            odd = axis_slope * along
        else:
            even = side_weight * (base + along * along)
            odd = side_slope * along
        result.append((even + odd) - 0.2 * state[2 * k + 1])
        result.append((even - odd) - 0.2 * state[2 * k + 2])
    return result


def spread(level, slope):
    x, y, z = slope
    result = [level]
    for along in (x, y, z, x + y, x - y, x + z, x - z, y + z, y - z):
        result.append(level + along)
        result.append(level - along)
    return result


def pull(source, plane, word):
    here = [source[m, plane] for m in range(19)]
    result = [here[0]]
    for m in range(1, 19):
        step_x, step_y, step_z = VELOCITY[m]
        moved = here[m] if step_x == 0 else source[m, plane - step_x]
        moved = rolled(moved, step_y, step_z)
        result.append(jnp.where((word & (1 << m)) != 0, moved, here[OPP[m]]))
    return result


def link_word(behind, here, ahead):
    rows = lax.broadcasted_iota(jnp.int32, here.shape, 0)
    columns = lax.broadcasted_iota(jnp.int32, here.shape, 1)
    joined = behind + 2 * here + 4 * ahead
    word = jnp.zeros_like(here)
    for step_y in (-1, 0, 1):
        for step_z in (-1, 0, 1):
            if step_y and step_z:
                inner = {0: 1}
            else:
                inner = {1: 0, 0: 1, -1: 2}
            near = rolled(joined, step_y, step_z)
            if step_y == 1:
                near = jnp.where(rows == 0, 0, near)
            if step_y == -1:
                near = jnp.where(rows == here.shape[0] - 1, 0, near)
            if step_z == 1:
                near = jnp.where(columns == 0, 0, near)
            if step_z == -1:
                near = jnp.where(columns == here.shape[1] - 1, 0, near)
            for step_x, place in inner.items():
                if (step_x, step_y, step_z) == (0, 0, 0):
                    continue
                m = VELOCITY.index((step_x, step_y, step_z))
                word = word | ((near & (1 << place)) << (m - place))
    return jnp.where(here > 0, word, 0)


def run(bodies):
    for body in bodies:
        next(body)
    for body in bodies:
        next(body, None)


def each_plane(low, high, body, width=7):
    groups = (high - low) // width

    def group(index, carry):
        run([body(low + width * index + place) for place in range(width)])
        return carry

    lax.fori_loop(0, groups, group, 0)
    rest = range(low + groups * width, high)
    if rest:
        run([body(plane) for plane in rest])


def is_fluid_rate(mark):
    design = jnp.maximum(mark, 0.0)
    return (mark >= 0.0).astype(jnp.int32), (1.0 + 4.0 * design) / (1.6 + 3.4 * design)


def store(target, plane, values):
    for m, part in enumerate(values):
        target[m, plane] = part


def remember(history, step, plane, density, flow):
    history[4 * step, plane] = density
    for axis in range(3):
        history[4 * step + 1 + axis, plane] = flow[axis]


def drag_terms(flow, open_rate):
    return (flow[0] * flow[0] + flow[1] * flow[1] + flow[2] * flow[2]) / open_rate


def parity(axis="block"):
    return 1 - lax.rem(lax.axis_index(axis), 2)


def pick(flag, yes, no):
    return no + flag * (yes - no)


def edge_kernel(home, pops_far, design, mask, near, far, pops, marked, designs, masks, sems):
    up = parity()
    cuts = ((0, HALO), (home - HALO, HALO), (HALO, home - 2 * HALO))
    copies = [
        pltpu.make_async_copy(design, designs, sems.at[0]),
        pltpu.make_async_copy(mask, masks, sems.at[1]),
    ] + [
        pltpu.make_async_copy(
            pops_far.at[:, pl.ds(first, planes)], pops.at[:, pl.ds(first, planes)], sems.at[2 + place]
        )
        for place, (first, planes) in enumerate(cuts)
    ]
    for copy in copies:
        copy.start()
    for copy in copies[:2]:
        copy.wait()
    for plane in range(home):
        marked[plane] = jnp.where(masks[plane] > 0, designs[plane], -1.0)
    for copy in copies[2:4]:
        copy.wait()
    for out, ahead in ((near, up), (far, 1 - up)):
        first = ahead * (home - RAW)
        for plane in range(RAW):
            for m in range(19):
                out[m, plane] = pops[m, first + plane]
            out[19, plane] = marked[first + plane]
        third = ahead * (home - 1) + (1 - 2 * ahead) * RAW
        last = marked[third]
        out[22, 1] = last
        _, open_rate = is_fluid_rate(last)
        state = [pops[m, third] for m in range(19)]
        density, flow = density_velocity(state)
        collided = collide(state, density, flow, open_rate)
        for slot in range(5):
            value = jnp.where(ahead > 0, collided[AHEAD[slot]], collided[BEHIND[slot]])
            out[20 + slot // 2, slot % 2] = value
    copies[4].wait()


def count_blocks(home_blocks, owner, where):
    rank = lax.axis_index("block")
    below = jnp.int32(0)
    own = jnp.int32(0)
    for block in range(owner.shape[0]):
        holder = owner[block]
        below += (holder < rank).astype(jnp.int32)
        own += (holder == rank).astype(jnp.int32)
    stray = jnp.int32(0)
    for device in range(owner.shape[0] // home_blocks):
        late = owner[home_blocks * device + 1] < device
        early = owner[home_blocks * device + home_blocks - 2] > device
        stray = stray | late.astype(jnp.int32) | early.astype(jnp.int32)
    where[0] = below - home_blocks * rank
    where[1] = own
    where[2] = stray


def interior_kernel(
    home,
    owner_far,
    pops,
    marked,
    to_near,
    to_far,
    edges,
    history,
    final,
    opens,
    fluid,
    words,
    drag,
    where,
    even,
    odd,
    owner,
    sem,
):
    up = parity()
    copy = pltpu.make_async_copy(owner_far, owner, sem)
    copy.start()

    def start(plane):
        is_fluid, open_rate = is_fluid_rate(marked[plane])
        state = [pops[m, plane] for m in range(19)]
        density, flow = density_velocity(state)
        collided = collide(state, density, flow, open_rate)
        yield
        fluid[plane] = is_fluid
        opens[plane] = open_rate
        remember(history, 0, plane, density, flow)
        store(even, plane, collided)

    def link(plane):
        word = link_word(fluid[plane - 1], fluid[plane], fluid[plane + 1])
        yield
        words[plane] = word

    def advance(step, source, target, plane):
        state = pull(source, plane, words[plane])
        density, flow = density_velocity(state)
        collided = collide(state, density, flow, opens[plane])
        yield
        remember(history, step, plane, density, flow)
        store(target, plane, collided)

    def finish(plane):
        state = pull(even, plane, words[plane])
        density, flow = density_velocity(state)
        here = fluid[plane] > 0
        placed = [jnp.where(here, state[m], pops[m, plane]) for m in range(19)]
        part = jnp.where(here, drag_terms(flow, opens[plane]), 0.0)
        yield
        remember(history, 3, plane, density, flow)
        store(final, plane, placed)
        drag[...] += part

    def keep(step, source):
        for m in range(19):
            for side in range(2):
                edges[m, 4 * step + side] = source[m, step + side]
                edges[m, 4 * step + 2 + side] = source[m, home - 2 - step + side]

    def send(out, ahead, step, source):
        outer = ahead * (home - 1) + (1 - 2 * ahead) * RAW
        if step == 1:
            for slot in range(5):
                out[slot] = source[AHEAD[slot] + 1 - ahead, outer]
            return
        inner = ahead * (home - 1) + (1 - 2 * ahead) * HALO
        here = fluid[outer] > 0
        for slot in range(5):
            out[5 + slot] = source[AHEAD[slot] + 1 - ahead, inner]
        for m in range(19):
            out[10 + m] = jnp.where(here, source[m, outer], pops[m, outer])
        out[29] = marked[inner]

    drag[...] = jnp.zeros_like(drag)
    each_plane(0, home, start)
    keep(0, even)
    each_plane(1, home - 1, link)
    each_plane(1, home - 1, functools.partial(advance, 1, even, odd))
    keep(1, odd)
    each_plane(2, home - 2, functools.partial(advance, 2, odd, even))
    keep(2, even)
    for out, ahead in ((to_near, up), (to_far, 1 - up)):
        send(out, ahead, 1, odd)
        send(out, ahead, 2, even)
    each_plane(3, home - 3, finish)
    for m in range(19):
        for plane in range(STEPS):
            final[m, plane] = pops[m, plane]
            final[m, home - STEPS + plane] = pops[m, home - STEPS + plane]
        for out, ahead in ((to_near, up), (to_far, 1 - up)):
            out[30 + m] = final[m, STEPS + ahead * (home - 1 - 2 * STEPS)]
    copy.wait()
    count_blocks(home // BX, owner, where)


def boundary_kernel(
    home,
    far,
    near,
    edges,
    inner_history,
    inner_final,
    inner_opens,
    inner_fluid,
    inner_words,
    inner_drag,
    final,
    history,
    opens,
    fluid,
    words,
    drag,
    even,
    odd,
    sems,
):
    span = home + 2 * HALO
    up = parity()
    sides = ((up, near), (1 - up, far))
    copies = [
        pltpu.make_async_copy(
            inner_history.at[pl.ds(4 * step, 4), pl.ds(step, home - 2 * step)],
            history.at[pl.ds(4 * step, 4), pl.ds(HALO + step, home - 2 * step)],
            sems.at[step],
        )
        for step in range(4)
    ]
    copies.append(
        pltpu.make_async_copy(
            inner_final.at[:, pl.ds(STEPS, home - 2 * STEPS)],
            final.at[:, pl.ds(STEPS, home - 2 * STEPS)],
            sems.at[4],
        )
    )
    for copy in copies:
        copy.start()

    for plane in range(home):
        fluid[plane + HALO] = inner_fluid[plane]
        opens[plane + HALO] = inner_opens[plane]
    for plane in range(1, home - 1):
        words[plane + HALO] = inner_words[plane]
    for ahead, side in sides:
        fluid[ahead * (span - 1)], opens[ahead * (span - 1)] = is_fluid_rate(side[22, 1])
        for slot in range(5):
            even[AHEAD[slot] + ahead, ahead * (span - 1)] = side[20 + slot // 2, slot % 2]

    def begin(plane, ahead, side):
        index = plane + 1 + ahead * (home + RAW)
        is_fluid, open_rate = is_fluid_rate(side[19, plane])
        state = [side[m, plane] for m in range(19)]
        density, flow = density_velocity(state)
        collided = collide(state, density, flow, open_rate)
        yield
        fluid[index] = is_fluid
        opens[index] = open_rate
        store(even, index, collided)

    run([begin(plane, *side) for plane in range(RAW) for side in sides])

    def receive(step, target):
        for m in range(19):
            for side in range(2):
                target[m, HALO + step + side] = edges[m, 4 * step + side]
                target[m, HALO + home - 2 - step + side] = edges[m, 4 * step + 2 + side]

    def both(step, body):
        run(
            [
                body(first + place, place, ahead)
                for place in range(3)
                for ahead, first in enumerate((step, span - 3 - step))
            ]
        )

    def link(index, place, ahead):
        word = link_word(fluid[index - 1], fluid[index], fluid[index + 1])
        yield
        words[index] = word

    def advance(step, source, target, index, place, ahead):
        state = pull(source, index, words[index])
        density, flow = density_velocity(state)
        collided = collide(state, density, flow, opens[index])
        yield
        remember(history, step, index, density, flow)
        store(target, index, collided)

    both(1, link)
    receive(0, even)
    both(1, functools.partial(advance, 1, even, odd))
    receive(1, odd)
    both(2, functools.partial(advance, 2, odd, even))
    receive(2, even)
    drag[...] = jnp.zeros_like(drag)
    drag[0] = inner_drag[...]

    def finish(index, place, ahead):
        state = pull(even, index, words[index])
        density, flow = density_velocity(state)
        here = fluid[index] > 0
        placed = [jnp.where(here, state[m], inner_final[m, index - HALO]) for m in range(19)]
        part = jnp.where(here, drag_terms(flow, opens[index]), 0.0)
        yield
        remember(history, 3, index, density, flow)
        store(final, index - HALO, placed)
        drag[1 + place] += part

    both(3, finish)
    for copy in copies:
        copy.wait()


def recall(history, step, plane):
    return history[4 * step, plane], [history[4 * step + 1 + axis, plane] for axis in range(3)]


def retreat(opens, words, share, source, target, plane, density, flow):
    mirrored = pull(source, plane, words[plane])
    adjoint = [mirrored[OPP[m]] for m in range(19)]
    open_rate = opens[plane]
    force_flow = [flow[0] + FORCE, flow[1], flow[2]]
    x, y, z = [open_rate * part for part in force_flow]
    plus, minus = pairs(adjoint)
    mx, my, mz = [part * (1.0 / 12.0) for part in first_moments(minus, 2.0)]
    xy_plus, xz_plus, yz_plus = plus[3] + plus[4], plus[5] + plus[6], plus[7] + plus[8]
    axes = [2.0 * plus[k] for k in range(3)]
    whole = 12.0 * adjoint[0] + (axes[0] + axes[1] + axes[2]) + (xy_plus + xz_plus + yz_plus)
    third = whole * (1.0 / 3.0)
    xx = axes[0] + (xy_plus + xz_plus) - third
    yy = axes[1] + (xy_plus + yz_plus) - third
    zz = axes[2] + (xz_plus + yz_plus) - third
    xy, xz, yz = plus[3] - plus[4], plus[5] - plus[6], plus[7] - plus[8]
    hx = 0.25 * (xx * x + xy * y + xz * z)
    hy = 0.25 * (xy * x + yy * y + yz * z)
    hz = 0.25 * (xz * x + yz * y + zz * z)
    rate = 1.2 * open_rate
    slope = [rate * (mx + hx), rate * (my + hy), rate * (mz + hz)]
    pushed = slope[0] * force_flow[0] + slope[1] * force_flow[1] + slope[2] * force_flow[2]
    gained = share[plane] + density * pushed
    if target is None:
        yield
        share[plane] = gained
        return
    level = whole * (1.2 / 36.0) + 1.2 * (
        x * (mx + 0.5 * hx) + y * (my + 0.5 * hy) + z * (mz + 0.5 * hz)
    )
    level = level - (slope[0] * flow[0] + slope[1] * flow[1] + slope[2] * flow[2])
    values = [part - 0.2 * old for part, old in zip(spread(level, slope), adjoint)]
    yield
    share[plane] = gained
    for m in range(19):
        target[OPP[m], plane] = values[m]


def outer_kernel(
    home,
    history,
    opens,
    fluid,
    words,
    even_state,
    odd_state,
    far,
    near,
    from_far,
    from_near,
    summed,
    counted,
    outer,
    share,
    odd,
    even,
    first,
    second,
    second_flow,
):
    del summed, counted
    span = home + 2 * HALO
    up = parity()

    def seed(plane, density, flow):
        damping = 1.0 / opens[plane]
        square = flow[0] * flow[0] + flow[1] * flow[1] + flow[2] * flow[2]
        factor = 2.0 * damping / density
        slope = [part * factor for part in flow]
        values = spread(-square * factor, slope)
        yield
        share[plane] = -square * damping
        for m in range(19):
            even[OPP[m], plane] = values[m]

    sides = ((up, near, from_near), (1 - up, far, from_far))
    edge_words = []
    for ahead, _, message in sides:
        for m in range(19):
            for place in range(HALO):
                first[ahead, m, place] = odd_state[m, ahead * (span - HALO) + place]
            for place in range(2):
                second[ahead, m, 3 - 3 * ahead + place] = even_state[m, 2 + ahead * (span - 6) + place]
            second[ahead, m, 1 + 2 * ahead] = message[10 + m]
        for slot in range(5):
            first[ahead, AHEAD[slot] + ahead, ahead * RAW] = message[slot]
            second[ahead, AHEAD[slot] + ahead, 4 * ahead] = message[5 + slot]
        beyond = (message[29] >= 0.0).astype(jnp.int32)
        within = fluid[1 + ahead * (span - 3)]
        edge_words.append(
            link_word(
                beyond + ahead * (within - beyond),
                fluid[ahead * (span - 1)],
                within + ahead * (beyond - within),
            )
        )

    def second_out(ahead):
        index = 1 + ahead * (span - 3)
        state = pull(first.at[ahead], 1, words[index])
        density, flow = density_velocity(state)
        collided = collide(state, density, flow, opens[index])
        yield
        for place, part in enumerate([density] + flow):
            second_flow[ahead, place] = part
        store(second.at[ahead], 2, collided)

    run([second_out(side[0]) for side in sides])

    def last_step(ahead, raw, message, edge_word, place):
        spot = 1 + place
        index = place + ahead * (span - 3)
        two = second.at[ahead]
        word = words[index]
        if place == 0:
            word = edge_word + ahead * (word - edge_word)
        if place == 2:
            word = word + ahead * (edge_word - word)
        state = pull(two, spot, word)
        density, flow = density_velocity(state)
        seeded = seed(index, density, flow)
        next(seeded)
        here = fluid[index] > 0
        placed = []
        for m in range(19):
            if place == 1:
                initial = raw[m, ahead]
            else:
                initial = jnp.where((ahead > 0) == (place == 2), two[m, spot], raw[m, place // 2])
            placed.append(jnp.where(here, state[m], initial))
        yield
        next(seeded, None)
        store(outer.at[ahead], spot - ahead, placed)

    run(
        [
            last_step(*side, edge_word, place)
            for place in range(HALO)
            for side, edge_word in zip(sides, edge_words)
        ]
    )
    for ahead, _, message in sides:
        for m in range(19):
            outer[ahead, m, ahead * (BX - 1)] = message[30 + m]

    def seed_home(plane):
        return seed(plane, *recall(history, STEPS, plane))

    each_plane(HALO, HALO + home, seed_home)

    def ends(side):
        flow = [second_flow[side, 1 + axis] for axis in range(3)]
        return retreat(opens, words, share, even, odd, 1 + side * (span - 3), second_flow[side, 0], flow)

    run([ends(0), ends(1)])

    def step_two(plane):
        return retreat(opens, words, share, even, odd, plane, *recall(history, 2, plane))

    each_plane(HALO - 1, HALO + home + 1, step_two)


def gradient_kernel(
    home, history, opens, words, share, odd, marked, summed, gradient, to_near, to_far, total, even
):
    del summed
    up = parity()
    for plane in range(share.shape[0]):
        total[plane] = share[plane]

    def step_one(plane):
        return retreat(opens, words, total, odd, even, plane, *recall(history, 1, plane))

    def step_zero(plane):
        return retreat(opens, words, total, even, None, plane, *recall(history, 0, plane))

    each_plane(HALO - 1, HALO + home + 1, step_one)
    each_plane(HALO, HALO + home, step_zero)
    for plane in range(home):
        design = marked[plane]
        slope = 3.0 / ((1.6 + 3.4 * design) * (1.0 + 4.0 * design))
        gradient[plane] = jnp.where(design >= 0.0, total[plane + HALO] * slope, 0.0)
    for out, ahead in ((to_near, up), (to_far, 1 - up)):
        for plane in range(BX):
            out[plane] = gradient[ahead * (home - BX) + plane]


def scaled(home, cells, where, drag, joined, out):
    factor = cells / jnp.sum(drag[...])
    reach = (joined.shape[0] - home) // 2
    for plane in range(out.shape[0]):
        spot = jnp.clip(where[0] * BX + reach + plane, 0, joined.shape[0] - 1)
        live = plane < where[1] * BX
        out[plane] = jnp.where(live, joined[spot] * factor, 0.0)


def near_gradient(home, cells, where, drag, gradient, from_far, from_near, out, joined):
    up = parity()
    for ahead, message in ((up, from_near), (1 - up, from_far)):
        joined[pl.ds(ahead * (BX + home), BX)] = message[...]
    joined[pl.ds(BX, home)] = gradient[...]
    scaled(home, cells, where, drag, joined, out)


def far_gradient(home, cells, where, drag, gradient, from_left, from_right, out, joined):
    joined[pl.ds(0, home)] = from_left[...]
    joined[pl.ds(home, home)] = gradient[...]
    joined[pl.ds(2 * home, home)] = from_right[...]
    scaled(home, cells, where, drag, joined, out)


def place_kernel(where, final, outer, later, out, zeros, sems):
    del later
    blocks = out.shape[1] // BX
    home_blocks = final.shape[1] // BX
    beyond = outer.shape[2] // BX
    zeros[...] = jnp.zeros_like(zeros)
    for slot in range(blocks):
        target = out.at[:, pl.ds(slot * BX, BX)]
        live = slot < where[1]
        block = jnp.clip(where[0] + slot, -beyond, home_blocks + beyond - 1)
        inside = (block >= 0) & (block < home_blocks)

        @pl.when(live & inside)
        def _():
            source = final.at[:, pl.ds(block * BX, BX)]
            pltpu.make_async_copy(source, target, sems.at[slot]).start()

        @pl.when(live & jnp.logical_not(inside))
        def _():
            after = (block >= 0).astype(jnp.int32)
            within = block + beyond - after * (home_blocks + beyond)
            source = outer.at[after, :, pl.ds(within * BX, BX)]
            pltpu.make_async_copy(source, target, sems.at[slot]).start()

        @pl.when(jnp.logical_not(live))
        def _():
            pltpu.make_async_copy(zeros, target, sems.at[slot]).start()

    for slot in range(blocks):
        pltpu.make_async_copy(zeros, out.at[:, pl.ds(slot * BX, BX)], sems.at[slot]).wait()


def body(populations, design, fluid_mask, owner_after):
    count = lax.axis_size("block")
    home, width_y, width_z = design.shape
    slots = home // BX + 2
    span = home + 2 * HALO
    plane = (width_y, width_z)
    vmem = pl.BlockSpec(memory_space=pltpu.VMEM)
    hbm = pl.BlockSpec(memory_space=pltpu.HBM)
    anywhere = pl.BlockSpec(memory_space=pl.ANY)
    smem = pl.BlockSpec(memory_space=pltpu.SMEM)
    cells = float(count * home * width_y * width_z)
    near_pairs = [(i, i ^ 1) for i in range(count)]
    far_pairs = [(i, (i + 1 if i % 2 else i - 1) % count) for i in range(count)]
    inner_pairs = far_pairs[1:-1]

    def planes(*lead, dtype=jnp.float32):
        return jax.ShapeDtypeStruct(lead + plane, dtype)

    def scratch(*lead, dtype=jnp.float32):
        return pltpu.VMEM(lead + plane, dtype)

    def call(kernel, name, ins, outs, scratches, limit, moved, *operands):
        return pl.pallas_call(
            kernel,
            out_shape=[shape for shape, _ in outs],
            in_specs=ins,
            out_specs=[spec for _, spec in outs],
            scratch_shapes=scratches,
            compiler_params=pltpu.CompilerParams(vmem_limit_bytes=limit * MIB),
            cost_estimate=pl.CostEstimate(flops=20 * moved, bytes_accessed=moved, transcendentals=0),
            name=name,
        )(*operands)

    own_near, own_far, pops, marked = call(
        functools.partial(edge_kernel, home),
        "edge_planes",
        [hbm] * 3,
        [(planes(23, RAW), vmem)] * 2 + [(planes(19, home), vmem), (planes(home), vmem)],
        [scratch(home), scratch(home, dtype=jnp.int32), pltpu.SemaphoreType.DMA((5,))],
        4,
        1_000_000,
        *[
            pltpu.with_memory_space_constraint(part, pltpu.HBM)
            for part in (populations, design, fluid_mask)
        ],
    )
    near = lax.ppermute(own_near, "block", near_pairs)
    far = lax.ppermute(own_far, "block", far_pairs)

    inner_shapes = (
        planes(49),
        planes(49),
        planes(19, 12),
        planes(16, home),
        planes(19, home),
        planes(home),
        planes(home, dtype=jnp.int32),
        planes(home, dtype=jnp.int32),
        planes(),
    )
    (
        to_near,
        to_far,
        edges,
        inner_history,
        inner_final,
        inner_opens,
        inner_fluid,
        inner_words,
        inner_drag,
        where,
    ) = call(
        functools.partial(interior_kernel, home),
        "interior_steps",
        [hbm] + [vmem] * 2,
        [(shape, vmem) for shape in inner_shapes] + [(jax.ShapeDtypeStruct((3,), jnp.int32), smem)],
        [scratch(19, home)] * 2
        + [pltpu.SMEM(owner_after.shape, jnp.int32), pltpu.SemaphoreType.DMA(())],
        16,
        6_000_000,
        pltpu.with_memory_space_constraint(owner_after, pltpu.HBM),
        pops,
        marked,
    )
    from_near = lax.ppermute(to_near, "block", near_pairs)
    from_far = lax.ppermute(to_far, "block", far_pairs)

    boundary_shapes = (
        planes(19, home),
        planes(16, span),
        planes(span),
        planes(span, dtype=jnp.int32),
        planes(span, dtype=jnp.int32),
        planes(1 + STEPS),
        planes(19, span),
        planes(19, span),
    )
    final, history, opens, fluid, words, drag, even_state, odd_state = call(
        functools.partial(boundary_kernel, home),
        "boundary_steps",
        [vmem] * 3 + [anywhere] + [vmem] * 5,
        [(shape, vmem) for shape in boundary_shapes],
        [pltpu.SemaphoreType.DMA((5,))],
        20,
        8_000_000,
        far,
        near,
        edges,
        inner_history,
        inner_final,
        inner_opens,
        inner_fluid,
        inner_words,
        inner_drag,
    )

    distances = [1 << bit for bit in range(count.bit_length() - 1)]
    sums = [drag]
    for distance in distances[:1] + distances[2:3] + distances[1:2] + distances[3:]:
        swap = [(i, i ^ distance) for i in range(count)]
        sums.append(sums[-1] + lax.ppermute(sums[-1], "block", swap))
    drag = sums[-1]

    is_far = where[2] > 0
    outer, share, odd = call(
        functools.partial(outer_kernel, home),
        "outer_steps",
        [vmem] * 10 + [anywhere] * 2,
        [(planes(2, 19, BX), vmem), (planes(span), vmem), (planes(19, span), vmem)],
        [scratch(19, span), scratch(2, 19, HALO), scratch(2, 19, HALO + 2), scratch(2, 4)],
        20,
        12_000_000,
        history,
        opens,
        fluid,
        words,
        even_state,
        odd_state,
        far,
        near,
        from_far,
        from_near,
        sums[2],
        is_far.astype(jnp.int32).reshape(1),
    )
    gradient, to_near, to_far = call(
        functools.partial(gradient_kernel, home),
        "gradient_steps",
        [vmem] * 6 + [anywhere],
        [(planes(home), vmem), (planes(BX), vmem), (planes(BX), vmem)],
        [scratch(span), scratch(19, span)],
        20,
        6_000_000,
        history,
        opens,
        words,
        share,
        odd,
        marked,
        sums[3],
    )
    from_near = lax.ppermute(to_near, "block", near_pairs)
    from_far = lax.ppermute(to_far, "block", inner_pairs)

    ring = [(i, i + 1) for i in range(count - 1)]
    back = [(i + 1, i) for i in range(count - 1)]

    def place(outer):
        (out,) = call(
            place_kernel,
            "place_populations",
            [smem, anywhere, anywhere, vmem],
            [(planes(19, slots * BX), anywhere)],
            [scratch(19, BX), pltpu.SemaphoreType.DMA((slots,))],
            8,
            4_000_000,
            where,
            final,
            outer,
            gradient,
        )
        return out

    def place_far(_):
        wide = [lax.ppermute(final, "block", route) for route in (ring, back)]
        return place(jnp.stack(wide))

    def slope(kernel, name, reach, *messages):
        (out,) = call(
            functools.partial(kernel, home, cells),
            name,
            [smem] + [vmem] * 4,
            [(planes(slots * BX), vmem)],
            [scratch(home + 2 * reach)],
            4,
            1_000_000,
            where,
            drag,
            gradient,
            *messages,
        )
        return out

    def slope_near(*messages):
        return slope(near_gradient, "near_gradient", BX, *messages)

    def slope_far(*_):
        wide = [lax.ppermute(gradient, "block", route) for route in (ring, back)]
        return slope(far_gradient, "far_gradient", home, *wide)

    populations_after = lax.cond(is_far, place_far, place, outer)
    sensitivity = lax.cond(is_far, slope_far, slope_near, from_far, from_near)
    return (populations_after, sensitivity)


def solution(mesh):
    placed = (
        P(None, ("group", "block"), None, None),
        P(("group", "block"), None, None),
        P(("group", "block"), None, None),
        P("group"),
    )
    return jax.shard_map(
        body,
        mesh=mesh,
        in_specs=placed,
        out_specs=(P(None, ("group", "block"), None, None), P(("group", "block"), None, None)),
        check_vma=False,
    )
```

```python
import functools
import math

import jax
import jax.numpy as jnp
from jax import lax
from jax.experimental import pallas as pl
from jax.experimental.pallas import tpu as pltpu
from jax.sharding import PartitionSpec as P

BX = 4
STEPS = 3
HALO = STEPS
RAW = HALO - 1
MIB = 2**20

VELOCITY = (
    (0, 0, 0),
    (1, 0, 0),
    (-1, 0, 0),
    (0, 1, 0),
    (0, -1, 0),
    (0, 0, 1),
    (0, 0, -1),
    (1, 1, 0),
    (-1, -1, 0),
    (1, -1, 0),
    (-1, 1, 0),
    (1, 0, 1),
    (-1, 0, -1),
    (1, 0, -1),
    (-1, 0, 1),
    (0, 1, 1),
    (0, -1, -1),
    (0, 1, -1),
    (0, -1, 1),
)
OPP = (0,) + tuple(m + 1 if m % 2 else m - 1 for m in range(1, 19))
AHEAD = tuple(m for m in range(19) if VELOCITY[m][0] == 1)
BEHIND = tuple(m for m in range(19) if VELOCITY[m][0] == -1)
FORCE = 0.02
ROOT_45 = math.sqrt(4.5)
ROOT_2 = math.sqrt(2.0)


def rolled(field, step_y, step_z):
    if step_y:
        field = pltpu.roll(field, step_y % field.shape[0], 0)
    if step_z:
        field = pltpu.roll(field, step_z % field.shape[1], 1)
    return field


def pairs(values):
    plus = [values[2 * k + 1] + values[2 * k + 2] for k in range(9)]
    minus = [values[2 * k + 1] - values[2 * k + 2] for k in range(9)]
    return plus, minus


def first_moments(minus, scale):
    along_x, along_y, along_z = minus[:3]
    if scale != 1.0:
        along_x, along_y, along_z = scale * along_x, scale * along_y, scale * along_z
    along_x = along_x + ((minus[3] + minus[4]) + (minus[5] + minus[6]))
    along_y = along_y + ((minus[3] - minus[4]) + (minus[7] + minus[8]))
    along_z = along_z + ((minus[5] - minus[6]) + (minus[7] - minus[8]))
    return along_x, along_y, along_z


def density_velocity(state):
    plus, minus = pairs(state)
    axes = (plus[0] + plus[1]) + (plus[2] + state[0])
    diagonals = (plus[3] + plus[4]) + (plus[5] + plus[6]) + (plus[7] + plus[8])
    density = axes + diagonals
    inverse = 1.0 / density
    momentum = first_moments(minus, 1.0)
    return density, [part * inverse for part in momentum]


def collide(state, density, flow, open_rate):
    rate = ROOT_45 * open_rate
    x, y, z = (flow[0] + FORCE) * rate, flow[1] * rate, flow[2] * rate
    xx, yy, zz = x * x, y * y, z * z
    base = 1.0 - (xx + yy + zz) * (1.0 / 3.0)
    axis_weight = density * (1.2 / 18.0)
    axis_slope = density * (1.2 * ROOT_2 / 18.0)
    side_weight = density * (1.2 / 36.0)
    side_slope = density * (1.2 * ROOT_2 / 36.0)
    result = [density * 0.4 * base - 0.2 * state[0]]
    for k, along in enumerate((x, y, z, x + y, x - y, x + z, x - z, y + z, y - z)):
        if k < 3:
            even = axis_weight * (base + (xx, yy, zz)[k])
            odd = axis_slope * along
        else:
            even = side_weight * (base + along * along)
            odd = side_slope * along
        result.append((even + odd) - 0.2 * state[2 * k + 1])
        result.append((even - odd) - 0.2 * state[2 * k + 2])
    return result


def spread(level, slope):
    x, y, z = slope
    result = [level]
    for along in (x, y, z, x + y, x - y, x + z, x - z, y + z, y - z):
        result.append(level + along)
        result.append(level - along)
    return result


def pull(source, plane, word):
    here = [source[m, plane] for m in range(19)]
    result = [here[0]]
    for m in range(1, 19):
        step_x, step_y, step_z = VELOCITY[m]
        moved = here[m] if step_x == 0 else source[m, plane - step_x]
        moved = rolled(moved, step_y, step_z)
        result.append(jnp.where((word & (1 << m)) != 0, moved, here[OPP[m]]))
    return result


def link_word(behind, here, ahead):
    rows = lax.broadcasted_iota(jnp.int32, here.shape, 0)
    columns = lax.broadcasted_iota(jnp.int32, here.shape, 1)
    joined = behind + 2 * here + 4 * ahead
    word = jnp.zeros_like(here)
    for step_y in (-1, 0, 1):
        for step_z in (-1, 0, 1):
            if step_y and step_z:
                inner = {0: 1}
            else:
                inner = {1: 0, 0: 1, -1: 2}
            near = rolled(joined, step_y, step_z)
            if step_y == 1:
                near = jnp.where(rows == 0, 0, near)
            if step_y == -1:
                near = jnp.where(rows == here.shape[0] - 1, 0, near)
            if step_z == 1:
                near = jnp.where(columns == 0, 0, near)
            if step_z == -1:
                near = jnp.where(columns == here.shape[1] - 1, 0, near)
            for step_x, place in inner.items():
                if (step_x, step_y, step_z) == (0, 0, 0):
                    continue
                m = VELOCITY.index((step_x, step_y, step_z))
                word = word | ((near & (1 << place)) << (m - place))
    return jnp.where(here > 0, word, 0)


def run(bodies):
    for body in bodies:
        next(body)
    for body in bodies:
        next(body, None)


def each_plane(low, high, body, width=7):
    groups = (high - low) // width

    def group(index, carry):
        run([body(low + width * index + place) for place in range(width)])
        return carry

    lax.fori_loop(0, groups, group, 0)
    rest = range(low + groups * width, high)
    if rest:
        run([body(plane) for plane in rest])


def is_fluid_rate(mark):
    design = jnp.maximum(mark, 0.0)
    return (mark >= 0.0).astype(jnp.int32), (1.0 + 4.0 * design) / (1.6 + 3.4 * design)


def store(target, plane, values):
    for m, part in enumerate(values):
        target[m, plane] = part


def remember(history, step, plane, density, flow):
    history[4 * step, plane] = density
    for axis in range(3):
        history[4 * step + 1 + axis, plane] = flow[axis]


def drag_terms(flow, open_rate):
    return (flow[0] * flow[0] + flow[1] * flow[1] + flow[2] * flow[2]) / open_rate


def parity(axis="block"):
    return 1 - lax.rem(lax.axis_index(axis), 2)


def pick(flag, yes, no):
    return no + flag * (yes - no)


def edge_kernel(home, pops_far, design, mask, near, far, pops, marked, designs, masks, sems):
    up = parity()
    cuts = ((0, HALO), (home - HALO, HALO), (HALO, home - 2 * HALO))
    copies = [
        pltpu.make_async_copy(design, designs, sems.at[0]),
        pltpu.make_async_copy(mask, masks, sems.at[1]),
    ] + [
        pltpu.make_async_copy(
            pops_far.at[:, pl.ds(first, planes)], pops.at[:, pl.ds(first, planes)], sems.at[2 + place]
        )
        for place, (first, planes) in enumerate(cuts)
    ]
    for copy in copies:
        copy.start()
    for copy in copies[:2]:
        copy.wait()
    for plane in range(home):
        marked[plane] = jnp.where(masks[plane] > 0, designs[plane], -1.0)
    for copy in copies[2:4]:
        copy.wait()
    for out, ahead in ((near, up), (far, 1 - up)):
        first = ahead * (home - RAW)
        for plane in range(RAW):
            for m in range(19):
                out[m, plane] = pops[m, first + plane]
            out[19, plane] = marked[first + plane]
        third = ahead * (home - 1) + (1 - 2 * ahead) * RAW
        last = marked[third]
        out[22, 1] = last
        _, open_rate = is_fluid_rate(last)
        state = [pops[m, third] for m in range(19)]
        density, flow = density_velocity(state)
        collided = collide(state, density, flow, open_rate)
        for slot in range(5):
            value = jnp.where(ahead > 0, collided[AHEAD[slot]], collided[BEHIND[slot]])
            out[20 + slot // 2, slot % 2] = value
    copies[4].wait()


def count_blocks(home_blocks, owner, where):
    rank = lax.axis_index("block")
    below = jnp.int32(0)
    own = jnp.int32(0)
    for block in range(owner.shape[0]):
        holder = owner[block]
        below += (holder < rank).astype(jnp.int32)
        own += (holder == rank).astype(jnp.int32)
    stray = jnp.int32(0)
    for device in range(owner.shape[0] // home_blocks):
        late = owner[home_blocks * device + 1] < device
        early = owner[home_blocks * device + home_blocks - 2] > device
        stray = stray | late.astype(jnp.int32) | early.astype(jnp.int32)
    where[0] = below - home_blocks * rank
    where[1] = own
    where[2] = stray


def interior_kernel(
    home,
    owner_far,
    pops,
    marked,
    to_near,
    to_far,
    edges,
    history,
    final,
    opens,
    fluid,
    words,
    drag,
    where,
    even,
    odd,
    owner,
    sem,
):
    up = parity()
    copy = pltpu.make_async_copy(owner_far, owner, sem)
    copy.start()

    def start(plane):
        is_fluid, open_rate = is_fluid_rate(marked[plane])
        state = [pops[m, plane] for m in range(19)]
        density, flow = density_velocity(state)
        collided = collide(state, density, flow, open_rate)
        yield
        fluid[plane] = is_fluid
        opens[plane] = open_rate
        remember(history, 0, plane, density, flow)
        store(even, plane, collided)

    def link(plane):
        word = link_word(fluid[plane - 1], fluid[plane], fluid[plane + 1])
        yield
        words[plane] = word

    def advance(step, source, target, plane):
        state = pull(source, plane, words[plane])
        density, flow = density_velocity(state)
        collided = collide(state, density, flow, opens[plane])
        yield
        remember(history, step, plane, density, flow)
        store(target, plane, collided)

    def finish(plane):
        state = pull(even, plane, words[plane])
        density, flow = density_velocity(state)
        here = fluid[plane] > 0
        placed = [jnp.where(here, state[m], pops[m, plane]) for m in range(19)]
        part = jnp.where(here, drag_terms(flow, opens[plane]), 0.0)
        yield
        remember(history, 3, plane, density, flow)
        store(final, plane, placed)
        drag[...] += part

    def keep(step, source):
        for m in range(19):
            for side in range(2):
                edges[m, 4 * step + side] = source[m, step + side]
                edges[m, 4 * step + 2 + side] = source[m, home - 2 - step + side]

    def send(out, ahead, step, source):
        outer = ahead * (home - 1) + (1 - 2 * ahead) * RAW
        if step == 1:
            for slot in range(5):
                out[slot] = source[AHEAD[slot] + 1 - ahead, outer]
            return
        inner = ahead * (home - 1) + (1 - 2 * ahead) * HALO
        here = fluid[outer] > 0
        for slot in range(5):
            out[5 + slot] = source[AHEAD[slot] + 1 - ahead, inner]
        for m in range(19):
            out[10 + m] = jnp.where(here, source[m, outer], pops[m, outer])
        out[29] = marked[inner]

    drag[...] = jnp.zeros_like(drag)
    each_plane(0, home, start)
    keep(0, even)
    each_plane(1, home - 1, link)
    each_plane(1, home - 1, functools.partial(advance, 1, even, odd))
    keep(1, odd)
    each_plane(2, home - 2, functools.partial(advance, 2, odd, even))
    keep(2, even)
    for out, ahead in ((to_near, up), (to_far, 1 - up)):
        send(out, ahead, 1, odd)
        send(out, ahead, 2, even)
    each_plane(3, home - 3, finish)
    for m in range(19):
        for plane in range(STEPS):
            final[m, plane] = pops[m, plane]
            final[m, home - STEPS + plane] = pops[m, home - STEPS + plane]
        for out, ahead in ((to_near, up), (to_far, 1 - up)):
            out[30 + m] = final[m, STEPS + ahead * (home - 1 - 2 * STEPS)]
    copy.wait()
    count_blocks(home // BX, owner, where)


def boundary_kernel(
    home,
    far,
    near,
    edges,
    inner_history,
    inner_final,
    inner_opens,
    inner_fluid,
    inner_words,
    inner_drag,
    final,
    history,
    opens,
    fluid,
    words,
    drag,
    even,
    odd,
    sems,
):
    span = home + 2 * HALO
    up = parity()
    sides = ((up, near), (1 - up, far))
    copies = [
        pltpu.make_async_copy(
            inner_history.at[pl.ds(4 * step, 4), pl.ds(step, home - 2 * step)],
            history.at[pl.ds(4 * step, 4), pl.ds(HALO + step, home - 2 * step)],
            sems.at[step],
        )
        for step in range(4)
    ]
    copies.append(
        pltpu.make_async_copy(
            inner_final.at[:, pl.ds(STEPS, home - 2 * STEPS)],
            final.at[:, pl.ds(STEPS, home - 2 * STEPS)],
            sems.at[4],
        )
    )
    for copy in copies:
        copy.start()

    for plane in range(home):
        fluid[plane + HALO] = inner_fluid[plane]
        opens[plane + HALO] = inner_opens[plane]
    for plane in range(1, home - 1):
        words[plane + HALO] = inner_words[plane]
    for ahead, side in sides:
        fluid[ahead * (span - 1)], opens[ahead * (span - 1)] = is_fluid_rate(side[22, 1])
        for slot in range(5):
            even[AHEAD[slot] + ahead, ahead * (span - 1)] = side[20 + slot // 2, slot % 2]

    def begin(plane, ahead, side):
        index = plane + 1 + ahead * (home + RAW)
        is_fluid, open_rate = is_fluid_rate(side[19, plane])
        state = [side[m, plane] for m in range(19)]
        density, flow = density_velocity(state)
        collided = collide(state, density, flow, open_rate)
        yield
        fluid[index] = is_fluid
        opens[index] = open_rate
        store(even, index, collided)

    run([begin(plane, *side) for plane in range(RAW) for side in sides])

    def receive(step, target):
        for m in range(19):
            for side in range(2):
                target[m, HALO + step + side] = edges[m, 4 * step + side]
                target[m, HALO + home - 2 - step + side] = edges[m, 4 * step + 2 + side]

    def both(step, body):
        run(
            [
                body(first + place, place, ahead)
                for place in range(3)
                for ahead, first in enumerate((step, span - 3 - step))
            ]
        )

    def link(index, place, ahead):
        word = link_word(fluid[index - 1], fluid[index], fluid[index + 1])
        yield
        words[index] = word

    def advance(step, source, target, index, place, ahead):
        state = pull(source, index, words[index])
        density, flow = density_velocity(state)
        collided = collide(state, density, flow, opens[index])
        yield
        remember(history, step, index, density, flow)
        store(target, index, collided)

    both(1, link)
    receive(0, even)
    both(1, functools.partial(advance, 1, even, odd))
    receive(1, odd)
    both(2, functools.partial(advance, 2, odd, even))
    receive(2, even)
    drag[...] = jnp.zeros_like(drag)
    drag[0] = inner_drag[...]

    def finish(index, place, ahead):
        state = pull(even, index, words[index])
        density, flow = density_velocity(state)
        here = fluid[index] > 0
        placed = [jnp.where(here, state[m], inner_final[m, index - HALO]) for m in range(19)]
        part = jnp.where(here, drag_terms(flow, opens[index]), 0.0)
        yield
        remember(history, 3, index, density, flow)
        store(final, index - HALO, placed)
        drag[1 + place] += part

    both(3, finish)
    for copy in copies:
        copy.wait()


def recall(history, step, plane):
    return history[4 * step, plane], [history[4 * step + 1 + axis, plane] for axis in range(3)]


def retreat(opens, words, share, source, target, plane, density, flow):
    mirrored = pull(source, plane, words[plane])
    adjoint = [mirrored[OPP[m]] for m in range(19)]
    open_rate = opens[plane]
    force_flow = [flow[0] + FORCE, flow[1], flow[2]]
    x, y, z = [open_rate * part for part in force_flow]
    plus, minus = pairs(adjoint)
    mx, my, mz = [part * (1.0 / 12.0) for part in first_moments(minus, 2.0)]
    xy_plus, xz_plus, yz_plus = plus[3] + plus[4], plus[5] + plus[6], plus[7] + plus[8]
    axes = [2.0 * plus[k] for k in range(3)]
    whole = 12.0 * adjoint[0] + (axes[0] + axes[1] + axes[2]) + (xy_plus + xz_plus + yz_plus)
    third = whole * (1.0 / 3.0)
    xx = axes[0] + (xy_plus + xz_plus) - third
    yy = axes[1] + (xy_plus + yz_plus) - third
    zz = axes[2] + (xz_plus + yz_plus) - third
    xy, xz, yz = plus[3] - plus[4], plus[5] - plus[6], plus[7] - plus[8]
    hx = 0.25 * (xx * x + xy * y + xz * z)
    hy = 0.25 * (xy * x + yy * y + yz * z)
    hz = 0.25 * (xz * x + yz * y + zz * z)
    rate = 1.2 * open_rate
    slope = [rate * (mx + hx), rate * (my + hy), rate * (mz + hz)]
    pushed = slope[0] * force_flow[0] + slope[1] * force_flow[1] + slope[2] * force_flow[2]
    gained = share[plane] + density * pushed
    if target is None:
        yield
        share[plane] = gained
        return
    level = whole * (1.2 / 36.0) + 1.2 * (
        x * (mx + 0.5 * hx) + y * (my + 0.5 * hy) + z * (mz + 0.5 * hz)
    )
    level = level - (slope[0] * flow[0] + slope[1] * flow[1] + slope[2] * flow[2])
    values = [part - 0.2 * old for part, old in zip(spread(level, slope), adjoint)]
    yield
    share[plane] = gained
    for m in range(19):
        target[OPP[m], plane] = values[m]


def outer_kernel(
    home,
    history,
    opens,
    fluid,
    words,
    even_state,
    odd_state,
    far,
    near,
    from_far,
    from_near,
    summed,
    counted,
    outer,
    share,
    odd,
    even,
    first,
    second,
    second_flow,
):
    del summed, counted
    span = home + 2 * HALO
    up = parity()

    def seed(plane, density, flow):
        damping = 1.0 / opens[plane]
        square = flow[0] * flow[0] + flow[1] * flow[1] + flow[2] * flow[2]
        factor = 2.0 * damping / density
        slope = [part * factor for part in flow]
        values = spread(-square * factor, slope)
        yield
        share[plane] = -square * damping
        for m in range(19):
            even[OPP[m], plane] = values[m]

    sides = ((up, near, from_near), (1 - up, far, from_far))
    edge_words = []
    for ahead, _, message in sides:
        for m in range(19):
            for place in range(HALO):
                first[ahead, m, place] = odd_state[m, ahead * (span - HALO) + place]
            for place in range(2):
                second[ahead, m, 3 - 3 * ahead + place] = even_state[m, 2 + ahead * (span - 6) + place]
            second[ahead, m, 1 + 2 * ahead] = message[10 + m]
        for slot in range(5):
            first[ahead, AHEAD[slot] + ahead, ahead * RAW] = message[slot]
            second[ahead, AHEAD[slot] + ahead, 4 * ahead] = message[5 + slot]
        beyond = (message[29] >= 0.0).astype(jnp.int32)
        within = fluid[1 + ahead * (span - 3)]
        edge_words.append(
            link_word(
                beyond + ahead * (within - beyond),
                fluid[ahead * (span - 1)],
                within + ahead * (beyond - within),
            )
        )

    def second_out(ahead):
        index = 1 + ahead * (span - 3)
        state = pull(first.at[ahead], 1, words[index])
        density, flow = density_velocity(state)
        collided = collide(state, density, flow, opens[index])
        yield
        for place, part in enumerate([density] + flow):
            second_flow[ahead, place] = part
        store(second.at[ahead], 2, collided)

    run([second_out(side[0]) for side in sides])

    def last_step(ahead, raw, message, edge_word, place):
        spot = 1 + place
        index = place + ahead * (span - 3)
        two = second.at[ahead]
        word = words[index]
        if place == 0:
            word = edge_word + ahead * (word - edge_word)
        if place == 2:
            word = word + ahead * (edge_word - word)
        state = pull(two, spot, word)
        density, flow = density_velocity(state)
        seeded = seed(index, density, flow)
        next(seeded)
        here = fluid[index] > 0
        placed = []
        for m in range(19):
            if place == 1:
                initial = raw[m, ahead]
            else:
                initial = jnp.where((ahead > 0) == (place == 2), two[m, spot], raw[m, place // 2])
            placed.append(jnp.where(here, state[m], initial))
        yield
        next(seeded, None)
        store(outer.at[ahead], spot - ahead, placed)

    run(
        [
            last_step(*side, edge_word, place)
            for place in range(HALO)
            for side, edge_word in zip(sides, edge_words)
        ]
    )
    for ahead, _, message in sides:
        for m in range(19):
            outer[ahead, m, ahead * (BX - 1)] = message[30 + m]

    def seed_home(plane):
        return seed(plane, *recall(history, STEPS, plane))

    each_plane(HALO, HALO + home, seed_home, home)

    def ends(side):
        flow = [second_flow[side, 1 + axis] for axis in range(3)]
        return retreat(opens, words, share, even, odd, 1 + side * (span - 3), second_flow[side, 0], flow)

    run([ends(0), ends(1)])

    def step_two(plane):
        return retreat(opens, words, share, even, odd, plane, *recall(history, 2, plane))

    each_plane(HALO - 1, HALO + home + 1, step_two, home + 2)


def gradient_kernel(
    home, history, opens, words, share, odd, marked, summed, gradient, to_near, to_far, total, even
):
    del summed
    up = parity()
    for plane in range(share.shape[0]):
        total[plane] = share[plane]

    def step_one(plane):
        return retreat(opens, words, total, odd, even, plane, *recall(history, 1, plane))

    def step_zero(plane):
        return retreat(opens, words, total, even, None, plane, *recall(history, 0, plane))

    each_plane(HALO - 1, HALO + home + 1, step_one, home + 2)
    each_plane(HALO, HALO + home, step_zero, home)
    for plane in range(home):
        design = marked[plane]
        slope = 3.0 / ((1.6 + 3.4 * design) * (1.0 + 4.0 * design))
        gradient[plane] = jnp.where(design >= 0.0, total[plane + HALO] * slope, 0.0)
    for out, ahead in ((to_near, up), (to_far, 1 - up)):
        for plane in range(BX):
            out[plane] = gradient[ahead * (home - BX) + plane]


def scaled(home, cells, where, drag, joined, out):
    factor = cells / jnp.sum(drag[...])
    reach = (joined.shape[0] - home) // 2
    for plane in range(out.shape[0]):
        spot = jnp.clip(where[0] * BX + reach + plane, 0, joined.shape[0] - 1)
        live = plane < where[1] * BX
        out[plane] = jnp.where(live, joined[spot] * factor, 0.0)


def near_gradient(home, cells, where, drag, gradient, from_far, from_near, out, joined):
    up = parity()
    for ahead, message in ((up, from_near), (1 - up, from_far)):
        joined[pl.ds(ahead * (BX + home), BX)] = message[...]
    joined[pl.ds(BX, home)] = gradient[...]
    scaled(home, cells, where, drag, joined, out)


def far_gradient(home, cells, where, drag, gradient, from_left, from_right, out, joined):
    joined[pl.ds(0, home)] = from_left[...]
    joined[pl.ds(home, home)] = gradient[...]
    joined[pl.ds(2 * home, home)] = from_right[...]
    scaled(home, cells, where, drag, joined, out)


def place_kernel(where, final, outer, later, out, zeros, sems):
    del later
    blocks = out.shape[1] // BX
    home_blocks = final.shape[1] // BX
    beyond = outer.shape[2] // BX
    zeros[...] = jnp.zeros_like(zeros)
    for slot in range(blocks):
        target = out.at[:, pl.ds(slot * BX, BX)]
        live = slot < where[1]
        block = jnp.clip(where[0] + slot, -beyond, home_blocks + beyond - 1)
        inside = (block >= 0) & (block < home_blocks)

        @pl.when(live & inside)
        def _():
            source = final.at[:, pl.ds(block * BX, BX)]
            pltpu.make_async_copy(source, target, sems.at[slot]).start()

        @pl.when(live & jnp.logical_not(inside))
        def _():
            after = (block >= 0).astype(jnp.int32)
            within = block + beyond - after * (home_blocks + beyond)
            source = outer.at[after, :, pl.ds(within * BX, BX)]
            pltpu.make_async_copy(source, target, sems.at[slot]).start()

        @pl.when(jnp.logical_not(live))
        def _():
            pltpu.make_async_copy(zeros, target, sems.at[slot]).start()

    for slot in range(blocks):
        pltpu.make_async_copy(zeros, out.at[:, pl.ds(slot * BX, BX)], sems.at[slot]).wait()


def body(populations, design, fluid_mask, owner_after):
    count = lax.axis_size("block")
    home, width_y, width_z = design.shape
    slots = home // BX + 2
    span = home + 2 * HALO
    plane = (width_y, width_z)
    vmem = pl.BlockSpec(memory_space=pltpu.VMEM)
    hbm = pl.BlockSpec(memory_space=pltpu.HBM)
    anywhere = pl.BlockSpec(memory_space=pl.ANY)
    smem = pl.BlockSpec(memory_space=pltpu.SMEM)
    cells = float(count * home * width_y * width_z)
    near_pairs = [(i, i ^ 1) for i in range(count)]
    far_pairs = [(i, (i + 1 if i % 2 else i - 1) % count) for i in range(count)]
    inner_pairs = far_pairs[1:-1]

    def planes(*lead, dtype=jnp.float32):
        return jax.ShapeDtypeStruct(lead + plane, dtype)

    def scratch(*lead, dtype=jnp.float32):
        return pltpu.VMEM(lead + plane, dtype)

    def call(kernel, name, ins, outs, scratches, limit, moved, *operands):
        return pl.pallas_call(
            kernel,
            out_shape=[shape for shape, _ in outs],
            in_specs=ins,
            out_specs=[spec for _, spec in outs],
            scratch_shapes=scratches,
            compiler_params=pltpu.CompilerParams(vmem_limit_bytes=limit * MIB),
            cost_estimate=pl.CostEstimate(flops=20 * moved, bytes_accessed=moved, transcendentals=0),
            name=name,
        )(*operands)

    own_near, own_far, pops, marked = call(
        functools.partial(edge_kernel, home),
        "edge_planes",
        [hbm] * 3,
        [(planes(23, RAW), vmem)] * 2 + [(planes(19, home), vmem), (planes(home), vmem)],
        [scratch(home), scratch(home, dtype=jnp.int32), pltpu.SemaphoreType.DMA((5,))],
        4,
        1_000_000,
        *[
            pltpu.with_memory_space_constraint(part, pltpu.HBM)
            for part in (populations, design, fluid_mask)
        ],
    )
    near = lax.ppermute(own_near, "block", near_pairs)
    far = lax.ppermute(own_far, "block", far_pairs)

    inner_shapes = (
        planes(49),
        planes(49),
        planes(19, 12),
        planes(16, home),
        planes(19, home),
        planes(home),
        planes(home, dtype=jnp.int32),
        planes(home, dtype=jnp.int32),
        planes(),
    )
    (
        to_near,
        to_far,
        edges,
        inner_history,
        inner_final,
        inner_opens,
        inner_fluid,
        inner_words,
        inner_drag,
        where,
    ) = call(
        functools.partial(interior_kernel, home),
        "interior_steps",
        [hbm] + [vmem] * 2,
        [(shape, vmem) for shape in inner_shapes] + [(jax.ShapeDtypeStruct((3,), jnp.int32), smem)],
        [scratch(19, home)] * 2
        + [pltpu.SMEM(owner_after.shape, jnp.int32), pltpu.SemaphoreType.DMA(())],
        16,
        6_000_000,
        pltpu.with_memory_space_constraint(owner_after, pltpu.HBM),
        pops,
        marked,
    )
    from_near = lax.ppermute(to_near, "block", near_pairs)
    from_far = lax.ppermute(to_far, "block", far_pairs)

    boundary_shapes = (
        planes(19, home),
        planes(16, span),
        planes(span),
        planes(span, dtype=jnp.int32),
        planes(span, dtype=jnp.int32),
        planes(1 + STEPS),
        planes(19, span),
        planes(19, span),
    )
    final, history, opens, fluid, words, drag, even_state, odd_state = call(
        functools.partial(boundary_kernel, home),
        "boundary_steps",
        [vmem] * 3 + [anywhere] + [vmem] * 5,
        [(shape, vmem) for shape in boundary_shapes],
        [pltpu.SemaphoreType.DMA((5,))],
        20,
        8_000_000,
        far,
        near,
        edges,
        inner_history,
        inner_final,
        inner_opens,
        inner_fluid,
        inner_words,
        inner_drag,
    )

    distances = [1 << bit for bit in range(count.bit_length() - 1)]
    sums = [drag]
    for distance in distances[:1] + distances[2:3] + distances[1:2] + distances[3:]:
        swap = [(i, i ^ distance) for i in range(count)]
        sums.append(sums[-1] + lax.ppermute(sums[-1], "block", swap))
    drag = sums[-1]

    is_far = where[2] > 0
    outer, share, odd = call(
        functools.partial(outer_kernel, home),
        "outer_steps",
        [vmem] * 10 + [anywhere] * 2,
        [(planes(2, 19, BX), vmem), (planes(span), vmem), (planes(19, span), vmem)],
        [scratch(19, span), scratch(2, 19, HALO), scratch(2, 19, HALO + 2), scratch(2, 4)],
        20,
        12_000_000,
        history,
        opens,
        fluid,
        words,
        even_state,
        odd_state,
        far,
        near,
        from_far,
        from_near,
        sums[2],
        is_far.astype(jnp.int32).reshape(1),
    )
    gradient, to_near, to_far = call(
        functools.partial(gradient_kernel, home),
        "gradient_steps",
        [vmem] * 6 + [anywhere],
        [(planes(home), vmem), (planes(BX), vmem), (planes(BX), vmem)],
        [scratch(span), scratch(19, span)],
        20,
        6_000_000,
        history,
        opens,
        words,
        share,
        odd,
        marked,
        sums[3],
    )
    from_near = lax.ppermute(to_near, "block", near_pairs)
    from_far = lax.ppermute(to_far, "block", inner_pairs)

    ring = [(i, i + 1) for i in range(count - 1)]
    back = [(i + 1, i) for i in range(count - 1)]

    def place(outer):
        (out,) = call(
            place_kernel,
            "place_populations",
            [smem, anywhere, anywhere, vmem],
            [(planes(19, slots * BX), anywhere)],
            [scratch(19, BX), pltpu.SemaphoreType.DMA((slots,))],
            8,
            4_000_000,
            where,
            final,
            outer,
            gradient,
        )
        return out

    def place_far(_):
        wide = [lax.ppermute(final, "block", route) for route in (ring, back)]
        return place(jnp.stack(wide))

    def slope(kernel, name, reach, *messages):
        (out,) = call(
            functools.partial(kernel, home, cells),
            name,
            [smem] + [vmem] * 4,
            [(planes(slots * BX), vmem)],
            [scratch(home + 2 * reach)],
            4,
            1_000_000,
            where,
            drag,
            gradient,
            *messages,
        )
        return out

    def slope_near(*messages):
        return slope(near_gradient, "near_gradient", BX, *messages)

    def slope_far(*_):
        wide = [lax.ppermute(gradient, "block", route) for route in (ring, back)]
        return slope(far_gradient, "far_gradient", home, *wide)

    populations_after = lax.cond(is_far, place_far, place, outer)
    sensitivity = lax.cond(is_far, slope_far, slope_near, from_far, from_near)
    return (populations_after, sensitivity)


def solution(mesh):
    placed = (
        P(None, ("group", "block"), None, None),
        P(("group", "block"), None, None),
        P(("group", "block"), None, None),
        P("group"),
    )
    return jax.shard_map(
        body,
        mesh=mesh,
        in_specs=placed,
        out_specs=(P(None, ("group", "block"), None, None), P(("group", "block"), None, None)),
        check_vma=False,
    )
```
